32 devices in a mesh: row: 4 (over y, core), col: 8 (over z, x).
Axes of the slice: x: 2, y: 2, z: 4, core: 2. Of those that a mesh axis runs over, the one named last changes fastest.
Arguments:
- latents: bfloat16 [16384, 1152], P(('row', 'col')), may hold values from -6 to 6
- condition: bfloat16 [16, 1152], P('row'), may hold values from -6 to 6
- ada_weight: bfloat16 [1152, 6, 1152], P('row', None, 'col'), may hold values from -0.1875 to 0.1875
- ada_bias: bfloat16 [6, 1152], P(None, 'col'), may hold values from -3 to 3
- qkv_weight: bfloat16 [1152, 3, 1152], P('row', None, 'col'), may hold values from -0.1875 to 0.1875
- qv_bias: bfloat16 [2, 1152], P(None, 'col'), may hold values from -3 to 3
- proj_weight: bfloat16 [1152, 1152], P('col', 'row'), may hold values from -0.75 to 0.75
- proj_bias: bfloat16 [1152], P('col'), may hold values from -2 to 2
- fc1_weight: bfloat16 [1152, 4608], P('row', 'col'), may hold values from -0.1875 to 0.1875
- fc1_bias: bfloat16 [4608], P('col'), may hold values from -3 to 3
- fc2_weight: bfloat16 [4608, 1152], P('col', 'row'), may hold values from -0.125 to 0.125
- fc2_bias: bfloat16 [1152], P('col'), may hold values from -2 to 2
- cotangent: bfloat16 [16384, 1152], P(('row', 'col')), may hold values from -6 to 6
Outputs:
- output: bfloat16 [16384, 1152], P(('row', 'col'))
- latents_grad: float32 [16384, 1152], P(('row', 'col'))
- condition_grad: float32 [16, 1152], P('row')
- ada_weight_grad: float32 [1152, 6, 1152], P('row', None, 'col')
- ada_bias_grad: float32 [6, 1152], P(None, 'col')
- qkv_weight_grad: float32 [1152, 3, 1152], P('row', None, 'col')
- qv_bias_grad: float32 [2, 1152], P(None, 'col')
- proj_weight_grad: float32 [1152, 1152], P('col', 'row')
- proj_bias_grad: float32 [1152], P('col')
- fc1_weight_grad: float32 [1152, 4608], P('row', 'col')
- fc1_bias_grad: float32 [4608], P('col')
- fc2_weight_grad: float32 [4608, 1152], P('col', 'row')
- fc2_bias_grad: float32 [1152], P('col')
The draws below stay inside these ranges and needn't reach their ends.
All inputs are finite; a program needn't handle non-finite values.
Results may differ from the reference program's by a relative error of at most 0.02.
Values may be sent and summed in bfloat16 or wider, within the bound.
A program may use at most 256 MiB of HBM per device.

```python
import math
import jax
import jax.numpy as jnp
from jax import lax

D = 1152
HEADS = 16
HEAD_DIM = 72
FF = 4608
SEQ = 1024
LATENTS = 16
TOKENS = 16384


def block_scale(key, shape, cuts, smallest, largest):
    loudness, own = 1.0, jax.random.fold_in(key, 6)
    for axis_at, parts in cuts:
        heights = jnp.exp(jax.random.uniform(jax.random.fold_in(own, axis_at), (parts,), jnp.float32, smallest / len(cuts), largest / len(cuts)))
        loudness = loudness * jnp.repeat(heights, shape[axis_at] // parts).reshape([-1 if axis == axis_at else 1 for axis in range(len(shape))])
    return loudness


def noise(key, shape, width, limit, split=(), dtype=jnp.bfloat16):
    gain = block_scale(key, shape, split, -0.22, 0.18) if split else 1.0
    array = jax.random.normal(key, shape, jnp.float32) * width * gain
    return jnp.minimum(jnp.maximum(array, -limit), limit).astype(dtype)


def setup_inputs(seed: int = 0) -> dict:
    keys = jax.random.split(jax.random.key(seed), 14)
    latents = noise(keys[0], (TOKENS, D), 1.0, 6.0, ((0, 32),))
    condition = noise(keys[1], (LATENTS, D), 1.0, 6.0, ((0, 4),))
    ada_weight = noise(keys[2], (D, 6, D), D ** -0.5, 0.1875, ((0, 4), (2, 8)))
    ada_bias = noise(keys[3], (6, D), 0.5, 3.0, ((1, 8),))
    qkv_weight = noise(keys[4], (D, 3, D), D ** -0.5, 0.1875, ((0, 4), (2, 8)))
    qv_bias = noise(keys[5], (2, D), 0.5, 3.0, ((1, 8),))
    proj_weight = noise(keys[6], (D, D), (D // 16) ** -0.5, 0.75, ((0, 8), (1, 4)))
    proj_bias = noise(keys[7], (D,), 0.3, 2.0, ((0, 8),))
    fc1_weight = noise(keys[8], (D, FF), D ** -0.5, 0.1875, ((0, 4), (1, 8)))
    fc1_bias = noise(keys[9], (FF,), 0.5, 3.0, ((0, 8),))
    fc2_weight = noise(keys[10], (FF, D), (FF // 2) ** -0.5, 0.125, ((0, 8), (1, 4)))
    fc2_bias = noise(keys[11], (D,), 0.3, 2.0, ((0, 8),))
    cotangent = noise(keys[12], (TOKENS, D), 1.0, 6.0, ((0, 32),))
    return dict(latents=latents, condition=condition, ada_weight=ada_weight, ada_bias=ada_bias, qkv_weight=qkv_weight, qv_bias=qv_bias, proj_weight=proj_weight, proj_bias=proj_bias, fc1_weight=fc1_weight, fc1_bias=fc1_bias, fc2_weight=fc2_weight, fc2_bias=fc2_bias, cotangent=cotangent)


norm_eps = 1e-06
highest = lax.Precision.HIGHEST

@jax.custom_vjp
def low(v):
    return lax.optimization_barrier(v.astype(jnp.bfloat16)).astype(jnp.float32)

@jax.custom_vjp
def low_back(v):
    return v

def low_keep(v):
    return (low(v), None)

def low_pass(kept, grad):
    return (grad,)

def back_keep(v):
    return (v, None)

def back_low(kept, grad):
    return (low(grad),)
low.defvjp(low_keep, low_pass)
low_back.defvjp(back_keep, back_low)

def modulate(values, shift, scale):
    mean = lax.optimization_barrier(jnp.mean(values, axis=-1, keepdims=True))
    centred = values - mean
    variance = lax.optimization_barrier(jnp.mean(centred * centred, axis=-1, keepdims=True))
    normal = centred * lax.rsqrt(variance + norm_eps)
    return low(normal * (1.0 + scale[:, None, :]) + shift[:, None, :])

def attend_one(triple):
    query, key_vec, value = triple
    scores = low_back(jnp.einsum('qhe,khe->hqk', query, key_vec, precision=highest)) * HEAD_DIM ** (-0.5)
    probs = low(jax.nn.softmax(scores, axis=-1))
    return low(low_back(jnp.einsum('hqk,khe->qhe', probs, value, precision=highest)))

def layer_forward(tokens, cond, ada_w, ada_b, qkv_w, qv_b, proj_w, proj_b, fc1_w, fc1_b, fc2_w, fc2_b):
    groups = cond.shape[0]
    cond_act = low(jax.nn.silu(cond))
    modulation = low_back(jnp.einsum('bd,dkc->bkc', cond_act, ada_w, precision=highest)) + ada_b
    values = tokens.reshape(groups, SEQ, D)
    normed1 = modulate(values, modulation[:, 0], modulation[:, 1])
    projected = jnp.einsum('bsd,dkc->bskc', normed1, qkv_w, precision=highest)
    query = low(low_back(projected[:, :, 0]) + qv_b[0])
    key_vec = low(low_back(projected[:, :, 1]))
    value = low(low_back(projected[:, :, 2]) + qv_b[1])
    shaped = (query.reshape(groups, SEQ, HEADS, HEAD_DIM), key_vec.reshape(groups, SEQ, HEADS, HEAD_DIM), value.reshape(groups, SEQ, HEADS, HEAD_DIM))
    attended = lax.map(jax.checkpoint(attend_one), shaped).reshape(groups, SEQ, D)
    branch_a = low_back(jnp.einsum('bsd,de->bse', attended, proj_w, precision=highest)) + proj_b
    middle = values + modulation[:, 2][:, None, :] * branch_a
    normed2 = modulate(middle, modulation[:, 3], modulation[:, 4])
    pre_act = low_back(jnp.einsum('bsd,df->bsf', normed2, fc1_w, precision=highest)) + fc1_b
    hidden = low(jax.nn.gelu(pre_act, approximate=True))
    branch_m = low_back(jnp.einsum('bsf,fd->bsd', hidden, fc2_w, precision=highest)) + fc2_b
    return (middle + modulation[:, 5][:, None, :] * branch_m).reshape(groups * SEQ, D)

def reference(latents, condition, ada_weight, ada_bias, qkv_weight, qv_bias, proj_weight, proj_bias, fc1_weight, fc1_bias, fc2_weight, fc2_bias, cotangent):
    weights = tuple((w.astype(jnp.float32) for w in (ada_weight, ada_bias, qkv_weight, qv_bias, proj_weight, proj_bias, fc1_weight, fc1_bias, fc2_weight, fc2_bias)))
    group = math.gcd(LATENTS, 4)
    count = LATENTS // group
    tok_groups = latents.astype(jnp.float32).reshape(count, group * SEQ, D)
    cond_groups = condition.astype(jnp.float32).reshape(count, group, D)
    grad_groups = cotangent.astype(jnp.float32).reshape(count, group * SEQ, D)

    def one_group(totals, item):
        tokens, cond, grad_out = item
        result, pull = jax.vjp(layer_forward, tokens, cond, *weights)
        grads = pull(grad_out)
        totals = tuple((a + b for a, b in zip(totals, grads[2:])))
        return (totals, (result.astype(jnp.bfloat16), grads[0], grads[1]))
    start = tuple((jnp.zeros_like(w) for w in weights))
    totals, (outputs, token_grads, cond_grads) = lax.scan(one_group, start, (tok_groups, cond_groups, grad_groups))
    return (outputs.reshape(TOKENS, D), token_grads.reshape(TOKENS, D), cond_grads.reshape(LATENTS, D), totals[0], totals[1], totals[2], totals[3], totals[4], totals[5], totals[6], totals[7], totals[8], totals[9])
```

```python
import functools
import math
import jax
import jax.numpy as jnp
from jax import lax
from jax.experimental import pallas as pl
from jax.experimental.pallas import tpu as pltpu
from jax.sharding import PartitionSpec as P

HEAD_DIM = 72
SEQ = 1024
norm_eps = 1e-06
bf16, f32 = jnp.bfloat16, jnp.float32

MESH = pl.DeviceIdType.MESH
ANY = pl.BlockSpec(memory_space=pl.ANY)


class Place:
    def __init__(self):
        row, col = lax.axis_index("row"), lax.axis_index("col")
        self.row, self.col = row, col
        self.depth = lax.axis_size("col") // 2
        self.y, self.h = row // 2, row % 2
        self.z, self.x = col // 2, col % 2
        self.p = jnp.where(self.h == 0, self.y, self.x)
        self.q = jnp.where(self.h == 0, self.x, self.y)
        flip_x, flip_y = (row, col + 1 - 2 * self.x), (row + 2 - 4 * self.y, col)
        self.to_q = tuple(jnp.where(self.h == 0, a, b) for a, b in zip(flip_x, flip_y))
        self.to_p = tuple(jnp.where(self.h == 0, b, a) for a, b in zip(flip_x, flip_y))
        self.to_core = (row + 1 - 2 * self.h, col)

    def to_z(self, z):
        return (self.row, 2 * z + self.x)

    def yx(self, p, q):
        return jnp.where(self.h == 0, p, q), jnp.where(self.h == 0, q, p)

    def partners(self):
        near = [self.to_q, self.to_p, self.to_core]
        return near + [self.to_z((self.z + k) % self.depth) for k in range(1, self.depth)]


def greet(partners):
    barrier = pltpu.get_barrier_semaphore()
    for partner in partners:
        pl.semaphore_signal(barrier, inc=1, device_id=partner, device_id_type=MESH)
    pl.semaphore_wait(barrier, len(partners))


def block_at(ref, rows, lanes, r, c):
    return ref.at[pl.ds(pl.multiple_of(r * rows, 16), rows), pl.ds(pl.multiple_of(c * lanes, 128), lanes)]


class Gather:
    sems = (1, 2, 2, 4, 8)

    def __init__(self, place, ins, outs, sems):
        self.at, self.ins, self.outs = place, ins, outs
        self.local, self.zs, self.qs, self.ps, self.ks = sems

    @staticmethod
    def scratch(count, depth):
        dma = pltpu.SemaphoreType.DMA
        return [dma((count,)), dma((count, 2, depth)), dma((count, 2, depth)), dma((count, 2, depth, 2)), dma((count, 2, depth, 4))]

    def block(self, a, p, q, z, h=None):
        y, x = self.at.yx(p, q)
        rows, lanes = self.ins[a].shape
        h = self.at.h if h is None else h
        return block_at(self.outs[a], rows, lanes, 2 * y + h, 2 * z + x)

    def zc(self, t):
        return (self.at.z + self.at.depth - t) % self.at.depth

    def copy(self, src, dst, sems, index, to):
        return pltpu.make_async_remote_copy(
            src_ref=src, dst_ref=dst, send_sem=sems.at[(index[0], 0) + index[1:]], recv_sem=sems.at[(index[0], 1) + index[1:]],
            device_id=to, device_id_type=MESH)

    def own(self, a):
        return self.block(a, self.at.p, self.at.q, self.at.z)

    def c_local(self, a):
        return pltpu.make_async_copy(self.ins[a], self.own(a), self.local.at[a])

    def c_z(self, a, k):
        place = self.at
        return pltpu.make_async_remote_copy(
            src_ref=self.ins[a], dst_ref=self.own(a), send_sem=self.zs.at[a, 0, k], recv_sem=self.zs.at[a, 1, place.z],
            device_id=place.to_z((place.z + k) % place.depth), device_id_type=MESH)

    def r_z(self, a, t):
        place = self.at
        here = self.block(a, place.p, place.q, self.zc(t))
        return pltpu.make_async_remote_copy(
            src_ref=self.ins[a], dst_ref=here, send_sem=self.zs.at[a, 0, 0], recv_sem=self.zs.at[a, 1, self.zc(t)],
            device_id=place.to_z(place.z), device_id_type=MESH)

    def c_q(self, a, t):
        place = self.at
        spot = self.block(a, place.p, place.q, self.zc(t))
        return self.copy(self.ins[a] if t == 0 else spot, spot, self.qs, (a, self.zc(t)), place.to_q)

    def c_p(self, a, t, j):
        place = self.at
        spot = self.block(a, place.p, place.q if j == 0 else 1 - place.q, self.zc(t))
        return self.copy(self.ins[a] if t == 0 and j == 0 else spot, spot, self.ps, (a, self.zc(t), j), place.to_p)

    def c_k(self, a, t, j):
        place = self.at
        spot = self.block(a, place.p if j < 2 else 1 - place.p, place.q if j % 2 == 0 else 1 - place.q, self.zc(t))
        return self.copy(self.ins[a] if t == 0 and j == 0 else spot, spot, self.ks, (a, self.zc(t), j), place.to_core)

    def start(self, a):
        for k in range(1, self.at.depth):
            self.c_z(a, k).start()
        self.c_local(a).start()

    def stage(self, a, t, n):
        if n == 0:
            if t > 0:
                self.r_z(a, t).wait_recv()
            self.c_q(a, t).start()
            self.c_p(a, t, 0).start()
            self.c_k(a, t, 0).start()
        elif n == 1:
            self.c_q(a, t).wait_recv()
            self.c_p(a, t, 1).start()
            self.c_k(a, t, 1).start()
        elif n == 2:
            self.c_p(a, t, 0).wait_recv()
            self.c_k(a, t, 2).start()
        elif n == 3:
            self.c_p(a, t, 1).wait_recv()
            self.c_k(a, t, 3).start()
        else:
            for j in range(4):
                self.c_k(a, t, j).wait_recv()

    def finish(self, a):
        for k in range(1, self.at.depth):
            self.c_z(a, k).wait_send()
        self.c_local(a).wait()
        for t in range(self.at.depth):
            self.c_q(a, t).wait_send()
            for j in range(2):
                self.c_p(a, t, j).wait_send()
            for j in range(4):
                self.c_k(a, t, j).wait_send()


def gather_kernel(groups, *refs):
    count = sum(groups)
    ins, outs, sems = refs[:count], refs[count:2 * count], refs[2 * count:]
    place = Place()
    greet(place.partners())
    work = Gather(place, ins, outs, sems)
    for a in range(count):
        work.start(a)
    chunks, first = [], 0
    for size in groups:
        for t in range(place.depth):
            chunks.append([(a, t) for a in range(first, first + size)])
        first += size
    for s in range(len(chunks) + 4):
        for n in range(5):
            if 0 <= s - n < len(chunks):
                for a, t in chunks[s - n]:
                    work.stage(a, t, n)
    for a in range(count):
        work.finish(a)


def gather_all(blocks, groups, collective_id):
    rows, cols = lax.axis_size("row"), lax.axis_size("col")
    return pl.pallas_call(
        functools.partial(gather_kernel, groups),
        out_shape=[jax.ShapeDtypeStruct((rows * b.shape[0], cols * b.shape[1]), b.dtype) for b in blocks],
        in_specs=[ANY] * len(blocks),
        out_specs=[ANY] * len(blocks),
        scratch_shapes=Gather.scratch(len(blocks), cols // 2),
        compiler_params=pltpu.CompilerParams(collective_id=collective_id, has_side_effects=True),
        name="gather_weights",
    )(*blocks)


class Scatter:
    def __init__(self, place, ins, outs, bufs, sems):
        self.at, self.ins, self.outs = place, ins, outs
        self.r0, self.own, self.r1, self.r2, self.r3 = bufs
        self.s0, self.ld, self.s1, self.s2, self.s3 = sems

    @staticmethod
    def scratch(shapes, depth):
        dma, count = pltpu.SemaphoreType.DMA, len(shapes)
        bufs = []
        for lead in ((depth, 2, 2), (2, 2, 2), (depth, 2), (depth,), (depth - 1,)):
            bufs += [pltpu.VMEM(lead + s, jnp.bfloat16) for s in shapes]
        return bufs + [dma((count, 2, depth, 4)), dma((count, 2, 4)), dma((count, 2, depth, 2)), dma((count, 2, depth)), dma((count, 2, depth))]

    @staticmethod
    def split(refs, count):
        return [refs[i * count:(i + 1) * count] for i in range(5)], refs[5 * count:]

    def zc(self, t):
        return lax.rem(self.at.z + 1 + t, self.at.depth)

    def block(self, a, p, q, z, h):
        y, x = jnp.where(h == 0, p, q), jnp.where(h == 0, q, p)
        rows, lanes = self.outs[a].shape
        return block_at(self.ins[a], rows, lanes, 2 * y + h, 2 * z + x)

    def c0(self, a, t, j):
        place = self.at
        return pltpu.make_async_remote_copy(
            src_ref=self.block(a, j // 2, j % 2, self.zc(t), 1 - place.h), dst_ref=self.r0[a].at[t, j // 2, j % 2],
            send_sem=self.s0.at[a, 0, t, j], recv_sem=self.s0.at[a, 1, t, j], device_id=place.to_core, device_id_type=MESH)

    def load(self, a, t, j):
        return pltpu.make_async_copy(
            self.block(a, j // 2, j % 2, self.zc(t), self.at.h), self.own[a].at[t % 2, j // 2, j % 2], self.ld.at[a, t % 2, j])

    def c1(self, a, t, j):
        place = self.at
        return pltpu.make_async_remote_copy(
            src_ref=self.r0[a].at[t, 1 - place.p, j], dst_ref=self.r1[a].at[t, j],
            send_sem=self.s1.at[a, 0, t, j], recv_sem=self.s1.at[a, 1, t, j], device_id=place.to_p, device_id_type=MESH)

    def c2(self, a, t):
        place = self.at
        return pltpu.make_async_remote_copy(
            src_ref=self.r0[a].at[t, place.p, 1 - place.q], dst_ref=self.r2[a].at[t],
            send_sem=self.s2.at[a, 0, t], recv_sem=self.s2.at[a, 1, t], device_id=place.to_q, device_id_type=MESH)

    def c3(self, a, t):
        place = self.at
        return pltpu.make_async_remote_copy(
            src_ref=self.r0[a].at[t, place.p, place.q], dst_ref=self.r3[a].at[t],
            send_sem=self.s3.at[a, 0, t], recv_sem=self.s3.at[a, 1, t], device_id=place.to_z(self.zc(t)), device_id_type=MESH)

    def add(self, a, into, other):
        rows = self.outs[a].shape[0]
        step = 48 if rows % 48 == 0 else 16

        @pl.loop(0, rows // step)
        def _(i):
            part = pl.ds(pl.multiple_of(i * step, 16), step)
            into[part, :] = into[part, :] + other[part, :]

    def stage(self, a, t, n):
        place = self.at
        last = t == place.depth - 1
        if n == 0:
            for j in range(4):
                self.c0(a, t, j).start()
                self.load(a, t, j).start()
        elif n == 1:
            for j in range(4):
                self.c0(a, t, j).wait_recv()
                self.load(a, t, j).wait()
            for j in range(2):
                self.add(a, self.r0[a].at[t, 1 - place.p, j], self.own[a].at[t % 2, 1 - place.p, j])
                self.c1(a, t, j).start()
            for j in range(2):
                self.add(a, self.r0[a].at[t, place.p, j], self.own[a].at[t % 2, place.p, j])
        elif n == 2:
            for j in range(2):
                self.c1(a, t, j).wait_recv()
            self.add(a, self.r0[a].at[t, place.p, 1 - place.q], self.r1[a].at[t, 1 - place.q])
            self.c2(a, t).start()
            self.add(a, self.r0[a].at[t, place.p, place.q], self.r1[a].at[t, place.q])
        elif n == 3:
            self.c2(a, t).wait_recv()
            self.add(a, self.r0[a].at[t, place.p, place.q], self.r2[a].at[t])
            if not last:
                self.c3(a, t).start()
        elif last:
            self.total(a)

    def total(self, a):
        place, depth = self.at, self.at.depth
        for t in range(depth - 1):
            self.c3(a, t).wait_recv()
        rows = self.outs[a].shape[0]
        step = 48 if rows % 48 == 0 else 16
        mine, others, out = self.r0[a].at[depth - 1, place.p, place.q], self.r3[a], self.outs[a]

        @pl.loop(0, rows // step)
        def _(i):
            part = pl.ds(pl.multiple_of(i * step, 16), step)
            value = mine[part, :].astype(jnp.float32)
            for t in range(depth - 1):
                value = value + others[t, part, :].astype(jnp.float32)
            out[part, :] = value

    def finish(self, a):
        for t in range(self.at.depth):
            for j in range(4):
                self.c0(a, t, j).wait_send()
            for j in range(2):
                self.c1(a, t, j).wait_send()
            self.c2(a, t).wait_send()
            if t < self.at.depth - 1:
                self.c3(a, t).wait_send()


def chunk_list(groups, depth):
    chunks, first = [], 0
    for size in groups:
        for t in range(depth):
            chunks.append([(a, t) for a in range(first, first + size)])
        first += size
    return chunks


def scatter_kernel(groups, *refs):
    count = sum(groups)
    ins, outs = refs[:count], refs[count:2 * count]
    bufs, sems = Scatter.split(refs[2 * count:], count)
    place = Place()
    greet(place.partners())
    work = Scatter(place, ins, outs, bufs, sems)
    chunks = chunk_list(groups, place.depth)
    for s in range(len(chunks) + 4):
        for n in range(5):
            if 0 <= s - n < len(chunks):
                for a, t in chunks[s - n]:
                    work.stage(a, t, n)
    for a in range(count):
        work.finish(a)


def scatter_all(fulls, groups, collective_id):
    rows, cols = lax.axis_size("row"), lax.axis_size("col")
    shapes = [(g.shape[0] // rows, g.shape[1] // cols) for g in fulls]
    return pl.pallas_call(
        functools.partial(scatter_kernel, groups),
        out_shape=[jax.ShapeDtypeStruct(s, jnp.float32) for s in shapes],
        in_specs=[ANY] * len(fulls),
        out_specs=[pl.BlockSpec(memory_space=pltpu.VMEM)] * len(fulls),
        scratch_shapes=Scatter.scratch(shapes, cols // 2),
        compiler_params=pltpu.CompilerParams(collective_id=collective_id, has_side_effects=True, vmem_limit_bytes=58 * 2**20),
        name="scatter_grads",
    )(*fulls)


def nt(a, b):
    return lax.dot_general(a, b, (((1,), (1,)), ((), ())), preferred_element_type=f32)


def nn(a, b):
    return lax.dot_general(a, b, (((1,), (0,)), ((), ())), preferred_element_type=f32)


def tn(a, b):
    return lax.dot_general(a, b, (((0,), (0,)), ((), ())), preferred_element_type=f32)


SOFT = HEAD_DIM ** (-0.5) * math.log2(math.e)


def attend_kernel(q_ref, k_ref, v_ref, att_ref, lse_ref, k2_ref, v2_ref, sems):
    place = Place()
    greet([place.to_core])
    heads, rows, width = q_ref.shape

    def swap(i, h):
        src, dst = ((k_ref, k2_ref), (v_ref, v2_ref))[i]
        return pltpu.make_async_remote_copy(
            src_ref=src.at[h], dst_ref=dst.at[h], send_sem=sems.at[0, i, h], recv_sem=sems.at[1, i, h],
            device_id=place.to_core, device_id_type=MESH)

    for h in range(heads):
        swap(0, h).start()
        swap(1, h).start()

    @pl.loop(0, heads)
    def _(h):
        swap(0, h).wait_recv()
        swap(1, h).wait_recv()
        q = q_ref[h]
        one = nt(k_ref[h], q)
        two = nt(k2_ref[h], q)
        top = jnp.maximum(jnp.max(one, axis=0, keepdims=True), jnp.max(two, axis=0, keepdims=True)) * SOFT
        one = jnp.exp2(one * SOFT - top)
        two = jnp.exp2(two * SOFT - top)
        total = jnp.sum(one, axis=0, keepdims=True) + jnp.sum(two, axis=0, keepdims=True)
        result = tn(v_ref[h], one.astype(bf16)) + tn(v2_ref[h], two.astype(bf16))
        att_ref[h] = (result / total).T.astype(bf16)
        lse_ref[h] = top + jnp.log2(total)

    for h in range(heads):
        swap(0, h).wait_send()
        swap(1, h).wait_send()


def attend(q, k, v, collective_id):
    heads, rows, width = q.shape
    vmem = pl.BlockSpec(memory_space=pltpu.VMEM)
    return pl.pallas_call(
        attend_kernel,
        out_shape=[jax.ShapeDtypeStruct(q.shape, bf16), jax.ShapeDtypeStruct((heads, 1, rows), f32)]
        + [jax.ShapeDtypeStruct(q.shape, bf16)] * 2,
        in_specs=[vmem] * 3,
        out_specs=[vmem] * 4,
        scratch_shapes=[pltpu.SemaphoreType.DMA((2, 2, heads))],
        compiler_params=pltpu.CompilerParams(collective_id=collective_id, has_side_effects=True, vmem_limit_bytes=50 * 2**20),
        name="attend",
    )(q, k, v)


def attend_back_kernel(q_ref, k_ref, v_ref, k2_ref, v2_ref, lse_ref, o_ref, do_ref, dq_ref, dk_ref, dv_ref, send, recv, sems):
    place = Place()
    greet([place.to_core])
    heads = q_ref.shape[0]

    def swap(i, h):
        return pltpu.make_async_remote_copy(
            src_ref=send.at[i, h], dst_ref=recv.at[i, h], send_sem=sems.at[0, i, h], recv_sem=sems.at[1, i, h],
            device_id=place.to_core, device_id_type=MESH)

    @pl.loop(0, heads)
    def _(h):
        q, out_grad, lse = q_ref[h], do_ref[h], lse_ref[h]
        delta = jnp.sum(out_grad.astype(f32).T * o_ref[h].astype(f32).T, axis=0, keepdims=True)

        def half(k, v):
            probs = jnp.exp2(nt(k, q) * SOFT - lse)
            grad = (probs * (nt(v, out_grad) - delta)).astype(bf16)
            return nn(grad, q) * HEAD_DIM ** (-0.5), nn(probs.astype(bf16), out_grad), tn(k, grad)

        dk, dv, dq_two = half(k2_ref[h], v2_ref[h])
        send[0, h] = dk.astype(bf16)
        send[1, h] = dv.astype(bf16)
        swap(0, h).start()
        swap(1, h).start()
        dk, dv, dq_one = half(k_ref[h], v_ref[h])
        dk_ref[h] = dk
        dv_ref[h] = dv
        dq_ref[h] = ((dq_one + dq_two) * HEAD_DIM ** (-0.5)).T

    @pl.loop(0, heads)
    def _(h):
        swap(0, h).wait_recv()
        swap(1, h).wait_recv()
        dk_ref[h] = dk_ref[h] + recv[0, h].astype(f32)
        dv_ref[h] = dv_ref[h] + recv[1, h].astype(f32)

    for h in range(heads):
        swap(0, h).wait_send()
        swap(1, h).wait_send()


def attend_back(q, k, v, k2, v2, lse, att, att_grad, collective_id):
    heads, rows, width = q.shape
    vmem = pl.BlockSpec(memory_space=pltpu.VMEM)
    return pl.pallas_call(
        attend_back_kernel,
        out_shape=[jax.ShapeDtypeStruct(q.shape, f32)] * 3,
        in_specs=[vmem] * 8,
        out_specs=[vmem] * 3,
        scratch_shapes=[pltpu.VMEM((2,) + q.shape, bf16), pltpu.VMEM((2,) + q.shape, bf16), pltpu.SemaphoreType.DMA((2, 2, heads))],
        compiler_params=pltpu.CompilerParams(collective_id=collective_id, has_side_effects=True, vmem_limit_bytes=58 * 2**20),
        name="attend_back",
    )(q, k, v, k2, v2, lse, att, att_grad)


class Plan:
    def __init__(self, latents, condition, qkv_weight, fc1_weight):
        self.rows, self.cols = lax.axis_size("row"), lax.axis_size("col")
        self.tokens, self.width = latents.shape
        self.lats = condition.shape[0]
        self.depth_rows = qkv_weight.shape[0]
        self.head_cols = qkv_weight.shape[2]
        self.ff_cols = fc1_weight.shape[1]
        self.share = SEQ // self.tokens
        q_left, p_left, f_left = (3 * self.head_cols) % 128, self.head_cols % 128, self.ff_cols % 128
        self.near = (
            self.rows == 4 and self.share == 2 and self.cols % 2 == 0 and self.lats == self.cols // 2
            and self.depth_rows % 32 == 0 and self.tokens % 128 == 0 and q_left + p_left == 64 and f_left == 64)
        self.q_left, self.p_left, self.f_left = (q_left, p_left, f_left) if self.near else (0, 0, 0)
        self.q_main, self.p_main = 3 * self.head_cols - self.q_left, self.head_cols - self.p_left
        self.f_main = self.ff_cols - self.f_left

    def fold(self, left):
        rows, lanes = left.shape
        return left.reshape(2, rows // 2, lanes).transpose(1, 0, 2).reshape(rows // 2, 2 * lanes)

    def unfold(self, left):
        rows, lanes = left.shape
        return left.reshape(rows, 2, lanes // 2).transpose(1, 0, 2).reshape(2 * rows, lanes // 2)

    def fold_full(self, left):
        half = self.depth_rows // 2
        return left.reshape(self.rows, 2, half, self.cols, 64).transpose(0, 2, 3, 1, 4).reshape(self.rows * half, self.cols * 128)

    def unfold_full(self, left):
        half = self.depth_rows // 2
        return left.reshape(self.rows, half, self.cols, 2, 64).transpose(0, 3, 1, 2, 4).reshape(self.width, self.cols * 64)

    def swap_pairs(self):
        pairs = []
        for row in range(self.rows):
            for col in range(self.cols):
                there = (row - row % 2 + col % 2) * self.cols + col - col % 2 + row % 2
                pairs.append((row * self.cols + col, there))
        return pairs

    def swap(self, value):
        return lax.ppermute(value, ("row", "col"), self.swap_pairs()) if self.near else value


def gather_plain(blocks):
    return [lax.all_gather(lax.all_gather(b, "row", axis=0, tiled=True), "col", axis=1, tiled=True) for b in blocks]


def scatter_plain(fulls):
    parts = [lax.psum_scatter(g, "row", scatter_dimension=0, tiled=True) for g in fulls]
    return [lax.psum_scatter(g, "col", scatter_dimension=1, tiled=True).astype(f32) for g in parts]


def attend_plain(q, k, v):
    def one(item):
        scores = nt(item[0], item[1]) * HEAD_DIM ** (-0.5)
        top = jnp.max(scores, axis=-1, keepdims=True)
        probs = jnp.exp(scores - top)
        total = jnp.sum(probs, axis=-1, keepdims=True)
        return nn((probs / total).astype(bf16), item[2]).astype(bf16), top + jnp.log(total)

    return lax.map(one, (q, k, v))


def attend_back_plain(q, k, v, lse, att_grad):
    def one(item):
        q, k, v, lse, out_grad = item
        probs = jnp.exp(nt(q, k) * HEAD_DIM ** (-0.5) - lse)
        probs_grad = nt(out_grad, v)
        inner = jnp.sum(probs * probs_grad, axis=-1, keepdims=True)
        grad = (probs * (probs_grad - inner) * HEAD_DIM ** (-0.5)).astype(bf16)
        return nn(grad, k), tn(grad, q), tn(probs.astype(bf16), out_grad)

    return lax.map(one, (q, k, v, lse, att_grad))


def gelu_and_slope(u):
    c = math.sqrt(2.0 / math.pi)
    inner = jnp.tanh(c * (u + 0.044715 * u * u * u))
    value = 0.5 * u * (1.0 + inner)
    slope = 0.5 * (1.0 + inner) + 0.5 * u * (1.0 - inner * inner) * c * (1.0 + 3 * 0.044715 * u * u)
    return value, slope


def layer_norm(values):
    mean = jnp.mean(values, axis=-1, keepdims=True)
    centred = values - mean
    inverse = lax.rsqrt(jnp.mean(centred * centred, axis=-1, keepdims=True) + norm_eps)
    return centred * inverse, inverse


def norm_back(rows_grad, normal, inverse, scale):
    normal_grad = rows_grad * (1.0 + scale)
    first = jnp.mean(normal_grad, axis=-1, keepdims=True)
    second = jnp.mean(normal_grad * normal, axis=-1, keepdims=True)
    value_grad = inverse * (normal_grad - first - normal * second)
    return value_grad, jnp.sum(rows_grad, axis=0), jnp.sum(rows_grad * normal, axis=0)


def shards(latents, condition, ada_weight, ada_bias, qkv_weight, qv_bias, proj_weight, proj_bias,
           fc1_weight, fc1_bias, fc2_weight, fc2_bias, cotangent):
    plan = Plan(latents, condition, qkv_weight, fc1_weight)
    row, col = lax.axis_index("row"), lax.axis_index("col")
    rows, cols, width, tokens = plan.rows, plan.cols, plan.width, plan.tokens
    depth, hc, fc = plan.depth_rows, plan.head_cols, plan.ff_cols
    heads = cols * hc // HEAD_DIM
    groups = rows * plan.lats

    qkv_flat = qkv_weight.reshape(depth, 3 * hc)
    proj_t, fc2_t = proj_weight.T, fc2_weight.T
    blocks = [qkv_flat[:, :plan.q_main], proj_t[:, :plan.p_main], fc1_weight[:, :plan.f_main], fc2_t[:, :plan.f_main]]
    if plan.near:
        left_a = plan.fold(jnp.concatenate([qkv_flat[:, plan.q_main:], proj_t[:, plan.p_main:]], axis=1))
        blocks += [left_a, plan.fold(fc1_weight[:, plan.f_main:]), plan.fold(fc2_t[:, plan.f_main:])]
        order = (0, 1, 4, 2, 5, 3, 6)
        full = [None] * 7
        for i, w in zip(order, gather_all([blocks[i] for i in order], (3, 2, 2), 0)):
            full[i] = w
        full[4:] = [plan.unfold_full(w) for w in full[4:]]
    else:
        full = gather_plain(blocks)

    if plan.near:
        home = (row - row % 2 + col % 2) * plan.lats + col // 2
    else:
        home = row * plan.lats + col // plan.share
    values = plan.swap(latents).astype(f32)
    grad_out = plan.swap(cotangent).astype(f32)

    cond_all = lax.all_gather(condition, "row", axis=0, tiled=True).astype(f32)
    cond_act = jax.nn.silu(cond_all).astype(bf16)
    cond_mine = lax.dynamic_slice(cond_act, (0, row * depth), (groups, depth))
    ada_flat = ada_weight.reshape(depth, 6 * hc)
    partial = lax.psum(nn(cond_mine, ada_flat), "row") + ada_bias.astype(f32).reshape(1, 6 * hc)
    small = jnp.concatenate(
        [partial.reshape(-1)] + [b.astype(f32).reshape(-1) for b in (proj_bias, fc2_bias, fc1_bias, qv_bias)])
    small = lax.all_gather(small, "col", axis=0, tiled=False)
    sizes = [groups * 6 * hc, hc, hc, fc, 2 * hc]
    mod_all, proj_b, fc2_b, fc1_b, qv_b = jnp.split(small, [sum(sizes[:i + 1]) for i in range(4)], axis=1)
    mod = lax.dynamic_index_in_dim(mod_all.reshape(cols, groups, 6, hc), home, 1, keepdims=False)
    mod = mod.transpose(1, 0, 2).reshape(6, 1, width)
    shift_one, scale_one, gate_one, shift_two, scale_two, gate_two = (mod[k] for k in range(6))
    proj_b, fc2_b = proj_b.reshape(width), fc2_b.reshape(width)
    q_b, v_b = qv_b[:, :hc].reshape(heads, 1, HEAD_DIM), qv_b[:, hc:].reshape(heads, 1, HEAD_DIM)
    fc1_parts = [fc1_b[:, :plan.f_main].reshape(-1)]
    if plan.near:
        fc1_parts.append(fc1_b[:, plan.f_main:].reshape(-1))

    def to_heads(flat):
        return flat.reshape(tokens, heads, HEAD_DIM).transpose(1, 0, 2)

    def from_heads(value):
        return value.transpose(1, 0, 2).reshape(tokens, cols, hc)

    normal_one, inverse_one = layer_norm(values)
    normed_one = (normal_one * (1.0 + scale_one) + shift_one).astype(bf16)
    projected = nn(normed_one, full[0]).reshape(tokens, cols, plan.q_main)
    if plan.near:
        left_w = full[4].reshape(width, cols, 64)
        left_q, left_p = left_w[:, :, :plan.q_left].reshape(width, -1), left_w[:, :, plan.q_left:].reshape(width, -1)
        projected = jnp.concatenate([projected, nn(normed_one, left_q).reshape(tokens, cols, plan.q_left)], axis=2)
    query = (to_heads(projected[:, :, :hc]) + q_b).astype(bf16)
    key = to_heads(projected[:, :, hc:2 * hc]).astype(bf16)
    value = (to_heads(projected[:, :, 2 * hc:]) + v_b).astype(bf16)
    if plan.near:
        att, lse, key_two, value_two = attend(query, key, value, 2)
    else:
        cuts = [[s * plan.share + i for i in range(plan.share)] for s in range(cols // plan.share)]
        key_all = lax.all_gather(key, "col", axis=1, tiled=True, axis_index_groups=cuts)
        value_all = lax.all_gather(value, "col", axis=1, tiled=True, axis_index_groups=cuts)
        att, lse = attend_plain(query, key_all, value_all)
    att_flat = from_heads(att)
    att_main = att_flat[:, :, :plan.p_main].reshape(tokens, -1)
    branch_a = nt(att_main, full[1])
    if plan.near:
        att_left = att_flat[:, :, plan.p_main:]
        branch_a = branch_a + nt(att_left.reshape(tokens, -1), left_p)
    branch_a = branch_a + proj_b
    middle = values + gate_one * branch_a

    count = len(fc1_parts)
    fc1_w, fc2_w = (full[2], full[5])[:count] if plan.near else (full[2],), (full[3], full[6])[:count] if plan.near else (full[3],)
    normal_two, inverse_two = layer_norm(middle)
    normed_two = (normal_two * (1.0 + scale_two) + shift_two).astype(bf16)
    pre = [nn(normed_two, w) + b for w, b in zip(fc1_w, fc1_parts)]
    hidden, slope = zip(*[gelu_and_slope(u) for u in pre])
    hidden = [u.astype(bf16) for u in hidden]
    branch_m = sum(nt(u, w) for u, w in zip(hidden, fc2_w)) + fc2_b
    output = plan.swap((middle + gate_two * branch_m).astype(bf16))

    gate_two_grad = jnp.sum(grad_out * branch_m, axis=0)
    m_grad = grad_out * gate_two
    fc2_bias_part = jnp.sum(m_grad, axis=0)
    m_low = m_grad.astype(bf16)
    fc2_grads = [tn(m_low, u).astype(bf16) for u in hidden]
    pre_grads = [nn(m_low, w) * s for w, s in zip(fc2_w, slope)]
    fc1_bias_parts = [jnp.sum(u, axis=0) for u in pre_grads]
    pre_low = [u.astype(bf16) for u in pre_grads]
    fc1_grads = [tn(normed_two, u).astype(bf16) for u in pre_low]
    normed_two_grad = sum(nt(u, w) for u, w in zip(pre_low, fc1_w))
    middle_part, shift_two_grad, scale_two_grad = norm_back(normed_two_grad, normal_two, inverse_two, scale_two)
    middle_grad = grad_out + middle_part
    gate_one_grad = jnp.sum(middle_grad * branch_a, axis=0)
    a_grad = middle_grad * gate_one
    proj_bias_part = jnp.sum(a_grad, axis=0)
    a_low = a_grad.astype(bf16)
    proj_grad = tn(a_low, att_main).astype(bf16)
    att_grad = nn(a_low, full[1]).reshape(tokens, cols, plan.p_main)
    if plan.near:
        att_grad = jnp.concatenate([att_grad, nn(a_low, left_p).reshape(tokens, cols, plan.p_left)], axis=2)
    att_grad = to_heads(att_grad.astype(bf16))
    if plan.near:
        query_grad, key_grad, value_grad = attend_back(query, key, value, key_two, value_two, lse, att, att_grad, 3)
    else:
        query_grad, key_grad, value_grad = attend_back_plain(query, key_all, value_all, lse, att_grad)
        key_grad, value_grad = (
            lax.psum_scatter(g.astype(bf16), "col", scatter_dimension=1, tiled=True, axis_index_groups=cuts).astype(f32)
            for g in (key_grad, value_grad))
    q_bias_part, v_bias_part = jnp.sum(query_grad, axis=1), jnp.sum(value_grad, axis=1)
    qkv_low = jnp.concatenate([from_heads(g.astype(bf16)) for g in (query_grad, key_grad, value_grad)], axis=2)
    low_main = qkv_low[:, :, :plan.q_main].reshape(tokens, -1)
    qkv_grad = tn(normed_one, low_main).astype(bf16)
    normed_one_grad = nt(low_main, full[0])
    if plan.near:
        low_left = qkv_low[:, :, plan.q_main:]
        normed_one_grad = normed_one_grad + nt(low_left.reshape(tokens, -1), left_q)
        left_grad = jnp.concatenate(
            [tn(normed_one, low_left.reshape(tokens, -1)).reshape(width, cols, -1),
             tn(a_low, att_left.reshape(tokens, -1)).reshape(width, cols, -1)], axis=2).reshape(width, cols * 64).astype(bf16)
        grads = [fc2_grads[0], plan.fold_full(fc2_grads[1]), fc1_grads[0], plan.fold_full(fc1_grads[1]),
                 qkv_grad, proj_grad, plan.fold_full(left_grad)]
        sums = scatter_all(grads, (2, 2, 3), 1)
        fc2_sum = jnp.concatenate([sums[0], plan.unfold(sums[1])], axis=1)
        fc1_sum = jnp.concatenate([sums[2], plan.unfold(sums[3])], axis=1)
        left_sum = plan.unfold(sums[6])
        qkv_sum = jnp.concatenate([sums[4], left_sum[:, :plan.q_left]], axis=1)
        proj_sum = jnp.concatenate([sums[5], left_sum[:, plan.q_left:]], axis=1)
    else:
        fc2_sum, fc1_sum, qkv_sum, proj_sum = scatter_plain([fc2_grads[0], fc1_grads[0], qkv_grad, proj_grad])
    input_part, shift_one_grad, scale_one_grad = norm_back(normed_one_grad, normal_one, inverse_one, scale_one)
    latents_grad = plan.swap((middle_grad + input_part).astype(bf16)).astype(f32)

    mod_grad = jnp.stack(
        [shift_one_grad, scale_one_grad, gate_one_grad, shift_two_grad, scale_two_grad, gate_two_grad], axis=0)
    mod_grad = lax.all_gather(mod_grad, ("row", "col"), axis=0, tiled=False)
    if plan.near:
        mod_grad = mod_grad.reshape(rows // 2, 2, cols // 2, 2, 6, width).sum(axis=1).transpose(0, 2, 1, 3, 4)
    else:
        mod_grad = mod_grad.reshape(rows, cols // plan.share, plan.share, 6, width).sum(axis=2)
    mod_grad = mod_grad.reshape(groups, 6, width)
    mod_mine = lax.dynamic_slice(mod_grad, (0, 0, col * hc), (groups, 6, hc))
    ada_bsum = jnp.sum(mod_mine, axis=0)
    mod_low = mod_mine.astype(bf16).reshape(groups, 6 * hc)
    ada_wsum = tn(cond_mine, mod_low).reshape(depth, 6, hc)
    cond_part = lax.dynamic_update_slice(jnp.zeros((groups, width), f32), nt(mod_low, ada_flat), (0, row * depth))
    parts = [cond_part, proj_bias_part, fc2_bias_part, q_bias_part, v_bias_part] + fc1_bias_parts
    totals = lax.psum(jnp.concatenate([part.reshape(-1) for part in parts]), ("row", "col"))
    ends, spot = [], 0
    for part in parts:
        ends.append(totals[spot:spot + part.size])
        spot += part.size

    def mine(flat, size):
        return lax.dynamic_slice(flat, (col * size,), (size,))

    cond_summed = lax.dynamic_slice(ends[0].reshape(groups, width), (row * plan.lats, 0), (plan.lats, width))
    silu_value, silu_pull = jax.vjp(jax.nn.silu, condition.astype(f32))
    condition_grad = silu_pull(cond_summed)[0]
    proj_bsum, fc2_bsum = mine(ends[1], hc), mine(ends[2], hc)
    qv_bsum = jnp.stack([mine(ends[3], hc), mine(ends[4], hc)], axis=0)
    fc1_bsum = jnp.concatenate([mine(flat, flat.size // cols) for flat in ends[5:]])
    return (
        output, latents_grad, condition_grad, ada_wsum, ada_bsum, qkv_sum.reshape(depth, 3, hc), qv_bsum,
        proj_sum.T, proj_bsum, fc1_sum, fc1_bsum, fc2_sum.T, fc2_bsum)


def solution(mesh):
    token, grid, turned = P(("row", "col"), None), P("row", "col"), P("col", "row")
    cube, wide, flat = P("row", None, "col"), P(None, "col"), P("col")
    return jax.shard_map(
        shards,
        mesh=mesh,
        in_specs=(token, P("row", None), cube, wide, cube, wide, turned, flat, grid, flat, turned, flat, token),
        out_specs=(token, token, P("row", None), cube, wide, cube, wide, turned, flat, grid, flat, turned, flat),
        check_vma=False,
    )
```

```python
import functools
import math
import jax
import jax.numpy as jnp
from jax import lax
from jax.experimental import pallas as pl
from jax.experimental.pallas import tpu as pltpu
from jax.sharding import PartitionSpec as P

HEAD_DIM = 72
SEQ = 1024
norm_eps = 1e-06
bf16, f32 = jnp.bfloat16, jnp.float32

MESH = pl.DeviceIdType.MESH
ANY = pl.BlockSpec(memory_space=pl.ANY)


class Place:
    def __init__(self):
        row, col = lax.axis_index("row"), lax.axis_index("col")
        self.row, self.col = row, col
        self.depth = lax.axis_size("col") // 2
        self.y, self.h = row // 2, row % 2
        self.z, self.x = col // 2, col % 2
        self.p = jnp.where(self.h == 0, self.y, self.x)
        self.q = jnp.where(self.h == 0, self.x, self.y)
        flip_x, flip_y = (row, col + 1 - 2 * self.x), (row + 2 - 4 * self.y, col)
        self.to_q = tuple(jnp.where(self.h == 0, a, b) for a, b in zip(flip_x, flip_y))
        self.to_p = tuple(jnp.where(self.h == 0, b, a) for a, b in zip(flip_x, flip_y))
        self.to_core = (row + 1 - 2 * self.h, col)

    def to_z(self, z):
        return (self.row, 2 * z + self.x)

    def diagonal(self):
        return (self.row + 1 - 2 * self.h, self.col + 1 - 2 * self.x)

    def yx(self, p, q):
        return jnp.where(self.h == 0, p, q), jnp.where(self.h == 0, q, p)

    def partners(self):
        near = [self.to_q, self.to_p, self.to_core]
        return near + [self.to_z((self.z + k) % self.depth) for k in range(1, self.depth)]


def greet(partners):
    barrier = pltpu.get_barrier_semaphore()
    for partner in partners:
        pl.semaphore_signal(barrier, inc=1, device_id=partner, device_id_type=MESH)
    pl.semaphore_wait(barrier, len(partners))


def block_at(ref, rows, lanes, r, c):
    return ref.at[pl.ds(pl.multiple_of(r * rows, 16), rows), pl.ds(pl.multiple_of(c * lanes, 128), lanes)]


class Gather:
    sems = (1, 2, 2, 4, 8)

    def __init__(self, place, ins, outs, sems):
        self.at, self.ins, self.outs = place, ins, outs
        self.local, self.zs, self.qs, self.ps, self.ks = sems

    @staticmethod
    def scratch(count, depth):
        dma = pltpu.SemaphoreType.DMA
        return [dma((count,)), dma((count, 2, depth)), dma((count, 2, depth)), dma((count, 2, depth, 2)), dma((count, 2, depth, 4))]

    def block(self, a, p, q, z, h=None):
        y, x = self.at.yx(p, q)
        rows, lanes = self.ins[a].shape
        h = self.at.h if h is None else h
        return block_at(self.outs[a], rows, lanes, 2 * y + h, 2 * z + x)

    def zc(self, t):
        return (self.at.z + self.at.depth - t) % self.at.depth

    def copy(self, src, dst, sems, index, to):
        return pltpu.make_async_remote_copy(
            src_ref=src, dst_ref=dst, send_sem=sems.at[(index[0], 0) + index[1:]], recv_sem=sems.at[(index[0], 1) + index[1:]],
            device_id=to, device_id_type=MESH)

    def own(self, a):
        return self.block(a, self.at.p, self.at.q, self.at.z)

    def c_local(self, a):
        return pltpu.make_async_copy(self.ins[a], self.own(a), self.local.at[a])

    def c_z(self, a, k):
        place = self.at
        return pltpu.make_async_remote_copy(
            src_ref=self.ins[a], dst_ref=self.own(a), send_sem=self.zs.at[a, 0, k], recv_sem=self.zs.at[a, 1, place.z],
            device_id=place.to_z((place.z + k) % place.depth), device_id_type=MESH)

    def r_z(self, a, t):
        place = self.at
        here = self.block(a, place.p, place.q, self.zc(t))
        return pltpu.make_async_remote_copy(
            src_ref=self.ins[a], dst_ref=here, send_sem=self.zs.at[a, 0, 0], recv_sem=self.zs.at[a, 1, self.zc(t)],
            device_id=place.to_z(place.z), device_id_type=MESH)

    def c_q(self, a, t):
        place = self.at
        spot = self.block(a, place.p, place.q, self.zc(t))
        return self.copy(self.ins[a] if t == 0 else spot, spot, self.qs, (a, self.zc(t)), place.to_q)

    def c_p(self, a, t, j):
        place = self.at
        spot = self.block(a, place.p, place.q if j == 0 else 1 - place.q, self.zc(t))
        return self.copy(self.ins[a] if t == 0 and j == 0 else spot, spot, self.ps, (a, self.zc(t), j), place.to_p)

    def c_k(self, a, t, j):
        place = self.at
        spot = self.block(a, place.p if j < 2 else 1 - place.p, place.q if j % 2 == 0 else 1 - place.q, self.zc(t))
        return self.copy(self.ins[a] if t == 0 and j == 0 else spot, spot, self.ks, (a, self.zc(t), j), place.to_core)

    def start(self, a):
        for k in range(1, self.at.depth):
            self.c_z(a, k).start()
        self.c_local(a).start()

    def stage(self, a, t, n):
        if n == 0:
            if t > 0:
                self.r_z(a, t).wait_recv()
            self.c_q(a, t).start()
            self.c_p(a, t, 0).start()
            self.c_k(a, t, 0).start()
        elif n == 1:
            self.c_q(a, t).wait_recv()
            self.c_p(a, t, 1).start()
            self.c_k(a, t, 1).start()
        elif n == 2:
            self.c_p(a, t, 0).wait_recv()
            self.c_k(a, t, 2).start()
        elif n == 3:
            self.c_p(a, t, 1).wait_recv()
            self.c_k(a, t, 3).start()
        else:
            if t == 0:
                self.c_local(a).wait()
            for j in range(4):
                self.c_k(a, t, j).wait_recv()

    def finish(self, a):
        for k in range(1, self.at.depth):
            self.c_z(a, k).wait_send()
        for t in range(self.at.depth):
            self.c_q(a, t).wait_send()
            for j in range(2):
                self.c_p(a, t, j).wait_send()
            for j in range(4):
                self.c_k(a, t, j).wait_send()


def gather_kernel(groups, *refs):
    count = sum(groups)
    ins, outs, sems = refs[:count], refs[count:2 * count], refs[2 * count:]
    place = Place()
    greet(place.partners())
    work = Gather(place, ins, outs, sems)
    for a in range(count):
        work.start(a)
    chunks, first = [], 0
    for size in groups:
        for t in range(place.depth):
            chunks.append([(a, t) for a in range(first, first + size)])
        first += size
    for s in range(len(chunks) + 4):
        for n in range(5):
            if 0 <= s - n < len(chunks):
                for a, t in chunks[s - n]:
                    work.stage(a, t, n)
    for a in range(count):
        work.finish(a)


def gather_all(blocks, groups, collective_id):
    rows, cols = lax.axis_size("row"), lax.axis_size("col")
    return pl.pallas_call(
        functools.partial(gather_kernel, groups),
        out_shape=[jax.ShapeDtypeStruct((rows * b.shape[0], cols * b.shape[1]), b.dtype) for b in blocks],
        in_specs=[ANY] * len(blocks),
        out_specs=[ANY] * len(blocks),
        scratch_shapes=Gather.scratch(len(blocks), cols // 2),
        compiler_params=pltpu.CompilerParams(collective_id=collective_id, has_side_effects=True),
        name="gather_weights",
    )(*blocks)


class Scatter:
    def __init__(self, place, ins, outs, bufs, sems):
        self.at, self.ins, self.outs = place, ins, outs
        self.r0, self.own, self.r1, self.r2, self.r3 = bufs
        self.s0, self.ld, self.s1, self.s2, self.s3 = sems

    @staticmethod
    def scratch(shapes, depth):
        dma, count = pltpu.SemaphoreType.DMA, len(shapes)
        bufs = []
        for lead in ((depth, 2, 2), (2, 2, 2), (depth, 2), (depth,), (depth - 1,)):
            bufs += [pltpu.VMEM(lead + s, jnp.bfloat16) for s in shapes]
        return bufs + [dma((count, 2, depth, 4)), dma((count, 2, 4)), dma((count, 2, depth, 2)), dma((count, 2, depth)), dma((count, 2, depth))]

    @staticmethod
    def split(refs, count):
        return [refs[i * count:(i + 1) * count] for i in range(5)], refs[5 * count:]

    def zc(self, t):
        return lax.rem(self.at.z + 1 + t, self.at.depth)

    def block(self, a, p, q, z, h):
        y, x = jnp.where(h == 0, p, q), jnp.where(h == 0, q, p)
        rows, lanes = self.outs[a].shape
        return block_at(self.ins[a], rows, lanes, 2 * y + h, 2 * z + x)

    def c0(self, a, t, j):
        place = self.at
        return pltpu.make_async_remote_copy(
            src_ref=self.block(a, j // 2, j % 2, self.zc(t), 1 - place.h), dst_ref=self.r0[a].at[t, j // 2, j % 2],
            send_sem=self.s0.at[a, 0, t, j], recv_sem=self.s0.at[a, 1, t, j], device_id=place.to_core, device_id_type=MESH)

    def load(self, a, t, j):
        return pltpu.make_async_copy(
            self.block(a, j // 2, j % 2, self.zc(t), self.at.h), self.own[a].at[t % 2, j // 2, j % 2], self.ld.at[a, t % 2, j])

    def c1(self, a, t, j):
        place = self.at
        return pltpu.make_async_remote_copy(
            src_ref=self.r0[a].at[t, 1 - place.p, j], dst_ref=self.r1[a].at[t, j],
            send_sem=self.s1.at[a, 0, t, j], recv_sem=self.s1.at[a, 1, t, j], device_id=place.to_p, device_id_type=MESH)

    def c2(self, a, t):
        place = self.at
        return pltpu.make_async_remote_copy(
            src_ref=self.r0[a].at[t, place.p, 1 - place.q], dst_ref=self.r2[a].at[t],
            send_sem=self.s2.at[a, 0, t], recv_sem=self.s2.at[a, 1, t], device_id=place.to_q, device_id_type=MESH)

    def c3(self, a, t):
        place = self.at
        return pltpu.make_async_remote_copy(
            src_ref=self.r0[a].at[t, place.p, place.q], dst_ref=self.r3[a].at[t],
            send_sem=self.s3.at[a, 0, t], recv_sem=self.s3.at[a, 1, t], device_id=place.to_z(self.zc(t)), device_id_type=MESH)

    def add(self, a, into, other):
        rows = self.outs[a].shape[0]
        step = 48 if rows % 48 == 0 else 16

        @pl.loop(0, rows // step)
        def _(i):
            part = pl.ds(pl.multiple_of(i * step, 16), step)
            into[part, :] = into[part, :] + other[part, :]

    def stage(self, a, t, n):
        place = self.at
        last = t == place.depth - 1
        if n == 0:
            for j in range(4):
                self.c0(a, t, j).start()
                self.load(a, t, j).start()
        elif n == 1:
            for j in range(4):
                self.c0(a, t, j).wait_recv()
                self.load(a, t, j).wait()
            for j in range(2):
                self.add(a, self.r0[a].at[t, 1 - place.p, j], self.own[a].at[t % 2, 1 - place.p, j])
                self.c1(a, t, j).start()
            for j in range(2):
                self.add(a, self.r0[a].at[t, place.p, j], self.own[a].at[t % 2, place.p, j])
        elif n == 2:
            for j in range(2):
                self.c1(a, t, j).wait_recv()
            self.add(a, self.r0[a].at[t, place.p, 1 - place.q], self.r1[a].at[t, 1 - place.q])
            self.c2(a, t).start()
            self.add(a, self.r0[a].at[t, place.p, place.q], self.r1[a].at[t, place.q])
        elif n == 3:
            self.c2(a, t).wait_recv()
            self.add(a, self.r0[a].at[t, place.p, place.q], self.r2[a].at[t])
            if not last:
                self.c3(a, t).start()
        elif last:
            self.total(a)

    def total(self, a):
        place, depth = self.at, self.at.depth
        for t in range(depth - 1):
            self.c3(a, t).wait_recv()
        rows = self.outs[a].shape[0]
        step = 48 if rows % 48 == 0 else 16
        mine, others, out = self.r0[a].at[depth - 1, place.p, place.q], self.r3[a], self.outs[a]

        @pl.loop(0, rows // step)
        def _(i):
            part = pl.ds(pl.multiple_of(i * step, 16), step)
            value = mine[part, :].astype(jnp.float32)
            for t in range(depth - 1):
                value = value + others[t, part, :].astype(jnp.float32)
            out[part, :] = value

    def finish(self, a):
        for t in range(self.at.depth):
            for j in range(4):
                self.c0(a, t, j).wait_send()
            for j in range(2):
                self.c1(a, t, j).wait_send()
            self.c2(a, t).wait_send()
            if t < self.at.depth - 1:
                self.c3(a, t).wait_send()


def chunk_list(groups, depth):
    chunks, first = [], 0
    for size in groups:
        for t in range(depth):
            chunks.append([(a, t) for a in range(first, first + size)])
        first += size
    return chunks


def scatter_kernel(groups, *refs):
    count = sum(groups)
    ins, outs = refs[:count], refs[count:2 * count]
    bufs, sems = Scatter.split(refs[2 * count:], count)
    place = Place()
    greet(place.partners())
    work = Scatter(place, ins, outs, bufs, sems)
    chunks = chunk_list(groups, place.depth)
    for s in range(len(chunks) + 4):
        for n in range(5):
            if 0 <= s - n < len(chunks):
                for a, t in chunks[s - n]:
                    work.stage(a, t, n)
    for a in range(count):
        work.finish(a)


def scatter_all(fulls, groups, collective_id):
    rows, cols = lax.axis_size("row"), lax.axis_size("col")
    shapes = [(g.shape[0] // rows, g.shape[1] // cols) for g in fulls]
    return pl.pallas_call(
        functools.partial(scatter_kernel, groups),
        out_shape=[jax.ShapeDtypeStruct(s, jnp.float32) for s in shapes],
        in_specs=[ANY] * len(fulls),
        out_specs=[pl.BlockSpec(memory_space=pltpu.VMEM)] * len(fulls),
        scratch_shapes=Scatter.scratch(shapes, cols // 2),
        compiler_params=pltpu.CompilerParams(collective_id=collective_id, has_side_effects=True, vmem_limit_bytes=58 * 2**20),
        name="scatter_grads",
    )(*fulls)


def nt(a, b):
    return lax.dot_general(a, b, (((1,), (1,)), ((), ())), preferred_element_type=f32)


def nn(a, b):
    return lax.dot_general(a, b, (((1,), (0,)), ((), ())), preferred_element_type=f32)


def tn(a, b):
    return lax.dot_general(a, b, (((0,), (0,)), ((), ())), preferred_element_type=f32)


SOFT = HEAD_DIM ** (-0.5) * math.log2(math.e)


def attend_kernel(q_ref, k_ref, v_ref, att_ref, lse_ref, k2_ref, v2_ref, sems):
    place = Place()
    greet([place.to_core])
    heads, rows, width = q_ref.shape

    def swap(i, h):
        src, dst = ((k_ref, k2_ref), (v_ref, v2_ref))[i]
        return pltpu.make_async_remote_copy(
            src_ref=src.at[h], dst_ref=dst.at[h], send_sem=sems.at[0, i, h], recv_sem=sems.at[1, i, h],
            device_id=place.to_core, device_id_type=MESH)

    for h in range(heads):
        swap(0, h).start()
        swap(1, h).start()

    @pl.loop(0, heads)
    def _(h):
        swap(0, h).wait_recv()
        swap(1, h).wait_recv()
        q = q_ref[h]
        one = nt(k_ref[h], q)
        two = nt(k2_ref[h], q)
        top = jnp.maximum(jnp.max(one, axis=0, keepdims=True), jnp.max(two, axis=0, keepdims=True)) * SOFT
        one = jnp.exp2(one * SOFT - top)
        two = jnp.exp2(two * SOFT - top)
        total = jnp.sum(one, axis=0, keepdims=True) + jnp.sum(two, axis=0, keepdims=True)
        result = tn(v_ref[h], one.astype(bf16)) + tn(v2_ref[h], two.astype(bf16))
        att_ref[h] = (result / total).T.astype(bf16)
        lse_ref[h] = top + jnp.log2(total)

    for h in range(heads):
        swap(0, h).wait_send()
        swap(1, h).wait_send()


def attend(q, k, v, collective_id):
    heads, rows, width = q.shape
    vmem = pl.BlockSpec(memory_space=pltpu.VMEM)
    return pl.pallas_call(
        attend_kernel,
        out_shape=[jax.ShapeDtypeStruct(q.shape, bf16), jax.ShapeDtypeStruct((heads, 1, rows), f32)]
        + [jax.ShapeDtypeStruct(q.shape, bf16)] * 2,
        in_specs=[vmem] * 3,
        out_specs=[vmem] * 4,
        scratch_shapes=[pltpu.SemaphoreType.DMA((2, 2, heads))],
        compiler_params=pltpu.CompilerParams(collective_id=collective_id, has_side_effects=True, vmem_limit_bytes=50 * 2**20),
        name="attend",
    )(q, k, v)


def attend_back_kernel(q_ref, k_ref, v_ref, k2_ref, v2_ref, lse_ref, o_ref, do_ref, dq_ref, dk_ref, dv_ref, send, recv, sems):
    place = Place()
    greet([place.to_core])
    heads = q_ref.shape[0]

    def swap(i, h):
        return pltpu.make_async_remote_copy(
            src_ref=send.at[i, h], dst_ref=recv.at[i, h], send_sem=sems.at[0, i, h], recv_sem=sems.at[1, i, h],
            device_id=place.to_core, device_id_type=MESH)

    @pl.loop(0, heads)
    def _(h):
        q, out_grad, lse = q_ref[h], do_ref[h], lse_ref[h]
        delta = jnp.sum(out_grad.astype(f32).T * o_ref[h].astype(f32).T, axis=0, keepdims=True)

        def half(k, v):
            probs = jnp.exp2(nt(k, q) * SOFT - lse)
            grad = (probs * (nt(v, out_grad) - delta)).astype(bf16)
            return nn(grad, q) * HEAD_DIM ** (-0.5), nn(probs.astype(bf16), out_grad), tn(k, grad)

        dk, dv, dq_two = half(k2_ref[h], v2_ref[h])
        send[0, h] = dk.astype(bf16)
        send[1, h] = dv.astype(bf16)
        swap(0, h).start()
        swap(1, h).start()
        dk, dv, dq_one = half(k_ref[h], v_ref[h])
        dk_ref[h] = dk
        dv_ref[h] = dv
        dq_ref[h] = ((dq_one + dq_two) * HEAD_DIM ** (-0.5)).T

    @pl.loop(0, heads)
    def _(h):
        swap(0, h).wait_recv()
        swap(1, h).wait_recv()
        dk_ref[h] = dk_ref[h] + recv[0, h].astype(f32)
        dv_ref[h] = dv_ref[h] + recv[1, h].astype(f32)

    for h in range(heads):
        swap(0, h).wait_send()
        swap(1, h).wait_send()


def attend_back(q, k, v, k2, v2, lse, att, att_grad, collective_id):
    heads, rows, width = q.shape
    vmem = pl.BlockSpec(memory_space=pltpu.VMEM)
    return pl.pallas_call(
        attend_back_kernel,
        out_shape=[jax.ShapeDtypeStruct(q.shape, f32)] * 3,
        in_specs=[vmem] * 8,
        out_specs=[vmem] * 3,
        scratch_shapes=[pltpu.VMEM((2,) + q.shape, bf16), pltpu.VMEM((2,) + q.shape, bf16), pltpu.SemaphoreType.DMA((2, 2, heads))],
        compiler_params=pltpu.CompilerParams(collective_id=collective_id, has_side_effects=True, vmem_limit_bytes=58 * 2**20),
        name="attend_back",
    )(q, k, v, k2, v2, lse, att, att_grad)


VECS = 24


def softmax_head(q, k, k2):
    one, two = nt(k, q), nt(k2, q)
    top = jnp.maximum(jnp.max(one, axis=0, keepdims=True), jnp.max(two, axis=0, keepdims=True)) * SOFT
    one, two = jnp.exp2(one * SOFT - top), jnp.exp2(two * SOFT - top)
    total = jnp.sum(one, axis=0, keepdims=True) + jnp.sum(two, axis=0, keepdims=True)
    return one.astype(bf16), two.astype(bf16), total, top + jnp.log2(total)


def norm_rows(values):
    mean = jnp.mean(values, axis=-1, keepdims=True)
    centred = values - mean
    inverse = lax.rsqrt(jnp.mean(centred * centred, axis=-1, keepdims=True) + norm_eps)
    return centred * inverse, inverse


def gelu_both(u):
    c = math.sqrt(2.0 / math.pi)
    square = u * u
    inner = jnp.tanh(u * (c + (c * 0.044715) * square))
    half = 0.5 * (1.0 + inner)
    slope = half + (0.5 * u) * (1.0 - inner * inner) * (c + (3 * c * 0.044715) * square)
    return u * half, slope


class Swap:
    def __init__(self, place, src, dst, sems, i):
        self.stay = place.h == place.x
        self.local = pltpu.make_async_copy(src, dst, sems.at[i, 0])
        self.remote = pltpu.make_async_remote_copy(
            src_ref=src, dst_ref=dst, send_sem=sems.at[i, 0], recv_sem=sems.at[i, 1],
            device_id=place.diagonal(), device_id_type=MESH)

    def start(self):
        pl.when(self.stay)(self.local.start)
        pl.when(jnp.logical_not(self.stay))(self.remote.start)

    def wait(self):
        pl.when(self.stay)(self.local.wait)
        pl.when(jnp.logical_not(self.stay))(self.remote.wait)


def unfold_into(left, target):
    rows = target.shape[0] // 4
    half = rows // 2
    for r in range(4):
        tile = left[r * half:(r + 1) * half, :].astype(f32)
        target[r * rows:r * rows + half, :] = jnp.concatenate([tile[:, :64], tile[:, 128:192]], axis=1).astype(bf16)
        target[r * rows + half:(r + 1) * rows, :] = jnp.concatenate([tile[:, 64:128], tile[:, 192:]], axis=1).astype(bf16)


GROUPS = (3, 2, 2)


def forward_kernel(*refs):
    lat, cot, cond, ada, bias = refs[:5]
    blocks, refs = refs[5:12], refs[12:]
    fulls, refs = refs[:7], refs[7:]
    (o_w, o_cot, o_x, o_n1, o_q, o_k, o_v, o_k2, o_v2, o_lse, o_att, o_ba, o_mid, o_n2, o_hid, o_slo, o_out, o_vec), refs = refs[:18], refs[18:]
    (x_v, n1, q_v, k_v, v_v, k2_v, v2_v, lse_v, ot, att, ba, mid, n2, hid, slo, acc, wbuf, lbuf, out_v, cot_v, vec,
     c_send, c_recv, s_send, s_recv, m_own, m_oth), refs = refs[:27], refs[27:]
    ag_sems, (swap_sems, c_sems, s_sems, m_sems, o_sems, kv_sems, w_sems, save_sems, wsave_sems) = refs[:5], refs[5:]

    place = Place()
    depth, rows_n = place.depth, 4
    row, col = place.row, place.col
    cols_n = 2 * depth
    tokens, width = x_v.shape
    hc = width // cols_n
    drows = ada.shape[0]
    q_main, p_main = blocks[0].shape[1], blocks[1].shape[1]
    half = tokens // 2

    row_peers = [((row + k) % rows_n, col) for k in range(1, rows_n)]
    col_peers = [(row, (col + k) % cols_n) for k in range(1, cols_n)]
    greet(place.partners() + row_peers + col_peers + [place.diagonal()])

    def send(src, dst, s_sem, r_sem, to):
        return pltpu.make_async_remote_copy(
            src_ref=src, dst_ref=dst, send_sem=s_sem, recv_sem=r_sem, device_id=to, device_id_type=MESH)

    cond_value = cond[...]
    act = (cond_value / (1.0 + jnp.exp(-cond_value))).astype(bf16).astype(f32)
    for r in range(rows_n):
        c_send[r] = act[:, r * drows:(r + 1) * drows]

    def cond_copy(k):
        to = (row + k) % rows_n
        return send(c_send.at[to], c_recv.at[row], c_sems.at[0, k], c_sems.at[1, row], (to, col))

    def cond_got(k):
        src = (row + k) % rows_n
        return send(c_send.at[src], c_recv.at[src], c_sems.at[0, k], c_sems.at[1, src], (src, col))

    for k in range(1, rows_n):
        cond_copy(k).start()
    swap_x = Swap(place, lat, x_v, swap_sems, 0)
    swap_x.start()

    work = Gather(place, blocks, fulls, ag_sems)
    for a in range(3):
        work.start(a)

    members, first = [], 0
    for size in GROUPS:
        members.append(list(range(first, first + size)))
        first += size
    chunks = [(g, t) for g in range(len(GROUPS)) for t in range(depth)]
    events = [(s - n, n) for s in range(len(chunks) + 4) for n in range(5) if 0 <= s - n < len(chunks)]
    at = [0]

    def pump(count):
        for s, n in events[at[0]:at[0] + count]:
            if n == 0 and s in (2, depth + 2):
                for a in members[1 if s == 2 else 2]:
                    work.start(a)
            g, t = chunks[s]
            for a in members[g]:
                work.stage(a, t, n)
        at[0] += count

    def pump_to(s, n):
        pump(max(0, events.index((s, n)) + 1 - at[0]))

    pump_to(0, 0)
    c_recv[row] = c_send[row]
    for k in range(1, rows_n):
        cond_got(k).wait_recv()
    act_all = c_recv[...].reshape(rows_n * 8, drows).astype(bf16)
    s_send[...] = nn(act_all, ada[...]).reshape(rows_n, 8, 6 * hc)

    def sum_copy(k):
        to = (row + k) % rows_n
        return send(s_send.at[to], s_recv.at[row], s_sems.at[0, k], s_sems.at[1, row], (to, col))

    def sum_got(k):
        src = (row + k) % rows_n
        return send(s_send.at[src], s_recv.at[src], s_sems.at[0, k], s_sems.at[1, src], (src, col))

    for k in range(1, rows_n):
        sum_copy(k).start()
    pump_to(0, 1)
    s_recv[row] = s_send[row]
    for k in range(1, rows_n):
        sum_got(k).wait_recv()
    m_own[col] = s_recv[0] + s_recv[1] + s_recv[2] + s_recv[3] + bias[...]

    def mod_copy(k):
        return send(m_own.at[col], m_own.at[col], m_sems.at[0, k], m_sems.at[1, col], (row, (col + k) % cols_n))

    def mod_got(k):
        src = (col + k) % cols_n
        return send(m_own.at[src], m_own.at[src], m_sems.at[0, k], m_sems.at[1, src], (row, src))

    for k in range(1, cols_n):
        mod_copy(k).start()
    pump_to(0, 2)
    for k in range(1, cols_n):
        mod_got(k).wait_recv()
    other = send(m_own, m_oth, o_sems.at[0], o_sems.at[1], place.to_core)
    other.start()
    pump_to(0, 3)
    other.wait_recv()
    stay = place.h == place.x
    for c in range(cols_n):
        line = jnp.where(stay, m_own[c, pl.ds(place.z, 1), :], m_oth[c, pl.ds(place.z, 1), :])
        for k in range(6):
            vec[k:k + 1, c * hc:(c + 1) * hc] = line[:, k * hc:(k + 1) * hc]
        line = m_own[c, 4:5, :]
        vec[6:7, c * hc:(c + 1) * hc] = line[:, 576:576 + hc]
        vec[7:8, c * hc:(c + 1) * hc] = line[:, 576 + hc:]
        z, i = c // 2, c % 2
        vec[16 + z:17 + z, i * 512:(i + 1) * 512] = line[:, :512]
        vec[16 + z:17 + z, 1024 + i * 64:1024 + (i + 1) * 64] = line[:, 512:576]

    swap_x.wait()
    swap_dy = Swap(place, cot, o_cot, swap_sems, 1)
    swap_dy.start()
    part = 128

    def row_parts(body):
        @pl.loop(0, tokens // part)
        def _(i):
            body(pl.ds(pl.multiple_of(i * part, part), part))

    def first_norm(at_rows):
        normal, _ = norm_rows(x_v[at_rows, :].astype(f32))
        n1[at_rows, :] = (normal * (1.0 + vec[1:2, :]) + vec[0:1, :]).astype(bf16)

    row_parts(first_norm)

    saves = []

    def save(src, dst):
        copy = pltpu.make_async_copy(src, dst, save_sems.at[len(saves)])
        copy.start()
        saves.append(copy)

    save(x_v, o_x)
    save(n1, o_n1)

    def fetch(s):
        g, t = chunks[s]
        zc, slot = work.zc(t), s % depth
        lanes = [q_main, p_main] if g == 0 else [blocks[members[g][0]].shape[1]]
        spot, copies = 0, []
        for i, n in enumerate(lanes):
            src = fulls[members[g][i]].at[:, pl.ds(pl.multiple_of(zc * 2 * n, 128), 2 * n)]
            copies.append(pltpu.make_async_copy(src, wbuf.at[slot, :, spot:spot + 2 * n], w_sems.at[s % 2, i]))
            spot += 2 * n
        src = fulls[members[g][-1]].at[:, pl.ds(pl.multiple_of(zc * 256, 128), 256)]
        copies.append(pltpu.make_async_copy(src, lbuf.at[s % 2], w_sems.at[s % 2, 2]))
        return copies

    def fetch_start(s):
        pump_to(s, 4)
        if s >= depth:
            weight_save(s - depth).wait()
        for copy in fetch(s):
            copy.start()

    def fetch_wait(s):
        for copy in fetch(s):
            copy.wait()
        unfold_into(lbuf.at[s % 2], wbuf.at[s % depth, :, 1024:1152])
        weight_save(s).start()

    def weight_save(s):
        g, t = chunks[s]
        return pltpu.make_async_copy(wbuf.at[s % depth], o_w.at[g, work.zc(t)], wsave_sems.at[s])

    def swap_kv(i, h):
        src, dst = ((k_v, k2_v), (v_v, v2_v))[i]
        return send(src.at[h], dst.at[h], kv_sems.at[0, i, h], kv_sems.at[1, i, h], place.to_core)

    def project(s):
        t, slot = chunks[s][1], s % depth
        zc = work.zc(t)

        @pl.loop(0, 2)
        def _(i):
            at_rows = pl.ds(pl.multiple_of(i * half, half), half)
            main = nn(n1[at_rows, :], wbuf[slot, :, :2 * q_main])
            left = nn(n1[at_rows, :], wbuf[slot, :, 1024:1152])
            for j in range(2):
                biases = m_own[2 * zc + j]
                own = main[:, j * q_main:(j + 1) * q_main]
                tail = left[:, j * 64:j * 64 + 3 * hc - q_main]
                for e in range(2):
                    h = 4 * zc + 2 * j + e
                    a = e * HEAD_DIM
                    q_v[h, at_rows, :] = (own[:, a:a + HEAD_DIM] + biases[5:6, a:a + HEAD_DIM]).astype(bf16)
                    k_v[h, at_rows, :] = own[:, hc + a:hc + a + HEAD_DIM].astype(bf16)
                    if e == 0:
                        value = own[:, 2 * hc:2 * hc + HEAD_DIM]
                    else:
                        value = jnp.concatenate([own[:, 2 * hc + HEAD_DIM:], tail], axis=1)
                    v_v[h, at_rows, :] = (value + biases[5:6, hc + a:hc + a + HEAD_DIM]).astype(bf16)

        for i in range(4):
            swap_kv(0, 4 * zc + i).start()
            swap_kv(1, 4 * zc + i).start()

    def attention(s):
        zc = work.zc(chunks[s][1])
        start = at[0]

        @pl.loop(0, 4)
        def _(i):
            h = 4 * zc + i
            swap_kv(0, h).wait_recv()
            swap_kv(1, h).wait_recv()
            one, two, total, lse = softmax_head(q_v[h], k_v[h], k2_v[h])
            ot[i] = (tn(v_v[h], one) + tn(v2_v[h], two)) / total
            lse_v[h] = lse
            for k in range(4):
                at[0] = start + k

                @pl.when(i == k)
                def _():
                    pump(1)

        at[0] = start + 4
        att[zc, :, 2 * p_main:] = jnp.zeros((tokens, 128), bf16)
        for j in range(2):
            pair = jnp.concatenate([ot[2 * j], ot[2 * j + 1]], axis=0).T.astype(bf16)
            att[zc, :, j * p_main:(j + 1) * p_main] = pair[:, :p_main]
            att[zc, :, 2 * p_main + 64 * j + 48:2 * p_main + 64 * j + 64] = pair[:, p_main:]

        @pl.loop(0, 2)
        def _(i):
            at_rows = pl.ds(pl.multiple_of(i * half, half), half)
            term = nt(att[zc, at_rows, :], wbuf[s % depth, :, 2 * q_main:])
            if s == 0:
                acc[at_rows, :] = term
            else:
                acc[at_rows, :] += term

    for s in range(depth):
        fetch_start(s)
        fetch_wait(s)
        project(s)
        if s > 0:
            attention(s - 1)
    attention(depth - 1)
    for src, dst in ((q_v, o_q), (k_v, o_k), (v_v, o_v), (k2_v, o_k2), (v2_v, o_v2), (lse_v, o_lse), (att, o_att)):
        save(src, dst)

    def second_norm(at_rows):
        branch = acc[at_rows, :] + vec[6:7, :]
        ba[at_rows, :] = branch.astype(bf16)
        middle = x_v[at_rows, :].astype(f32) + vec[2:3, :] * branch
        mid[at_rows, :] = middle
        normal, _ = norm_rows(middle)
        n2[at_rows, :] = (normal * (1.0 + vec[4:5, :]) + vec[3:4, :]).astype(bf16)

    row_parts(second_norm)
    for src, dst in ((ba, o_ba), (mid, o_mid), (n2, o_n2)):
        save(src, dst)

    for s in range(depth, 2 * depth):
        fetch_start(s)
        fetch_wait(s)
        zc = work.zc(chunks[s][1])

        def up(at_rows):
            u = nn(n2[at_rows, :], wbuf[s % depth]) + vec[pl.ds(16 + zc, 1), :]
            value, slope = gelu_both(u)
            hid[zc, at_rows, :] = value.astype(bf16)
            slo[zc, at_rows, :] = slope.astype(bf16)

        row_parts(up)
    save(hid, o_hid)
    save(slo, o_slo)
    for s in range(2 * depth, 3 * depth):
        fetch_start(s)
        fetch_wait(s)
        zc = work.zc(chunks[s][1])

        def down(at_rows):
            term = nt(hid[zc, at_rows, :], wbuf[s % depth])
            if s == 2 * depth:
                acc[at_rows, :] = term
            else:
                acc[at_rows, :] += term

        row_parts(down)

    swap_dy.wait()
    load_dy = pltpu.make_async_copy(o_cot, cot_v, w_sems.at[0, 0])
    load_dy.start()
    load_dy.wait()
    vec[8:9, :] = jnp.zeros((1, width), f32)

    def finish(at_rows):
        branch = acc[at_rows, :] + vec[7:8, :]
        out_v[at_rows, :] = (mid[at_rows, :] + vec[5:6, :] * branch).astype(bf16)
        vec[8:9, :] += jnp.sum(cot_v[at_rows, :].astype(f32) * branch, axis=0, keepdims=True)

    row_parts(finish)
    save(out_v, o_out)
    save(vec, o_vec)

    for a in range(7):
        work.finish(a)
    for k in range(1, rows_n):
        cond_copy(k).wait_send()
        sum_copy(k).wait_send()
    for k in range(1, cols_n):
        mod_copy(k).wait_send()
    other.wait_send()

    @pl.loop(0, 4 * depth)
    def _(h):
        swap_kv(0, h).wait_send()
        swap_kv(1, h).wait_send()

    for s in range(2 * depth, 3 * depth):
        weight_save(s).wait()
    for copy in saves:
        copy.wait()


def forward(lat, cot, cond, ada, bias, blocks, collective_id):
    rows, cols = lax.axis_size("row"), lax.axis_size("col")
    depth = cols // 2
    tokens, width = lat.shape
    heads = width // HEAD_DIM
    lanes = 1152
    hc6 = ada.shape[1]
    shape = jax.ShapeDtypeStruct
    head = shape((heads, tokens, HEAD_DIM), bf16)
    token = shape((tokens, width), bf16)
    outs = [shape((rows * b.shape[0], cols * b.shape[1]), bf16) for b in blocks] + [
        shape((3, depth, width, lanes), bf16), token, token, token, head, head, head, head, head,
        shape((heads, 1, tokens), f32), shape((depth, tokens, 384), bf16), token, shape((tokens, width), f32), token,
        shape((depth, tokens, lanes), bf16), shape((depth, tokens, lanes), bf16), token, shape((VECS, width), f32)]
    dma, vm = pltpu.SemaphoreType.DMA, pltpu.VMEM
    t16, h16 = vm((tokens, width), bf16), vm((heads, tokens, HEAD_DIM), bf16)
    drows = ada.shape[0]
    scratch = [
        t16, t16, h16, h16, h16, h16, h16, vm((heads, 1, tokens), f32), vm((4, HEAD_DIM, tokens), f32),
        vm((depth, tokens, 384), bf16), t16, vm((tokens, width), f32), t16, vm((depth, tokens, lanes), bf16),
        vm((depth, tokens, lanes), bf16), vm((tokens, width), f32), vm((depth, width, lanes), bf16), vm((2, width // 2, 256), bf16),
        t16, t16, vm((VECS, width), f32), vm((rows, 8, drows), f32), vm((rows, 8, drows), f32), vm((rows, 8, hc6), f32),
        vm((rows, 8, hc6), f32), vm((cols, 8, hc6), f32), vm((cols, 8, hc6), f32)]
    scratch += Gather.scratch(len(blocks), depth)
    scratch += [dma((2, 2)), dma((2, rows)), dma((2, rows)), dma((2, cols)), dma((2,)), dma((2, 2, heads)), dma((2, 3)), dma((32,)),
                dma((3 * depth,))]
    vmem = pl.BlockSpec(memory_space=pltpu.VMEM)
    got = pl.pallas_call(
        forward_kernel,
        out_shape=outs,
        in_specs=[ANY, ANY, vmem, vmem, vmem] + [ANY] * len(blocks),
        out_specs=[ANY] * len(outs),
        scratch_shapes=scratch,
        compiler_params=pltpu.CompilerParams(collective_id=collective_id, has_side_effects=True, vmem_limit_bytes=62 * 2**20),
        name="forward",
    )(lat, cot, cond, ada, bias, *blocks)
    return got[len(blocks):]


class ZScatter(Scatter):
    def __init__(self, place, sources, outs, bufs, sems, parts):
        super().__init__(place, sources, outs, bufs, sems)
        self.parts = parts

    def block(self, a, p, q, z, h):
        y, x = jnp.where(h == 0, p, q), jnp.where(h == 0, q, p)
        rows, lanes = self.outs[a].shape
        g, first, depth_rows = self.parts[a]
        r = 2 * y + h
        if first is None:
            spot, lane = r * depth_rows + x * rows, 1024
        else:
            spot, lane = r * depth_rows, first + x * lanes
        return self.ins[g].at[z, pl.ds(pl.multiple_of(spot, 16), rows), pl.ds(pl.multiple_of(lane, 128) if first is not None else lane, lanes)]


def zscatter_kernel(groups, parts, *refs):
    count = sum(groups)
    ins, outs = refs[:3], refs[3:3 + count]
    bufs, sems = Scatter.split(refs[3 + count:], count)
    place = Place()
    greet(place.partners())
    work = ZScatter(place, ins, outs, bufs, sems, parts)
    chunks = chunk_list(groups, place.depth)
    for s in range(len(chunks) + 4):
        for n in range(5):
            if 0 <= s - n < len(chunks):
                for a, t in chunks[s - n]:
                    work.stage(a, t, n)
    for a in range(count):
        work.finish(a)


def zscatter_all(fulls, shapes, groups, parts, collective_id):
    cols = lax.axis_size("col")
    return pl.pallas_call(
        functools.partial(zscatter_kernel, groups, parts),
        out_shape=[jax.ShapeDtypeStruct(s, jnp.float32) for s in shapes],
        in_specs=[ANY] * len(fulls),
        out_specs=[pl.BlockSpec(memory_space=pltpu.VMEM)] * len(shapes),
        scratch_shapes=Scatter.scratch(shapes, cols // 2),
        compiler_params=pltpu.CompilerParams(collective_id=collective_id, has_side_effects=True, vmem_limit_bytes=58 * 2**20),
        name="scatter_grads",
    )(*fulls)


class Plan:
    def __init__(self, latents, condition, qkv_weight, fc1_weight):
        self.rows, self.cols = lax.axis_size("row"), lax.axis_size("col")
        self.tokens, self.width = latents.shape
        self.lats = condition.shape[0]
        self.depth_rows = qkv_weight.shape[0]
        self.head_cols = qkv_weight.shape[2]
        self.ff_cols = fc1_weight.shape[1]
        self.share = SEQ // self.tokens
        q_left, p_left, f_left = (3 * self.head_cols) % 128, self.head_cols % 128, self.ff_cols % 128
        self.near = (
            self.rows == 4 and self.share == 2 and self.cols % 2 == 0 and self.lats == self.cols // 2
            and self.depth_rows % 32 == 0 and self.tokens % 128 == 0 and q_left + p_left == 64 and f_left == 64)
        self.q_left, self.p_left, self.f_left = (q_left, p_left, f_left) if self.near else (0, 0, 0)
        self.q_main, self.p_main = 3 * self.head_cols - self.q_left, self.head_cols - self.p_left
        self.f_main = self.ff_cols - self.f_left

    def fold(self, left):
        rows, lanes = left.shape
        return left.reshape(2, rows // 2, lanes).transpose(1, 0, 2).reshape(rows // 2, 2 * lanes)

    def unfold(self, left):
        rows, lanes = left.shape
        return left.reshape(rows, 2, lanes // 2).transpose(1, 0, 2).reshape(2 * rows, lanes // 2)

    def fold_full(self, left):
        half = self.depth_rows // 2
        return left.reshape(self.rows, 2, half, self.cols, 64).transpose(0, 2, 3, 1, 4).reshape(self.rows * half, self.cols * 128)

    def unfold_full(self, left):
        half = self.depth_rows // 2
        return left.reshape(self.rows, half, self.cols, 2, 64).transpose(0, 3, 1, 2, 4).reshape(self.width, self.cols * 64)

    def swap_pairs(self):
        pairs = []
        for row in range(self.rows):
            for col in range(self.cols):
                there = (row - row % 2 + col % 2) * self.cols + col - col % 2 + row % 2
                pairs.append((row * self.cols + col, there))
        return pairs

    def swap(self, value):
        return lax.ppermute(value, ("row", "col"), self.swap_pairs()) if self.near else value


def gather_plain(blocks):
    return [lax.all_gather(lax.all_gather(b, "row", axis=0, tiled=True), "col", axis=1, tiled=True) for b in blocks]


def scatter_plain(fulls):
    parts = [lax.psum_scatter(g, "row", scatter_dimension=0, tiled=True) for g in fulls]
    return [lax.psum_scatter(g, "col", scatter_dimension=1, tiled=True).astype(f32) for g in parts]


def attend_plain(q, k, v):
    def one(item):
        scores = nt(item[0], item[1]) * HEAD_DIM ** (-0.5)
        top = jnp.max(scores, axis=-1, keepdims=True)
        probs = jnp.exp(scores - top)
        total = jnp.sum(probs, axis=-1, keepdims=True)
        return nn((probs / total).astype(bf16), item[2]).astype(bf16), top + jnp.log(total)

    return lax.map(one, (q, k, v))


def attend_back_plain(q, k, v, lse, att_grad):
    def one(item):
        q, k, v, lse, out_grad = item
        probs = jnp.exp(nt(q, k) * HEAD_DIM ** (-0.5) - lse)
        probs_grad = nt(out_grad, v)
        inner = jnp.sum(probs * probs_grad, axis=-1, keepdims=True)
        grad = (probs * (probs_grad - inner) * HEAD_DIM ** (-0.5)).astype(bf16)
        return nn(grad, k), tn(grad, q), tn(probs.astype(bf16), out_grad)

    return lax.map(one, (q, k, v, lse, att_grad))


def gelu_and_slope(u):
    c = math.sqrt(2.0 / math.pi)
    inner = jnp.tanh(c * (u + 0.044715 * u * u * u))
    value = 0.5 * u * (1.0 + inner)
    slope = 0.5 * (1.0 + inner) + 0.5 * u * (1.0 - inner * inner) * c * (1.0 + 3 * 0.044715 * u * u)
    return value, slope


def layer_norm(values):
    mean = jnp.mean(values, axis=-1, keepdims=True)
    centred = values - mean
    inverse = lax.rsqrt(jnp.mean(centred * centred, axis=-1, keepdims=True) + norm_eps)
    return centred * inverse, inverse


def norm_back(rows_grad, normal, inverse, scale):
    normal_grad = rows_grad * (1.0 + scale)
    first = jnp.mean(normal_grad, axis=-1, keepdims=True)
    second = jnp.mean(normal_grad * normal, axis=-1, keepdims=True)
    value_grad = inverse * (normal_grad - first - normal * second)
    return value_grad, jnp.sum(rows_grad, axis=0), jnp.sum(rows_grad * normal, axis=0)


def shards_near(plan, latents, condition, ada_weight, ada_bias, qkv_weight, qv_bias, proj_weight, proj_bias,
                fc1_weight, fc1_bias, fc2_weight, fc2_bias, cotangent):
    row, col = lax.axis_index("row"), lax.axis_index("col")
    rows, cols, width, tokens = plan.rows, plan.cols, plan.width, plan.tokens
    depth, hc, fc = plan.depth_rows, plan.head_cols, plan.ff_cols
    zs = cols // 2
    heads = cols * hc // HEAD_DIM
    groups = rows * plan.lats
    qkv_flat = qkv_weight.reshape(depth, 3 * hc)
    proj_t, fc2_t = proj_weight.T, fc2_weight.T
    left_a = plan.fold(jnp.concatenate([qkv_flat[:, plan.q_main:], proj_t[:, plan.p_main:]], axis=1))
    blocks = [qkv_flat[:, :plan.q_main], proj_t[:, :plan.p_main], left_a,
              fc1_weight[:, :plan.f_main], plan.fold(fc1_weight[:, plan.f_main:]),
              fc2_t[:, :plan.f_main], plan.fold(fc2_t[:, plan.f_main:])]
    cond8 = jnp.pad(condition.astype(f32), ((0, 8 - plan.lats), (0, 0)))
    ada_flat = ada_weight.reshape(depth, 6 * hc)
    line = jnp.concatenate([fc1_bias, proj_bias, fc2_bias]).astype(f32).reshape(1, 6 * hc)
    tail = jnp.pad(qv_bias.astype(f32).reshape(1, 2 * hc), ((0, 0), (0, 4 * hc)))
    bias = jnp.concatenate([jnp.broadcast_to(ada_bias.astype(f32).reshape(1, 6 * hc), (plan.lats, 6 * hc)), line, tail,
                            jnp.zeros((8 - plan.lats - 2, 6 * hc), f32)], axis=0)
    (w, grad_out, values, normed_one, query, key, value, key_two, value_two, lse, att, branch_a, middle, normed_two,
     hidden, slope, out, vec) = forward(latents, cotangent, cond8, ada_flat, bias, blocks, 0)
    output = plan.swap(out)
    values, grad_out, branch_a = values.astype(f32), grad_out.astype(f32), branch_a.astype(f32)
    shift_one, scale_one, gate_one, shift_two, scale_two, gate_two = (vec[k:k + 1] for k in range(6))
    gate_two_grad = vec[8]
    normal_one, inverse_one = layer_norm(values)
    normal_two, inverse_two = layer_norm(middle)
    cond_all = lax.all_gather(condition, "row", axis=0, tiled=True).astype(f32)
    cond_act = jax.nn.silu(cond_all).astype(bf16)
    cond_mine = lax.dynamic_slice(cond_act, (0, row * depth), (groups, depth))

    def to_heads(flat):
        return flat.reshape(tokens, heads, HEAD_DIM).transpose(1, 0, 2)

    def from_heads(value):
        return value.transpose(1, 0, 2).reshape(tokens, cols, hc)

    m_grad = grad_out * gate_two
    fc2_bias_part = jnp.sum(m_grad, axis=0)
    m_low = m_grad.astype(bf16)
    fc2_grad = jnp.stack([tn(m_low, hidden[z]).astype(bf16) for z in range(zs)])
    pre_grad = [nn(m_low, w[2, z]) * slope[z] for z in range(zs)]
    fc1_bias_part = jnp.stack([jnp.sum(u, axis=0) for u in pre_grad])
    pre_low = [u.astype(bf16) for u in pre_grad]
    fc1_grad = jnp.stack([tn(normed_two, u).astype(bf16) for u in pre_low])
    normed_two_grad = sum(nt(u, w[1, z]) for z, u in enumerate(pre_low))
    middle_part, shift_two_grad, scale_two_grad = norm_back(normed_two_grad, normal_two, inverse_two, scale_two)
    middle_grad = grad_out + middle_part
    gate_one_grad = jnp.sum(middle_grad * branch_a, axis=0)
    a_grad = middle_grad * gate_one
    proj_bias_part = jnp.sum(a_grad, axis=0)
    a_low = a_grad.astype(bf16)
    qm, pm, ql = 2 * plan.q_main, 2 * plan.p_main, plan.q_left

    att_grads, proj_grads = [], []
    for z in range(zs):
        got = nn(a_low, w[0, z, :, qm:])
        for j in range(2):
            att_grads.append(jnp.concatenate(
                [got[:, j * plan.p_main:(j + 1) * plan.p_main], got[:, pm + 64 * j + ql:pm + 64 * (j + 1)]], axis=1))
        proj_grads.append(tn(a_low, att[z]))
    att_grad = to_heads(jnp.concatenate(att_grads, axis=1).astype(bf16))
    att_pairs = []
    for z in range(zs):
        for j in range(2):
            att_pairs.append(jnp.concatenate(
                [att[z][:, j * plan.p_main:(j + 1) * plan.p_main], att[z][:, pm + 64 * j + ql:pm + 64 * (j + 1)]], axis=1))
    att_heads = to_heads(jnp.concatenate(att_pairs, axis=1))
    query_grad, key_grad, value_grad = attend_back(query, key, value, key_two, value_two, lse, att_heads, att_grad, 3)
    q_bias_part, v_bias_part = jnp.sum(query_grad, axis=1), jnp.sum(value_grad, axis=1)
    qkv_low = jnp.concatenate([from_heads(g.astype(bf16)) for g in (query_grad, key_grad, value_grad)], axis=2)
    att_wgrads, normed_one_grad = [], 0.0
    for z in range(zs):
        pair = qkv_low[:, 2 * z:2 * z + 2]
        main = pair[:, :, :plan.q_main].reshape(tokens, qm)
        left = jnp.pad(pair[:, :, plan.q_main:], ((0, 0), (0, 0), (0, 64 - ql))).reshape(tokens, 128)
        both = jnp.concatenate([main, left], axis=1)
        normed_one_grad = normed_one_grad + nt(main, w[0, z, :, :qm]) + nt(left, w[0, z, :, qm + pm:])
        got = tn(normed_one, both)
        att_wgrads.append(jnp.concatenate(
            [got[:, :qm], proj_grads[z][:, :pm], got[:, qm:] + proj_grads[z][:, pm:]], axis=1).astype(bf16))
    att_wgrad = jnp.stack(att_wgrads)
    half = depth // 2
    shapes = [(depth, plan.f_main), (half, 128), (depth, plan.f_main), (half, 128), (depth, plan.q_main), (depth, plan.p_main), (half, 128)]
    parts = [(0, 0, depth), (0, None, depth), (1, 0, depth), (1, None, depth), (2, 0, depth), (2, qm, depth), (2, None, depth)]
    sums = zscatter_all([fc2_grad, fc1_grad, att_wgrad], shapes, (2, 2, 3), parts, 1)
    lefts = jnp.stack([sums[1], sums[3], sums[6]])
    x = col % 2
    give = jnp.where(x == 0, lefts[:, :, 64:], lefts[:, :, :64])
    keep = jnp.where(x == 0, lefts[:, :, :64], lefts[:, :, 64:])
    got = lax.ppermute(give, "col", [(i, i + 1 - 2 * (i % 2)) for i in range(cols)])
    lefts = jnp.where(x == 0, jnp.concatenate([keep, got], axis=1), jnp.concatenate([got, keep], axis=1))
    fc2_sum = jnp.concatenate([sums[0], lefts[0]], axis=1)
    fc1_sum = jnp.concatenate([sums[2], lefts[1]], axis=1)
    qkv_sum = jnp.concatenate([sums[4], lefts[2][:, :ql]], axis=1)
    proj_sum = jnp.concatenate([sums[5], lefts[2][:, ql:]], axis=1)
    input_part, shift_one_grad, scale_one_grad = norm_back(normed_one_grad, normal_one, inverse_one, scale_one)
    latents_grad = plan.swap((middle_grad + input_part).astype(bf16)).astype(f32)
    mod_grad = jnp.stack(
        [shift_one_grad, scale_one_grad, gate_one_grad, shift_two_grad, scale_two_grad, gate_two_grad], axis=0)
    fc1_flat = jnp.concatenate([fc1_bias_part[:, :1024].reshape(-1), fc1_bias_part[:, 1024:].reshape(-1)])
    fc1_parts = [fc1_flat[:cols * plan.f_main], fc1_flat[cols * plan.f_main:]]
    return finish(plan, condition, cond_mine, ada_flat, mod_grad,
                  [proj_bias_part, fc2_bias_part, q_bias_part, v_bias_part] + fc1_parts,
                  (output, latents_grad, qkv_sum, proj_sum, fc1_sum, fc2_sum))


def finish(plan, condition, cond_mine, ada_flat, mod_grad, bias_parts, done):
    output, latents_grad, qkv_sum, proj_sum, fc1_sum, fc2_sum = done
    row, col = lax.axis_index("row"), lax.axis_index("col")
    rows, cols, width, depth, hc = plan.rows, plan.cols, plan.width, plan.depth_rows, plan.head_cols
    groups = rows * plan.lats
    mod_grad = lax.all_gather(mod_grad, ("row", "col"), axis=0, tiled=False)
    if plan.near:
        mod_grad = mod_grad.reshape(rows // 2, 2, cols // 2, 2, 6, width).sum(axis=1).transpose(0, 2, 1, 3, 4)
    else:
        mod_grad = mod_grad.reshape(rows, cols // plan.share, plan.share, 6, width).sum(axis=2)
    mod_grad = mod_grad.reshape(groups, 6, width)
    mod_mine = lax.dynamic_slice(mod_grad, (0, 0, col * hc), (groups, 6, hc))
    ada_bsum = jnp.sum(mod_mine, axis=0)
    mod_low = mod_mine.astype(bf16).reshape(groups, 6 * hc)
    ada_wsum = tn(cond_mine, mod_low).reshape(depth, 6, hc)
    cond_part = lax.dynamic_update_slice(jnp.zeros((groups, width), f32), nt(mod_low, ada_flat), (0, row * depth))
    parts = [cond_part] + bias_parts
    totals = lax.psum(jnp.concatenate([part.reshape(-1) for part in parts]), ("row", "col"))
    ends, spot = [], 0
    for part in parts:
        ends.append(totals[spot:spot + part.size])
        spot += part.size

    def mine(flat, size):
        return lax.dynamic_slice(flat, (col * size,), (size,))

    cond_summed = lax.dynamic_slice(ends[0].reshape(groups, width), (row * plan.lats, 0), (plan.lats, width))
    silu_value, silu_pull = jax.vjp(jax.nn.silu, condition.astype(f32))
    condition_grad = silu_pull(cond_summed)[0]
    proj_bsum, fc2_bsum = mine(ends[1], hc), mine(ends[2], hc)
    qv_bsum = jnp.stack([mine(ends[3], hc), mine(ends[4], hc)], axis=0)
    fc1_bsum = jnp.concatenate([mine(flat, flat.size // cols) for flat in ends[5:]])
    return (
        output, latents_grad, condition_grad, ada_wsum, ada_bsum, qkv_sum.reshape(depth, 3, hc), qv_bsum,
        proj_sum.T, proj_bsum, fc1_sum, fc1_bsum, fc2_sum.T, fc2_bsum)


def shards(latents, condition, ada_weight, ada_bias, qkv_weight, qv_bias, proj_weight, proj_bias,
           fc1_weight, fc1_bias, fc2_weight, fc2_bias, cotangent):
    plan = Plan(latents, condition, qkv_weight, fc1_weight)
    if plan.near:
        return shards_near(plan, latents, condition, ada_weight, ada_bias, qkv_weight, qv_bias, proj_weight, proj_bias,
                           fc1_weight, fc1_bias, fc2_weight, fc2_bias, cotangent)
    row, col = lax.axis_index("row"), lax.axis_index("col")
    rows, cols, width, tokens = plan.rows, plan.cols, plan.width, plan.tokens
    depth, hc, fc = plan.depth_rows, plan.head_cols, plan.ff_cols
    heads = cols * hc // HEAD_DIM
    groups = rows * plan.lats

    qkv_flat = qkv_weight.reshape(depth, 3 * hc)
    proj_t, fc2_t = proj_weight.T, fc2_weight.T
    blocks = [qkv_flat[:, :plan.q_main], proj_t[:, :plan.p_main], fc1_weight[:, :plan.f_main], fc2_t[:, :plan.f_main]]
    if plan.near:
        left_a = plan.fold(jnp.concatenate([qkv_flat[:, plan.q_main:], proj_t[:, plan.p_main:]], axis=1))
        blocks += [left_a, plan.fold(fc1_weight[:, plan.f_main:]), plan.fold(fc2_t[:, plan.f_main:])]
        order = (0, 1, 4, 2, 5, 3, 6)
        full = [None] * 7
        for i, w in zip(order, gather_all([blocks[i] for i in order], (3, 2, 2), 0)):
            full[i] = w
        full[4:] = [plan.unfold_full(w) for w in full[4:]]
    else:
        full = gather_plain(blocks)

    if plan.near:
        home = (row - row % 2 + col % 2) * plan.lats + col // 2
    else:
        home = row * plan.lats + col // plan.share
    values = plan.swap(latents).astype(f32)
    grad_out = plan.swap(cotangent).astype(f32)

    cond_all = lax.all_gather(condition, "row", axis=0, tiled=True).astype(f32)
    cond_act = jax.nn.silu(cond_all).astype(bf16)
    cond_mine = lax.dynamic_slice(cond_act, (0, row * depth), (groups, depth))
    ada_flat = ada_weight.reshape(depth, 6 * hc)
    partial = lax.psum(nn(cond_mine, ada_flat), "row") + ada_bias.astype(f32).reshape(1, 6 * hc)
    small = jnp.concatenate(
        [partial.reshape(-1)] + [b.astype(f32).reshape(-1) for b in (proj_bias, fc2_bias, fc1_bias, qv_bias)])
    small = lax.all_gather(small, "col", axis=0, tiled=False)
    sizes = [groups * 6 * hc, hc, hc, fc, 2 * hc]
    mod_all, proj_b, fc2_b, fc1_b, qv_b = jnp.split(small, [sum(sizes[:i + 1]) for i in range(4)], axis=1)
    mod = lax.dynamic_index_in_dim(mod_all.reshape(cols, groups, 6, hc), home, 1, keepdims=False)
    mod = mod.transpose(1, 0, 2).reshape(6, 1, width)
    shift_one, scale_one, gate_one, shift_two, scale_two, gate_two = (mod[k] for k in range(6))
    proj_b, fc2_b = proj_b.reshape(width), fc2_b.reshape(width)
    q_b, v_b = qv_b[:, :hc].reshape(heads, 1, HEAD_DIM), qv_b[:, hc:].reshape(heads, 1, HEAD_DIM)
    fc1_parts = [fc1_b[:, :plan.f_main].reshape(-1)]
    if plan.near:
        fc1_parts.append(fc1_b[:, plan.f_main:].reshape(-1))

    def to_heads(flat):
        return flat.reshape(tokens, heads, HEAD_DIM).transpose(1, 0, 2)

    def from_heads(value):
        return value.transpose(1, 0, 2).reshape(tokens, cols, hc)

    normal_one, inverse_one = layer_norm(values)
    normed_one = (normal_one * (1.0 + scale_one) + shift_one).astype(bf16)
    projected = nn(normed_one, full[0]).reshape(tokens, cols, plan.q_main)
    if plan.near:
        left_w = full[4].reshape(width, cols, 64)
        left_q, left_p = left_w[:, :, :plan.q_left].reshape(width, -1), left_w[:, :, plan.q_left:].reshape(width, -1)
        projected = jnp.concatenate([projected, nn(normed_one, left_q).reshape(tokens, cols, plan.q_left)], axis=2)
    query = (to_heads(projected[:, :, :hc]) + q_b).astype(bf16)
    key = to_heads(projected[:, :, hc:2 * hc]).astype(bf16)
    value = (to_heads(projected[:, :, 2 * hc:]) + v_b).astype(bf16)
    if plan.near:
        att, lse, key_two, value_two = attend(query, key, value, 2)
    else:
        cuts = [[s * plan.share + i for i in range(plan.share)] for s in range(cols // plan.share)]
        key_all = lax.all_gather(key, "col", axis=1, tiled=True, axis_index_groups=cuts)
        value_all = lax.all_gather(value, "col", axis=1, tiled=True, axis_index_groups=cuts)
        att, lse = attend_plain(query, key_all, value_all)
    att_flat = from_heads(att)
    att_main = att_flat[:, :, :plan.p_main].reshape(tokens, -1)
    branch_a = nt(att_main, full[1])
    if plan.near:
        att_left = att_flat[:, :, plan.p_main:]
        branch_a = branch_a + nt(att_left.reshape(tokens, -1), left_p)
    branch_a = branch_a + proj_b
    middle = values + gate_one * branch_a

    count = len(fc1_parts)
    fc1_w, fc2_w = (full[2], full[5])[:count] if plan.near else (full[2],), (full[3], full[6])[:count] if plan.near else (full[3],)
    normal_two, inverse_two = layer_norm(middle)
    normed_two = (normal_two * (1.0 + scale_two) + shift_two).astype(bf16)
    pre = [nn(normed_two, w) + b for w, b in zip(fc1_w, fc1_parts)]
    hidden, slope = zip(*[gelu_and_slope(u) for u in pre])
    hidden = [u.astype(bf16) for u in hidden]
    branch_m = sum(nt(u, w) for u, w in zip(hidden, fc2_w)) + fc2_b
    output = plan.swap((middle + gate_two * branch_m).astype(bf16))

    gate_two_grad = jnp.sum(grad_out * branch_m, axis=0)
    m_grad = grad_out * gate_two
    fc2_bias_part = jnp.sum(m_grad, axis=0)
    m_low = m_grad.astype(bf16)
    fc2_grads = [tn(m_low, u).astype(bf16) for u in hidden]
    pre_grads = [nn(m_low, w) * s for w, s in zip(fc2_w, slope)]
    fc1_bias_parts = [jnp.sum(u, axis=0) for u in pre_grads]
    pre_low = [u.astype(bf16) for u in pre_grads]
    fc1_grads = [tn(normed_two, u).astype(bf16) for u in pre_low]
    normed_two_grad = sum(nt(u, w) for u, w in zip(pre_low, fc1_w))
    middle_part, shift_two_grad, scale_two_grad = norm_back(normed_two_grad, normal_two, inverse_two, scale_two)
    middle_grad = grad_out + middle_part
    gate_one_grad = jnp.sum(middle_grad * branch_a, axis=0)
    a_grad = middle_grad * gate_one
    proj_bias_part = jnp.sum(a_grad, axis=0)
    a_low = a_grad.astype(bf16)
    proj_grad = tn(a_low, att_main).astype(bf16)
    att_grad = nn(a_low, full[1]).reshape(tokens, cols, plan.p_main)
    if plan.near:
        att_grad = jnp.concatenate([att_grad, nn(a_low, left_p).reshape(tokens, cols, plan.p_left)], axis=2)
    att_grad = to_heads(att_grad.astype(bf16))
    if plan.near:
        query_grad, key_grad, value_grad = attend_back(query, key, value, key_two, value_two, lse, att, att_grad, 3)
    else:
        query_grad, key_grad, value_grad = attend_back_plain(query, key_all, value_all, lse, att_grad)
        key_grad, value_grad = (
            lax.psum_scatter(g.astype(bf16), "col", scatter_dimension=1, tiled=True, axis_index_groups=cuts).astype(f32)
            for g in (key_grad, value_grad))
    q_bias_part, v_bias_part = jnp.sum(query_grad, axis=1), jnp.sum(value_grad, axis=1)
    qkv_low = jnp.concatenate([from_heads(g.astype(bf16)) for g in (query_grad, key_grad, value_grad)], axis=2)
    low_main = qkv_low[:, :, :plan.q_main].reshape(tokens, -1)
    qkv_grad = tn(normed_one, low_main).astype(bf16)
    normed_one_grad = nt(low_main, full[0])
    if plan.near:
        low_left = qkv_low[:, :, plan.q_main:]
        normed_one_grad = normed_one_grad + nt(low_left.reshape(tokens, -1), left_q)
        left_grad = jnp.concatenate(
            [tn(normed_one, low_left.reshape(tokens, -1)).reshape(width, cols, -1),
             tn(a_low, att_left.reshape(tokens, -1)).reshape(width, cols, -1)], axis=2).reshape(width, cols * 64).astype(bf16)
        grads = [fc2_grads[0], plan.fold_full(fc2_grads[1]), fc1_grads[0], plan.fold_full(fc1_grads[1]),
                 qkv_grad, proj_grad, plan.fold_full(left_grad)]
        sums = scatter_all(grads, (2, 2, 3), 1)
        fc2_sum = jnp.concatenate([sums[0], plan.unfold(sums[1])], axis=1)
        fc1_sum = jnp.concatenate([sums[2], plan.unfold(sums[3])], axis=1)
        left_sum = plan.unfold(sums[6])
        qkv_sum = jnp.concatenate([sums[4], left_sum[:, :plan.q_left]], axis=1)
        proj_sum = jnp.concatenate([sums[5], left_sum[:, plan.q_left:]], axis=1)
    else:
        fc2_sum, fc1_sum, qkv_sum, proj_sum = scatter_plain([fc2_grads[0], fc1_grads[0], qkv_grad, proj_grad])
    input_part, shift_one_grad, scale_one_grad = norm_back(normed_one_grad, normal_one, inverse_one, scale_one)
    latents_grad = plan.swap((middle_grad + input_part).astype(bf16)).astype(f32)

    mod_grad = jnp.stack(
        [shift_one_grad, scale_one_grad, gate_one_grad, shift_two_grad, scale_two_grad, gate_two_grad], axis=0)
    return finish(plan, condition, cond_mine, ada_flat, mod_grad,
                  [proj_bias_part, fc2_bias_part, q_bias_part, v_bias_part] + fc1_bias_parts,
                  (output, latents_grad, qkv_sum, proj_sum, fc1_sum, fc2_sum))


def solution(mesh):
    token, grid, turned = P(("row", "col"), None), P("row", "col"), P("col", "row")
    cube, wide, flat = P("row", None, "col"), P(None, "col"), P("col")
    return jax.shard_map(
        shards,
        mesh=mesh,
        in_specs=(token, P("row", None), cube, wide, cube, wide, turned, flat, grid, flat, turned, flat, token),
        out_specs=(token, token, P("row", None), cube, wide, cube, wide, turned, flat, grid, flat, turned, flat),
        check_vma=False,
    )
```

```python
import functools
import math
import jax
import jax.numpy as jnp
from jax import lax
from jax.experimental import pallas as pl
from jax.experimental.pallas import tpu as pltpu
from jax.sharding import PartitionSpec as P

HEAD_DIM = 72
SEQ = 1024
norm_eps = 1e-06
bf16, f32 = jnp.bfloat16, jnp.float32

MESH = pl.DeviceIdType.MESH
ANY = pl.BlockSpec(memory_space=pl.ANY)


class Place:
    def __init__(self):
        row, col = lax.axis_index("row"), lax.axis_index("col")
        self.row, self.col = row, col
        self.depth = lax.axis_size("col") // 2
        self.y, self.h = row // 2, row % 2
        self.z, self.x = col // 2, col % 2
        self.p = jnp.where(self.h == 0, self.y, self.x)
        self.q = jnp.where(self.h == 0, self.x, self.y)
        flip_x, flip_y = (row, col + 1 - 2 * self.x), (row + 2 - 4 * self.y, col)
        self.to_q = tuple(jnp.where(self.h == 0, a, b) for a, b in zip(flip_x, flip_y))
        self.to_p = tuple(jnp.where(self.h == 0, b, a) for a, b in zip(flip_x, flip_y))
        self.to_core = (row + 1 - 2 * self.h, col)

    def to_z(self, z):
        return (self.row, 2 * z + self.x)

    def diagonal(self):
        return (self.row + 1 - 2 * self.h, self.col + 1 - 2 * self.x)

    def yx(self, p, q):
        return jnp.where(self.h == 0, p, q), jnp.where(self.h == 0, q, p)

    def partners(self):
        near = [self.to_q, self.to_p, self.to_core]
        return near + [self.to_z((self.z + k) % self.depth) for k in range(1, self.depth)]


def greet(partners):
    barrier = pltpu.get_barrier_semaphore()
    for partner in partners:
        pl.semaphore_signal(barrier, inc=1, device_id=partner, device_id_type=MESH)
    pl.semaphore_wait(barrier, len(partners))


def block_at(ref, rows, lanes, r, c):
    return ref.at[pl.ds(pl.multiple_of(r * rows, 16), rows), pl.ds(pl.multiple_of(c * lanes, 128), lanes)]


class Gather:
    sems = (1, 2, 2, 4, 8)

    def __init__(self, place, ins, outs, sems):
        self.at, self.ins, self.outs = place, ins, outs
        self.local, self.zs, self.qs, self.ps, self.ks = sems

    @staticmethod
    def scratch(count, depth):
        dma = pltpu.SemaphoreType.DMA
        return [dma((count,)), dma((count, 2, depth)), dma((count, 2, depth)), dma((count, 2, depth, 2)), dma((count, 2, depth, 4))]

    def block(self, a, p, q, z, h=None):
        y, x = self.at.yx(p, q)
        rows, lanes = self.ins[a].shape
        h = self.at.h if h is None else h
        return block_at(self.outs[a], rows, lanes, 2 * y + h, 2 * z + x)

    def zc(self, t):
        return (self.at.z + self.at.depth - t) % self.at.depth

    def copy(self, src, dst, sems, index, to):
        return pltpu.make_async_remote_copy(
            src_ref=src, dst_ref=dst, send_sem=sems.at[(index[0], 0) + index[1:]], recv_sem=sems.at[(index[0], 1) + index[1:]],
            device_id=to, device_id_type=MESH)

    def own(self, a):
        return self.block(a, self.at.p, self.at.q, self.at.z)

    def c_local(self, a):
        return pltpu.make_async_copy(self.ins[a], self.own(a), self.local.at[a])

    def c_z(self, a, k):
        place = self.at
        return pltpu.make_async_remote_copy(
            src_ref=self.ins[a], dst_ref=self.own(a), send_sem=self.zs.at[a, 0, k], recv_sem=self.zs.at[a, 1, place.z],
            device_id=place.to_z((place.z + k) % place.depth), device_id_type=MESH)

    def r_z(self, a, t):
        place = self.at
        here = self.block(a, place.p, place.q, self.zc(t))
        return pltpu.make_async_remote_copy(
            src_ref=self.ins[a], dst_ref=here, send_sem=self.zs.at[a, 0, 0], recv_sem=self.zs.at[a, 1, self.zc(t)],
            device_id=place.to_z(place.z), device_id_type=MESH)

    def c_q(self, a, t):
        place = self.at
        spot = self.block(a, place.p, place.q, self.zc(t))
        return self.copy(self.ins[a] if t == 0 else spot, spot, self.qs, (a, self.zc(t)), place.to_q)

    def c_p(self, a, t, j):
        place = self.at
        spot = self.block(a, place.p, place.q if j == 0 else 1 - place.q, self.zc(t))
        return self.copy(self.ins[a] if t == 0 and j == 0 else spot, spot, self.ps, (a, self.zc(t), j), place.to_p)

    def c_k(self, a, t, j):
        place = self.at
        spot = self.block(a, place.p if j < 2 else 1 - place.p, place.q if j % 2 == 0 else 1 - place.q, self.zc(t))
        return self.copy(self.ins[a] if t == 0 and j == 0 else spot, spot, self.ks, (a, self.zc(t), j), place.to_core)

    def start(self, a):
        for k in range(1, self.at.depth):
            self.c_z(a, k).start()
        self.c_local(a).start()

    def stage(self, a, t, n):
        if n == 0:
            if t > 0:
                self.r_z(a, t).wait_recv()
            self.c_q(a, t).start()
            self.c_p(a, t, 0).start()
            self.c_k(a, t, 0).start()
        elif n == 1:
            self.c_q(a, t).wait_recv()
            self.c_p(a, t, 1).start()
            self.c_k(a, t, 1).start()
        elif n == 2:
            self.c_p(a, t, 0).wait_recv()
            self.c_k(a, t, 2).start()
        elif n == 3:
            self.c_p(a, t, 1).wait_recv()
            self.c_k(a, t, 3).start()
        else:
            if t == 0:
                self.c_local(a).wait()
            for j in range(4):
                self.c_k(a, t, j).wait_recv()

    def finish(self, a):
        for k in range(1, self.at.depth):
            self.c_z(a, k).wait_send()
        for t in range(self.at.depth):
            self.c_q(a, t).wait_send()
            for j in range(2):
                self.c_p(a, t, j).wait_send()
            for j in range(4):
                self.c_k(a, t, j).wait_send()


def nt(a, b):
    return lax.dot_general(a, b, (((1,), (1,)), ((), ())), preferred_element_type=f32)


def nn(a, b):
    return lax.dot_general(a, b, (((1,), (0,)), ((), ())), preferred_element_type=f32)


def tn(a, b):
    return lax.dot_general(a, b, (((0,), (0,)), ((), ())), preferred_element_type=f32)


SOFT = HEAD_DIM ** (-0.5) * math.log2(math.e)


VECS = 24


def softmax_head(q, k, k2):
    one, two = nt(k, q), nt(k2, q)
    top = jnp.maximum(jnp.max(one, axis=0, keepdims=True), jnp.max(two, axis=0, keepdims=True)) * SOFT
    one, two = jnp.exp2(one * SOFT - top), jnp.exp2(two * SOFT - top)
    total = jnp.sum(one, axis=0, keepdims=True) + jnp.sum(two, axis=0, keepdims=True)
    return one.astype(bf16), two.astype(bf16), total, top + jnp.log2(total)


def norm_rows(values):
    mean = jnp.mean(values, axis=-1, keepdims=True)
    centred = values - mean
    inverse = lax.rsqrt(jnp.mean(centred * centred, axis=-1, keepdims=True) + norm_eps)
    return centred * inverse, inverse


def gelu_both(u):
    c = math.sqrt(2.0 / math.pi)
    square = u * u
    inner = jnp.tanh(u * (c + (c * 0.044715) * square))
    half = 0.5 * (1.0 + inner)
    slope = half + (0.5 * u) * (1.0 - inner * inner) * (c + (3 * c * 0.044715) * square)
    return u * half, slope


class Swap:
    def __init__(self, place, src, dst, sems, i):
        self.stay = place.h == place.x
        self.local = pltpu.make_async_copy(src, dst, sems.at[i, 0])
        self.remote = pltpu.make_async_remote_copy(
            src_ref=src, dst_ref=dst, send_sem=sems.at[i, 0], recv_sem=sems.at[i, 1],
            device_id=place.diagonal(), device_id_type=MESH)

    def start(self):
        pl.when(self.stay)(self.local.start)
        pl.when(jnp.logical_not(self.stay))(self.remote.start)

    def wait(self):
        pl.when(self.stay)(self.local.wait)
        pl.when(jnp.logical_not(self.stay))(self.remote.wait)


def unfold_into(left, target):
    rows = target.shape[0] // 4
    half = rows // 2
    for r in range(4):
        tile = left[r * half:(r + 1) * half, :].astype(f32)
        target[r * rows:r * rows + half, :] = jnp.concatenate([tile[:, :64], tile[:, 128:192]], axis=1).astype(bf16)
        target[r * rows + half:(r + 1) * rows, :] = jnp.concatenate([tile[:, 64:128], tile[:, 192:]], axis=1).astype(bf16)


GROUPS = (3, 2, 2)


def forward_kernel(*refs):
    lat, cot, cond, ada, bias = refs[:5]
    blocks, refs = refs[5:12], refs[12:]
    fulls, refs = refs[:7], refs[7:]
    (o_w, o_cot, o_x, o_n1, o_q, o_k, o_v, o_k2, o_v2, o_lse, o_att, o_ba, o_mid, o_n2, o_hid, o_slo, o_out, o_vec, o_act), refs = refs[:19], refs[19:]
    (x_v, n1, q_v, k_v, v_v, k2_v, v2_v, lse_v, ot, att, ba, mid, n2, hid, slo, acc, wbuf, lbuf, out_v, cot_v, vec,
     c_send, c_recv, s_send, s_recv, m_own, m_oth), refs = refs[:27], refs[27:]
    ag_sems, (swap_sems, c_sems, s_sems, m_sems, o_sems, kv_sems, w_sems, save_sems, wsave_sems) = refs[:5], refs[5:]

    place = Place()
    depth, rows_n = place.depth, 4
    row, col = place.row, place.col
    cols_n = 2 * depth
    tokens, width = x_v.shape
    hc = width // cols_n
    drows = ada.shape[0]
    q_main, p_main = blocks[0].shape[1], blocks[1].shape[1]
    half = tokens // 2

    row_peers = [((row + k) % rows_n, col) for k in range(1, rows_n)]
    col_peers = [(row, (col + k) % cols_n) for k in range(1, cols_n)]
    greet(place.partners() + row_peers + col_peers + [place.diagonal()])

    def send(src, dst, s_sem, r_sem, to):
        return pltpu.make_async_remote_copy(
            src_ref=src, dst_ref=dst, send_sem=s_sem, recv_sem=r_sem, device_id=to, device_id_type=MESH)

    cond_value = cond[...]
    act = (cond_value / (1.0 + jnp.exp(-cond_value))).astype(bf16).astype(f32)
    for r in range(rows_n):
        c_send[r] = act[:, r * drows:(r + 1) * drows]

    def cond_copy(k):
        to = (row + k) % rows_n
        return send(c_send.at[to], c_recv.at[row], c_sems.at[0, k], c_sems.at[1, row], (to, col))

    def cond_got(k):
        src = (row + k) % rows_n
        return send(c_send.at[src], c_recv.at[src], c_sems.at[0, k], c_sems.at[1, src], (src, col))

    for k in range(1, rows_n):
        cond_copy(k).start()
    swap_x = Swap(place, lat, x_v, swap_sems, 0)
    swap_x.start()

    work = Gather(place, blocks, fulls, ag_sems)
    for a in range(3):
        work.start(a)

    members, first = [], 0
    for size in GROUPS:
        members.append(list(range(first, first + size)))
        first += size
    chunks = [(g, t) for g in range(len(GROUPS)) for t in range(depth)]
    events = [(s - n, n) for s in range(len(chunks) + 4) for n in range(5) if 0 <= s - n < len(chunks)]
    at = [0]

    def pump(count):
        for s, n in events[at[0]:at[0] + count]:
            if n == 0 and s in (2, depth + 2):
                for a in members[1 if s == 2 else 2]:
                    work.start(a)
            g, t = chunks[s]
            for a in members[g]:
                work.stage(a, t, n)
        at[0] += count

    def pump_to(s, n):
        pump(max(0, events.index((s, n)) + 1 - at[0]))

    pump_to(0, 0)
    c_recv[row] = c_send[row]
    for k in range(1, rows_n):
        cond_got(k).wait_recv()
    act_all = c_recv[...].reshape(rows_n * 8, drows).astype(bf16)
    s_send[...] = nn(act_all, ada[...]).reshape(rows_n, 8, 6 * hc)

    def sum_copy(k):
        to = (row + k) % rows_n
        return send(s_send.at[to], s_recv.at[row], s_sems.at[0, k], s_sems.at[1, row], (to, col))

    def sum_got(k):
        src = (row + k) % rows_n
        return send(s_send.at[src], s_recv.at[src], s_sems.at[0, k], s_sems.at[1, src], (src, col))

    for k in range(1, rows_n):
        sum_copy(k).start()
    pump_to(0, 1)
    s_recv[row] = s_send[row]
    for k in range(1, rows_n):
        sum_got(k).wait_recv()
    m_own[col] = s_recv[0] + s_recv[1] + s_recv[2] + s_recv[3] + bias[...]

    def mod_copy(k):
        return send(m_own.at[col], m_own.at[col], m_sems.at[0, k], m_sems.at[1, col], (row, (col + k) % cols_n))

    def mod_got(k):
        src = (col + k) % cols_n
        return send(m_own.at[src], m_own.at[src], m_sems.at[0, k], m_sems.at[1, src], (row, src))

    for k in range(1, cols_n):
        mod_copy(k).start()
    pump_to(0, 2)
    for k in range(1, cols_n):
        mod_got(k).wait_recv()
    other = send(m_own, m_oth, o_sems.at[0], o_sems.at[1], place.to_core)
    other.start()
    pump_to(0, 3)
    other.wait_recv()
    stay = place.h == place.x
    for c in range(cols_n):
        line = jnp.where(stay, m_own[c, pl.ds(place.z, 1), :], m_oth[c, pl.ds(place.z, 1), :])
        for k in range(6):
            vec[k:k + 1, c * hc:(c + 1) * hc] = line[:, k * hc:(k + 1) * hc]
        line = m_own[c, 4:5, :]
        vec[6:7, c * hc:(c + 1) * hc] = line[:, 576:576 + hc]
        vec[7:8, c * hc:(c + 1) * hc] = line[:, 576 + hc:]
        z, i = c // 2, c % 2
        vec[16 + z:17 + z, i * 512:(i + 1) * 512] = line[:, :512]
        vec[16 + z:17 + z, 1024 + i * 64:1024 + (i + 1) * 64] = line[:, 512:576]

    swap_x.wait()
    swap_dy = Swap(place, cot, o_cot, swap_sems, 1)
    swap_dy.start()
    part = 128

    def row_parts(body):
        @pl.loop(0, tokens // part)
        def _(i):
            body(pl.ds(pl.multiple_of(i * part, part), part))

    def first_norm(at_rows):
        normal, _ = norm_rows(x_v[at_rows, :].astype(f32))
        n1[at_rows, :] = (normal * (1.0 + vec[1:2, :]) + vec[0:1, :]).astype(bf16)

    row_parts(first_norm)

    saves = []

    def save(src, dst):
        copy = pltpu.make_async_copy(src, dst, save_sems.at[len(saves)])
        copy.start()
        saves.append(copy)

    save(x_v, o_x)
    save(n1, o_n1)
    save(c_recv, o_act)

    def fetch(s):
        g, t = chunks[s]
        zc, slot = work.zc(t), s % depth
        lanes = [q_main, p_main] if g == 0 else [blocks[members[g][0]].shape[1]]
        spot, copies = 0, []
        for i, n in enumerate(lanes):
            src = fulls[members[g][i]].at[:, pl.ds(pl.multiple_of(zc * 2 * n, 128), 2 * n)]
            copies.append(pltpu.make_async_copy(src, wbuf.at[slot, :, spot:spot + 2 * n], w_sems.at[s % 2, i]))
            spot += 2 * n
        src = fulls[members[g][-1]].at[:, pl.ds(pl.multiple_of(zc * 256, 128), 256)]
        copies.append(pltpu.make_async_copy(src, lbuf.at[s % 2], w_sems.at[s % 2, 2]))
        return copies

    def fetch_start(s):
        pump_to(s, 4)
        if s >= depth:
            weight_save(s - depth).wait()
        for copy in fetch(s):
            copy.start()

    def fetch_wait(s):
        for copy in fetch(s):
            copy.wait()
        unfold_into(lbuf.at[s % 2], wbuf.at[s % depth, :, 1024:1152])
        weight_save(s).start()

    def weight_save(s):
        g, t = chunks[s]
        return pltpu.make_async_copy(wbuf.at[s % depth], o_w.at[g, work.zc(t)], wsave_sems.at[s])

    def swap_kv(i, h):
        src, dst = ((k_v, k2_v), (v_v, v2_v))[i]
        return send(src.at[h], dst.at[h], kv_sems.at[0, i, h], kv_sems.at[1, i, h], place.to_core)

    def project(s):
        t, slot = chunks[s][1], s % depth
        zc = work.zc(t)

        @pl.loop(0, 2)
        def _(i):
            at_rows = pl.ds(pl.multiple_of(i * half, half), half)
            main = nn(n1[at_rows, :], wbuf[slot, :, :2 * q_main])
            left = nn(n1[at_rows, :], wbuf[slot, :, 1024:1152])
            for j in range(2):
                biases = m_own[2 * zc + j]
                own = main[:, j * q_main:(j + 1) * q_main]
                tail = left[:, j * 64:j * 64 + 3 * hc - q_main]
                for e in range(2):
                    h = 4 * zc + 2 * j + e
                    a = e * HEAD_DIM
                    q_v[h, at_rows, :] = (own[:, a:a + HEAD_DIM] + biases[5:6, a:a + HEAD_DIM]).astype(bf16)
                    k_v[h, at_rows, :] = own[:, hc + a:hc + a + HEAD_DIM].astype(bf16)
                    if e == 0:
                        value = own[:, 2 * hc:2 * hc + HEAD_DIM]
                    else:
                        value = jnp.concatenate([own[:, 2 * hc + HEAD_DIM:], tail], axis=1)
                    v_v[h, at_rows, :] = (value + biases[5:6, hc + a:hc + a + HEAD_DIM]).astype(bf16)

        for i in range(4):
            swap_kv(0, 4 * zc + i).start()
            swap_kv(1, 4 * zc + i).start()

    def attention(s):
        zc = work.zc(chunks[s][1])
        start = at[0]

        @pl.loop(0, 4)
        def _(i):
            h = 4 * zc + i
            swap_kv(0, h).wait_recv()
            swap_kv(1, h).wait_recv()
            one, two, total, lse = softmax_head(q_v[h], k_v[h], k2_v[h])
            ot[i] = (tn(v_v[h], one) + tn(v2_v[h], two)) / total
            lse_v[h] = lse
            for k in range(4):
                at[0] = start + k

                @pl.when(i == k)
                def _():
                    pump(1)

        at[0] = start + 4
        att[zc, :, 2 * p_main:] = jnp.zeros((tokens, 128), bf16)
        for j in range(2):
            pair = jnp.concatenate([ot[2 * j], ot[2 * j + 1]], axis=0).T.astype(bf16)
            att[zc, :, j * p_main:(j + 1) * p_main] = pair[:, :p_main]
            att[zc, :, 2 * p_main + 64 * j + 48:2 * p_main + 64 * j + 64] = pair[:, p_main:]

        @pl.loop(0, 2)
        def _(i):
            at_rows = pl.ds(pl.multiple_of(i * half, half), half)
            term = nt(att[zc, at_rows, :], wbuf[s % depth, :, 2 * q_main:])
            if s == 0:
                acc[at_rows, :] = term
            else:
                acc[at_rows, :] += term

    for s in range(depth):
        fetch_start(s)
        fetch_wait(s)
        project(s)
        if s > 0:
            attention(s - 1)
    attention(depth - 1)
    for src, dst in ((q_v, o_q), (k_v, o_k), (v_v, o_v), (k2_v, o_k2), (v2_v, o_v2), (lse_v, o_lse), (att, o_att)):
        save(src, dst)

    def second_norm(at_rows):
        branch = acc[at_rows, :] + vec[6:7, :]
        ba[at_rows, :] = branch.astype(bf16)
        middle = x_v[at_rows, :].astype(f32) + vec[2:3, :] * branch
        mid[at_rows, :] = middle
        normal, _ = norm_rows(middle)
        n2[at_rows, :] = (normal * (1.0 + vec[4:5, :]) + vec[3:4, :]).astype(bf16)

    row_parts(second_norm)
    for src, dst in ((ba, o_ba), (mid, o_mid), (n2, o_n2)):
        save(src, dst)

    for s in range(depth, 2 * depth):
        fetch_start(s)
        fetch_wait(s)
        zc = work.zc(chunks[s][1])

        def up(at_rows):
            u = nn(n2[at_rows, :], wbuf[s % depth]) + vec[pl.ds(16 + zc, 1), :]
            value, slope = gelu_both(u)
            hid[zc, at_rows, :] = value.astype(bf16)
            slo[zc, at_rows, :] = slope.astype(bf16)

        row_parts(up)
    save(hid, o_hid)
    save(slo, o_slo)
    for s in range(2 * depth, 3 * depth):
        fetch_start(s)
        fetch_wait(s)
        zc = work.zc(chunks[s][1])

        def down(at_rows):
            term = nt(hid[zc, at_rows, :], wbuf[s % depth])
            if s == 2 * depth:
                acc[at_rows, :] = term
            else:
                acc[at_rows, :] += term

        row_parts(down)

    swap_dy.wait()
    load_dy = pltpu.make_async_copy(o_cot, cot_v, w_sems.at[0, 0])
    load_dy.start()
    load_dy.wait()
    vec[8:9, :] = jnp.zeros((1, width), f32)

    def finish(at_rows):
        branch = acc[at_rows, :] + vec[7:8, :]
        out_v[at_rows, :] = (mid[at_rows, :] + vec[5:6, :] * branch).astype(bf16)
        vec[8:9, :] += jnp.sum(cot_v[at_rows, :].astype(f32) * branch, axis=0, keepdims=True)

    row_parts(finish)
    save(out_v, o_out)
    save(vec, o_vec)

    for a in range(7):
        work.finish(a)
    for k in range(1, rows_n):
        cond_copy(k).wait_send()
        sum_copy(k).wait_send()
    for k in range(1, cols_n):
        mod_copy(k).wait_send()
    other.wait_send()

    @pl.loop(0, 4 * depth)
    def _(h):
        swap_kv(0, h).wait_send()
        swap_kv(1, h).wait_send()

    for s in range(2 * depth, 3 * depth):
        weight_save(s).wait()
    for copy in saves:
        copy.wait()


def forward(lat, cot, cond, ada, bias, blocks, collective_id):
    rows, cols = lax.axis_size("row"), lax.axis_size("col")
    depth = cols // 2
    tokens, width = lat.shape
    heads = width // HEAD_DIM
    lanes = 1152
    hc6 = ada.shape[1]
    shape = jax.ShapeDtypeStruct
    head = shape((heads, tokens, HEAD_DIM), bf16)
    token = shape((tokens, width), bf16)
    outs = [shape((rows * b.shape[0], cols * b.shape[1]), bf16) for b in blocks] + [
        shape((3, depth, width, lanes), bf16), token, token, token, head, head, head, head, head,
        shape((heads, 1, tokens), f32), shape((depth, tokens, 384), bf16), token, shape((tokens, width), f32), token,
        shape((depth, tokens, lanes), bf16), shape((depth, tokens, lanes), bf16), token, shape((VECS, width), f32), shape((rows, 8, ada.shape[0]), f32)]
    dma, vm = pltpu.SemaphoreType.DMA, pltpu.VMEM
    t16, h16 = vm((tokens, width), bf16), vm((heads, tokens, HEAD_DIM), bf16)
    drows = ada.shape[0]
    scratch = [
        t16, t16, h16, h16, h16, h16, h16, vm((heads, 1, tokens), f32), vm((4, HEAD_DIM, tokens), f32),
        vm((depth, tokens, 384), bf16), t16, vm((tokens, width), f32), t16, vm((depth, tokens, lanes), bf16),
        vm((depth, tokens, lanes), bf16), vm((tokens, width), f32), vm((depth, width, lanes), bf16), vm((2, width // 2, 256), bf16),
        t16, t16, vm((VECS, width), f32), vm((rows, 8, drows), f32), vm((rows, 8, drows), f32), vm((rows, 8, hc6), f32),
        vm((rows, 8, hc6), f32), vm((cols, 8, hc6), f32), vm((cols, 8, hc6), f32)]
    scratch += Gather.scratch(len(blocks), depth)
    scratch += [dma((2, 2)), dma((2, rows)), dma((2, rows)), dma((2, cols)), dma((2,)), dma((2, 2, heads)), dma((2, 3)), dma((32,)),
                dma((3 * depth,))]
    vmem = pl.BlockSpec(memory_space=pltpu.VMEM)
    got = pl.pallas_call(
        forward_kernel,
        out_shape=outs,
        in_specs=[ANY, ANY, vmem, vmem, vmem] + [ANY] * len(blocks),
        out_specs=[ANY] * len(outs),
        scratch_shapes=scratch,
        compiler_params=pltpu.CompilerParams(collective_id=collective_id, has_side_effects=True, vmem_limit_bytes=62 * 2**20),
        name="forward",
    )(lat, cot, cond, ada, bias, *blocks)
    return got[len(blocks):]


def backward_kernel(*refs):
    (w, dy_h, x_h, n1_h, q_h, k_h, v_h, k2_h, v2_h, att_h, ba_h, mid_h, n2_h, hid_h, slo_h, out_h), refs = refs[:16], refs[16:]
    (lse, vec, act, ada, cond), refs = refs[:5], refs[5:]
    (o_out, o_lat, o_pq, o_fc2, o_fc1, o_qkv, o_proj, o_ada, o_rows, o_cond), refs = refs[:10], refs[10:]
    (acc, give, r0, r1, r1l, r2, r2l, r3, r3l, lf, lx), refs = refs[:11], refs[11:]
    (wbuf, hs, pre, pq, turn, tmp, ml, gm, gx, slo, att, heads, grad_o, delta, kv_give, kv_got, own, gv), refs = refs[:18], refs[18:]
    (tt, tc, um, vm_, modl, cp, cr, cf), refs = refs[:8], refs[8:]
    (swap_sems, s0, s1, s2, s3, lx_sems, w_sems, hs_sems, slo_sems, tmp_sems, head_sems, kv_sems, pq_sems, t_sems, u_sems, v_sems, cr_sems, cf_sems) = refs

    place = Place()
    depth, rows_n = place.depth, 4
    row, col, h = place.row, place.col, place.h
    cols_n = 2 * depth
    tokens, width = ml.shape
    hc = width // cols_n
    drows = ada.shape[0]
    lrows = drows // 2
    half, part = tokens // 2, 128
    q_main, p_main = 384, 128
    scale = HEAD_DIM ** (-0.5)
    row_peers = [((row + k) % rows_n, col) for k in range(1, rows_n)]
    col_peers = [(row, (col + k) % cols_n) for k in range(1, cols_n)]
    flip_x, flip_y = (row, col + 1 - 2 * place.x), (row + 2 - 4 * place.y, col)
    greet(place.partners() + row_peers + col_peers + [place.diagonal()])

    def send(src, dst, s_sem, r_sem, to):
        return pltpu.make_async_remote_copy(
            src_ref=src, dst_ref=dst, send_sem=s_sem, recv_sem=r_sem, device_id=to, device_id_type=MESH)

    def row_parts(body):
        @pl.loop(0, tokens // part)
        def _(i):
            body(pl.ds(pl.multiple_of(i * part, part), part))

    def row_halves(body):
        @pl.loop(0, 2)
        def _(i):
            body(pl.ds(pl.multiple_of(i * half, half), half))

    def zc(t):
        return lax.rem(place.z + 1 + t, depth)

    def load(src, i):
        copy = pltpu.make_async_copy(src, tmp.at[i], tmp_sems.at[i])
        copy.start()
        return copy

    def weight_load(u):
        return pltpu.make_async_copy(w.at[2 - u // depth, zc(u % depth)], wbuf.at[u % 2], w_sems.at[u % 2])

    def slope_load(u):
        return pltpu.make_async_copy(slo_h.at[zc(u)], slo.at[u % 2], slo_sems.at[u % 2])

    def weight_use(u):
        weight_load(u).wait()
        if u + 1 < 3 * depth:
            weight_load(u + 1).start()


    def tick_loads(s):
        g, t = s // depth, s % depth
        if g == 0:
            return [pltpu.make_async_copy(hid_h.at[zc(t)], hs.at[s % 2], hs_sems.at[s % 2, 0])]
        if g == 1:
            return []
        return [pltpu.make_async_copy(o_pq.at[zc(t)], hs.at[s % 2, :, :896], hs_sems.at[s % 2, 0]),
                pltpu.make_async_copy(att_h.at[zc(t)], att.at[s % 2], hs_sems.at[s % 2, 1])]

    def tick_prefetch(s):
        if s < 3 * depth:
            for copy in tick_loads(s):
                copy.start()

    def pq_save(t):
        return pltpu.make_async_copy(pq, o_pq.at[zc(t)], pq_sems.at[t])

    def c0(s, y):
        return send(give.at[s % 2, y], r0.at[s % 2, y], s0.at[0, s % 2, y], s0.at[1, s % 2, y], place.to_core)

    def spots(s, y, x):
        return (acc.at[s % 4, y, :, pl.ds(pl.multiple_of(x * 512, 512), 512)],
                acc.at[s % 4, y, pl.ds(pl.multiple_of(x * lrows, 16), lrows), 1024:1152])

    def c1(s, j):
        main, left = spots(s, *place.yx(1 - place.p, j))
        k = s % 4
        return [send(main, r1.at[k, j], s1.at[0, k, j, 0], s1.at[1, k, j, 0], place.to_p),
                send(left, r1l.at[k, j], s1.at[0, k, j, 1], s1.at[1, k, j, 1], place.to_p)]

    def c2(s):
        main, left = spots(s, *place.yx(place.p, 1 - place.q))
        k = s % 4
        return [send(main, r2.at[k], s2.at[0, k, 0], s2.at[1, k, 0], place.to_q),
                send(left, r2l.at[k], s2.at[0, k, 1], s2.at[1, k, 1], place.to_q)]

    def c3(s):
        g, t = s // depth, s % depth
        main, left = spots(s, *place.yx(place.p, place.q))
        to = place.to_z(zc(t))
        return [send(main, r3.at[g, t], s3.at[0, g, t, 0], s3.at[1, g, t, 0], to),
                send(left, r3l.at[g, t], s3.at[0, g, t, 1], s3.at[1, g, t, 1], to)]

    def add_into(into, other):
        n = into.shape[0]

        @pl.loop(0, n // 48)
        def _(i):
            at_rows = pl.ds(pl.multiple_of(i * 48, 16), 48)
            into[at_rows, :] = into[at_rows, :] + other[at_rows, :]

    def tick_a(s):
        g, t = s // depth, s % depth
        k = s % 4
        if s >= 4:
            for j in range(2):
                for copy in c1(s - 4, j):
                    copy.wait_send()
            for copy in c2(s - 4):
                copy.wait_send()
            if (s - 4) % depth < depth - 1:
                for copy in c3(s - 4):
                    copy.wait_send()
        if s >= 2:
            for y in range(2):
                c0(s - 2, y).wait_send()
        for copy in tick_loads(s):
            copy.wait()

        def rows_of(r):
            at_rows = pl.ds(pl.multiple_of(r * drows, 16), drows)
            if g == 0:
                return nn(turn[0, at_rows, :], hs[s % 2]).astype(bf16)
            if g == 1:
                return nn(turn[0, at_rows, :], pre[zc(t)]).astype(bf16)
            one = nn(turn[1, at_rows, :], hs[s % 2, :, :896])
            two = nn(turn[0, at_rows, :], att[s % 2])
            return jnp.concatenate(
                [one[:, :q_main], two[:, :p_main], one[:, q_main:2 * q_main], two[:, p_main:2 * p_main],
                 one[:, 2 * q_main:] + two[:, 2 * p_main:]], axis=1).astype(bf16)

        @pl.loop(0, 2)
        def _(y):
            give[s % 2, y] = rows_of(2 * y + 1 - h)
            acc[k, y] = rows_of(2 * y + h)

        for y in range(2):
            c0(s, y).start()
        tick_prefetch(s + 1)

    def tick_b(s):
        if 0 <= s - 1 < 3 * depth:
            n = s - 1
            for j in range(2):
                for copy in c1(n, j):
                    copy.wait_recv()
            for into, other in zip(spots(n, *place.yx(place.p, 1 - place.q)), (r1.at[n % 4, 1 - place.q], r1l.at[n % 4, 1 - place.q])):
                add_into(into, other)
            for copy in c2(n):
                copy.start()
            for into, other in zip(spots(n, *place.yx(place.p, place.q)), (r1.at[n % 4, place.q], r1l.at[n % 4, place.q])):
                add_into(into, other)
        if s < 3 * depth:
            for y in range(2):
                c0(s, y).wait_recv()
            for y in range(2):
                add_into(acc.at[s % 4, y], r0.at[s % 2, y])
            for j in range(2):
                for copy in c1(s, j):
                    copy.start()
        if 0 <= s - 2 < 3 * depth:
            n = s - 2
            for copy in c2(n):
                copy.wait_recv()
            for into, other in zip(spots(n, *place.yx(place.p, place.q)), (r2.at[n % 4], r2l.at[n % 4])):
                add_into(into, other)
            if n % depth < depth - 1:
                for copy in c3(n):
                    copy.start()
        if 0 <= s - 3 < 3 * depth and (s - 3) % depth == depth - 1:
            total((s - 3) // depth)

    def left_copy(g):
        return send(lf.at[g], lx.at[g], lx_sems.at[0, g], lx_sems.at[1, g], flip_x)

    def total(g):
        last = (g + 1) * depth - 1
        for t in range(depth - 1):
            for copy in c3(g * depth + t):
                copy.wait_recv()
        main, left = spots(last, *place.yx(place.p, place.q))

        @pl.loop(0, drows // 48)
        def _(i):
            at_rows = pl.ds(pl.multiple_of(i * 48, 16), 48)
            value = main[at_rows, :].astype(f32)
            for t in range(depth - 1):
                value = value + r3[g, t, at_rows, :].astype(f32)
            if g == 0:
                o_fc2[at_rows, :512] = value
            elif g == 1:
                o_fc1[at_rows, :512] = value
            else:
                o_qkv[at_rows, :q_main] = value[:, :q_main]
                o_proj[at_rows, :p_main] = value[:, q_main:]

        value = left[...].astype(f32)
        for t in range(depth - 1):
            value = value + r3l[g, t].astype(f32)
        lf[g] = value
        left_copy(g).start()

    def left_finish(g):
        left_copy(g).wait_recv()
        first = place.x == 0
        top = jnp.where(first, lf[g][:, :64], lx[g][:, 64:])
        bottom = jnp.where(first, lx[g][:, :64], lf[g][:, 64:])
        tail = 3 * hc - q_main
        for spot, value in ((0, top), (lrows, bottom)):
            if g == 0:
                o_fc2[spot:spot + lrows, 512:] = value
            elif g == 1:
                o_fc1[spot:spot + lrows, 512:] = value
            else:
                o_qkv[spot:spot + lrows, q_main:] = value[:, :tail]
                o_proj[spot:spot + lrows, p_main:] = value[:, tail:]

    def turn_into(i, src):
        @pl.loop(0, width // 128)
        def _(n):
            spot = pl.ds(pl.multiple_of(n * 128, 128), 128)
            turn[i, spot, :] = src[:, spot].T

    swap_out = Swap(place, out_h, o_out, swap_sems, 0)
    load_dy = load(dy_h, 0)
    weight_load(0).start()
    slope_load(0).start()
    tick_prefetch(0)
    swap_out.start()
    gv[...] = jnp.zeros_like(gv)
    tt[...] = jnp.zeros_like(tt)
    gv[5:6, :] = vec[8:9, :]
    load_dy.wait()

    def first(at_rows):
        grad = tmp[0, at_rows, :].astype(f32) * vec[5:6, :]
        gv[7:8, :] += jnp.sum(grad, axis=0, keepdims=True)
        ml[at_rows, :] = grad.astype(bf16)

    row_parts(first)
    turn_into(0, ml)

    def hidden_back(u):
        z = zc(u)
        weight_use(u)
        slope_load(u).wait()
        if u + 1 < depth:
            slope_load(u + 1).start()
        sums = gv.at[8:9, :]
        sums[...] = jnp.zeros((1, width), f32)

        def body(at_rows):
            grad = nn(ml[at_rows, :], wbuf[u % 2]) * slo[u % 2, at_rows, :].astype(f32)
            sums[...] += jnp.sum(grad, axis=0, keepdims=True)
            pre[z, at_rows, :] = grad.astype(bf16)

        row_parts(body)
        for j in range(2):
            tt[2 * z + j, 1:2, :512] = sums[:, 512 * j:512 * (j + 1)]
            tt[2 * z + j, 1:2, 512:576] = sums[:, 1024 + 64 * j:1024 + 64 * (j + 1)]

    def normed_back(u):
        z = zc(u % depth)
        weight_use(u)

        def body(at_rows):
            term = nt(pre[z, at_rows, :], wbuf[u % 2])
            if u == depth:
                gx[at_rows, :] = term
            else:
                gx[at_rows, :] += term

        row_parts(body)

    tick_a(0)
    hidden_back(0)
    tick_b(0)
    hidden_back(1)
    tick_a(1)
    hidden_back(2)
    tick_b(1)
    hidden_back(3)
    for u in range(depth, 2 * depth):
        if u == depth + 1:
            tick_a(2)
        if u == depth + 3:
            tick_b(2)
        normed_back(u)

    load_mid = pltpu.make_async_copy(mid_h, gm, tmp_sems.at[2])
    load_mid.start()
    load_ba, load_dy = load(ba_h, 1), load(dy_h, 0)
    load_mid.wait()
    load_ba.wait()
    load_dy.wait()

    def norm_grad(values, grads, shift_row, scale_row, scale_vec):
        normal, inverse = norm_rows(values)
        gv[shift_row:shift_row + 1, :] += jnp.sum(grads, axis=0, keepdims=True)
        gv[scale_row:scale_row + 1, :] += jnp.sum(grads * normal, axis=0, keepdims=True)
        inner = grads * (1.0 + scale_vec)
        one = jnp.mean(inner, axis=-1, keepdims=True)
        two = jnp.mean(inner * normal, axis=-1, keepdims=True)
        return inverse * (inner - one - normal * two)

    def second(at_rows):
        grad = norm_grad(gm[at_rows, :], gx[at_rows, :], 3, 4, vec[4:5, :]) + tmp[0, at_rows, :].astype(f32)
        gm[at_rows, :] = grad
        gv[2:3, :] += jnp.sum(grad * tmp[1, at_rows, :].astype(f32), axis=0, keepdims=True)
        grad = grad * vec[2:3, :]
        gv[6:7, :] += jnp.sum(grad, axis=0, keepdims=True)
        ml[at_rows, :] = grad.astype(bf16)

    row_parts(second)

    def heads_load(t):
        spot = pl.ds(4 * zc(t), 4)
        return [pltpu.make_async_copy(src.at[spot], heads.at[i], head_sems.at[i])
                for i, src in enumerate((q_h, k_h, v_h, k2_h, v2_h))]

    def att_load(t):
        return pltpu.make_async_copy(att_h.at[zc(t)], att.at[t % 2], hs_sems.at[t % 2, 1])

    def kv_swap(t, kind, i):
        return send(kv_give.at[kind, i], kv_got.at[t % 2, kind, i], kv_sems.at[0, 0, kind, i], kv_sems.at[1, t % 2, kind, i], place.to_core)

    def pair_of(value, j):
        spot = 2 * p_main + 64 * j + 48
        return jnp.concatenate([value[:, j * p_main:(j + 1) * p_main], value[:, spot:spot + 16]], axis=1)

    def attention_open(t):
        u = 2 * depth + t
        weight_use(u)
        att_load(t).wait()

        def body(at_rows):
            grads = nn(ml[at_rows, :], wbuf[u % 2, :, 2 * q_main:])
            results = att[t % 2, at_rows, :].astype(f32)
            for j in range(2):
                grad = pair_of(grads, j).astype(bf16)
                product = (grad.astype(f32) * pair_of(results, j)).T
                for e in range(2):
                    grad_o[2 * j + e, at_rows, :] = grad[:, e * HEAD_DIM:(e + 1) * HEAD_DIM]
                    delta[2 * j + e, :, at_rows] = jnp.sum(product[e * HEAD_DIM:(e + 1) * HEAD_DIM, :], axis=0, keepdims=True)

        row_halves(body)
        for copy in heads_load(t):
            copy.wait()

    def attention_heads(t, between):
        @pl.loop(0, 4)
        def _(i):
            q, out_grad, shift, less = heads[0, i], grad_o[i], lse[4 * zc(t) + i], delta[i]

            def side(k, v):
                probs = jnp.exp2(nt(k, q) * SOFT - shift)
                grad = (probs * (nt(v, out_grad) - less)).astype(bf16)
                return nn(grad, q) * scale, nn(probs.astype(bf16), out_grad), tn(k, grad)

            dk, dv, dq_two = side(heads[3, i], heads[4, i])
            kv_give[0, i] = dk.astype(bf16)
            kv_give[1, i] = dv.astype(bf16)
            kv_swap(t, 0, i).start()
            kv_swap(t, 1, i).start()
            dk, dv, dq_one = side(heads[1, i], heads[2, i])
            own[1, i] = dk
            own[2, i] = dv
            own[0, i] = ((dq_one + dq_two) * scale).T
            for n, action in between:
                pl.when(i == n)(action)

    def attention_close(t):
        u = 2 * depth + t
        z = zc(t)
        if t + 1 < depth:
            for copy in heads_load(t + 1):
                copy.start()
            att_load(t + 1).start()
        for kind in range(2):
            for i in range(4):
                kv_swap(t, kind, i).wait()
        if t > 0:
            pq_save(t - 1).wait()

        def body(at_rows):
            for j in range(2):
                pieces, tails = [[], [], []], None
                for e in range(2):
                    i = 2 * j + e
                    dq = own[0, i, at_rows, :]
                    dk = own[1, i, at_rows, :] + kv_got[t % 2, 0, i, at_rows, :].astype(f32)
                    dv = own[2, i, at_rows, :] + kv_got[t % 2, 1, i, at_rows, :].astype(f32)
                    tt[2 * z + j, 2:3, e * HEAD_DIM:(e + 1) * HEAD_DIM] += jnp.sum(dq, axis=0, keepdims=True)
                    tt[2 * z + j, 2:3, hc + e * HEAD_DIM:hc + (e + 1) * HEAD_DIM] += jnp.sum(dv, axis=0, keepdims=True)
                    for n, value in enumerate((dq, dk, dv)):
                        pieces[n].append(value)
                last = pieces[2][1]
                cut = q_main - 2 * hc - HEAD_DIM
                line = pieces[0] + pieces[1] + [pieces[2][0], last[:, :cut]]
                pq[at_rows, j * q_main:(j + 1) * q_main] = jnp.concatenate(line, axis=1).astype(bf16)
                rest = jnp.concatenate([last[:, cut:], jnp.zeros((last.shape[0], 64 - HEAD_DIM + cut), f32)], axis=1)
                pq[at_rows, 2 * q_main + 64 * j:2 * q_main + 64 * (j + 1)] = rest.astype(bf16)
            term = nt(pq[at_rows, :2 * q_main], wbuf[u % 2, :, :2 * q_main]) + nt(pq[at_rows, 2 * q_main:], wbuf[u % 2, :, 1024:])
            if t == 0:
                gx[at_rows, :] = term
            else:
                gx[at_rows, :] += term

        row_halves(body)
        pq_save(t).start()

    for copy in heads_load(0):
        copy.start()
    att_load(0).start()
    load_n2 = load(n2_h, 0)
    tick_a(3)
    load_n2.wait()
    turn_into(0, tmp.at[0])
    attention_open(0)
    tick_b(3)
    attention_heads(0, [(1, lambda: tick_a(4)), (3, lambda: tick_b(4))])
    attention_close(0)
    attention_open(1)
    tick_a(5)
    attention_heads(1, [(0, lambda: tick_b(5)), (2, lambda: tick_a(6))])
    attention_close(1)
    tick_b(6)
    attention_open(2)
    attention_heads(2, [(1, lambda: tick_a(7))])
    load_x, load_n1 = load(x_h, 0), load(n1_h, 1)
    tick_b(7)
    load_n1.wait()
    turn_into(1, tmp.at[1])
    turn_into(0, ml)
    attention_close(2)
    attention_open(3)
    tick_a(8)
    attention_heads(3, [(1, lambda: tick_b(8))])
    attention_close(3)
    pq_save(3).wait()
    tick_a(9)
    load_x.wait()

    def third(at_rows):
        grad = norm_grad(tmp[0, at_rows, :].astype(f32), gx[at_rows, :], 0, 1, vec[1:2, :]) + gm[at_rows, :]
        tmp[1, at_rows, :] = grad.astype(bf16)

    row_parts(third)
    swap_lat = Swap(place, tmp.at[1], o_lat, swap_sems, 1)
    swap_lat.start()

    for c in range(cols_n):
        spot = slice(c * hc, (c + 1) * hc)
        for k in range(6):
            tt[c, 0:1, k * hc:(k + 1) * hc] = gv[k:k + 1, spot]
        tt[c, 1:2, 576:576 + hc] = gv[6:7, spot]
        tt[c, 1:2, 576 + hc:] = gv[7:8, spot]
    copy_t = send(tt, tc, t_sems.at[0], t_sems.at[1], place.to_core)
    copy_t.start()
    tick_b(9)
    copy_t.wait()
    tt[...] = tt[...] + tc[...]

    def u_copy(k):
        to = (col + k) % cols_n
        return send(tt.at[to], um.at[col], u_sems.at[0, k], u_sems.at[1, col], (row, to))

    def u_got(k):
        src = (col + k) % cols_n
        return send(tt.at[src], um.at[src], u_sems.at[0, k], u_sems.at[1, src], (row, src))

    for k in range(1, cols_n):
        u_copy(k).start()
    um[col] = tt[col]
    tick_a(10)
    for k in range(1, cols_n):
        u_got(k).wait_recv()
    copy_v = send(um, vm_, v_sems.at[0], v_sems.at[1], flip_y)
    copy_v.start()
    tick_b(10)
    copy_v.wait_recv()
    modl[...] = jnp.zeros_like(modl)
    sums = um[0] + vm_[0]
    for c in range(1, cols_n):
        sums = sums + um[c] + vm_[c]
    o_rows[...] = sums
    for c in range(cols_n):
        modl[2 * place.y + c % 2, c // 2:c // 2 + 1, :] = um[c, 0:1, :]
        modl[2 - 2 * place.y + c % 2, c // 2:c // 2 + 1, :] = vm_[c, 0:1, :]
    low = modl[...].reshape(rows_n * 8, 6 * hc).astype(bf16)
    o_ada[...] = tn(act[...].reshape(rows_n * 8, drows).astype(bf16), low)
    cp[...] = nt(low, ada[...]).reshape(rows_n, 8, drows)

    def cr_copy(k):
        return send(cp, cr.at[col], cr_sems.at[0, k], cr_sems.at[1, col], (row, (col + k) % cols_n))

    def cr_got(k):
        src = (col + k) % cols_n
        return send(cp, cr.at[src], cr_sems.at[0, k], cr_sems.at[1, src], (row, src))

    for k in range(1, cols_n):
        cr_copy(k).start()
    tick_a(11)
    tick_b(11)
    for k in range(1, cols_n):
        cr_got(k).wait_recv()
        cr_copy(k).wait_send()
    cr[col] = cp[...]
    cp[...] = sum(cr[c] for c in range(cols_n))

    def cf_copy(k):
        to = (row + k) % rows_n
        return send(cp.at[to], cf.at[row], cf_sems.at[0, k], cf_sems.at[1, row], (to, col))

    def cf_got(k):
        src = (row + k) % rows_n
        return send(cp.at[src], cf.at[src], cf_sems.at[0, k], cf_sems.at[1, src], (src, col))

    for k in range(1, rows_n):
        cf_copy(k).start()
    cf[row] = cp[row]
    tick_b(12)
    for k in range(1, rows_n):
        cf_got(k).wait_recv()
    cond_value = cond[...]
    gate = 1.0 / (1.0 + jnp.exp(-cond_value))
    slope = gate * (1.0 + cond_value * (1.0 - gate))
    for r in range(rows_n):
        spot = slice(r * drows, (r + 1) * drows)
        o_cond[:, spot] = cf[r] * slope[:, spot]
    tick_b(13)
    left_finish(0)
    left_finish(1)
    tick_b(14)
    left_finish(2)

    for s in range(3 * depth - 4, 3 * depth):
        for j in range(2):
            for copy in c1(s, j):
                copy.wait_send()
        for copy in c2(s):
            copy.wait_send()
        if s % depth < depth - 1:
            for copy in c3(s):
                copy.wait_send()
    for s in range(3 * depth - 2, 3 * depth):
        for y in range(2):
            c0(s, y).wait_send()
    for g in range(3):
        left_copy(g).wait_send()
    for k in range(1, cols_n):
        u_copy(k).wait_send()
    copy_v.wait_send()
    for k in range(1, rows_n):
        cf_copy(k).wait_send()
    swap_lat.wait()
    swap_out.wait()


def backward(saved, out, lse, vec, act, ada, cond, collective_id):
    rows, cols = lax.axis_size("row"), lax.axis_size("col")
    depth = cols // 2
    tokens, width = out.shape
    heads, drows, hc6 = width // HEAD_DIM, ada.shape[0], ada.shape[1]
    hc, lanes, lrows = width // cols, 1152, drows // 2
    shape, dma, vm = jax.ShapeDtypeStruct, pltpu.SemaphoreType.DMA, pltpu.VMEM
    token = shape((tokens, width), bf16)
    outs = [token, token, shape((depth, tokens, 896), bf16), shape((drows, 576), f32), shape((drows, 576), f32),
            shape((drows, 3 * hc), f32), shape((drows, hc), f32), shape((drows, hc6), f32), shape((8, hc6), f32),
            shape((8, width), f32)]
    head = (tokens, HEAD_DIM)
    scratch = [
        vm((4, 2, drows, lanes), bf16), vm((2, 2, drows, lanes), bf16), vm((2, 2, drows, lanes), bf16),
        vm((4, 2, drows, 512), bf16), vm((4, 2, lrows, 128), bf16), vm((4, drows, 512), bf16), vm((4, lrows, 128), bf16),
        vm((3, depth - 1, drows, 512), bf16), vm((3, depth - 1, lrows, 128), bf16), vm((3, lrows, 128), f32), vm((3, lrows, 128), f32),
        vm((2, width, lanes), bf16), vm((2, tokens, lanes), bf16), vm((depth, tokens, lanes), bf16), vm((tokens, 896), bf16),
        vm((2, width, tokens), bf16), vm((2, tokens, width), bf16), vm((tokens, width), bf16), vm((tokens, width), f32),
        vm((tokens, width), f32), vm((2, tokens, lanes), bf16), vm((2, tokens, 384), bf16), vm((5, 4) + head, bf16),
        vm((4,) + head, bf16), vm((4, 1, tokens), f32), vm((2, 4) + head, bf16), vm((2, 2, 4) + head, bf16), vm((3, 4) + head, f32),
        vm((16, width), f32),
        vm((cols, 8, hc6), f32), vm((cols, 8, hc6), f32), vm((cols, 8, hc6), f32), vm((cols, 8, hc6), f32), vm((rows, 8, hc6), f32),
        vm((rows, 8, drows), f32), vm((cols, rows, 8, drows), f32), vm((rows, 8, drows), f32)]
    scratch += [
        dma((2, 2)), dma((2, 2, 2)), dma((2, 4, 2, 2)), dma((2, 4, 2)), dma((2, 3, depth, 2)), dma((2, 3)), dma((2,)), dma((2, 2)),
        dma((2,)), dma((3,)), dma((5,)), dma((2, 2, 2, 4)), dma((depth,)), dma((2,)), dma((2, cols)), dma((2,)), dma((2, cols)),
        dma((2, rows))]
    vmem = pl.BlockSpec(memory_space=pltpu.VMEM)
    return pl.pallas_call(
        backward_kernel,
        out_shape=outs,
        in_specs=[ANY] * 16 + [vmem] * 5,
        out_specs=[ANY] * 3 + [vmem] * 7,
        scratch_shapes=scratch,
        compiler_params=pltpu.CompilerParams(collective_id=collective_id, has_side_effects=True, vmem_limit_bytes=63 * 2**20),
        name="backward",
    )(*saved, out, lse, vec, act, ada, cond)


class Plan:
    def __init__(self, latents, condition, qkv_weight, fc1_weight):
        self.rows, self.cols = lax.axis_size("row"), lax.axis_size("col")
        self.tokens, self.width = latents.shape
        self.lats = condition.shape[0]
        self.depth_rows = qkv_weight.shape[0]
        self.head_cols = qkv_weight.shape[2]
        self.ff_cols = fc1_weight.shape[1]
        self.share = SEQ // self.tokens
        self.near = (
            self.rows == 4 and self.share == 2 and self.cols == 8 and self.lats == self.cols // 2
            and (self.depth_rows, self.head_cols, self.ff_cols) == (288, 2 * HEAD_DIM, 576) and self.width == 1152)


def fold(left):
    rows, lanes = left.shape
    return left.reshape(2, rows // 2, lanes).transpose(1, 0, 2).reshape(rows // 2, 2 * lanes)


def gather_plain(blocks):
    return [lax.all_gather(lax.all_gather(b, "row", axis=0, tiled=True), "col", axis=1, tiled=True) for b in blocks]


def scatter_plain(fulls):
    parts = [lax.psum_scatter(g, "row", scatter_dimension=0, tiled=True) for g in fulls]
    return [lax.psum_scatter(g, "col", scatter_dimension=1, tiled=True).astype(f32) for g in parts]


def attend_plain(q, k, v):
    def one(item):
        scores = nt(item[0], item[1]) * HEAD_DIM ** (-0.5)
        top = jnp.max(scores, axis=-1, keepdims=True)
        probs = jnp.exp(scores - top)
        total = jnp.sum(probs, axis=-1, keepdims=True)
        return nn((probs / total).astype(bf16), item[2]).astype(bf16), top + jnp.log(total)

    return lax.map(one, (q, k, v))


def attend_back_plain(q, k, v, lse, att_grad):
    def one(item):
        q, k, v, lse, out_grad = item
        probs = jnp.exp(nt(q, k) * HEAD_DIM ** (-0.5) - lse)
        probs_grad = nt(out_grad, v)
        inner = jnp.sum(probs * probs_grad, axis=-1, keepdims=True)
        grad = (probs * (probs_grad - inner) * HEAD_DIM ** (-0.5)).astype(bf16)
        return nn(grad, k), tn(grad, q), tn(probs.astype(bf16), out_grad)

    return lax.map(one, (q, k, v, lse, att_grad))


def gelu_and_slope(u):
    c = math.sqrt(2.0 / math.pi)
    inner = jnp.tanh(c * (u + 0.044715 * u * u * u))
    value = 0.5 * u * (1.0 + inner)
    slope = 0.5 * (1.0 + inner) + 0.5 * u * (1.0 - inner * inner) * c * (1.0 + 3 * 0.044715 * u * u)
    return value, slope


def layer_norm(values):
    mean = jnp.mean(values, axis=-1, keepdims=True)
    centred = values - mean
    inverse = lax.rsqrt(jnp.mean(centred * centred, axis=-1, keepdims=True) + norm_eps)
    return centred * inverse, inverse


def norm_back(rows_grad, normal, inverse, scale):
    normal_grad = rows_grad * (1.0 + scale)
    first = jnp.mean(normal_grad, axis=-1, keepdims=True)
    second = jnp.mean(normal_grad * normal, axis=-1, keepdims=True)
    value_grad = inverse * (normal_grad - first - normal * second)
    return value_grad, jnp.sum(rows_grad, axis=0), jnp.sum(rows_grad * normal, axis=0)


def shards_near(plan, latents, condition, ada_weight, ada_bias, qkv_weight, qv_bias, proj_weight, proj_bias,
                fc1_weight, fc1_bias, fc2_weight, fc2_bias, cotangent):
    depth, hc, fc = plan.depth_rows, plan.head_cols, plan.ff_cols
    q_main, p_main, f_main = 384, 128, 512
    qkv_flat = qkv_weight.reshape(depth, 3 * hc)
    proj_t, fc2_t = proj_weight.T, fc2_weight.T
    left_a = fold(jnp.concatenate([qkv_flat[:, q_main:], proj_t[:, p_main:]], axis=1))
    blocks = [qkv_flat[:, :q_main], proj_t[:, :p_main], left_a,
              fc1_weight[:, :f_main], fold(fc1_weight[:, f_main:]), fc2_t[:, :f_main], fold(fc2_t[:, f_main:])]
    cond = jnp.pad(condition.astype(f32), ((0, 8 - plan.lats), (0, 0)))
    ada = ada_weight.reshape(depth, 6 * hc)
    line = jnp.concatenate([fc1_bias, proj_bias, fc2_bias]).astype(f32).reshape(1, 6 * hc)
    tail = jnp.pad(qv_bias.astype(f32).reshape(1, 2 * hc), ((0, 0), (0, 4 * hc)))
    bias = jnp.concatenate([jnp.broadcast_to(ada_bias.astype(f32).reshape(1, 6 * hc), (plan.lats, 6 * hc)), line, tail,
                            jnp.zeros((8 - plan.lats - 2, 6 * hc), f32)], axis=0)
    (w, dy, x, n1, q, k, v, k2, v2, lse, att, ba, mid, n2, hid, slo, out, vec, act) = forward(
        latents, cotangent, cond, ada, bias, blocks, 0)
    output, lat_grad, _, fc2_sum, fc1_sum, qkv_sum, proj_sum, ada_sum, rows, cond_grad = backward(
        (w, dy, x, n1, q, k, v, k2, v2, att, ba, mid, n2, hid, slo), out, lse, vec, act, ada, cond, 1)
    return (
        output, lat_grad.astype(f32), cond_grad[:plan.lats], ada_sum.reshape(depth, 6, hc), rows[0].reshape(6, hc),
        qkv_sum.reshape(depth, 3, hc), rows[2, :2 * hc].reshape(2, hc), proj_sum.T, rows[1, fc:fc + hc],
        fc1_sum, rows[1, :fc], fc2_sum.T, rows[1, fc + hc:])


def shards(latents, condition, ada_weight, ada_bias, qkv_weight, qv_bias, proj_weight, proj_bias,
           fc1_weight, fc1_bias, fc2_weight, fc2_bias, cotangent):
    plan = Plan(latents, condition, qkv_weight, fc1_weight)
    if plan.near:
        return shards_near(plan, latents, condition, ada_weight, ada_bias, qkv_weight, qv_bias, proj_weight, proj_bias,
                           fc1_weight, fc1_bias, fc2_weight, fc2_bias, cotangent)
    row, col = lax.axis_index("row"), lax.axis_index("col")
    rows, cols, width, tokens = plan.rows, plan.cols, plan.width, plan.tokens
    depth, hc, fc = plan.depth_rows, plan.head_cols, plan.ff_cols
    heads = cols * hc // HEAD_DIM
    groups = rows * plan.lats

    blocks = [qkv_weight.reshape(depth, 3 * hc), proj_weight.T, fc1_weight, fc2_weight.T]
    qkv_w, proj_w, fc1_w, fc2_w = gather_plain(blocks)
    home = row * plan.lats + col // plan.share
    values, grad_out = latents.astype(f32), cotangent.astype(f32)

    cond_all = lax.all_gather(condition, "row", axis=0, tiled=True).astype(f32)
    cond_act = jax.nn.silu(cond_all).astype(bf16)
    cond_mine = lax.dynamic_slice(cond_act, (0, row * depth), (groups, depth))
    ada_flat = ada_weight.reshape(depth, 6 * hc)
    partial = lax.psum(nn(cond_mine, ada_flat), "row") + ada_bias.astype(f32).reshape(1, 6 * hc)
    small = jnp.concatenate(
        [partial.reshape(-1)] + [b.astype(f32).reshape(-1) for b in (proj_bias, fc2_bias, fc1_bias, qv_bias)])
    small = lax.all_gather(small, "col", axis=0, tiled=False)
    sizes = [groups * 6 * hc, hc, hc, fc, 2 * hc]
    mod_all, proj_b, fc2_b, fc1_b, qv_b = jnp.split(small, [sum(sizes[:i + 1]) for i in range(4)], axis=1)
    mod = lax.dynamic_index_in_dim(mod_all.reshape(cols, groups, 6, hc), home, 1, keepdims=False)
    mod = mod.transpose(1, 0, 2).reshape(6, 1, width)
    shift_one, scale_one, gate_one, shift_two, scale_two, gate_two = (mod[k] for k in range(6))
    proj_b, fc2_b, fc1_b = proj_b.reshape(width), fc2_b.reshape(width), fc1_b.reshape(-1)
    q_b, v_b = qv_b[:, :hc].reshape(heads, 1, HEAD_DIM), qv_b[:, hc:].reshape(heads, 1, HEAD_DIM)

    def to_heads(flat):
        return flat.reshape(tokens, heads, HEAD_DIM).transpose(1, 0, 2)

    def from_heads(value):
        return value.transpose(1, 0, 2).reshape(tokens, cols, hc)

    normal_one, inverse_one = layer_norm(values)
    normed_one = (normal_one * (1.0 + scale_one) + shift_one).astype(bf16)
    projected = nn(normed_one, qkv_w).reshape(tokens, cols, 3 * hc)
    query = (to_heads(projected[:, :, :hc]) + q_b).astype(bf16)
    key = to_heads(projected[:, :, hc:2 * hc]).astype(bf16)
    value = (to_heads(projected[:, :, 2 * hc:]) + v_b).astype(bf16)
    cuts = [[s * plan.share + i for i in range(plan.share)] for s in range(cols // plan.share)]
    key_all = lax.all_gather(key, "col", axis=1, tiled=True, axis_index_groups=cuts)
    value_all = lax.all_gather(value, "col", axis=1, tiled=True, axis_index_groups=cuts)
    att, lse = attend_plain(query, key_all, value_all)
    att_flat = from_heads(att).reshape(tokens, width)
    branch_a = nt(att_flat, proj_w) + proj_b
    middle = values + gate_one * branch_a

    normal_two, inverse_two = layer_norm(middle)
    normed_two = (normal_two * (1.0 + scale_two) + shift_two).astype(bf16)
    hidden, slope = gelu_and_slope(nn(normed_two, fc1_w) + fc1_b)
    hidden = hidden.astype(bf16)
    branch_m = nt(hidden, fc2_w) + fc2_b
    output = (middle + gate_two * branch_m).astype(bf16)

    gate_two_grad = jnp.sum(grad_out * branch_m, axis=0)
    m_grad = grad_out * gate_two
    fc2_bias_part = jnp.sum(m_grad, axis=0)
    m_low = m_grad.astype(bf16)
    fc2_grad = tn(m_low, hidden).astype(bf16)
    pre_grad = nn(m_low, fc2_w) * slope
    fc1_bias_part = jnp.sum(pre_grad, axis=0)
    pre_low = pre_grad.astype(bf16)
    fc1_grad = tn(normed_two, pre_low).astype(bf16)
    normed_two_grad = nt(pre_low, fc1_w)
    middle_part, shift_two_grad, scale_two_grad = norm_back(normed_two_grad, normal_two, inverse_two, scale_two)
    middle_grad = grad_out + middle_part
    gate_one_grad = jnp.sum(middle_grad * branch_a, axis=0)
    a_grad = middle_grad * gate_one
    proj_bias_part = jnp.sum(a_grad, axis=0)
    a_low = a_grad.astype(bf16)
    proj_grad = tn(a_low, att_flat).astype(bf16)
    att_grad = to_heads(nn(a_low, proj_w).astype(bf16))
    query_grad, key_grad, value_grad = attend_back_plain(query, key_all, value_all, lse, att_grad)
    key_grad, value_grad = (
        lax.psum_scatter(g.astype(bf16), "col", scatter_dimension=1, tiled=True, axis_index_groups=cuts).astype(f32)
        for g in (key_grad, value_grad))
    q_bias_part, v_bias_part = jnp.sum(query_grad, axis=1), jnp.sum(value_grad, axis=1)
    qkv_low = jnp.concatenate([from_heads(g.astype(bf16)) for g in (query_grad, key_grad, value_grad)], axis=2)
    qkv_low = qkv_low.reshape(tokens, 3 * width)
    qkv_grad = tn(normed_one, qkv_low).astype(bf16)
    normed_one_grad = nt(qkv_low, qkv_w)
    fc2_sum, fc1_sum, qkv_sum, proj_sum = scatter_plain([fc2_grad, fc1_grad, qkv_grad, proj_grad])
    input_part, shift_one_grad, scale_one_grad = norm_back(normed_one_grad, normal_one, inverse_one, scale_one)
    latents_grad = middle_grad + input_part

    mod_grad = jnp.stack(
        [shift_one_grad, scale_one_grad, gate_one_grad, shift_two_grad, scale_two_grad, gate_two_grad], axis=0)
    mod_grad = lax.all_gather(mod_grad, ("row", "col"), axis=0, tiled=False)
    mod_grad = mod_grad.reshape(groups, plan.share, 6, width).sum(axis=1)
    mod_mine = lax.dynamic_slice(mod_grad, (0, 0, col * hc), (groups, 6, hc))
    ada_bsum = jnp.sum(mod_mine, axis=0)
    mod_low = mod_mine.astype(bf16).reshape(groups, 6 * hc)
    ada_wsum = tn(cond_mine, mod_low).reshape(depth, 6, hc)
    cond_part = lax.dynamic_update_slice(jnp.zeros((groups, width), f32), nt(mod_low, ada_flat), (0, row * depth))
    parts = [cond_part, proj_bias_part, fc2_bias_part, q_bias_part, v_bias_part, fc1_bias_part]
    totals = lax.psum(jnp.concatenate([part.reshape(-1) for part in parts]), ("row", "col"))
    ends, spot = [], 0
    for part in parts:
        ends.append(totals[spot:spot + part.size])
        spot += part.size

    def mine(flat):
        size = flat.size // cols
        return lax.dynamic_slice(flat, (col * size,), (size,))

    cond_summed = lax.dynamic_slice(ends[0].reshape(groups, width), (row * plan.lats, 0), (plan.lats, width))
    silu_value, silu_pull = jax.vjp(jax.nn.silu, condition.astype(f32))
    condition_grad = silu_pull(cond_summed)[0]
    qv_bsum = jnp.stack([mine(ends[3]), mine(ends[4])], axis=0)
    return (
        output, latents_grad, condition_grad, ada_wsum, ada_bsum, qkv_sum.reshape(depth, 3, hc), qv_bsum,
        proj_sum.T, mine(ends[1]), fc1_sum, mine(ends[5]), fc2_sum.T, mine(ends[2]))


def solution(mesh):
    token, grid, turned = P(("row", "col"), None), P("row", "col"), P("col", "row")
    cube, wide, flat = P("row", None, "col"), P(None, "col"), P("col")
    return jax.shard_map(
        shards,
        mesh=mesh,
        in_specs=(token, P("row", None), cube, wide, cube, wide, turned, flat, grid, flat, turned, flat, token),
        out_specs=(token, token, P("row", None), cube, wide, cube, wide, turned, flat, grid, flat, turned, flat),
        check_vma=False,
    )
```

```python
import functools
import math
import jax
import jax.numpy as jnp
from jax import lax
from jax.experimental import pallas as pl
from jax.experimental.pallas import tpu as pltpu
from jax.sharding import PartitionSpec as P

HEAD_DIM = 72
SEQ = 1024
norm_eps = 1e-06
bf16, f32 = jnp.bfloat16, jnp.float32

MESH = pl.DeviceIdType.MESH
ANY = pl.BlockSpec(memory_space=pl.ANY)


class Place:
    def __init__(self):
        row, col = lax.axis_index("row"), lax.axis_index("col")
        self.row, self.col = row, col
        self.depth = lax.axis_size("col") // 2
        self.y, self.h = row // 2, row % 2
        self.z, self.x = col // 2, col % 2
        self.p = jnp.where(self.h == 0, self.y, self.x)
        self.q = jnp.where(self.h == 0, self.x, self.y)
        flip_x, flip_y = (row, col + 1 - 2 * self.x), (row + 2 - 4 * self.y, col)
        self.to_q = tuple(jnp.where(self.h == 0, a, b) for a, b in zip(flip_x, flip_y))
        self.to_p = tuple(jnp.where(self.h == 0, b, a) for a, b in zip(flip_x, flip_y))
        self.to_core = (row + 1 - 2 * self.h, col)

    def to_z(self, z):
        return (self.row, 2 * z + self.x)

    def diagonal(self):
        return (self.row + 1 - 2 * self.h, self.col + 1 - 2 * self.x)

    def yx(self, p, q):
        return jnp.where(self.h == 0, p, q), jnp.where(self.h == 0, q, p)

    def partners(self):
        near = [self.to_q, self.to_p, self.to_core]
        return near + [self.to_z((self.z + k) % self.depth) for k in range(1, self.depth)]


def greet(partners):
    barrier = pltpu.get_barrier_semaphore()
    for partner in partners:
        pl.semaphore_signal(barrier, inc=1, device_id=partner, device_id_type=MESH)
    pl.semaphore_wait(barrier, len(partners))


def block_at(ref, rows, lanes, r, c):
    return ref.at[pl.ds(pl.multiple_of(r * rows, 16), rows), pl.ds(pl.multiple_of(c * lanes, 128), lanes)]


class Gather:
    def __init__(self, place, ins, outs, sems):
        self.at, self.ins, self.outs = place, ins, outs
        self.local, self.zs, self.zzs, self.qs, self.ps, self.ks = sems
        self.early = place.h == 0

    @staticmethod
    def scratch(count, depth):
        dma = pltpu.SemaphoreType.DMA
        return [dma((count,)), dma((count, 2, depth)), dma((count, 2, depth)), dma((count, 2, depth)), dma((count, 2, depth, 2)),
                dma((count, 2, depth, 4))]

    def block(self, a, p, q, z):
        y, x = self.at.yx(p, q)
        rows, lanes = self.ins[a].shape
        return block_at(self.outs[a], rows, lanes, 2 * y + self.at.h, 2 * z + x)

    def zc(self, t):
        return (self.at.z + self.at.depth - t) % self.at.depth

    def copy(self, src, dst, sems, index, to):
        return pltpu.make_async_remote_copy(
            src_ref=src, dst_ref=dst, send_sem=sems.at[(index[0], 0) + index[1:]], recv_sem=sems.at[(index[0], 1) + index[1:]],
            device_id=to, device_id_type=MESH)

    def spot(self, a, t, j=0):
        p, q = self.at.p, self.at.q
        return self.block(a, p if j < 2 else 1 - p, q if j % 2 == 0 else 1 - q, self.zc(t))

    def source(self, a, t, j=0):
        return self.ins[a] if t == 0 and j == 0 else self.spot(a, t, j)

    def c_local(self, a):
        return pltpu.make_async_copy(self.ins[a], self.spot(a, 0), self.local.at[a])

    def c_z(self, a, k, j):
        place, sems = self.at, (self.zs, self.zzs)[j]
        return pltpu.make_async_remote_copy(
            src_ref=self.source(a, 0, j), dst_ref=self.spot(a, 0, j), send_sem=sems.at[a, 0, k], recv_sem=sems.at[a, 1, place.z],
            device_id=place.to_z((place.z + k) % place.depth), device_id_type=MESH)

    def r_z(self, a, t, j):
        place, sems = self.at, (self.zs, self.zzs)[j]
        return pltpu.make_async_remote_copy(
            src_ref=self.source(a, 0, j), dst_ref=self.spot(a, t, j), send_sem=sems.at[a, 0, 0], recv_sem=sems.at[a, 1, self.zc(t)],
            device_id=place.to_q, device_id_type=MESH)

    def c_q(self, a, t):
        return self.copy(self.source(a, t), self.spot(a, t), self.qs, (a, self.zc(t)), self.at.to_q)

    def c_p(self, a, t, j):
        return self.copy(self.source(a, t, j), self.spot(a, t, j), self.ps, (a, self.zc(t), j), self.at.to_p)

    def c_k(self, a, t, j):
        return self.copy(self.source(a, t, j), self.spot(a, t, j), self.ks, (a, self.zc(t), j), self.at.to_core)

    def start(self, a):
        self.c_q(a, 0).start()
        for k in range(1, self.at.depth):
            self.c_z(a, k, 0).start()
        self.c_local(a).start()

    def forward(self, a):
        @pl.when(self.early)
        def _():
            self.c_q(a, 0).wait_recv()
            for k in range(1, self.at.depth):
                self.c_z(a, k, 1).start()

    def stage(self, a, t, n):
        late = jnp.logical_not(self.early)
        if n == 0:
            if t > 0:
                self.r_z(a, t, 0).wait_recv()
                pl.when(late)(self.c_q(a, t).start)
            self.c_p(a, t, 0).start()
            self.c_k(a, t, 0).start()
        elif n == 1:
            pl.when(late)(self.c_q(a, t).wait_recv)
            if t > 0:
                pl.when(self.early)(self.r_z(a, t, 1).wait_recv)
            self.c_p(a, t, 1).start()
            self.c_k(a, t, 1).start()
        elif n == 2:
            self.c_p(a, t, 0).wait_recv()
            self.c_k(a, t, 2).start()
        elif n == 3:
            self.c_p(a, t, 1).wait_recv()
            self.c_k(a, t, 3).start()
        else:
            if t == 0:
                self.c_local(a).wait()
            for j in range(4):
                self.c_k(a, t, j).wait_recv()

    def finish(self, a):
        self.c_q(a, 0).wait_send()
        for k in range(1, self.at.depth):
            self.c_z(a, k, 0).wait_send()

        @pl.when(self.early)
        def _():
            for k in range(1, self.at.depth):
                self.c_z(a, k, 1).wait_send()

        @pl.when(jnp.logical_not(self.early))
        def _():
            for t in range(1, self.at.depth):
                self.c_q(a, t).wait_send()

        for t in range(self.at.depth):
            for j in range(2):
                self.c_p(a, t, j).wait_send()
            for j in range(4):
                self.c_k(a, t, j).wait_send()


class LineGather(Gather):
    def __init__(self, place, ins, outs, sems, mid=()):
        super().__init__(place, ins, outs, sems)
        z = place.z
        self.core0, self.mid = place.h == 0, mid
        self.middle = jnp.logical_and(z > 0, z < place.depth - 1)
        low = z < 2
        self.inner = place.to_z(jnp.where(low, z + 1, z - 1))
        self.outer = place.to_z(jnp.where(low, jnp.maximum(z - 1, 0), jnp.minimum(z + 1, place.depth - 1)))
        self.order = [z, z + 1 - 2 * (z % 2), jnp.where(low, 2, 1), jnp.where(low, 3, 0)]

    @staticmethod
    def scratch(count, depth):
        dma = pltpu.SemaphoreType.DMA
        return [dma((count,)), dma((count, 2, 5)), dma((count, 2, 5)), dma((count, 2, depth)), dma((count, 2, depth, 2)),
                dma((count, 2, depth, 4))]

    def early(self, a):
        return self.core0 if a in self.mid else jnp.logical_and(self.core0, False)

    def zc(self, t):
        return self.order[t]

    def c_z(self, a, t, j, n):
        sems = (self.zs, self.zzs)[j]
        return pltpu.make_async_remote_copy(
            src_ref=self.source(a, t, j), dst_ref=self.spot(a, t, j), send_sem=sems.at[a, 0, n], recv_sem=sems.at[a, 1, self.zc(t)],
            device_id=self.inner if n in (0, 2) else self.outer, device_id_type=MESH)

    def z_start(self, a, j):
        self.c_z(a, 0, j, 0).start()
        pl.when(self.middle)(self.c_z(a, 0, j, 1).start)

    def z_got(self, a, t, j):
        self.c_z(a, t, j, 0).wait_recv()
        pl.when(self.middle)(self.c_z(a, t, j, 1 + t).start)

    def z_sent(self, a, j):
        self.c_z(a, 0, j, 0).wait_send()

        @pl.when(self.middle)
        def _():
            self.c_z(a, 0, j, 1).wait_send()
            for t in range(1, self.at.depth):
                self.c_z(a, t, j, 1 + t).wait_send()

    def start(self, a):
        self.c_q(a, 0).start()
        self.z_start(a, 0)
        self.c_local(a).start()

    def forward(self, a):
        if a in self.mid:
            @pl.when(self.core0)
            def _():
                self.c_q(a, 0).wait_recv()
                self.z_start(a, 1)

    def stage(self, a, t, n):
        mid, early = a in self.mid, self.core0
        late = jnp.logical_not(early)
        if n == 0:
            if t > 0:
                self.z_got(a, t, 0)
                if mid:
                    pl.when(late)(self.c_q(a, t).start)
                else:
                    self.c_q(a, t).start()
            self.c_p(a, t, 0).start()
            self.c_k(a, t, 0).start()
        elif n == 1:
            if not mid:
                self.c_q(a, t).wait_recv()
            else:
                pl.when(late)(self.c_q(a, t).wait_recv)
                if t > 0:
                    pl.when(early)(lambda: self.z_got(a, t, 1))
            self.c_p(a, t, 1).start()
            self.c_k(a, t, 1).start()
        elif n == 2:
            self.c_p(a, t, 0).wait_recv()
            self.c_k(a, t, 2).start()
        elif n == 3:
            self.c_p(a, t, 1).wait_recv()
            self.c_k(a, t, 3).start()
        else:
            if t == 0:
                self.c_local(a).wait()
            for j in range(4):
                self.c_k(a, t, j).wait_recv()

    def finish(self, a):
        self.c_q(a, 0).wait_send()
        self.z_sent(a, 0)

        def rest():
            for t in range(1, self.at.depth):
                self.c_q(a, t).wait_send()

        if a in self.mid:
            pl.when(self.core0)(lambda: self.z_sent(a, 1))
            pl.when(jnp.logical_not(self.core0))(rest)
        else:
            rest()
        for t in range(self.at.depth):
            for j in range(2):
                self.c_p(a, t, j).wait_send()
            for j in range(4):
                self.c_k(a, t, j).wait_send()


def nt(a, b):
    return lax.dot_general(a, b, (((1,), (1,)), ((), ())), preferred_element_type=f32)


def nn(a, b):
    return lax.dot_general(a, b, (((1,), (0,)), ((), ())), preferred_element_type=f32)


def tn(a, b):
    return lax.dot_general(a, b, (((0,), (0,)), ((), ())), preferred_element_type=f32)


SOFT = HEAD_DIM ** (-0.5) * math.log2(math.e)


VECS = 24


def softmax_head(q, k, k2):
    one, two = nt(k, q), nt(k2, q)
    top = jnp.maximum(jnp.max(one, axis=0, keepdims=True), jnp.max(two, axis=0, keepdims=True)) * SOFT
    one, two = jnp.exp2(one * SOFT - top), jnp.exp2(two * SOFT - top)
    total = jnp.sum(one, axis=0, keepdims=True) + jnp.sum(two, axis=0, keepdims=True)
    return one.astype(bf16), two.astype(bf16), total, top + jnp.log2(total)


def norm_rows(values):
    mean = jnp.mean(values, axis=-1, keepdims=True)
    centred = values - mean
    inverse = lax.rsqrt(jnp.mean(centred * centred, axis=-1, keepdims=True) + norm_eps)
    return centred * inverse, inverse


def gelu_both(u):
    c = math.sqrt(2.0 / math.pi)
    square = u * u
    inner = jnp.tanh(u * (c + (c * 0.044715) * square))
    half = 0.5 * (1.0 + inner)
    slope = half + (0.5 * u) * (1.0 - inner * inner) * (c + (3 * c * 0.044715) * square)
    return u * half, slope


class Swap:
    def __init__(self, place, src, dst, sems, i):
        self.stay = place.h == place.x
        self.local = pltpu.make_async_copy(src, dst, sems.at[i, 0])
        self.remote = pltpu.make_async_remote_copy(
            src_ref=src, dst_ref=dst, send_sem=sems.at[i, 0], recv_sem=sems.at[i, 1],
            device_id=place.diagonal(), device_id_type=MESH)

    def start(self):
        pl.when(self.stay)(self.local.start)
        pl.when(jnp.logical_not(self.stay))(self.remote.start)

    def wait(self):
        pl.when(self.stay)(self.local.wait)
        pl.when(jnp.logical_not(self.stay))(self.remote.wait)


def unfold_into(left, target):
    rows = target.shape[0] // 4
    half = rows // 2
    for r in range(4):
        tile = left[r * half:(r + 1) * half, :].astype(f32)
        target[r * rows:r * rows + half, :] = jnp.concatenate([tile[:, :64], tile[:, 128:192]], axis=1).astype(bf16)
        target[r * rows + half:(r + 1) * rows, :] = jnp.concatenate([tile[:, 64:128], tile[:, 192:]], axis=1).astype(bf16)


GROUPS = (3, 2, 2)


def forward_kernel(*refs):
    lat, cot, cond, ada, bias = refs[:5]
    blocks, refs = refs[5:12], refs[12:]
    fulls, refs = refs[:7], refs[7:]
    (o_w, o_cot, o_x, o_n1, o_q, o_k, o_v, o_k2, o_v2, o_lse, o_att, o_ba, o_mid, o_n2, o_hid, o_slo, o_out, o_vec, o_act), refs = refs[:19], refs[19:]
    (x_v, n1, q_v, k_v, v_v, k2_v, v2_v, lse_v, ot, att, ba, mid, n2, hid, slo, acc, wbuf, lbuf, out_v, cot_v, vec,
     c_send, c_recv, s_send, s_recv, m_own, m_oth), refs = refs[:27], refs[27:]
    ag_sems, (swap_sems, c_sems, s_sems, m_sems, o_sems, kv_sems, w_sems, save_sems, wsave_sems) = refs[:6], refs[6:]

    place = Place()
    depth, rows_n = place.depth, 4
    row, col = place.row, place.col
    cols_n = 2 * depth
    tokens, width = x_v.shape
    hc = width // cols_n
    drows = ada.shape[0]
    q_main, p_main = blocks[0].shape[1], blocks[1].shape[1]
    half = tokens // 2

    row_peers = [((row + k) % rows_n, col) for k in range(1, rows_n)]
    col_peers = [(row, (col + k) % cols_n) for k in range(1, cols_n)]
    greet(place.partners() + row_peers + col_peers + [place.diagonal()])

    def send(src, dst, s_sem, r_sem, to):
        return pltpu.make_async_remote_copy(
            src_ref=src, dst_ref=dst, send_sem=s_sem, recv_sem=r_sem, device_id=to, device_id_type=MESH)

    cond_value = cond[...]
    act = (cond_value / (1.0 + jnp.exp(-cond_value))).astype(bf16).astype(f32)
    for r in range(rows_n):
        c_send[r] = act[:, r * drows:(r + 1) * drows]

    def cond_copy(k):
        to = (row + k) % rows_n
        return send(c_send.at[to], c_recv.at[row], c_sems.at[0, k], c_sems.at[1, row], (to, col))

    def cond_got(k):
        src = (row + k) % rows_n
        return send(c_send.at[src], c_recv.at[src], c_sems.at[0, k], c_sems.at[1, src], (src, col))

    for k in range(1, rows_n):
        cond_copy(k).start()
    swap_x = Swap(place, lat, x_v, swap_sems, 0)
    swap_x.start()

    work = LineGather(place, blocks, fulls, ag_sems, range(7))
    for a in range(3):
        work.start(a)

    members, first = [], 0
    for size in GROUPS:
        members.append(list(range(first, first + size)))
        first += size
    chunks = [(g, t) for g in range(len(GROUPS)) for t in range(depth)]
    events = []
    for s in range(len(chunks) + 4):
        if s % depth == 2 and s < 2 * depth:
            events.append((s // depth + 1, "start"))
        if s in (1, 3, depth + 3):
            events.append(((s + 1) // depth, "forward"))
        events += [(s - n, n) for n in range(5) if 0 <= s - n < len(chunks)]
    at = [0]

    def pump(count):
        for s, n in events[at[0]:at[0] + count]:
            if n in ("start", "forward"):
                for a in members[s]:
                    (work.start if n == "start" else work.forward)(a)
                continue
            g, t = chunks[s]
            for a in members[g]:
                work.stage(a, t, n)
        at[0] += count

    def pump_to(s, n):
        pump(max(0, events.index((s, n)) + 1 - at[0]))

    pump_to(0, 0)
    c_recv[row] = c_send[row]
    for k in range(1, rows_n):
        cond_got(k).wait_recv()
    act_all = c_recv[...].reshape(rows_n * 8, drows).astype(bf16)
    s_send[...] = nn(act_all, ada[...]).reshape(rows_n, 8, 6 * hc)

    def sum_copy(k):
        to = (row + k) % rows_n
        return send(s_send.at[to], s_recv.at[row], s_sems.at[0, k], s_sems.at[1, row], (to, col))

    def sum_got(k):
        src = (row + k) % rows_n
        return send(s_send.at[src], s_recv.at[src], s_sems.at[0, k], s_sems.at[1, src], (src, col))

    for k in range(1, rows_n):
        sum_copy(k).start()
    pump_to(0, 1)
    s_recv[row] = s_send[row]
    for k in range(1, rows_n):
        sum_got(k).wait_recv()
    m_own[col] = s_recv[0] + s_recv[1] + s_recv[2] + s_recv[3] + bias[...]

    def mod_copy(k):
        return send(m_own.at[col], m_own.at[col], m_sems.at[0, k], m_sems.at[1, col], (row, (col + k) % cols_n))

    def mod_got(k):
        src = (col + k) % cols_n
        return send(m_own.at[src], m_own.at[src], m_sems.at[0, k], m_sems.at[1, src], (row, src))

    for k in range(1, cols_n):
        mod_copy(k).start()
    pump_to(0, 2)
    for k in range(1, cols_n):
        mod_got(k).wait_recv()
    other = send(m_own, m_oth, o_sems.at[0], o_sems.at[1], place.to_core)
    other.start()
    pump_to(0, 3)
    other.wait_recv()
    stay = place.h == place.x
    for c in range(cols_n):
        line = jnp.where(stay, m_own[c, pl.ds(place.z, 1), :], m_oth[c, pl.ds(place.z, 1), :])
        for k in range(6):
            vec[k:k + 1, c * hc:(c + 1) * hc] = line[:, k * hc:(k + 1) * hc]
        line = m_own[c, 4:5, :]
        vec[6:7, c * hc:(c + 1) * hc] = line[:, 576:576 + hc]
        vec[7:8, c * hc:(c + 1) * hc] = line[:, 576 + hc:]
        z, i = c // 2, c % 2
        vec[16 + z:17 + z, i * 512:(i + 1) * 512] = line[:, :512]
        vec[16 + z:17 + z, 1024 + i * 64:1024 + (i + 1) * 64] = line[:, 512:576]

    swap_x.wait()
    swap_dy = Swap(place, cot, o_cot, swap_sems, 1)
    swap_dy.start()
    part = 128

    def row_parts(body):
        @pl.loop(0, tokens // part)
        def _(i):
            body(pl.ds(pl.multiple_of(i * part, part), part))

    def first_norm(at_rows):
        normal, _ = norm_rows(x_v[at_rows, :].astype(f32))
        n1[at_rows, :] = (normal * (1.0 + vec[1:2, :]) + vec[0:1, :]).astype(bf16)

    row_parts(first_norm)

    saves = []

    def save(src, dst):
        copy = pltpu.make_async_copy(src, dst, save_sems.at[len(saves)])
        copy.start()
        saves.append(copy)

    save(x_v, o_x)
    save(n1, o_n1)
    save(c_recv, o_act)

    def fetch(s):
        g, t = chunks[s]
        zc, slot = work.zc(t), s % depth
        lanes = [q_main, p_main] if g == 0 else [blocks[members[g][0]].shape[1]]
        spot, copies = 0, []
        for i, n in enumerate(lanes):
            src = fulls[members[g][i]].at[:, pl.ds(pl.multiple_of(zc * 2 * n, 128), 2 * n)]
            copies.append(pltpu.make_async_copy(src, wbuf.at[slot, :, spot:spot + 2 * n], w_sems.at[s % 2, i]))
            spot += 2 * n
        src = fulls[members[g][-1]].at[:, pl.ds(pl.multiple_of(zc * 256, 128), 256)]
        copies.append(pltpu.make_async_copy(src, lbuf.at[s % 2], w_sems.at[s % 2, 2]))
        return copies

    def fetch_start(s):
        pump_to(s, 4)
        if s >= depth:
            weight_save(s - depth).wait()
        for copy in fetch(s):
            copy.start()

    def fetch_wait(s):
        for copy in fetch(s):
            copy.wait()
        unfold_into(lbuf.at[s % 2], wbuf.at[s % depth, :, 1024:1152])
        weight_save(s).start()

    def weight_save(s):
        g, t = chunks[s]
        return pltpu.make_async_copy(wbuf.at[s % depth], o_w.at[g, work.zc(t)], wsave_sems.at[s])

    def swap_kv(i, h):
        src, dst = ((k_v, k2_v), (v_v, v2_v))[i]
        return send(src.at[h], dst.at[h], kv_sems.at[0, i, h], kv_sems.at[1, i, h], place.to_core)

    def project(s):
        t, slot = chunks[s][1], s % depth
        zc = work.zc(t)

        @pl.loop(0, 2)
        def _(i):
            at_rows = pl.ds(pl.multiple_of(i * half, half), half)
            main = nn(n1[at_rows, :], wbuf[slot, :, :2 * q_main])
            left = nn(n1[at_rows, :], wbuf[slot, :, 1024:1152])
            for j in range(2):
                biases = m_own[2 * zc + j]
                own = main[:, j * q_main:(j + 1) * q_main]
                tail = left[:, j * 64:j * 64 + 3 * hc - q_main]
                for e in range(2):
                    h = 4 * zc + 2 * j + e
                    a = e * HEAD_DIM
                    q_v[h, at_rows, :] = (own[:, a:a + HEAD_DIM] + biases[5:6, a:a + HEAD_DIM]).astype(bf16)
                    k_v[h, at_rows, :] = own[:, hc + a:hc + a + HEAD_DIM].astype(bf16)
                    if e == 0:
                        value = own[:, 2 * hc:2 * hc + HEAD_DIM]
                    else:
                        value = jnp.concatenate([own[:, 2 * hc + HEAD_DIM:], tail], axis=1)
                    v_v[h, at_rows, :] = (value + biases[5:6, hc + a:hc + a + HEAD_DIM]).astype(bf16)

        for i in range(4):
            swap_kv(0, 4 * zc + i).start()
            swap_kv(1, 4 * zc + i).start()

    def attention(s):
        zc = work.zc(chunks[s][1])
        start = at[0]

        @pl.loop(0, 4)
        def _(i):
            h = 4 * zc + i
            swap_kv(0, h).wait_recv()
            swap_kv(1, h).wait_recv()
            one, two, total, lse = softmax_head(q_v[h], k_v[h], k2_v[h])
            ot[i] = (tn(v_v[h], one) + tn(v2_v[h], two)) / total
            lse_v[h] = lse
            for k in range(4):
                at[0] = start + k

                @pl.when(i == k)
                def _():
                    pump(1)

        at[0] = start + 4
        att[zc, :, 2 * p_main:] = jnp.zeros((tokens, 128), bf16)
        for j in range(2):
            pair = jnp.concatenate([ot[2 * j], ot[2 * j + 1]], axis=0).T.astype(bf16)
            att[zc, :, j * p_main:(j + 1) * p_main] = pair[:, :p_main]
            att[zc, :, 2 * p_main + 64 * j + 48:2 * p_main + 64 * j + 64] = pair[:, p_main:]

        @pl.loop(0, 2)
        def _(i):
            at_rows = pl.ds(pl.multiple_of(i * half, half), half)
            term = nt(att[zc, at_rows, :], wbuf[s % depth, :, 2 * q_main:])
            if s == 0:
                acc[at_rows, :] = term
            else:
                acc[at_rows, :] += term

    for s in range(depth):
        fetch_start(s)
        fetch_wait(s)
        project(s)
        if s > 0:
            attention(s - 1)
    attention(depth - 1)
    for src, dst in ((q_v, o_q), (k_v, o_k), (v_v, o_v), (k2_v, o_k2), (v2_v, o_v2), (lse_v, o_lse), (att, o_att)):
        save(src, dst)

    def second_norm(at_rows):
        branch = acc[at_rows, :] + vec[6:7, :]
        ba[at_rows, :] = branch.astype(bf16)
        middle = x_v[at_rows, :].astype(f32) + vec[2:3, :] * branch
        mid[at_rows, :] = middle
        normal, _ = norm_rows(middle)
        n2[at_rows, :] = (normal * (1.0 + vec[4:5, :]) + vec[3:4, :]).astype(bf16)

    row_parts(second_norm)
    for src, dst in ((ba, o_ba), (mid, o_mid), (n2, o_n2)):
        save(src, dst)

    for s in range(depth, 2 * depth):
        fetch_start(s)
        fetch_wait(s)
        zc = work.zc(chunks[s][1])

        def up(at_rows):
            u = nn(n2[at_rows, :], wbuf[s % depth]) + vec[pl.ds(16 + zc, 1), :]
            value, slope = gelu_both(u)
            hid[zc, at_rows, :] = value.astype(bf16)
            slo[zc, at_rows, :] = slope.astype(bf16)

        row_parts(up)
    save(hid, o_hid)
    save(slo, o_slo)
    for s in range(2 * depth, 3 * depth):
        fetch_start(s)
        fetch_wait(s)
        zc = work.zc(chunks[s][1])

        def down(at_rows):
            term = nt(hid[zc, at_rows, :], wbuf[s % depth])
            if s == 2 * depth:
                acc[at_rows, :] = term
            else:
                acc[at_rows, :] += term

        row_parts(down)

    swap_dy.wait()
    load_dy = pltpu.make_async_copy(o_cot, cot_v, w_sems.at[0, 0])
    load_dy.start()
    load_dy.wait()
    vec[8:9, :] = jnp.zeros((1, width), f32)

    def finish(at_rows):
        branch = acc[at_rows, :] + vec[7:8, :]
        out_v[at_rows, :] = (mid[at_rows, :] + vec[5:6, :] * branch).astype(bf16)
        vec[8:9, :] += jnp.sum(cot_v[at_rows, :].astype(f32) * branch, axis=0, keepdims=True)

    row_parts(finish)
    save(out_v, o_out)
    save(vec, o_vec)

    for a in range(7):
        work.finish(a)
    for k in range(1, rows_n):
        cond_copy(k).wait_send()
        sum_copy(k).wait_send()
    for k in range(1, cols_n):
        mod_copy(k).wait_send()
    other.wait_send()

    @pl.loop(0, 4 * depth)
    def _(h):
        swap_kv(0, h).wait_send()
        swap_kv(1, h).wait_send()

    for s in range(2 * depth, 3 * depth):
        weight_save(s).wait()
    for copy in saves:
        copy.wait()


def forward(lat, cot, cond, ada, bias, blocks, collective_id):
    rows, cols = lax.axis_size("row"), lax.axis_size("col")
    depth = cols // 2
    tokens, width = lat.shape
    heads = width // HEAD_DIM
    lanes = 1152
    hc6 = ada.shape[1]
    shape = jax.ShapeDtypeStruct
    head = shape((heads, tokens, HEAD_DIM), bf16)
    token = shape((tokens, width), bf16)
    outs = [shape((rows * b.shape[0], cols * b.shape[1]), bf16) for b in blocks] + [
        shape((3, depth, width, lanes), bf16), token, token, token, head, head, head, head, head,
        shape((heads, 1, tokens), f32), shape((depth, tokens, 384), bf16), token, shape((tokens, width), f32), token,
        shape((depth, tokens, lanes), bf16), shape((depth, tokens, lanes), bf16), token, shape((VECS, width), f32), shape((rows, 8, ada.shape[0]), f32)]
    dma, vm = pltpu.SemaphoreType.DMA, pltpu.VMEM
    t16, h16 = vm((tokens, width), bf16), vm((heads, tokens, HEAD_DIM), bf16)
    drows = ada.shape[0]
    scratch = [
        t16, t16, h16, h16, h16, h16, h16, vm((heads, 1, tokens), f32), vm((4, HEAD_DIM, tokens), f32),
        vm((depth, tokens, 384), bf16), t16, vm((tokens, width), f32), t16, vm((depth, tokens, lanes), bf16),
        vm((depth, tokens, lanes), bf16), vm((tokens, width), f32), vm((depth, width, lanes), bf16), vm((2, width // 2, 256), bf16),
        t16, t16, vm((VECS, width), f32), vm((rows, 8, drows), f32), vm((rows, 8, drows), f32), vm((rows, 8, hc6), f32),
        vm((rows, 8, hc6), f32), vm((cols, 8, hc6), f32), vm((cols, 8, hc6), f32)]
    scratch += LineGather.scratch(len(blocks), depth)
    scratch += [dma((2, 2)), dma((2, rows)), dma((2, rows)), dma((2, cols)), dma((2,)), dma((2, 2, heads)), dma((2, 3)), dma((32,)),
                dma((3 * depth,))]
    vmem = pl.BlockSpec(memory_space=pltpu.VMEM)
    got = pl.pallas_call(
        forward_kernel,
        out_shape=outs,
        in_specs=[ANY, ANY, vmem, vmem, vmem] + [ANY] * len(blocks),
        out_specs=[ANY] * len(outs),
        scratch_shapes=scratch,
        compiler_params=pltpu.CompilerParams(collective_id=collective_id, has_side_effects=True, vmem_limit_bytes=62 * 2**20),
        name="forward",
    )(lat, cot, cond, ada, bias, *blocks)
    return got[len(blocks):]


SLOTS = 4


def backward_kernel(*refs):
    (w, dy_h, x_h, n1_h, q_h, k_h, v_h, k2_h, v2_h, att_h, ba_h, mid_h, n2_h, hid_h, slo_h, out_h), refs = refs[:16], refs[16:]
    (lse, vec, act, ada, cond), refs = refs[:5], refs[5:]
    (o_out, o_lat, o_pq, o_fc2, o_fc1, o_qkv, o_proj, o_ada, o_rows, o_cond), refs = refs[:10], refs[10:]
    (acc, give, r0, r1, r1l, r2, r2l, r3, r3l, lf, lx), refs = refs[:11], refs[11:]
    (wbuf, hs, pre, pq, turn, tmp, ml, gm, gx, att, heads, grad_o, delta, kv_give, kv_got, own, gv, att_w), refs = refs[:18], refs[18:]
    (tt, tc, um, vm_, modl, cp, cr, cf), refs = refs[:8], refs[8:]
    (swap_sems, s0, s1, s2, s3, lx_sems, w_sems, hs_sems, slo_sems, tmp_sems, head_sems, kv_sems, pq_sems, t_sems, u_sems, v_sems, cr_sems, cf_sems, att_sems) = refs

    place = Place()
    depth, rows_n = place.depth, 4
    row, col, h = place.row, place.col, place.h
    cols_n = 2 * depth
    tokens, width = ml.shape
    hc = width // cols_n
    drows = ada.shape[0]
    lrows = drows // 2
    half, part = tokens // 2, 128
    q_main, p_main = 384, 128
    scale = HEAD_DIM ** (-0.5)
    row_peers = [((row + k) % rows_n, col) for k in range(1, rows_n)]
    col_peers = [(row, (col + k) % cols_n) for k in range(1, cols_n)]
    flip_x, flip_y = (row, col + 1 - 2 * place.x), (row + 2 - 4 * place.y, col)
    greet(place.partners() + row_peers + col_peers + [place.diagonal()])

    def send(src, dst, s_sem, r_sem, to):
        return pltpu.make_async_remote_copy(
            src_ref=src, dst_ref=dst, send_sem=s_sem, recv_sem=r_sem, device_id=to, device_id_type=MESH)

    def row_parts(body):
        @pl.loop(0, tokens // part)
        def _(i):
            body(pl.ds(pl.multiple_of(i * part, part), part))

    def row_halves(body):
        @pl.loop(0, 2)
        def _(i):
            body(pl.ds(pl.multiple_of(i * half, half), half))

    low = place.z < 2
    middle = jnp.logical_and(place.z > 0, place.z < depth - 1)
    inner = place.to_z(jnp.where(low, place.z + 1, place.z - 1))
    outer = place.to_z(jnp.where(low, jnp.maximum(place.z - 1, 0), jnp.minimum(place.z + 1, depth - 1)))
    far = [jnp.where(low, 3, 0), jnp.where(low, 2, 1), place.z + 1 - 2 * (place.z % 2), place.z]

    def zc(t):
        return far[t]

    def load(src, i):
        copy = pltpu.make_async_copy(src, tmp.at[i], tmp_sems.at[i])
        copy.start()
        return copy

    def weight_load(u):
        return pltpu.make_async_copy(w.at[2 - u // depth, zc(u % depth)], wbuf.at[u % 2], w_sems.at[u % 2])

    def slope_load(u):
        return pltpu.make_async_copy(slo_h.at[zc(u)], pre.at[zc(u)], slo_sems.at[u])

    def weight_use(u):
        weight_load(u).wait()
        if u + 1 < 3 * depth:
            weight_load(u + 1).start()


    def tick_loads(s):
        g, t = s // depth, s % depth
        if g == 0:
            return [pltpu.make_async_copy(hid_h.at[zc(t)], hs.at[s % 2], hs_sems.at[s % 2, 0])]
        if g == 1:
            return []
        return [pltpu.make_async_copy(o_pq.at[zc(t)], hs.at[s % 2, :, :896], hs_sems.at[s % 2, 0]),
                pltpu.make_async_copy(att_h.at[zc(t)], att_w.at[s % 2], hs_sems.at[s % 2, 1])]

    def tick_prefetch(s):
        if s < 3 * depth:
            if s // depth == 2:
                pq_wait(s % depth)
            for copy in tick_loads(s):
                copy.start()

    saved = set()

    def pq_wait(t):
        if t not in saved:
            saved.add(t)
            pq_save(t).wait()

    def pq_save(t):
        return pltpu.make_async_copy(pq, o_pq.at[zc(t)], pq_sems.at[t])

    def c0(s, y):
        return send(give.at[s % 2, y], r0.at[s % 2, y], s0.at[0, s % 2, y], s0.at[1, s % 2, y], place.to_core)

    def spots(s, y, x):
        return (acc.at[s % SLOTS, y, :, pl.ds(pl.multiple_of(x * 512, 512), 512)],
                acc.at[s % SLOTS, y, pl.ds(pl.multiple_of(x * lrows, 16), lrows), 1024:1152])

    def c1(s, j):
        main, left = spots(s, *place.yx(1 - place.p, j))
        k = s % 4
        return [send(main, r1.at[k, j], s1.at[0, k, j, 0], s1.at[1, k, j, 0], place.to_p),
                send(left, r1l.at[k, j], s1.at[0, k, j, 1], s1.at[1, k, j, 1], place.to_p)]

    zq = h == 0
    qz = jnp.logical_not(zq)

    def c2(s):
        main, left = spots(s, *place.yx(place.p, 1 - place.q))
        k = jnp.where(zq, s // depth, s % 4) if s % depth == depth - 1 else s % 4
        return [send(main, r2.at[k], s2.at[0, k, 0], s2.at[1, k, 0], place.to_q),
                send(left, r2l.at[k], s2.at[0, k, 1], s2.at[1, k, 1], place.to_q)]

    def z_copy(s, j, inward, slot):
        g, t = s // depth, s % depth
        main, left = spots(s, *place.yx(place.p, place.q if j == 0 else 1 - place.q))
        to = inner if inward else outer
        return [send(main, r3.at[j, slot], s3.at[0, j, g, t, 0], s3.at[1, j, slot, 0, 0], to),
                send(left, r3l.at[j, slot], s3.at[0, j, g, t, 1], s3.at[1, j, slot, 0, 1], to)]

    def z_stage(s, j, inside):
        g, t = s // depth, s % depth
        par = g % 2
        if t == depth - 1:
            return
        if inside:
            slot = (par, 2, 3 + par)[t]
            for copy in z_copy(s, j, True, slot):
                copy.wait_recv()
            for into, other in zip(spots(s, *place.yx(place.p, place.q if j == 0 else 1 - place.q)), (r3.at[j, slot], r3l.at[j, slot])):
                add_into(into, other)
            copies = z_copy(s, j, t < 2, (3 + par, 5 + par, 5 + par)[t])
        else:
            copies = z_copy(s, j, True, (par, 2, 7 + par)[t])
        for copy in copies:
            copy.start()

    def z_stages(s, twice, inside):
        where = jnp.logical_and(zq if twice else qz, middle if inside else jnp.logical_not(middle))

        @pl.when(where)
        def _():
            z_stage(s, 0, inside)
            if twice:
                z_stage(s, 1, inside)

    def z_got(g, j):
        par = g % 2
        last = (g + 1) * depth - 1
        for copy in z_copy(last, j, True, 5 + par):
            copy.wait_recv()

        @pl.when(middle)
        def _():
            for copy in z_copy(last, j, True, 7 + par):
                copy.wait_recv()

    def z_sum(g, j, value, refs, index):
        par = g % 2
        value = value + refs[(j, 5 + par) + index].astype(f32)
        return jnp.where(middle, value + refs[(j, 7 + par) + index].astype(f32), value)

    def sent(s):
        for j in range(2):
            for copy in c1(s, j):
                copy.wait_send()
        if s % depth < depth - 1:
            for copy in z_copy(s, 0, True, 0):
                copy.wait_send()

            @pl.when(zq)
            def _():
                for copy in z_copy(s, 1, True, 0):
                    copy.wait_send()

            @pl.when(qz)
            def _():
                for copy in c2(s):
                    copy.wait_send()
        else:
            for copy in c2(s):
                copy.wait_send()

    def add_into(into, other):
        n = into.shape[0]

        @pl.loop(0, n // 48)
        def _(i):
            at_rows = pl.ds(pl.multiple_of(i * 48, 16), 48)
            into[at_rows, :] = into[at_rows, :] + other[at_rows, :]

    def tick_a(s):
        g, t = s // depth, s % depth
        k = s % SLOTS
        if s >= SLOTS:
            sent(s - SLOTS)
        if s >= 2:
            for y in range(2):
                c0(s - 2, y).wait_send()
        for copy in tick_loads(s):
            copy.wait()

        def rows_of(r):
            at_rows = pl.ds(pl.multiple_of(r * drows, 16), drows)
            if g == 0:
                return nn(turn[0, at_rows, :], hs[s % 2]).astype(bf16)
            if g == 1:
                return nn(turn[0, at_rows, :], pre[zc(t)]).astype(bf16)
            one = nn(turn[1, at_rows, :], hs[s % 2, :, :896])
            two = nn(turn[0, at_rows, :], att_w[s % 2])
            return jnp.concatenate(
                [one[:, :q_main], two[:, :p_main], one[:, q_main:2 * q_main], two[:, p_main:2 * p_main],
                 one[:, 2 * q_main:] + two[:, 2 * p_main:]], axis=1).astype(bf16)

        @pl.loop(0, 2)
        def _(y):
            give[s % 2, y] = rows_of(2 * y + 1 - h)
            acc[k, y] = rows_of(2 * y + h)

        for y in range(2):
            c0(s, y).start()
        if s + 1 < 3 * depth - 1:
            tick_prefetch(s + 1)

    def tick_b(s):
        if s < 3 * depth:
            for y in range(2):
                c0(s, y).wait_recv()
            for y in range(2):
                add_into(acc.at[s % SLOTS, y], r0.at[s % 2, y])
            for j in range(2):
                for copy in c1(s, j):
                    copy.start()
        if 0 <= s - 1 < 3 * depth:
            n = s - 1
            for j in range(2):
                for copy in c1(n, j):
                    copy.wait_recv()
            for into, other in zip(spots(n, *place.yx(place.p, 1 - place.q)), (r1.at[n % 4, 1 - place.q], r1l.at[n % 4, 1 - place.q])):
                add_into(into, other)

            @pl.when(qz)
            def _():
                for copy in c2(n):
                    copy.start()

            for into, other in zip(spots(n, *place.yx(place.p, place.q)), (r1.at[n % 4, place.q], r1l.at[n % 4, place.q])):
                add_into(into, other)
            z_stages(n, True, False)
        if 0 <= s - 2 < 3 * depth:
            n = s - 2

            @pl.when(qz)
            def _():
                for copy in c2(n):
                    copy.wait_recv()
                for into, other in zip(spots(n, *place.yx(place.p, place.q)), (r2.at[n % 4], r2l.at[n % 4])):
                    add_into(into, other)

            z_stages(n, False, False)
            z_stages(n, True, True)
            if n % depth == depth - 1:
                pl.when(zq)(lambda: hand_over(n))
        if 0 <= s - 3 < 3 * depth:
            z_stages(s - 3, False, True)
            if (s - 3) % depth == depth - 1:
                total((s - 3) // depth)

    def hand_over(n):
        g = n // depth
        z_got(g, 1)
        main, left = spots(n, *place.yx(place.p, 1 - place.q))

        @pl.loop(0, drows // 48)
        def _(i):
            at_rows = pl.ds(pl.multiple_of(i * 48, 16), 48)
            main[at_rows, :] = z_sum(g, 1, main[at_rows, :].astype(f32), r3, (at_rows,)).astype(bf16)

        left[...] = z_sum(g, 1, left[...].astype(f32), r3l, ()).astype(bf16)
        for copy in c2(n):
            copy.start()

    def left_copy(g):
        return send(lf.at[g], lx.at[g], lx_sems.at[0, g], lx_sems.at[1, g], flip_x)

    def total(g):
        last = (g + 1) * depth - 1
        z_got(g, 0)
        main, left = spots(last, *place.yx(place.p, place.q))

        def write(handed):
            if handed:
                for copy in c2(last):
                    copy.wait_recv()

            @pl.loop(0, drows // 48)
            def _(i):
                at_rows = pl.ds(pl.multiple_of(i * 48, 16), 48)
                value = z_sum(g, 0, main[at_rows, :].astype(f32), r3, (at_rows,))
                if handed:
                    value = value + r2[g, at_rows, :].astype(f32)
                if g == 0:
                    o_fc2[at_rows, :512] = value
                elif g == 1:
                    o_fc1[at_rows, :512] = value
                else:
                    o_qkv[at_rows, :q_main] = value[:, :q_main]
                    o_proj[at_rows, :p_main] = value[:, q_main:]

            value = z_sum(g, 0, left[...].astype(f32), r3l, ())
            lf[g] = value + r2l[g].astype(f32) if handed else value

        pl.when(zq)(lambda: write(True))
        pl.when(qz)(lambda: write(False))
        left_copy(g).start()

    def left_finish(g):
        left_copy(g).wait_recv()
        first = place.x == 0
        top = jnp.where(first, lf[g][:, :64], lx[g][:, 64:])
        bottom = jnp.where(first, lx[g][:, :64], lf[g][:, 64:])
        tail = 3 * hc - q_main
        for spot, value in ((0, top), (lrows, bottom)):
            if g == 0:
                o_fc2[spot:spot + lrows, 512:] = value
            elif g == 1:
                o_fc1[spot:spot + lrows, 512:] = value
            else:
                o_qkv[spot:spot + lrows, q_main:] = value[:, :tail]
                o_proj[spot:spot + lrows, p_main:] = value[:, tail:]

    def turn_into(i, src):
        @pl.loop(0, width // 128)
        def _(n):
            spot = pl.ds(pl.multiple_of(n * 128, 128), 128)
            turn[i, spot, :] = src[:, spot].T

    swap_out = Swap(place, out_h, o_out, swap_sems, 0)
    load_dy = load(dy_h, 0)
    weight_load(0).start()
    for u in range(depth):
        slope_load(u).start()
    tick_prefetch(0)
    swap_out.start()
    gv[...] = jnp.zeros_like(gv)
    tt[...] = jnp.zeros_like(tt)
    gv[5:6, :] = vec[8:9, :]
    load_dy.wait()

    def first(at_rows):
        grad = tmp[0, at_rows, :].astype(f32) * vec[5:6, :]
        gv[7:8, :] += jnp.sum(grad, axis=0, keepdims=True)
        ml[at_rows, :] = grad.astype(bf16)

    row_parts(first)
    turn_into(0, ml)

    def hidden_back(u):
        z = zc(u)
        weight_use(u)
        slope_load(u).wait()
        sums = gv.at[8:9, :]
        sums[...] = jnp.zeros((1, width), f32)

        def body(at_rows):
            grad = nn(ml[at_rows, :], wbuf[u % 2]) * pre[z, at_rows, :].astype(f32)
            sums[...] += jnp.sum(grad, axis=0, keepdims=True)
            pre[z, at_rows, :] = grad.astype(bf16)

        row_parts(body)
        for j in range(2):
            tt[2 * z + j, 1:2, :512] = sums[:, 512 * j:512 * (j + 1)]
            tt[2 * z + j, 1:2, 512:576] = sums[:, 1024 + 64 * j:1024 + 64 * (j + 1)]

    def normed_back(u):
        z = zc(u % depth)
        weight_use(u)

        def body(at_rows):
            term = nt(pre[z, at_rows, :], wbuf[u % 2])
            if u == depth:
                gx[at_rows, :] = term
            else:
                gx[at_rows, :] += term

        row_parts(body)

    tick_a(0)
    hidden_back(0)
    tick_b(0)
    hidden_back(1)
    hidden_back(2)
    tick_a(1)
    hidden_back(3)
    tick_b(1)
    normed_back(depth)
    normed_back(depth + 1)
    tick_a(2)
    normed_back(depth + 2)
    tick_b(2)
    normed_back(depth + 3)

    load_mid = pltpu.make_async_copy(mid_h, gm, tmp_sems.at[2])
    load_mid.start()
    load_ba, load_dy = load(ba_h, 1), load(dy_h, 0)
    load_mid.wait()
    load_ba.wait()
    load_dy.wait()

    def norm_grad(values, grads, shift_row, scale_row, scale_vec):
        normal, inverse = norm_rows(values)
        gv[shift_row:shift_row + 1, :] += jnp.sum(grads, axis=0, keepdims=True)
        gv[scale_row:scale_row + 1, :] += jnp.sum(grads * normal, axis=0, keepdims=True)
        inner = grads * (1.0 + scale_vec)
        one = jnp.mean(inner, axis=-1, keepdims=True)
        two = jnp.mean(inner * normal, axis=-1, keepdims=True)
        return inverse * (inner - one - normal * two)

    def second(at_rows):
        grad = norm_grad(gm[at_rows, :], gx[at_rows, :], 3, 4, vec[4:5, :]) + tmp[0, at_rows, :].astype(f32)
        gm[at_rows, :] = grad
        gv[2:3, :] += jnp.sum(grad * tmp[1, at_rows, :].astype(f32), axis=0, keepdims=True)
        grad = grad * vec[2:3, :]
        gv[6:7, :] += jnp.sum(grad, axis=0, keepdims=True)
        ml[at_rows, :] = grad.astype(bf16)

    row_parts(second)

    def heads_load(t):
        spot = pl.ds(4 * zc(t), 4)
        return [pltpu.make_async_copy(src.at[spot], heads.at[i], head_sems.at[i])
                for i, src in enumerate((q_h, k_h, v_h, k2_h, v2_h))]

    def att_load(t):
        return pltpu.make_async_copy(att_h.at[zc(t)], att, att_sems.at[0])

    def kv_swap(t, kind, i):
        return send(kv_give.at[kind, i], kv_got.at[t % 2, kind, i], kv_sems.at[0, 0, kind, i], kv_sems.at[1, t % 2, kind, i], place.to_core)

    def pair_of(value, j):
        spot = 2 * p_main + 64 * j + 48
        return jnp.concatenate([value[:, j * p_main:(j + 1) * p_main], value[:, spot:spot + 16]], axis=1)

    def attention_open(t):
        u = 2 * depth + t
        weight_use(u)
        att_load(t).wait()

        def body(at_rows):
            grads = nn(ml[at_rows, :], wbuf[u % 2, :, 2 * q_main:])
            results = att[at_rows, :].astype(f32)
            for j in range(2):
                grad = pair_of(grads, j).astype(bf16)
                product = (grad.astype(f32) * pair_of(results, j)).T
                for e in range(2):
                    grad_o[2 * j + e, at_rows, :] = grad[:, e * HEAD_DIM:(e + 1) * HEAD_DIM]
                    delta[2 * j + e, :, at_rows] = jnp.sum(product[e * HEAD_DIM:(e + 1) * HEAD_DIM, :], axis=0, keepdims=True)

        row_halves(body)
        for copy in heads_load(t):
            copy.wait()

    def attention_heads(t, between):
        @pl.loop(0, 4)
        def _(i):
            q, out_grad, shift, less = heads[0, i], grad_o[i], lse[4 * zc(t) + i], delta[i]

            def side(k, v):
                probs = jnp.exp2(nt(k, q) * SOFT - shift)
                grad = (probs * (nt(v, out_grad) - less)).astype(bf16)
                return nn(grad, q) * scale, nn(probs.astype(bf16), out_grad), tn(k, grad)

            dk, dv, dq_two = side(heads[3, i], heads[4, i])
            kv_give[0, i] = dk.astype(bf16)
            kv_give[1, i] = dv.astype(bf16)
            kv_swap(t, 0, i).start()
            kv_swap(t, 1, i).start()
            dk, dv, dq_one = side(heads[1, i], heads[2, i])
            own[1, i] = dk
            own[2, i] = dv
            own[0, i] = ((dq_one + dq_two) * scale).T
            for n, action in between:
                pl.when(i == n)(action)

    def attention_close(t):
        u = 2 * depth + t
        z = zc(t)
        if t + 1 < depth:
            for copy in heads_load(t + 1):
                copy.start()
            att_load(t + 1).start()
        for kind in range(2):
            for i in range(4):
                kv_swap(t, kind, i).wait()
        if t > 0:
            pq_wait(t - 1)

        def body(at_rows):
            for j in range(2):
                pieces, tails = [[], [], []], None
                for e in range(2):
                    i = 2 * j + e
                    dq = own[0, i, at_rows, :]
                    dk = own[1, i, at_rows, :] + kv_got[t % 2, 0, i, at_rows, :].astype(f32)
                    dv = own[2, i, at_rows, :] + kv_got[t % 2, 1, i, at_rows, :].astype(f32)
                    tt[2 * z + j, 2:3, e * HEAD_DIM:(e + 1) * HEAD_DIM] += jnp.sum(dq, axis=0, keepdims=True)
                    tt[2 * z + j, 2:3, hc + e * HEAD_DIM:hc + (e + 1) * HEAD_DIM] += jnp.sum(dv, axis=0, keepdims=True)
                    for n, value in enumerate((dq, dk, dv)):
                        pieces[n].append(value)
                last = pieces[2][1]
                cut = q_main - 2 * hc - HEAD_DIM
                line = pieces[0] + pieces[1] + [pieces[2][0], last[:, :cut]]
                pq[at_rows, j * q_main:(j + 1) * q_main] = jnp.concatenate(line, axis=1).astype(bf16)
                rest = jnp.concatenate([last[:, cut:], jnp.zeros((last.shape[0], 64 - HEAD_DIM + cut), f32)], axis=1)
                pq[at_rows, 2 * q_main + 64 * j:2 * q_main + 64 * (j + 1)] = rest.astype(bf16)
            term = nt(pq[at_rows, :2 * q_main], wbuf[u % 2, :, :2 * q_main]) + nt(pq[at_rows, 2 * q_main:], wbuf[u % 2, :, 1024:])
            if t == 0:
                gx[at_rows, :] = term
            else:
                gx[at_rows, :] += term

        row_halves(body)
        pq_save(t).start()

    for copy in heads_load(0):
        copy.start()
    att_load(0).start()
    load_n2 = load(n2_h, 0)
    tick_a(3)
    load_n2.wait()
    turn_into(0, tmp.at[0])
    load_x, load_n1 = load(x_h, 0), load(n1_h, 1)
    tick_b(3)
    attention_open(0)
    attention_heads(0, [(1, lambda: tick_a(4)), (3, lambda: tick_b(4))])
    attention_close(0)
    attention_open(1)
    tick_a(5)
    attention_heads(1, [(0, lambda: tick_b(5)), (2, lambda: tick_a(6)), (3, lambda: tick_b(6))])
    attention_close(1)
    tick_a(7)
    load_n1.wait()
    turn_into(1, tmp.at[1])
    turn_into(0, ml)
    attention_open(2)
    attention_heads(2, [(0, lambda: tick_b(7)), (2, lambda: tick_a(8))])
    tick_b(8)
    attention_close(2)
    attention_open(3)
    tick_a(9)
    attention_heads(3, [(0, lambda: tick_b(9)), (2, lambda: tick_a(10))])
    tick_b(10)
    attention_close(3)
    tick_prefetch(11)
    load_x.wait()

    def third(at_rows):
        grad = norm_grad(tmp[0, at_rows, :].astype(f32), gx[at_rows, :], 0, 1, vec[1:2, :]) + gm[at_rows, :]
        tmp[1, at_rows, :] = grad.astype(bf16)

    row_parts(third)
    swap_lat = Swap(place, tmp.at[1], o_lat, swap_sems, 1)
    swap_lat.start()
    tick_a(11)

    for c in range(cols_n):
        spot = slice(c * hc, (c + 1) * hc)
        for k in range(6):
            tt[c, 0:1, k * hc:(k + 1) * hc] = gv[k:k + 1, spot]
        tt[c, 1:2, 576:576 + hc] = gv[6:7, spot]
        tt[c, 1:2, 576 + hc:] = gv[7:8, spot]
    copy_t = send(tt, tc, t_sems.at[0], t_sems.at[1], place.to_core)
    copy_t.start()
    tick_b(11)
    copy_t.wait()
    tt[...] = tt[...] + tc[...]

    def u_copy(k):
        to = (col + k) % cols_n
        return send(tt.at[to], um.at[col], u_sems.at[0, k], u_sems.at[1, col], (row, to))

    def u_got(k):
        src = (col + k) % cols_n
        return send(tt.at[src], um.at[src], u_sems.at[0, k], u_sems.at[1, src], (row, src))

    for k in range(1, cols_n):
        u_copy(k).start()
    um[col] = tt[col]
    tick_b(12)
    for k in range(1, cols_n):
        u_got(k).wait_recv()
    copy_v = send(um, vm_, v_sems.at[0], v_sems.at[1], flip_y)
    copy_v.start()
    tick_b(13)
    copy_v.wait_recv()
    modl[...] = jnp.zeros_like(modl)
    sums = um[0] + vm_[0]
    for c in range(1, cols_n):
        sums = sums + um[c] + vm_[c]
    o_rows[...] = sums
    for c in range(cols_n):
        modl[2 * place.y + c % 2, c // 2:c // 2 + 1, :] = um[c, 0:1, :]
        modl[2 - 2 * place.y + c % 2, c // 2:c // 2 + 1, :] = vm_[c, 0:1, :]
    low = modl[...].reshape(rows_n * 8, 6 * hc).astype(bf16)
    o_ada[...] = tn(act[...].reshape(rows_n * 8, drows).astype(bf16), low)
    cp[...] = nt(low, ada[...]).reshape(rows_n, 8, drows)

    def cr_copy(k):
        return send(cp, cr.at[col], cr_sems.at[0, k], cr_sems.at[1, col], (row, (col + k) % cols_n))

    def cr_got(k):
        src = (col + k) % cols_n
        return send(cp, cr.at[src], cr_sems.at[0, k], cr_sems.at[1, src], (row, src))

    for k in range(1, cols_n):
        cr_copy(k).start()
    tick_b(14)
    left_finish(0)
    left_finish(1)
    for k in range(1, cols_n):
        cr_got(k).wait_recv()
        cr_copy(k).wait_send()
    cr[col] = cp[...]
    cp[...] = sum(cr[c] for c in range(cols_n))

    def cf_copy(k):
        to = (row + k) % rows_n
        return send(cp.at[to], cf.at[row], cf_sems.at[0, k], cf_sems.at[1, row], (to, col))

    def cf_got(k):
        src = (row + k) % rows_n
        return send(cp.at[src], cf.at[src], cf_sems.at[0, k], cf_sems.at[1, src], (src, col))

    for k in range(1, rows_n):
        cf_copy(k).start()
    cf[row] = cp[row]
    left_finish(2)
    for k in range(1, rows_n):
        cf_got(k).wait_recv()
    cond_value = cond[...]
    gate = 1.0 / (1.0 + jnp.exp(-cond_value))
    slope = gate * (1.0 + cond_value * (1.0 - gate))
    for r in range(rows_n):
        spot = slice(r * drows, (r + 1) * drows)
        o_cond[:, spot] = cf[r] * slope[:, spot]

    for s in range(3 * depth - SLOTS, 3 * depth):
        sent(s)
    for s in range(3 * depth - 2, 3 * depth):
        for y in range(2):
            c0(s, y).wait_send()
    for g in range(3):
        left_copy(g).wait_send()
    for k in range(1, cols_n):
        u_copy(k).wait_send()
    copy_v.wait_send()
    for k in range(1, rows_n):
        cf_copy(k).wait_send()
    swap_lat.wait()
    swap_out.wait()


def backward(saved, out, lse, vec, act, ada, cond, collective_id):
    rows, cols = lax.axis_size("row"), lax.axis_size("col")
    depth = cols // 2
    tokens, width = out.shape
    heads, drows, hc6 = width // HEAD_DIM, ada.shape[0], ada.shape[1]
    hc, lanes, lrows = width // cols, 1152, drows // 2
    shape, dma, vm = jax.ShapeDtypeStruct, pltpu.SemaphoreType.DMA, pltpu.VMEM
    token = shape((tokens, width), bf16)
    outs = [token, token, shape((depth, tokens, 896), bf16), shape((drows, 576), f32), shape((drows, 576), f32),
            shape((drows, 3 * hc), f32), shape((drows, hc), f32), shape((drows, hc6), f32), shape((8, hc6), f32),
            shape((8, width), f32)]
    head = (tokens, HEAD_DIM)
    scratch = [
        vm((SLOTS, 2, drows, lanes), bf16), vm((2, 2, drows, lanes), bf16), vm((2, 2, drows, lanes), bf16),
        vm((4, 2, drows, 512), bf16), vm((4, 2, lrows, 128), bf16), vm((4, drows, 512), bf16), vm((4, lrows, 128), bf16),
        vm((2, 9, drows, 512), bf16), vm((2, 9, lrows, 128), bf16), vm((3, lrows, 128), f32), vm((3, lrows, 128), f32),
        vm((2, width, lanes), bf16), vm((2, tokens, lanes), bf16), vm((depth, tokens, lanes), bf16), vm((tokens, 896), bf16),
        vm((2, width, tokens), bf16), vm((2, tokens, width), bf16), vm((tokens, width), bf16), vm((tokens, width), f32),
        vm((tokens, width), f32), vm((tokens, 384), bf16), vm((5, 4) + head, bf16),
        vm((4,) + head, bf16), vm((4, 1, tokens), f32), vm((2, 4) + head, bf16), vm((2, 2, 4) + head, bf16), vm((3, 4) + head, f32),
        vm((16, width), f32), vm((2, tokens, 384), bf16),
        vm((cols, 8, hc6), f32), vm((cols, 8, hc6), f32), vm((cols, 8, hc6), f32), vm((cols, 8, hc6), f32), vm((rows, 8, hc6), f32),
        vm((rows, 8, drows), f32), vm((cols, rows, 8, drows), f32), vm((rows, 8, drows), f32)]
    scratch += [
        dma((2, 2)), dma((2, 2, 2)), dma((2, 4, 2, 2)), dma((2, 4, 2)), dma((2, 2, 9, depth, 2)), dma((2, 3)), dma((2,)), dma((2, 2)),
        dma((depth,)), dma((3,)), dma((5,)), dma((2, 2, 2, 4)), dma((depth,)), dma((2,)), dma((2, cols)), dma((2,)), dma((2, cols)),
        dma((2, rows)), dma((2,))]
    vmem = pl.BlockSpec(memory_space=pltpu.VMEM)
    return pl.pallas_call(
        backward_kernel,
        out_shape=outs,
        in_specs=[ANY] * 16 + [vmem] * 5,
        out_specs=[ANY] * 3 + [vmem] * 7,
        scratch_shapes=scratch,
        compiler_params=pltpu.CompilerParams(collective_id=collective_id, has_side_effects=True, vmem_limit_bytes=63 * 2**20),
        name="backward",
    )(*saved, out, lse, vec, act, ada, cond)


class Plan:
    def __init__(self, latents, condition, qkv_weight, fc1_weight):
        self.rows, self.cols = lax.axis_size("row"), lax.axis_size("col")
        self.tokens, self.width = latents.shape
        self.lats = condition.shape[0]
        self.depth_rows = qkv_weight.shape[0]
        self.head_cols = qkv_weight.shape[2]
        self.ff_cols = fc1_weight.shape[1]
        self.share = SEQ // self.tokens
        self.near = (
            self.rows == 4 and self.share == 2 and self.cols == 8 and self.lats == self.cols // 2
            and (self.depth_rows, self.head_cols, self.ff_cols) == (288, 2 * HEAD_DIM, 576) and self.width == 1152)


def fold(left):
    rows, lanes = left.shape
    return left.reshape(2, rows // 2, lanes).transpose(1, 0, 2).reshape(rows // 2, 2 * lanes)


def gather_plain(blocks):
    return [lax.all_gather(lax.all_gather(b, "row", axis=0, tiled=True), "col", axis=1, tiled=True) for b in blocks]


def scatter_plain(fulls):
    parts = [lax.psum_scatter(g, "row", scatter_dimension=0, tiled=True) for g in fulls]
    return [lax.psum_scatter(g, "col", scatter_dimension=1, tiled=True).astype(f32) for g in parts]


def attend_plain(q, k, v):
    def one(item):
        scores = nt(item[0], item[1]) * HEAD_DIM ** (-0.5)
        top = jnp.max(scores, axis=-1, keepdims=True)
        probs = jnp.exp(scores - top)
        total = jnp.sum(probs, axis=-1, keepdims=True)
        return nn((probs / total).astype(bf16), item[2]).astype(bf16), top + jnp.log(total)

    return lax.map(one, (q, k, v))


def attend_back_plain(q, k, v, lse, att_grad):
    def one(item):
        q, k, v, lse, out_grad = item
        probs = jnp.exp(nt(q, k) * HEAD_DIM ** (-0.5) - lse)
        probs_grad = nt(out_grad, v)
        inner = jnp.sum(probs * probs_grad, axis=-1, keepdims=True)
        grad = (probs * (probs_grad - inner) * HEAD_DIM ** (-0.5)).astype(bf16)
        return nn(grad, k), tn(grad, q), tn(probs.astype(bf16), out_grad)

    return lax.map(one, (q, k, v, lse, att_grad))


def gelu_and_slope(u):
    c = math.sqrt(2.0 / math.pi)
    inner = jnp.tanh(c * (u + 0.044715 * u * u * u))
    value = 0.5 * u * (1.0 + inner)
    slope = 0.5 * (1.0 + inner) + 0.5 * u * (1.0 - inner * inner) * c * (1.0 + 3 * 0.044715 * u * u)
    return value, slope


def layer_norm(values):
    mean = jnp.mean(values, axis=-1, keepdims=True)
    centred = values - mean
    inverse = lax.rsqrt(jnp.mean(centred * centred, axis=-1, keepdims=True) + norm_eps)
    return centred * inverse, inverse


def norm_back(rows_grad, normal, inverse, scale):
    normal_grad = rows_grad * (1.0 + scale)
    first = jnp.mean(normal_grad, axis=-1, keepdims=True)
    second = jnp.mean(normal_grad * normal, axis=-1, keepdims=True)
    value_grad = inverse * (normal_grad - first - normal * second)
    return value_grad, jnp.sum(rows_grad, axis=0), jnp.sum(rows_grad * normal, axis=0)


def shards_near(plan, latents, condition, ada_weight, ada_bias, qkv_weight, qv_bias, proj_weight, proj_bias,
                fc1_weight, fc1_bias, fc2_weight, fc2_bias, cotangent):
    depth, hc, fc = plan.depth_rows, plan.head_cols, plan.ff_cols
    q_main, p_main, f_main = 384, 128, 512
    qkv_flat = qkv_weight.reshape(depth, 3 * hc)
    proj_t, fc2_t = proj_weight.T, fc2_weight.T
    left_a = fold(jnp.concatenate([qkv_flat[:, q_main:], proj_t[:, p_main:]], axis=1))
    blocks = [qkv_flat[:, :q_main], proj_t[:, :p_main], left_a,
              fc1_weight[:, :f_main], fold(fc1_weight[:, f_main:]), fc2_t[:, :f_main], fold(fc2_t[:, f_main:])]
    cond = jnp.pad(condition.astype(f32), ((0, 8 - plan.lats), (0, 0)))
    ada = ada_weight.reshape(depth, 6 * hc)
    line = jnp.concatenate([fc1_bias, proj_bias, fc2_bias]).astype(f32).reshape(1, 6 * hc)
    tail = jnp.pad(qv_bias.astype(f32).reshape(1, 2 * hc), ((0, 0), (0, 4 * hc)))
    bias = jnp.concatenate([jnp.broadcast_to(ada_bias.astype(f32).reshape(1, 6 * hc), (plan.lats, 6 * hc)), line, tail,
                            jnp.zeros((8 - plan.lats - 2, 6 * hc), f32)], axis=0)
    (w, dy, x, n1, q, k, v, k2, v2, lse, att, ba, mid, n2, hid, slo, out, vec, act) = forward(
        latents, cotangent, cond, ada, bias, blocks, 0)
    output, lat_grad, _, fc2_sum, fc1_sum, qkv_sum, proj_sum, ada_sum, rows, cond_grad = backward(
        (w, dy, x, n1, q, k, v, k2, v2, att, ba, mid, n2, hid, slo), out, lse, vec, act, ada, cond, 1)
    return (
        output, lat_grad.astype(f32), cond_grad[:plan.lats], ada_sum.reshape(depth, 6, hc), rows[0].reshape(6, hc),
        qkv_sum.reshape(depth, 3, hc), rows[2, :2 * hc].reshape(2, hc), proj_sum.T, rows[1, fc:fc + hc],
        fc1_sum, rows[1, :fc], fc2_sum.T, rows[1, fc + hc:])


def shards(latents, condition, ada_weight, ada_bias, qkv_weight, qv_bias, proj_weight, proj_bias,
           fc1_weight, fc1_bias, fc2_weight, fc2_bias, cotangent):
    plan = Plan(latents, condition, qkv_weight, fc1_weight)
    if plan.near:
        return shards_near(plan, latents, condition, ada_weight, ada_bias, qkv_weight, qv_bias, proj_weight, proj_bias,
                           fc1_weight, fc1_bias, fc2_weight, fc2_bias, cotangent)
    row, col = lax.axis_index("row"), lax.axis_index("col")
    rows, cols, width, tokens = plan.rows, plan.cols, plan.width, plan.tokens
    depth, hc, fc = plan.depth_rows, plan.head_cols, plan.ff_cols
    heads = cols * hc // HEAD_DIM
    groups = rows * plan.lats

    blocks = [qkv_weight.reshape(depth, 3 * hc), proj_weight.T, fc1_weight, fc2_weight.T]
    qkv_w, proj_w, fc1_w, fc2_w = gather_plain(blocks)
    home = row * plan.lats + col // plan.share
    values, grad_out = latents.astype(f32), cotangent.astype(f32)

    cond_all = lax.all_gather(condition, "row", axis=0, tiled=True).astype(f32)
    cond_act = jax.nn.silu(cond_all).astype(bf16)
    cond_mine = lax.dynamic_slice(cond_act, (0, row * depth), (groups, depth))
    ada_flat = ada_weight.reshape(depth, 6 * hc)
    partial = lax.psum(nn(cond_mine, ada_flat), "row") + ada_bias.astype(f32).reshape(1, 6 * hc)
    small = jnp.concatenate(
        [partial.reshape(-1)] + [b.astype(f32).reshape(-1) for b in (proj_bias, fc2_bias, fc1_bias, qv_bias)])
    small = lax.all_gather(small, "col", axis=0, tiled=False)
    sizes = [groups * 6 * hc, hc, hc, fc, 2 * hc]
    mod_all, proj_b, fc2_b, fc1_b, qv_b = jnp.split(small, [sum(sizes[:i + 1]) for i in range(4)], axis=1)
    mod = lax.dynamic_index_in_dim(mod_all.reshape(cols, groups, 6, hc), home, 1, keepdims=False)
    mod = mod.transpose(1, 0, 2).reshape(6, 1, width)
    shift_one, scale_one, gate_one, shift_two, scale_two, gate_two = (mod[k] for k in range(6))
    proj_b, fc2_b, fc1_b = proj_b.reshape(width), fc2_b.reshape(width), fc1_b.reshape(-1)
    q_b, v_b = qv_b[:, :hc].reshape(heads, 1, HEAD_DIM), qv_b[:, hc:].reshape(heads, 1, HEAD_DIM)

    def to_heads(flat):
        return flat.reshape(tokens, heads, HEAD_DIM).transpose(1, 0, 2)

    def from_heads(value):
        return value.transpose(1, 0, 2).reshape(tokens, cols, hc)

    normal_one, inverse_one = layer_norm(values)
    normed_one = (normal_one * (1.0 + scale_one) + shift_one).astype(bf16)
    projected = nn(normed_one, qkv_w).reshape(tokens, cols, 3 * hc)
    query = (to_heads(projected[:, :, :hc]) + q_b).astype(bf16)
    key = to_heads(projected[:, :, hc:2 * hc]).astype(bf16)
    value = (to_heads(projected[:, :, 2 * hc:]) + v_b).astype(bf16)
    cuts = [[s * plan.share + i for i in range(plan.share)] for s in range(cols // plan.share)]
    key_all = lax.all_gather(key, "col", axis=1, tiled=True, axis_index_groups=cuts)
    value_all = lax.all_gather(value, "col", axis=1, tiled=True, axis_index_groups=cuts)
    att, lse = attend_plain(query, key_all, value_all)
    att_flat = from_heads(att).reshape(tokens, width)
    branch_a = nt(att_flat, proj_w) + proj_b
    middle = values + gate_one * branch_a

    normal_two, inverse_two = layer_norm(middle)
    normed_two = (normal_two * (1.0 + scale_two) + shift_two).astype(bf16)
    hidden, slope = gelu_and_slope(nn(normed_two, fc1_w) + fc1_b)
    hidden = hidden.astype(bf16)
    branch_m = nt(hidden, fc2_w) + fc2_b
    output = (middle + gate_two * branch_m).astype(bf16)

    gate_two_grad = jnp.sum(grad_out * branch_m, axis=0)
    m_grad = grad_out * gate_two
    fc2_bias_part = jnp.sum(m_grad, axis=0)
    m_low = m_grad.astype(bf16)
    fc2_grad = tn(m_low, hidden).astype(bf16)
    pre_grad = nn(m_low, fc2_w) * slope
    fc1_bias_part = jnp.sum(pre_grad, axis=0)
    pre_low = pre_grad.astype(bf16)
    fc1_grad = tn(normed_two, pre_low).astype(bf16)
    normed_two_grad = nt(pre_low, fc1_w)
    middle_part, shift_two_grad, scale_two_grad = norm_back(normed_two_grad, normal_two, inverse_two, scale_two)
    middle_grad = grad_out + middle_part
    gate_one_grad = jnp.sum(middle_grad * branch_a, axis=0)
    a_grad = middle_grad * gate_one
    proj_bias_part = jnp.sum(a_grad, axis=0)
    a_low = a_grad.astype(bf16)
    proj_grad = tn(a_low, att_flat).astype(bf16)
    att_grad = to_heads(nn(a_low, proj_w).astype(bf16))
    query_grad, key_grad, value_grad = attend_back_plain(query, key_all, value_all, lse, att_grad)
    key_grad, value_grad = (
        lax.psum_scatter(g.astype(bf16), "col", scatter_dimension=1, tiled=True, axis_index_groups=cuts).astype(f32)
        for g in (key_grad, value_grad))
    q_bias_part, v_bias_part = jnp.sum(query_grad, axis=1), jnp.sum(value_grad, axis=1)
    qkv_low = jnp.concatenate([from_heads(g.astype(bf16)) for g in (query_grad, key_grad, value_grad)], axis=2)
    qkv_low = qkv_low.reshape(tokens, 3 * width)
    qkv_grad = tn(normed_one, qkv_low).astype(bf16)
    normed_one_grad = nt(qkv_low, qkv_w)
    fc2_sum, fc1_sum, qkv_sum, proj_sum = scatter_plain([fc2_grad, fc1_grad, qkv_grad, proj_grad])
    input_part, shift_one_grad, scale_one_grad = norm_back(normed_one_grad, normal_one, inverse_one, scale_one)
    latents_grad = middle_grad + input_part

    mod_grad = jnp.stack(
        [shift_one_grad, scale_one_grad, gate_one_grad, shift_two_grad, scale_two_grad, gate_two_grad], axis=0)
    mod_grad = lax.all_gather(mod_grad, ("row", "col"), axis=0, tiled=False)
    mod_grad = mod_grad.reshape(groups, plan.share, 6, width).sum(axis=1)
    mod_mine = lax.dynamic_slice(mod_grad, (0, 0, col * hc), (groups, 6, hc))
    ada_bsum = jnp.sum(mod_mine, axis=0)
    mod_low = mod_mine.astype(bf16).reshape(groups, 6 * hc)
    ada_wsum = tn(cond_mine, mod_low).reshape(depth, 6, hc)
    cond_part = lax.dynamic_update_slice(jnp.zeros((groups, width), f32), nt(mod_low, ada_flat), (0, row * depth))
    parts = [cond_part, proj_bias_part, fc2_bias_part, q_bias_part, v_bias_part, fc1_bias_part]
    totals = lax.psum(jnp.concatenate([part.reshape(-1) for part in parts]), ("row", "col"))
    ends, spot = [], 0
    for part in parts:
        ends.append(totals[spot:spot + part.size])
        spot += part.size

    def mine(flat):
        size = flat.size // cols
        return lax.dynamic_slice(flat, (col * size,), (size,))

    cond_summed = lax.dynamic_slice(ends[0].reshape(groups, width), (row * plan.lats, 0), (plan.lats, width))
    silu_value, silu_pull = jax.vjp(jax.nn.silu, condition.astype(f32))
    condition_grad = silu_pull(cond_summed)[0]
    qv_bsum = jnp.stack([mine(ends[3]), mine(ends[4])], axis=0)
    return (
        output, latents_grad, condition_grad, ada_wsum, ada_bsum, qkv_sum.reshape(depth, 3, hc), qv_bsum,
        proj_sum.T, mine(ends[1]), fc1_sum, mine(ends[5]), fc2_sum.T, mine(ends[2]))


def solution(mesh):
    token, grid, turned = P(("row", "col"), None), P("row", "col"), P("col", "row")
    cube, wide, flat = P("row", None, "col"), P(None, "col"), P("col")
    return jax.shard_map(
        shards,
        mesh=mesh,
        in_specs=(token, P("row", None), cube, wide, cube, wide, turned, flat, grid, flat, turned, flat, token),
        out_specs=(token, token, P("row", None), cube, wide, cube, wide, turned, flat, grid, flat, turned, flat),
        check_vma=False,
    )
```

```python
import functools
import math
import jax
import jax.numpy as jnp
from jax import lax
from jax.experimental import pallas as pl
from jax.experimental.pallas import tpu as pltpu
from jax.sharding import PartitionSpec as P

HEAD_DIM = 72
SEQ = 1024
norm_eps = 1e-06
bf16, f32 = jnp.bfloat16, jnp.float32

MESH = pl.DeviceIdType.MESH
ANY = pl.BlockSpec(memory_space=pl.ANY)


class Place:
    def __init__(self):
        row, col = lax.axis_index("row"), lax.axis_index("col")
        self.row, self.col = row, col
        self.depth = lax.axis_size("col") // 2
        self.y, self.h = row // 2, row % 2
        self.z, self.x = col // 2, col % 2
        self.p = jnp.where(self.h == 0, self.y, self.x)
        self.q = jnp.where(self.h == 0, self.x, self.y)
        flip_x, flip_y = (row, col + 1 - 2 * self.x), (row + 2 - 4 * self.y, col)
        self.to_q = tuple(jnp.where(self.h == 0, a, b) for a, b in zip(flip_x, flip_y))
        self.to_p = tuple(jnp.where(self.h == 0, b, a) for a, b in zip(flip_x, flip_y))
        self.to_core = (row + 1 - 2 * self.h, col)

    def to_z(self, z):
        return (self.row, 2 * z + self.x)

    def diagonal(self):
        return (self.row + 1 - 2 * self.h, self.col + 1 - 2 * self.x)

    def yx(self, p, q):
        return jnp.where(self.h == 0, p, q), jnp.where(self.h == 0, q, p)

    def partners(self):
        near = [self.to_q, self.to_p, self.to_core]
        return near + [self.to_z((self.z + k) % self.depth) for k in range(1, self.depth)]


def greet(partners):
    barrier = pltpu.get_barrier_semaphore()
    for partner in partners:
        pl.semaphore_signal(barrier, inc=1, device_id=partner, device_id_type=MESH)
    pl.semaphore_wait(barrier, len(partners))


def block_at(ref, rows, lanes, r, c):
    return ref.at[pl.ds(pl.multiple_of(r * rows, 16), rows), pl.ds(pl.multiple_of(c * lanes, 128), lanes)]


class Gather:
    def __init__(self, place, ins, outs, sems):
        self.at, self.ins, self.outs = place, ins, outs
        self.local, self.zs, self.zzs, self.qs, self.ps, self.ks = sems
        self.early = place.h == 0

    @staticmethod
    def scratch(count, depth):
        dma = pltpu.SemaphoreType.DMA
        return [dma((count,)), dma((count, 2, depth)), dma((count, 2, depth)), dma((count, 2, depth)), dma((count, 2, depth, 2)),
                dma((count, 2, depth, 2))]

    def block(self, a, p, q, z):
        y, x = self.at.yx(p, q)
        rows, lanes = self.ins[a].shape
        return block_at(self.outs[a], rows, lanes, 2 * y + self.at.h, 2 * z + x)

    def zc(self, t):
        return (self.at.z + self.at.depth - t) % self.at.depth

    def copy(self, src, dst, sems, index, to):
        return pltpu.make_async_remote_copy(
            src_ref=src, dst_ref=dst, send_sem=sems.at[(index[0], 0) + index[1:]], recv_sem=sems.at[(index[0], 1) + index[1:]],
            device_id=to, device_id_type=MESH)

    def spot(self, a, t, j=0):
        p, q = self.at.p, self.at.q
        return self.block(a, p if j < 2 else 1 - p, q if j % 2 == 0 else 1 - q, self.zc(t))

    def source(self, a, t, j=0):
        return self.ins[a] if t == 0 and j == 0 else self.spot(a, t, j)

    def c_local(self, a):
        return pltpu.make_async_copy(self.ins[a], self.spot(a, 0), self.local.at[a])

    def c_z(self, a, k, j):
        place, sems = self.at, (self.zs, self.zzs)[j]
        return pltpu.make_async_remote_copy(
            src_ref=self.source(a, 0, j), dst_ref=self.spot(a, 0, j), send_sem=sems.at[a, 0, k], recv_sem=sems.at[a, 1, place.z],
            device_id=place.to_z((place.z + k) % place.depth), device_id_type=MESH)

    def r_z(self, a, t, j):
        place, sems = self.at, (self.zs, self.zzs)[j]
        return pltpu.make_async_remote_copy(
            src_ref=self.source(a, 0, j), dst_ref=self.spot(a, t, j), send_sem=sems.at[a, 0, 0], recv_sem=sems.at[a, 1, self.zc(t)],
            device_id=place.to_q, device_id_type=MESH)

    def c_q(self, a, t):
        return self.copy(self.source(a, t), self.spot(a, t), self.qs, (a, self.zc(t)), self.at.to_q)

    def c_p(self, a, t, j):
        return self.copy(self.source(a, t, j), self.spot(a, t, j), self.ps, (a, self.zc(t), j), self.at.to_p)

    def c_k(self, a, t, j):
        rows, lanes = self.ins[a].shape
        r = 2 * j + self.at.h
        spot = block_at(self.outs[a], rows, 2 * lanes, r, self.zc(t))
        return self.copy(spot, spot, self.ks, (a, self.zc(t), j), self.at.to_core)

    def start(self, a):
        self.c_q(a, 0).start()
        for k in range(1, self.at.depth):
            self.c_z(a, k, 0).start()
        self.c_local(a).start()

    def forward(self, a):
        @pl.when(self.early)
        def _():
            self.c_q(a, 0).wait_recv()
            for k in range(1, self.at.depth):
                self.c_z(a, k, 1).start()

    def stage(self, a, t, n):
        late = jnp.logical_not(self.early)
        if n == 0:
            if t > 0:
                self.r_z(a, t, 0).wait_recv()
                pl.when(late)(self.c_q(a, t).start)
            self.c_p(a, t, 0).start()
        elif n == 1:
            pl.when(late)(self.c_q(a, t).wait_recv)
            if t > 0:
                pl.when(self.early)(self.r_z(a, t, 1).wait_recv)
            self.c_p(a, t, 1).start()
        elif n == 2:
            self.c_p(a, t, 0).wait_recv()
            if t == 0:
                self.c_local(a).wait()
        elif n == 3:
            self.c_p(a, t, 1).wait_recv()
            for j in range(2):
                self.c_k(a, t, j).start()
        else:
            for j in range(2):
                self.c_k(a, t, j).wait_recv()

    def finish(self, a):
        self.c_q(a, 0).wait_send()
        for k in range(1, self.at.depth):
            self.c_z(a, k, 0).wait_send()

        @pl.when(self.early)
        def _():
            for k in range(1, self.at.depth):
                self.c_z(a, k, 1).wait_send()

        @pl.when(jnp.logical_not(self.early))
        def _():
            for t in range(1, self.at.depth):
                self.c_q(a, t).wait_send()

        for t in range(self.at.depth):
            for j in range(2):
                self.c_p(a, t, j).wait_send()
            for j in range(2):
                self.c_k(a, t, j).wait_send()


class LineGather(Gather):
    def __init__(self, place, ins, outs, sems, mid=()):
        super().__init__(place, ins, outs, sems)
        z = place.z
        self.core0, self.mid = place.h == 0, mid
        self.middle = jnp.logical_and(z > 0, z < place.depth - 1)
        low = z < 2
        self.inner = place.to_z(jnp.where(low, z + 1, z - 1))
        self.outer = place.to_z(jnp.where(low, jnp.maximum(z - 1, 0), jnp.minimum(z + 1, place.depth - 1)))
        self.order = [z, z + 1 - 2 * (z % 2), jnp.where(low, 2, 1), jnp.where(low, 3, 0)]

    @staticmethod
    def scratch(count, depth):
        dma = pltpu.SemaphoreType.DMA
        return [dma((count,)), dma((count, 2, 5)), dma((count, 2, 5)), dma((count, 2, depth)), dma((count, 2, depth, 2)),
                dma((count, 2, depth, 2))]

    def early(self, a):
        return self.core0 if a in self.mid else jnp.logical_and(self.core0, False)

    def zc(self, t):
        return self.order[t]

    def c_z(self, a, t, j, n):
        sems = (self.zs, self.zzs)[j]
        return pltpu.make_async_remote_copy(
            src_ref=self.source(a, t, j), dst_ref=self.spot(a, t, j), send_sem=sems.at[a, 0, n], recv_sem=sems.at[a, 1, self.zc(t)],
            device_id=self.inner if n in (0, 2) else self.outer, device_id_type=MESH)

    def z_start(self, a, j):
        self.c_z(a, 0, j, 0).start()
        pl.when(self.middle)(self.c_z(a, 0, j, 1).start)

    def z_got(self, a, t, j):
        self.c_z(a, t, j, 0).wait_recv()
        pl.when(self.middle)(self.c_z(a, t, j, 1 + t).start)

    def z_sent(self, a, j):
        self.c_z(a, 0, j, 0).wait_send()

        @pl.when(self.middle)
        def _():
            self.c_z(a, 0, j, 1).wait_send()
            for t in range(1, self.at.depth):
                self.c_z(a, t, j, 1 + t).wait_send()

    def start(self, a):
        self.c_q(a, 0).start()
        self.z_start(a, 0)
        self.c_local(a).start()

    def forward(self, a):
        if a in self.mid:
            @pl.when(self.core0)
            def _():
                self.c_q(a, 0).wait_recv()
                self.z_start(a, 1)

    def stage(self, a, t, n):
        mid, early = a in self.mid, self.core0
        late = jnp.logical_not(early)
        if n == 0:
            if t > 0:
                self.z_got(a, t, 0)
                if mid:
                    pl.when(late)(self.c_q(a, t).start)
                else:
                    self.c_q(a, t).start()
            self.c_p(a, t, 0).start()
        elif n == 1:
            if not mid:
                self.c_q(a, t).wait_recv()
            else:
                pl.when(late)(self.c_q(a, t).wait_recv)
                if t > 0:
                    pl.when(early)(lambda: self.z_got(a, t, 1))
            self.c_p(a, t, 1).start()
        elif n == 2:
            self.c_p(a, t, 0).wait_recv()
            if t == 0:
                self.c_local(a).wait()
        elif n == 3:
            self.c_p(a, t, 1).wait_recv()
            for j in range(2):
                self.c_k(a, t, j).start()
        else:
            for j in range(2):
                self.c_k(a, t, j).wait_recv()

    def finish(self, a):
        self.c_q(a, 0).wait_send()
        self.z_sent(a, 0)

        def rest():
            for t in range(1, self.at.depth):
                self.c_q(a, t).wait_send()

        if a in self.mid:
            pl.when(self.core0)(lambda: self.z_sent(a, 1))
            pl.when(jnp.logical_not(self.core0))(rest)
        else:
            rest()
        for t in range(self.at.depth):
            for j in range(2):
                self.c_p(a, t, j).wait_send()
            for j in range(2):
                self.c_k(a, t, j).wait_send()


def nt(a, b):
    return lax.dot_general(a, b, (((1,), (1,)), ((), ())), preferred_element_type=f32)


def nn(a, b):
    return lax.dot_general(a, b, (((1,), (0,)), ((), ())), preferred_element_type=f32)


def tn(a, b):
    return lax.dot_general(a, b, (((0,), (0,)), ((), ())), preferred_element_type=f32)


SOFT = HEAD_DIM ** (-0.5) * math.log2(math.e)


VECS = 24


def softmax_head(q, k, k2):
    one, two = nt(k, q), nt(k2, q)
    top = jnp.maximum(jnp.max(one, axis=0, keepdims=True), jnp.max(two, axis=0, keepdims=True)) * SOFT
    one, two = jnp.exp2(one * SOFT - top), jnp.exp2(two * SOFT - top)
    total = jnp.sum(one, axis=0, keepdims=True) + jnp.sum(two, axis=0, keepdims=True)
    return one.astype(bf16), two.astype(bf16), total, top + jnp.log2(total)


def norm_rows(values):
    mean = jnp.mean(values, axis=-1, keepdims=True)
    centred = values - mean
    inverse = lax.rsqrt(jnp.mean(centred * centred, axis=-1, keepdims=True) + norm_eps)
    return centred * inverse, inverse


def gelu_both(u):
    c = math.sqrt(2.0 / math.pi)
    square = u * u
    inner = jnp.tanh(u * (c + (c * 0.044715) * square))
    half = 0.5 * (1.0 + inner)
    slope = half + (0.5 * u) * (1.0 - inner * inner) * (c + (3 * c * 0.044715) * square)
    return u * half, slope


class Swap:
    def __init__(self, place, src, dst, sems, i):
        self.stay = place.h == place.x
        self.local = pltpu.make_async_copy(src, dst, sems.at[i, 0])
        self.remote = pltpu.make_async_remote_copy(
            src_ref=src, dst_ref=dst, send_sem=sems.at[i, 0], recv_sem=sems.at[i, 1],
            device_id=place.diagonal(), device_id_type=MESH)

    def start(self):
        pl.when(self.stay)(self.local.start)
        pl.when(jnp.logical_not(self.stay))(self.remote.start)

    def wait(self):
        pl.when(self.stay)(self.local.wait)
        pl.when(jnp.logical_not(self.stay))(self.remote.wait)


def unfold_into(left, target):
    rows = target.shape[0] // 4
    half = rows // 2
    for r in range(4):
        tile = left[r * half:(r + 1) * half, :].astype(f32)
        target[r * rows:r * rows + half, :] = jnp.concatenate([tile[:, :64], tile[:, 128:192]], axis=1).astype(bf16)
        target[r * rows + half:(r + 1) * rows, :] = jnp.concatenate([tile[:, 64:128], tile[:, 192:]], axis=1).astype(bf16)


GROUPS = (2, 1, 1)


def forward_kernel(*refs):
    lat, cot, cond, ada, bias = refs[:5]
    blocks, refs = refs[5:9], refs[9:]
    fulls, refs = refs[:4], refs[4:]
    (o_w, o_cot, o_x, o_n1, o_q, o_k, o_v, o_k2, o_v2, o_lse, o_att, o_ba, o_mid, o_n2, o_hid, o_slo, o_out, o_vec, o_act), refs = refs[:19], refs[19:]
    (x_v, n1, q_v, k_v, v_v, k2_v, v2_v, lse_v, ot, att, ba, mid, n2, hid, slo, acc, wbuf, lbuf, out_v, cot_v, vec,
     c_send, c_recv, s_send, s_recv, m_own, m_oth), refs = refs[:27], refs[27:]
    ag_sems, (swap_sems, c_sems, s_sems, m_sems, o_sems, kv_sems, w_sems, save_sems, wsave_sems) = refs[:6], refs[6:]

    place = Place()
    depth, rows_n = place.depth, 4
    row, col = place.row, place.col
    cols_n = 2 * depth
    tokens, width = x_v.shape
    hc = width // cols_n
    drows = ada.shape[0]
    q_main, p_main = 384, 128
    half = tokens // 2

    row_peers = [((row + k) % rows_n, col) for k in range(1, rows_n)]
    col_peers = [(row, (col + k) % cols_n) for k in range(1, cols_n)]
    greet(place.partners() + row_peers + col_peers + [place.diagonal()])

    def send(src, dst, s_sem, r_sem, to):
        return pltpu.make_async_remote_copy(
            src_ref=src, dst_ref=dst, send_sem=s_sem, recv_sem=r_sem, device_id=to, device_id_type=MESH)

    cond_value = cond[...]
    act = (cond_value / (1.0 + jnp.exp(-cond_value))).astype(bf16).astype(f32)
    for r in range(rows_n):
        c_send[r] = act[:, r * drows:(r + 1) * drows]

    def cond_copy(k):
        to = (row + k) % rows_n
        return send(c_send.at[to], c_recv.at[row], c_sems.at[0, k], c_sems.at[1, row], (to, col))

    def cond_got(k):
        src = (row + k) % rows_n
        return send(c_send.at[src], c_recv.at[src], c_sems.at[0, k], c_sems.at[1, src], (src, col))

    for k in range(1, rows_n):
        cond_copy(k).start()
    swap_x = Swap(place, lat, x_v, swap_sems, 0)
    swap_x.start()

    work = LineGather(place, blocks, fulls, ag_sems, range(4))
    for a in range(2):
        work.start(a)

    members, first = [], 0
    for size in GROUPS:
        members.append(list(range(first, first + size)))
        first += size
    chunks = [(g, t) for g in range(len(GROUPS)) for t in range(depth)]
    events = []
    for s in range(len(chunks) + 4):
        if s % depth == 2 and s < 2 * depth:
            events.append((s // depth + 1, "start"))
        if s in (1, 3, depth + 3):
            events.append(((s + 1) // depth, "forward"))
        events += [(s - n, n) for n in range(5) if 0 <= s - n < len(chunks)]
    at = [0]

    def pump(count):
        for s, n in events[at[0]:at[0] + count]:
            if n in ("start", "forward"):
                for a in members[s]:
                    (work.start if n == "start" else work.forward)(a)
                continue
            g, t = chunks[s]
            for a in members[g]:
                work.stage(a, t, n)
        at[0] += count

    def pump_to(s, n):
        pump(max(0, events.index((s, n)) + 1 - at[0]))

    pump_to(0, 0)
    c_recv[row] = c_send[row]
    for k in range(1, rows_n):
        cond_got(k).wait_recv()
    act_all = c_recv[...].reshape(rows_n * 8, drows).astype(bf16)
    s_send[...] = nn(act_all, ada[...]).reshape(rows_n, 8, 6 * hc)

    def sum_copy(k):
        to = (row + k) % rows_n
        return send(s_send.at[to], s_recv.at[row], s_sems.at[0, k], s_sems.at[1, row], (to, col))

    def sum_got(k):
        src = (row + k) % rows_n
        return send(s_send.at[src], s_recv.at[src], s_sems.at[0, k], s_sems.at[1, src], (src, col))

    for k in range(1, rows_n):
        sum_copy(k).start()
    pump_to(0, 1)
    s_recv[row] = s_send[row]
    for k in range(1, rows_n):
        sum_got(k).wait_recv()
    m_own[col] = s_recv[0] + s_recv[1] + s_recv[2] + s_recv[3] + bias[...]

    def mod_copy(k):
        return send(m_own.at[col], m_own.at[col], m_sems.at[0, k], m_sems.at[1, col], (row, (col + k) % cols_n))

    def mod_got(k):
        src = (col + k) % cols_n
        return send(m_own.at[src], m_own.at[src], m_sems.at[0, k], m_sems.at[1, src], (row, src))

    for k in range(1, cols_n):
        mod_copy(k).start()
    pump_to(0, 2)
    for k in range(1, cols_n):
        mod_got(k).wait_recv()
    other = send(m_own, m_oth, o_sems.at[0], o_sems.at[1], place.to_core)
    other.start()
    pump_to(0, 3)
    other.wait_recv()
    stay = place.h == place.x
    for c in range(cols_n):
        line = jnp.where(stay, m_own[c, pl.ds(place.z, 1), :], m_oth[c, pl.ds(place.z, 1), :])
        for k in range(6):
            vec[k:k + 1, c * hc:(c + 1) * hc] = line[:, k * hc:(k + 1) * hc]
        line = m_own[c, 4:5, :]
        vec[6:7, c * hc:(c + 1) * hc] = line[:, 576:576 + hc]
        vec[7:8, c * hc:(c + 1) * hc] = line[:, 576 + hc:]
        z, i = c // 2, c % 2
        vec[16 + z:17 + z, i * 512:(i + 1) * 512] = line[:, :512]
        vec[16 + z:17 + z, 1024 + i * 64:1024 + (i + 1) * 64] = line[:, 512:576]

    swap_x.wait()
    swap_dy = Swap(place, cot, o_cot, swap_sems, 1)
    swap_dy.start()
    part = 128

    def row_parts(body):
        @pl.loop(0, tokens // part)
        def _(i):
            body(pl.ds(pl.multiple_of(i * part, part), part))

    def first_norm(at_rows):
        normal, _ = norm_rows(x_v[at_rows, :].astype(f32))
        n1[at_rows, :] = (normal * (1.0 + vec[1:2, :]) + vec[0:1, :]).astype(bf16)

    row_parts(first_norm)

    saves = []

    def save(src, dst):
        copy = pltpu.make_async_copy(src, dst, save_sems.at[len(saves)])
        copy.start()
        saves.append(copy)

    save(x_v, o_x)
    save(n1, o_n1)
    save(c_recv, o_act)

    def fetch(s):
        g, t = chunks[s]
        zc, slot = work.zc(t), s % depth
        main = fulls[members[g][0]]
        if g == 0:
            cuts = [(512 * i, q_main, q_main * i) for i in range(2)] + [(512 * i + q_main, p_main, 2 * q_main + p_main * i) for i in range(2)]
        else:
            cuts = [(256 * i, 256, 256 * i) for i in range(4)]
        copies = []
        for n, (spot, size, to) in enumerate(cuts):
            src = main.at[:, pl.ds(pl.multiple_of(zc * 1024 + spot, 128), size)]
            copies.append(pltpu.make_async_copy(src, wbuf.at[slot, :, to:to + size], w_sems.at[s % 2, n]))
        for i in range(2):
            src = fulls[1].at[:, pl.ds(pl.multiple_of(zc * 768 + 384 * i + 128 * g, 128), 128)]
            copies.append(pltpu.make_async_copy(src, lbuf.at[s % 2, :, 128 * i:128 * (i + 1)], w_sems.at[s % 2, 4 + i]))
        return copies

    def fetch_start(s):
        pump_to(s, 4)
        if s >= depth:
            weight_save(s - depth).wait()
        for copy in fetch(s):
            copy.start()

    def fetch_wait(s):
        for copy in fetch(s):
            copy.wait()
        unfold_into(lbuf.at[s % 2], wbuf.at[s % depth, :, 1024:1152])
        weight_save(s).start()

    def weight_save(s):
        g, t = chunks[s]
        return pltpu.make_async_copy(wbuf.at[s % depth], o_w.at[g, work.zc(t)], wsave_sems.at[s])

    def swap_kv(i, h):
        src, dst = ((k_v, k2_v), (v_v, v2_v))[i]
        return send(src.at[h], dst.at[h], kv_sems.at[0, i, h], kv_sems.at[1, i, h], place.to_core)

    def project(s):
        t, slot = chunks[s][1], s % depth
        zc = work.zc(t)

        @pl.loop(0, 2)
        def _(i):
            at_rows = pl.ds(pl.multiple_of(i * half, half), half)
            main = nn(n1[at_rows, :], wbuf[slot, :, :2 * q_main])
            left = nn(n1[at_rows, :], wbuf[slot, :, 1024:1152])
            for j in range(2):
                biases = m_own[2 * zc + j]
                own = main[:, j * q_main:(j + 1) * q_main]
                tail = left[:, j * 64:j * 64 + 3 * hc - q_main]
                for e in range(2):
                    h = 4 * zc + 2 * j + e
                    a = e * HEAD_DIM
                    q_v[h, at_rows, :] = (own[:, a:a + HEAD_DIM] + biases[5:6, a:a + HEAD_DIM]).astype(bf16)
                    k_v[h, at_rows, :] = own[:, hc + a:hc + a + HEAD_DIM].astype(bf16)
                    if e == 0:
                        value = own[:, 2 * hc:2 * hc + HEAD_DIM]
                    else:
                        value = jnp.concatenate([own[:, 2 * hc + HEAD_DIM:], tail], axis=1)
                    v_v[h, at_rows, :] = (value + biases[5:6, hc + a:hc + a + HEAD_DIM]).astype(bf16)

        for i in range(4):
            swap_kv(0, 4 * zc + i).start()
            swap_kv(1, 4 * zc + i).start()

    def attention(s):
        zc = work.zc(chunks[s][1])
        start = at[0]

        @pl.loop(0, 4)
        def _(i):
            h = 4 * zc + i
            swap_kv(0, h).wait_recv()
            swap_kv(1, h).wait_recv()
            one, two, total, lse = softmax_head(q_v[h], k_v[h], k2_v[h])
            ot[i] = (tn(v_v[h], one) + tn(v2_v[h], two)) / total
            lse_v[h] = lse
            for k in range(4):
                at[0] = start + k

                @pl.when(i == k)
                def _():
                    pump(1)

        at[0] = start + 4
        att[zc, :, 2 * p_main:] = jnp.zeros((tokens, 128), bf16)
        for j in range(2):
            pair = jnp.concatenate([ot[2 * j], ot[2 * j + 1]], axis=0).T.astype(bf16)
            att[zc, :, j * p_main:(j + 1) * p_main] = pair[:, :p_main]
            att[zc, :, 2 * p_main + 64 * j + 48:2 * p_main + 64 * j + 64] = pair[:, p_main:]

        @pl.loop(0, 2)
        def _(i):
            at_rows = pl.ds(pl.multiple_of(i * half, half), half)
            term = nt(att[zc, at_rows, :], wbuf[s % depth, :, 2 * q_main:])
            if s == 0:
                acc[at_rows, :] = term
            else:
                acc[at_rows, :] += term

    fetch_start(0)
    for s in range(depth):
        fetch_wait(s)
        project(s)
        fetch_start(s + 1)
        if s > 0:
            attention(s - 1)
    attention(depth - 1)
    for src, dst in ((q_v, o_q), (k_v, o_k), (v_v, o_v), (k2_v, o_k2), (v2_v, o_v2), (lse_v, o_lse), (att, o_att)):
        save(src, dst)

    def second_norm(at_rows):
        branch = acc[at_rows, :] + vec[6:7, :]
        ba[at_rows, :] = branch.astype(bf16)
        middle = x_v[at_rows, :].astype(f32) + vec[2:3, :] * branch
        mid[at_rows, :] = middle
        normal, _ = norm_rows(middle)
        n2[at_rows, :] = (normal * (1.0 + vec[4:5, :]) + vec[3:4, :]).astype(bf16)

    row_parts(second_norm)
    for src, dst in ((ba, o_ba), (mid, o_mid), (n2, o_n2)):
        save(src, dst)

    for s in range(depth, 2 * depth):
        fetch_wait(s)
        fetch_start(s + 1)
        zc = work.zc(chunks[s][1])

        def up(at_rows):
            u = nn(n2[at_rows, :], wbuf[s % depth]) + vec[pl.ds(16 + zc, 1), :]
            value, slope = gelu_both(u)
            hid[zc, at_rows, :] = value.astype(bf16)
            slo[zc, at_rows, :] = slope.astype(bf16)

        row_parts(up)
    save(hid, o_hid)
    save(slo, o_slo)
    for s in range(2 * depth, 3 * depth):
        fetch_wait(s)
        if s + 1 < 3 * depth:
            fetch_start(s + 1)
        zc = work.zc(chunks[s][1])

        def down(at_rows):
            term = nt(hid[zc, at_rows, :], wbuf[s % depth])
            if s == 2 * depth:
                acc[at_rows, :] = term
            else:
                acc[at_rows, :] += term

        row_parts(down)

    swap_dy.wait()
    load_dy = pltpu.make_async_copy(o_cot, cot_v, w_sems.at[0, 0])
    load_dy.start()
    load_dy.wait()
    vec[8:9, :] = jnp.zeros((1, width), f32)

    def finish(at_rows):
        branch = acc[at_rows, :] + vec[7:8, :]
        out_v[at_rows, :] = (mid[at_rows, :] + vec[5:6, :] * branch).astype(bf16)
        vec[8:9, :] += jnp.sum(cot_v[at_rows, :].astype(f32) * branch, axis=0, keepdims=True)

    row_parts(finish)
    save(out_v, o_out)
    save(vec, o_vec)

    for a in range(4):
        work.finish(a)
    for k in range(1, rows_n):
        cond_copy(k).wait_send()
        sum_copy(k).wait_send()
    for k in range(1, cols_n):
        mod_copy(k).wait_send()
    other.wait_send()

    @pl.loop(0, 4 * depth)
    def _(h):
        swap_kv(0, h).wait_send()
        swap_kv(1, h).wait_send()

    for s in range(2 * depth, 3 * depth):
        weight_save(s).wait()
    for copy in saves:
        copy.wait()


def forward(lat, cot, cond, ada, bias, blocks, collective_id):
    rows, cols = lax.axis_size("row"), lax.axis_size("col")
    depth = cols // 2
    tokens, width = lat.shape
    heads = width // HEAD_DIM
    lanes = 1152
    hc6 = ada.shape[1]
    shape = jax.ShapeDtypeStruct
    head = shape((heads, tokens, HEAD_DIM), bf16)
    token = shape((tokens, width), bf16)
    outs = [shape((rows * b.shape[0], cols * b.shape[1]), bf16) for b in blocks] + [
        shape((3, depth, width, lanes), bf16), token, token, token, head, head, head, head, head,
        shape((heads, 1, tokens), f32), shape((depth, tokens, 384), bf16), token, shape((tokens, width), f32), token,
        shape((depth, tokens, lanes), bf16), shape((depth, tokens, lanes), bf16), token, shape((VECS, width), f32), shape((rows, 8, ada.shape[0]), f32)]
    dma, vm = pltpu.SemaphoreType.DMA, pltpu.VMEM
    t16, h16 = vm((tokens, width), bf16), vm((heads, tokens, HEAD_DIM), bf16)
    drows = ada.shape[0]
    scratch = [
        t16, t16, h16, h16, h16, h16, h16, vm((heads, 1, tokens), f32), vm((4, HEAD_DIM, tokens), f32),
        vm((depth, tokens, 384), bf16), t16, vm((tokens, width), f32), t16, vm((depth, tokens, lanes), bf16),
        vm((depth, tokens, lanes), bf16), vm((tokens, width), f32), vm((depth, width, lanes), bf16), vm((2, width // 2, 256), bf16),
        t16, t16, vm((VECS, width), f32), vm((rows, 8, drows), f32), vm((rows, 8, drows), f32), vm((rows, 8, hc6), f32),
        vm((rows, 8, hc6), f32), vm((cols, 8, hc6), f32), vm((cols, 8, hc6), f32)]
    scratch += LineGather.scratch(len(blocks), depth)
    scratch += [dma((2, 2)), dma((2, rows)), dma((2, rows)), dma((2, cols)), dma((2,)), dma((2, 2, heads)), dma((2, 6)), dma((32,)),
                dma((3 * depth,))]
    vmem = pl.BlockSpec(memory_space=pltpu.VMEM)
    got = pl.pallas_call(
        forward_kernel,
        out_shape=outs,
        in_specs=[ANY, ANY, vmem, vmem, vmem] + [ANY] * len(blocks),
        out_specs=[ANY] * len(outs),
        scratch_shapes=scratch,
        compiler_params=pltpu.CompilerParams(collective_id=collective_id, has_side_effects=True, vmem_limit_bytes=62 * 2**20),
        name="forward",
    )(lat, cot, cond, ada, bias, *blocks)
    return got[len(blocks):]


SLOTS = 4


def backward_kernel(*refs):
    (w, dy_h, x_h, n1_h, q_h, k_h, v_h, k2_h, v2_h, att_h, ba_h, mid_h, n2_h, hid_h, slo_h, out_h), refs = refs[:16], refs[16:]
    (lse, vec, act, ada, cond), refs = refs[:5], refs[5:]
    (o_out, o_lat, o_pq, o_fc2, o_fc1, o_qkv, o_proj, o_ada, o_rows, o_cond), refs = refs[:10], refs[10:]
    (acc, give, r0, r1, r1l, r2, r2l, r3, r3l, lf, lx), refs = refs[:11], refs[11:]
    (wbuf, hs, pre, pq, turn, tmp, ml, gm, gx, att, heads, grad_o, delta, kv_give, kv_got, own, gv, att_w), refs = refs[:18], refs[18:]
    (tt, tc, um, vm_, modl, cp, cr, cf), refs = refs[:8], refs[8:]
    (swap_sems, s0, s1, s2, s3, lx_sems, w_sems, hs_sems, slo_sems, tmp_sems, head_sems, kv_sems, pq_sems, t_sems, u_sems, v_sems, cr_sems, cf_sems, att_sems) = refs

    place = Place()
    depth, rows_n = place.depth, 4
    row, col, h = place.row, place.col, place.h
    cols_n = 2 * depth
    tokens, width = ml.shape
    hc = width // cols_n
    drows = ada.shape[0]
    lrows = drows // 2
    half, part = tokens // 2, 128
    q_main, p_main = 384, 128
    scale = HEAD_DIM ** (-0.5)
    row_peers = [((row + k) % rows_n, col) for k in range(1, rows_n)]
    col_peers = [(row, (col + k) % cols_n) for k in range(1, cols_n)]
    flip_x, flip_y = (row, col + 1 - 2 * place.x), (row + 2 - 4 * place.y, col)
    greet(place.partners() + row_peers + col_peers + [place.diagonal()])

    def send(src, dst, s_sem, r_sem, to):
        return pltpu.make_async_remote_copy(
            src_ref=src, dst_ref=dst, send_sem=s_sem, recv_sem=r_sem, device_id=to, device_id_type=MESH)

    def row_parts(body):
        @pl.loop(0, tokens // part)
        def _(i):
            body(pl.ds(pl.multiple_of(i * part, part), part))

    def row_halves(body):
        @pl.loop(0, 2)
        def _(i):
            body(pl.ds(pl.multiple_of(i * half, half), half))

    low = place.z < 2
    middle = jnp.logical_and(place.z > 0, place.z < depth - 1)
    inner = place.to_z(jnp.where(low, place.z + 1, place.z - 1))
    outer = place.to_z(jnp.where(low, jnp.maximum(place.z - 1, 0), jnp.minimum(place.z + 1, depth - 1)))
    far = [jnp.where(low, 3, 0), jnp.where(low, 2, 1), place.z + 1 - 2 * (place.z % 2), place.z]

    def zc(t):
        return far[t]

    def load(src, i):
        copy = pltpu.make_async_copy(src, tmp.at[i], tmp_sems.at[i])
        copy.start()
        return copy

    def weight_load(u):
        return pltpu.make_async_copy(w.at[2 - u // depth, zc(u % depth)], wbuf.at[u % 2], w_sems.at[u % 2])

    def slope_load(u):
        return pltpu.make_async_copy(slo_h.at[zc(u)], pre.at[zc(u)], slo_sems.at[u])

    def weight_use(u):
        weight_load(u).wait()
        if u + 1 < 3 * depth:
            weight_load(u + 1).start()


    def tick_loads(s):
        g, t = s // depth, s % depth
        if g == 0:
            return [pltpu.make_async_copy(hid_h.at[zc(t)], hs.at[s % 2], hs_sems.at[s % 2, 0])]
        if g == 1:
            return []
        return [pltpu.make_async_copy(o_pq.at[zc(t)], hs.at[s % 2, :, :896], hs_sems.at[s % 2, 0]),
                pltpu.make_async_copy(att_h.at[zc(t)], att_w.at[s % 2], hs_sems.at[s % 2, 1])]

    def tick_prefetch(s):
        if s < 3 * depth:
            if s // depth == 2:
                pq_wait(s % depth)
            for copy in tick_loads(s):
                copy.start()

    saved = set()

    def pq_wait(t):
        if t not in saved:
            saved.add(t)
            pq_save(t).wait()

    def pq_save(t):
        return pltpu.make_async_copy(pq, o_pq.at[zc(t)], pq_sems.at[t])

    def c0(s, y):
        return send(give.at[s % 2, y], r0.at[s % 2, y], s0.at[0, s % 2, y], s0.at[1, s % 2, y], place.to_core)

    def spots(s, y, x):
        return (acc.at[s % SLOTS, y, :, pl.ds(pl.multiple_of(x * 512, 512), 512)],
                acc.at[s % SLOTS, y, pl.ds(pl.multiple_of(x * lrows, 16), lrows), 1024:1152])

    def c1(s, j):
        main, left = spots(s, *place.yx(1 - place.p, j))
        k = s % 4
        return [send(main, r1.at[k, j], s1.at[0, k, j, 0], s1.at[1, k, j, 0], place.to_p),
                send(left, r1l.at[k, j], s1.at[0, k, j, 1], s1.at[1, k, j, 1], place.to_p)]

    zq = h == 0
    qz = jnp.logical_not(zq)

    def c2(s):
        main, left = spots(s, *place.yx(place.p, 1 - place.q))
        k = jnp.where(zq, s // depth, s % 4) if s % depth == depth - 1 else s % 4
        return [send(main, r2.at[k], s2.at[0, k, 0], s2.at[1, k, 0], place.to_q),
                send(left, r2l.at[k], s2.at[0, k, 1], s2.at[1, k, 1], place.to_q)]

    def z_copy(s, j, inward, slot):
        g, t = s // depth, s % depth
        main, left = spots(s, *place.yx(place.p, place.q if j == 0 else 1 - place.q))
        to = inner if inward else outer
        return [send(main, r3.at[j, slot], s3.at[0, j, g, t, 0], s3.at[1, j, slot, 0, 0], to),
                send(left, r3l.at[j, slot], s3.at[0, j, g, t, 1], s3.at[1, j, slot, 0, 1], to)]

    def z_stage(s, j, inside):
        g, t = s // depth, s % depth
        par = g % 2
        if t == depth - 1:
            return
        if inside:
            slot = (par, 2, 3 + par)[t]
            for copy in z_copy(s, j, True, slot):
                copy.wait_recv()
            for into, other in zip(spots(s, *place.yx(place.p, place.q if j == 0 else 1 - place.q)), (r3.at[j, slot], r3l.at[j, slot])):
                add_into(into, other)
            copies = z_copy(s, j, t < 2, (3 + par, 5 + par, 5 + par)[t])
        else:
            copies = z_copy(s, j, True, (par, 2, 7 + par)[t])
        for copy in copies:
            copy.start()

    def z_stages(s, twice, inside):
        where = jnp.logical_and(zq if twice else qz, middle if inside else jnp.logical_not(middle))

        @pl.when(where)
        def _():
            z_stage(s, 0, inside)
            if twice:
                z_stage(s, 1, inside)

    def z_got(g, j):
        par = g % 2
        last = (g + 1) * depth - 1
        for copy in z_copy(last, j, True, 5 + par):
            copy.wait_recv()

        @pl.when(middle)
        def _():
            for copy in z_copy(last, j, True, 7 + par):
                copy.wait_recv()

    def z_sum(g, j, value, refs, index):
        par = g % 2
        value = value + refs[(j, 5 + par) + index].astype(f32)
        return jnp.where(middle, value + refs[(j, 7 + par) + index].astype(f32), value)

    def sent(s):
        for j in range(2):
            for copy in c1(s, j):
                copy.wait_send()
        if s % depth < depth - 1:
            for copy in z_copy(s, 0, True, 0):
                copy.wait_send()

            @pl.when(zq)
            def _():
                for copy in z_copy(s, 1, True, 0):
                    copy.wait_send()

            @pl.when(qz)
            def _():
                for copy in c2(s):
                    copy.wait_send()
        else:
            for copy in c2(s):
                copy.wait_send()

    def add_into(into, other):
        n = into.shape[0]

        @pl.loop(0, n // 48)
        def _(i):
            at_rows = pl.ds(pl.multiple_of(i * 48, 16), 48)
            into[at_rows, :] = into[at_rows, :] + other[at_rows, :]

    def tick_a(s):
        g, t = s // depth, s % depth
        k = s % SLOTS
        if s >= SLOTS:
            sent(s - SLOTS)
        if s >= 2:
            for y in range(2):
                c0(s - 2, y).wait_send()
        for copy in tick_loads(s):
            copy.wait()

        def rows_of(r):
            at_rows = pl.ds(pl.multiple_of(r * drows, 16), drows)
            if g == 0:
                return nn(turn[0, at_rows, :], hs[s % 2]).astype(bf16)
            if g == 1:
                return nn(turn[0, at_rows, :], pre[zc(t)]).astype(bf16)
            one = nn(turn[1, at_rows, :], hs[s % 2, :, :896])
            two = nn(turn[0, at_rows, :], att_w[s % 2])
            return jnp.concatenate(
                [one[:, :q_main], two[:, :p_main], one[:, q_main:2 * q_main], two[:, p_main:2 * p_main],
                 one[:, 2 * q_main:] + two[:, 2 * p_main:]], axis=1).astype(bf16)

        @pl.loop(0, 2)
        def _(y):
            give[s % 2, y] = rows_of(2 * y + 1 - h)
            acc[k, y] = rows_of(2 * y + h)

        for y in range(2):
            c0(s, y).start()
        if s + 1 < 3 * depth - 1:
            tick_prefetch(s + 1)

    def tick_b(s):
        if s < 3 * depth:
            for y in range(2):
                c0(s, y).wait_recv()
            for y in range(2):
                add_into(acc.at[s % SLOTS, y], r0.at[s % 2, y])
            for j in range(2):
                for copy in c1(s, j):
                    copy.start()
        if 0 <= s - 1 < 3 * depth:
            n = s - 1
            for j in range(2):
                for copy in c1(n, j):
                    copy.wait_recv()
            for into, other in zip(spots(n, *place.yx(place.p, 1 - place.q)), (r1.at[n % 4, 1 - place.q], r1l.at[n % 4, 1 - place.q])):
                add_into(into, other)

            @pl.when(qz)
            def _():
                for copy in c2(n):
                    copy.start()

            for into, other in zip(spots(n, *place.yx(place.p, place.q)), (r1.at[n % 4, place.q], r1l.at[n % 4, place.q])):
                add_into(into, other)
            z_stages(n, True, False)
        if 0 <= s - 2 < 3 * depth:
            n = s - 2

            @pl.when(qz)
            def _():
                for copy in c2(n):
                    copy.wait_recv()
                for into, other in zip(spots(n, *place.yx(place.p, place.q)), (r2.at[n % 4], r2l.at[n % 4])):
                    add_into(into, other)

            z_stages(n, False, False)
            z_stages(n, True, True)
            if n % depth == depth - 1:
                pl.when(zq)(lambda: hand_over(n))
        if 0 <= s - 3 < 3 * depth:
            z_stages(s - 3, False, True)
            if (s - 3) % depth == depth - 1:
                total((s - 3) // depth)

    def hand_over(n):
        g = n // depth
        z_got(g, 1)
        main, left = spots(n, *place.yx(place.p, 1 - place.q))

        @pl.loop(0, drows // 48)
        def _(i):
            at_rows = pl.ds(pl.multiple_of(i * 48, 16), 48)
            main[at_rows, :] = z_sum(g, 1, main[at_rows, :].astype(f32), r3, (at_rows,)).astype(bf16)

        left[...] = z_sum(g, 1, left[...].astype(f32), r3l, ()).astype(bf16)
        for copy in c2(n):
            copy.start()

    def left_copy(g):
        return send(lf.at[g], lx.at[g], lx_sems.at[0, g], lx_sems.at[1, g], flip_x)

    def total(g):
        last = (g + 1) * depth - 1
        z_got(g, 0)
        main, left = spots(last, *place.yx(place.p, place.q))

        def write(handed):
            if handed:
                for copy in c2(last):
                    copy.wait_recv()

            @pl.loop(0, drows // 48)
            def _(i):
                at_rows = pl.ds(pl.multiple_of(i * 48, 16), 48)
                value = z_sum(g, 0, main[at_rows, :].astype(f32), r3, (at_rows,))
                if handed:
                    value = value + r2[g, at_rows, :].astype(f32)
                if g == 0:
                    o_fc2[at_rows, :512] = value
                elif g == 1:
                    o_fc1[at_rows, :512] = value
                else:
                    o_qkv[at_rows, :q_main] = value[:, :q_main]
                    o_proj[at_rows, :p_main] = value[:, q_main:]

            value = z_sum(g, 0, left[...].astype(f32), r3l, ())
            lf[g] = value + r2l[g].astype(f32) if handed else value

        pl.when(zq)(lambda: write(True))
        pl.when(qz)(lambda: write(False))
        left_copy(g).start()

    def left_finish(g):
        left_copy(g).wait_recv()
        first = place.x == 0
        top = jnp.where(first, lf[g][:, :64], lx[g][:, 64:])
        bottom = jnp.where(first, lx[g][:, :64], lf[g][:, 64:])
        tail = 3 * hc - q_main
        for spot, value in ((0, top), (lrows, bottom)):
            if g == 0:
                o_fc2[spot:spot + lrows, 512:] = value
            elif g == 1:
                o_fc1[spot:spot + lrows, 512:] = value
            else:
                o_qkv[spot:spot + lrows, q_main:] = value[:, :tail]
                o_proj[spot:spot + lrows, p_main:] = value[:, tail:]

    def turn_into(i, src):
        @pl.loop(0, width // 128)
        def _(n):
            spot = pl.ds(pl.multiple_of(n * 128, 128), 128)
            turn[i, spot, :] = src[:, spot].T

    swap_out = Swap(place, out_h, o_out, swap_sems, 0)
    load_dy = load(dy_h, 0)
    weight_load(0).start()
    for u in range(depth):
        slope_load(u).start()
    tick_prefetch(0)
    swap_out.start()
    gv[...] = jnp.zeros_like(gv)
    tt[...] = jnp.zeros_like(tt)
    gv[5:6, :] = vec[8:9, :]
    load_dy.wait()

    def first(at_rows):
        grad = tmp[0, at_rows, :].astype(f32) * vec[5:6, :]
        gv[7:8, :] += jnp.sum(grad, axis=0, keepdims=True)
        ml[at_rows, :] = grad.astype(bf16)

    row_parts(first)
    turn_into(0, ml)

    def hidden_back(u):
        z = zc(u)
        weight_use(u)
        slope_load(u).wait()
        sums = gv.at[8:9, :]
        sums[...] = jnp.zeros((1, width), f32)

        def body(at_rows):
            grad = nn(ml[at_rows, :], wbuf[u % 2]) * pre[z, at_rows, :].astype(f32)
            sums[...] += jnp.sum(grad, axis=0, keepdims=True)
            pre[z, at_rows, :] = grad.astype(bf16)

        row_parts(body)
        for j in range(2):
            tt[2 * z + j, 1:2, :512] = sums[:, 512 * j:512 * (j + 1)]
            tt[2 * z + j, 1:2, 512:576] = sums[:, 1024 + 64 * j:1024 + 64 * (j + 1)]

    def normed_back(u):
        z = zc(u % depth)
        weight_use(u)

        def body(at_rows):
            term = nt(pre[z, at_rows, :], wbuf[u % 2])
            if u == depth:
                gx[at_rows, :] = term
            else:
                gx[at_rows, :] += term

        row_parts(body)

    tick_a(0)
    hidden_back(0)
    tick_b(0)
    hidden_back(1)
    hidden_back(2)
    tick_a(1)
    hidden_back(3)
    tick_b(1)
    normed_back(depth)
    normed_back(depth + 1)
    tick_a(2)
    normed_back(depth + 2)
    tick_b(2)
    normed_back(depth + 3)

    load_mid = pltpu.make_async_copy(mid_h, gm, tmp_sems.at[2])
    load_mid.start()
    load_ba, load_dy = load(ba_h, 1), load(dy_h, 0)
    load_mid.wait()
    load_ba.wait()
    load_dy.wait()

    def norm_grad(values, grads, shift_row, scale_row, scale_vec):
        normal, inverse = norm_rows(values)
        gv[shift_row:shift_row + 1, :] += jnp.sum(grads, axis=0, keepdims=True)
        gv[scale_row:scale_row + 1, :] += jnp.sum(grads * normal, axis=0, keepdims=True)
        inner = grads * (1.0 + scale_vec)
        one = jnp.mean(inner, axis=-1, keepdims=True)
        two = jnp.mean(inner * normal, axis=-1, keepdims=True)
        return inverse * (inner - one - normal * two)

    def second(at_rows):
        grad = norm_grad(gm[at_rows, :], gx[at_rows, :], 3, 4, vec[4:5, :]) + tmp[0, at_rows, :].astype(f32)
        gm[at_rows, :] = grad
        gv[2:3, :] += jnp.sum(grad * tmp[1, at_rows, :].astype(f32), axis=0, keepdims=True)
        grad = grad * vec[2:3, :]
        gv[6:7, :] += jnp.sum(grad, axis=0, keepdims=True)
        ml[at_rows, :] = grad.astype(bf16)

    row_parts(second)

    def heads_load(t):
        spot = pl.ds(4 * zc(t), 4)
        return [pltpu.make_async_copy(src.at[spot], heads.at[i], head_sems.at[i])
                for i, src in enumerate((q_h, k_h, v_h, k2_h, v2_h))]

    def att_load(t):
        return pltpu.make_async_copy(att_h.at[zc(t)], att, att_sems.at[0])

    def kv_swap(t, kind, i):
        return send(kv_give.at[kind, i], kv_got.at[t % 2, kind, i], kv_sems.at[0, 0, kind, i], kv_sems.at[1, t % 2, kind, i], place.to_core)

    def pair_of(value, j):
        spot = 2 * p_main + 64 * j + 48
        return jnp.concatenate([value[:, j * p_main:(j + 1) * p_main], value[:, spot:spot + 16]], axis=1)

    def attention_open(t):
        u = 2 * depth + t
        weight_use(u)
        att_load(t).wait()

        def body(at_rows):
            grads = nn(ml[at_rows, :], wbuf[u % 2, :, 2 * q_main:])
            results = att[at_rows, :].astype(f32)
            for j in range(2):
                grad = pair_of(grads, j).astype(bf16)
                product = (grad.astype(f32) * pair_of(results, j)).T
                for e in range(2):
                    grad_o[2 * j + e, at_rows, :] = grad[:, e * HEAD_DIM:(e + 1) * HEAD_DIM]
                    delta[2 * j + e, :, at_rows] = jnp.sum(product[e * HEAD_DIM:(e + 1) * HEAD_DIM, :], axis=0, keepdims=True)

        row_halves(body)
        for copy in heads_load(t):
            copy.wait()

    def attention_heads(t, between):
        @pl.loop(0, 4)
        def _(i):
            q, out_grad, shift, less = heads[0, i], grad_o[i], lse[4 * zc(t) + i], delta[i]

            def side(k, v):
                probs = jnp.exp2(nt(k, q) * SOFT - shift)
                grad = (probs * (nt(v, out_grad) - less)).astype(bf16)
                return nn(grad, q) * scale, nn(probs.astype(bf16), out_grad), tn(k, grad)

            dk, dv, dq_two = side(heads[3, i], heads[4, i])
            kv_give[0, i] = dk.astype(bf16)
            kv_give[1, i] = dv.astype(bf16)
            kv_swap(t, 0, i).start()
            kv_swap(t, 1, i).start()
            dk, dv, dq_one = side(heads[1, i], heads[2, i])
            own[1, i] = dk
            own[2, i] = dv
            own[0, i] = ((dq_one + dq_two) * scale).T
            for n, action in between:
                pl.when(i == n)(action)

    def attention_close(t):
        u = 2 * depth + t
        z = zc(t)
        if t + 1 < depth:
            for copy in heads_load(t + 1):
                copy.start()
            att_load(t + 1).start()
        for kind in range(2):
            for i in range(4):
                kv_swap(t, kind, i).wait()
        if t > 0:
            pq_wait(t - 1)

        def body(at_rows):
            for j in range(2):
                pieces, tails = [[], [], []], None
                for e in range(2):
                    i = 2 * j + e
                    dq = own[0, i, at_rows, :]
                    dk = own[1, i, at_rows, :] + kv_got[t % 2, 0, i, at_rows, :].astype(f32)
                    dv = own[2, i, at_rows, :] + kv_got[t % 2, 1, i, at_rows, :].astype(f32)
                    tt[2 * z + j, 2:3, e * HEAD_DIM:(e + 1) * HEAD_DIM] += jnp.sum(dq, axis=0, keepdims=True)
                    tt[2 * z + j, 2:3, hc + e * HEAD_DIM:hc + (e + 1) * HEAD_DIM] += jnp.sum(dv, axis=0, keepdims=True)
                    for n, value in enumerate((dq, dk, dv)):
                        pieces[n].append(value)
                last = pieces[2][1]
                cut = q_main - 2 * hc - HEAD_DIM
                line = pieces[0] + pieces[1] + [pieces[2][0], last[:, :cut]]
                pq[at_rows, j * q_main:(j + 1) * q_main] = jnp.concatenate(line, axis=1).astype(bf16)
                rest = jnp.concatenate([last[:, cut:], jnp.zeros((last.shape[0], 64 - HEAD_DIM + cut), f32)], axis=1)
                pq[at_rows, 2 * q_main + 64 * j:2 * q_main + 64 * (j + 1)] = rest.astype(bf16)
            term = nt(pq[at_rows, :2 * q_main], wbuf[u % 2, :, :2 * q_main]) + nt(pq[at_rows, 2 * q_main:], wbuf[u % 2, :, 1024:])
            if t == 0:
                gx[at_rows, :] = term
            else:
                gx[at_rows, :] += term

        row_halves(body)
        pq_save(t).start()

    for copy in heads_load(0):
        copy.start()
    att_load(0).start()
    load_n2 = load(n2_h, 0)
    tick_a(3)
    load_n2.wait()
    turn_into(0, tmp.at[0])
    load_x, load_n1 = load(x_h, 0), load(n1_h, 1)
    tick_b(3)
    attention_open(0)
    attention_heads(0, [(1, lambda: tick_a(4)), (3, lambda: tick_b(4))])
    attention_close(0)
    attention_open(1)
    tick_a(5)
    attention_heads(1, [(0, lambda: tick_b(5)), (2, lambda: tick_a(6)), (3, lambda: tick_b(6))])
    attention_close(1)
    tick_a(7)
    load_n1.wait()
    turn_into(1, tmp.at[1])
    turn_into(0, ml)
    attention_open(2)
    attention_heads(2, [(0, lambda: tick_b(7)), (2, lambda: tick_a(8))])
    tick_b(8)
    attention_close(2)
    attention_open(3)
    tick_a(9)
    attention_heads(3, [(0, lambda: tick_b(9)), (2, lambda: tick_a(10))])
    tick_b(10)
    attention_close(3)
    tick_prefetch(11)
    tick_a(11)
    load_x.wait()

    def third(at_rows):
        grad = norm_grad(tmp[0, at_rows, :].astype(f32), gx[at_rows, :], 0, 1, vec[1:2, :]) + gm[at_rows, :]
        tmp[1, at_rows, :] = grad.astype(bf16)

    row_parts(third)
    swap_lat = Swap(place, tmp.at[1], o_lat, swap_sems, 1)
    swap_lat.start()

    for c in range(cols_n):
        spot = slice(c * hc, (c + 1) * hc)
        for k in range(6):
            tt[c, 0:1, k * hc:(k + 1) * hc] = gv[k:k + 1, spot]
        tt[c, 1:2, 576:576 + hc] = gv[6:7, spot]
        tt[c, 1:2, 576 + hc:] = gv[7:8, spot]
    copy_t = send(tt, tc, t_sems.at[0], t_sems.at[1], place.to_core)
    copy_t.start()
    tick_b(11)
    copy_t.wait()
    tt[...] = tt[...] + tc[...]

    def u_copy(k):
        to = (col + k) % cols_n
        return send(tt.at[to], um.at[col], u_sems.at[0, k], u_sems.at[1, col], (row, to))

    def u_got(k):
        src = (col + k) % cols_n
        return send(tt.at[src], um.at[src], u_sems.at[0, k], u_sems.at[1, src], (row, src))

    for k in range(1, cols_n):
        u_copy(k).start()
    um[col] = tt[col]
    tick_b(12)
    for k in range(1, cols_n):
        u_got(k).wait_recv()
    copy_v = send(um, vm_, v_sems.at[0], v_sems.at[1], flip_y)
    copy_v.start()
    tick_b(13)
    copy_v.wait_recv()
    modl[...] = jnp.zeros_like(modl)
    sums = um[0] + vm_[0]
    for c in range(1, cols_n):
        sums = sums + um[c] + vm_[c]
    o_rows[...] = sums
    for c in range(cols_n):
        modl[2 * place.y + c % 2, c // 2:c // 2 + 1, :] = um[c, 0:1, :]
        modl[2 - 2 * place.y + c % 2, c // 2:c // 2 + 1, :] = vm_[c, 0:1, :]
    low = modl[...].reshape(rows_n * 8, 6 * hc).astype(bf16)
    o_ada[...] = tn(act[...].reshape(rows_n * 8, drows).astype(bf16), low)
    cp[...] = nt(low, ada[...]).reshape(rows_n, 8, drows)

    def cr_copy(k):
        return send(cp, cr.at[col], cr_sems.at[0, k], cr_sems.at[1, col], (row, (col + k) % cols_n))

    def cr_got(k):
        src = (col + k) % cols_n
        return send(cp, cr.at[src], cr_sems.at[0, k], cr_sems.at[1, src], (row, src))

    for k in range(1, cols_n):
        cr_copy(k).start()
    tick_b(14)
    left_finish(0)
    left_finish(1)
    for k in range(1, cols_n):
        cr_got(k).wait_recv()
        cr_copy(k).wait_send()
    cr[col] = cp[...]
    cp[...] = sum(cr[c] for c in range(cols_n))

    def cf_copy(k):
        to = (row + k) % rows_n
        return send(cp.at[to], cf.at[row], cf_sems.at[0, k], cf_sems.at[1, row], (to, col))

    def cf_got(k):
        src = (row + k) % rows_n
        return send(cp.at[src], cf.at[src], cf_sems.at[0, k], cf_sems.at[1, src], (src, col))

    for k in range(1, rows_n):
        cf_copy(k).start()
    cf[row] = cp[row]
    left_finish(2)
    for k in range(1, rows_n):
        cf_got(k).wait_recv()
    cond_value = cond[...]
    gate = 1.0 / (1.0 + jnp.exp(-cond_value))
    slope = gate * (1.0 + cond_value * (1.0 - gate))
    for r in range(rows_n):
        spot = slice(r * drows, (r + 1) * drows)
        o_cond[:, spot] = cf[r] * slope[:, spot]

    for s in range(3 * depth - SLOTS, 3 * depth):
        sent(s)
    for s in range(3 * depth - 2, 3 * depth):
        for y in range(2):
            c0(s, y).wait_send()
    for g in range(3):
        left_copy(g).wait_send()
    for k in range(1, cols_n):
        u_copy(k).wait_send()
    copy_v.wait_send()
    for k in range(1, rows_n):
        cf_copy(k).wait_send()
    swap_lat.wait()
    swap_out.wait()


def backward(saved, out, lse, vec, act, ada, cond, collective_id):
    rows, cols = lax.axis_size("row"), lax.axis_size("col")
    depth = cols // 2
    tokens, width = out.shape
    heads, drows, hc6 = width // HEAD_DIM, ada.shape[0], ada.shape[1]
    hc, lanes, lrows = width // cols, 1152, drows // 2
    shape, dma, vm = jax.ShapeDtypeStruct, pltpu.SemaphoreType.DMA, pltpu.VMEM
    token = shape((tokens, width), bf16)
    outs = [token, token, shape((depth, tokens, 896), bf16), shape((drows, 576), f32), shape((drows, 576), f32),
            shape((drows, 3 * hc), f32), shape((drows, hc), f32), shape((drows, hc6), f32), shape((8, hc6), f32),
            shape((8, width), f32)]
    head = (tokens, HEAD_DIM)
    scratch = [
        vm((SLOTS, 2, drows, lanes), bf16), vm((2, 2, drows, lanes), bf16), vm((2, 2, drows, lanes), bf16),
        vm((4, 2, drows, 512), bf16), vm((4, 2, lrows, 128), bf16), vm((4, drows, 512), bf16), vm((4, lrows, 128), bf16),
        vm((2, 9, drows, 512), bf16), vm((2, 9, lrows, 128), bf16), vm((3, lrows, 128), f32), vm((3, lrows, 128), f32),
        vm((2, width, lanes), bf16), vm((2, tokens, lanes), bf16), vm((depth, tokens, lanes), bf16), vm((tokens, 896), bf16),
        vm((2, width, tokens), bf16), vm((2, tokens, width), bf16), vm((tokens, width), bf16), vm((tokens, width), f32),
        vm((tokens, width), f32), vm((tokens, 384), bf16), vm((5, 4) + head, bf16),
        vm((4,) + head, bf16), vm((4, 1, tokens), f32), vm((2, 4) + head, bf16), vm((2, 2, 4) + head, bf16), vm((3, 4) + head, f32),
        vm((16, width), f32), vm((2, tokens, 384), bf16),
        vm((cols, 8, hc6), f32), vm((cols, 8, hc6), f32), vm((cols, 8, hc6), f32), vm((cols, 8, hc6), f32), vm((rows, 8, hc6), f32),
        vm((rows, 8, drows), f32), vm((cols, rows, 8, drows), f32), vm((rows, 8, drows), f32)]
    scratch += [
        dma((2, 2)), dma((2, 2, 2)), dma((2, 4, 2, 2)), dma((2, 4, 2)), dma((2, 2, 9, depth, 2)), dma((2, 3)), dma((2,)), dma((2, 2)),
        dma((depth,)), dma((3,)), dma((5,)), dma((2, 2, 2, 4)), dma((depth,)), dma((2,)), dma((2, cols)), dma((2,)), dma((2, cols)),
        dma((2, rows)), dma((2,))]
    vmem = pl.BlockSpec(memory_space=pltpu.VMEM)
    return pl.pallas_call(
        backward_kernel,
        out_shape=outs,
        in_specs=[ANY] * 16 + [vmem] * 5,
        out_specs=[ANY] * 3 + [vmem] * 7,
        scratch_shapes=scratch,
        compiler_params=pltpu.CompilerParams(collective_id=collective_id, has_side_effects=True, vmem_limit_bytes=63 * 2**20),
        name="backward",
    )(*saved, out, lse, vec, act, ada, cond)


class Plan:
    def __init__(self, latents, condition, qkv_weight, fc1_weight):
        self.rows, self.cols = lax.axis_size("row"), lax.axis_size("col")
        self.tokens, self.width = latents.shape
        self.lats = condition.shape[0]
        self.depth_rows = qkv_weight.shape[0]
        self.head_cols = qkv_weight.shape[2]
        self.ff_cols = fc1_weight.shape[1]
        self.share = SEQ // self.tokens
        self.near = (
            self.rows == 4 and self.share == 2 and self.cols == 8 and self.lats == self.cols // 2
            and (self.depth_rows, self.head_cols, self.ff_cols) == (288, 2 * HEAD_DIM, 576) and self.width == 1152)


def fold(left):
    rows, lanes = left.shape
    return left.reshape(2, rows // 2, lanes).transpose(1, 0, 2).reshape(rows // 2, 2 * lanes)


def gather_plain(blocks):
    return [lax.all_gather(lax.all_gather(b, "row", axis=0, tiled=True), "col", axis=1, tiled=True) for b in blocks]


def scatter_plain(fulls):
    parts = [lax.psum_scatter(g, "row", scatter_dimension=0, tiled=True) for g in fulls]
    return [lax.psum_scatter(g, "col", scatter_dimension=1, tiled=True).astype(f32) for g in parts]


def attend_plain(q, k, v):
    def one(item):
        scores = nt(item[0], item[1]) * HEAD_DIM ** (-0.5)
        top = jnp.max(scores, axis=-1, keepdims=True)
        probs = jnp.exp(scores - top)
        total = jnp.sum(probs, axis=-1, keepdims=True)
        return nn((probs / total).astype(bf16), item[2]).astype(bf16), top + jnp.log(total)

    return lax.map(one, (q, k, v))


def attend_back_plain(q, k, v, lse, att_grad):
    def one(item):
        q, k, v, lse, out_grad = item
        probs = jnp.exp(nt(q, k) * HEAD_DIM ** (-0.5) - lse)
        probs_grad = nt(out_grad, v)
        inner = jnp.sum(probs * probs_grad, axis=-1, keepdims=True)
        grad = (probs * (probs_grad - inner) * HEAD_DIM ** (-0.5)).astype(bf16)
        return nn(grad, k), tn(grad, q), tn(probs.astype(bf16), out_grad)

    return lax.map(one, (q, k, v, lse, att_grad))


def gelu_and_slope(u):
    c = math.sqrt(2.0 / math.pi)
    inner = jnp.tanh(c * (u + 0.044715 * u * u * u))
    value = 0.5 * u * (1.0 + inner)
    slope = 0.5 * (1.0 + inner) + 0.5 * u * (1.0 - inner * inner) * c * (1.0 + 3 * 0.044715 * u * u)
    return value, slope


def layer_norm(values):
    mean = jnp.mean(values, axis=-1, keepdims=True)
    centred = values - mean
    inverse = lax.rsqrt(jnp.mean(centred * centred, axis=-1, keepdims=True) + norm_eps)
    return centred * inverse, inverse


def norm_back(rows_grad, normal, inverse, scale):
    normal_grad = rows_grad * (1.0 + scale)
    first = jnp.mean(normal_grad, axis=-1, keepdims=True)
    second = jnp.mean(normal_grad * normal, axis=-1, keepdims=True)
    value_grad = inverse * (normal_grad - first - normal * second)
    return value_grad, jnp.sum(rows_grad, axis=0), jnp.sum(rows_grad * normal, axis=0)


def shards_near(plan, latents, condition, ada_weight, ada_bias, qkv_weight, qv_bias, proj_weight, proj_bias,
                fc1_weight, fc1_bias, fc2_weight, fc2_bias, cotangent):
    depth, hc, fc = plan.depth_rows, plan.head_cols, plan.ff_cols
    q_main, p_main, f_main = 384, 128, 512
    qkv_flat = qkv_weight.reshape(depth, 3 * hc)
    proj_t, fc2_t = proj_weight.T, fc2_weight.T
    main_a = jnp.concatenate([qkv_flat[:, :q_main], proj_t[:, :p_main]], axis=1)
    left = jnp.concatenate([fold(jnp.concatenate([qkv_flat[:, q_main:], proj_t[:, p_main:]], axis=1)),
                            fold(fc1_weight[:, f_main:]), fold(fc2_t[:, f_main:])], axis=1)
    blocks = [main_a, left, fc1_weight[:, :f_main], fc2_t[:, :f_main]]
    cond = jnp.pad(condition.astype(f32), ((0, 8 - plan.lats), (0, 0)))
    ada = ada_weight.reshape(depth, 6 * hc)
    line = jnp.concatenate([fc1_bias, proj_bias, fc2_bias]).astype(f32).reshape(1, 6 * hc)
    tail = jnp.pad(qv_bias.astype(f32).reshape(1, 2 * hc), ((0, 0), (0, 4 * hc)))
    bias = jnp.concatenate([jnp.broadcast_to(ada_bias.astype(f32).reshape(1, 6 * hc), (plan.lats, 6 * hc)), line, tail,
                            jnp.zeros((8 - plan.lats - 2, 6 * hc), f32)], axis=0)
    (w, dy, x, n1, q, k, v, k2, v2, lse, att, ba, mid, n2, hid, slo, out, vec, act) = forward(
        latents, cotangent, cond, ada, bias, blocks, 0)
    output, lat_grad, _, fc2_sum, fc1_sum, qkv_sum, proj_sum, ada_sum, rows, cond_grad = backward(
        (w, dy, x, n1, q, k, v, k2, v2, att, ba, mid, n2, hid, slo), out, lse, vec, act, ada, cond, 1)
    return (
        output, lat_grad.astype(f32), cond_grad[:plan.lats], ada_sum.reshape(depth, 6, hc), rows[0].reshape(6, hc),
        qkv_sum.reshape(depth, 3, hc), rows[2, :2 * hc].reshape(2, hc), proj_sum.T, rows[1, fc:fc + hc],
        fc1_sum, rows[1, :fc], fc2_sum.T, rows[1, fc + hc:])


def shards(latents, condition, ada_weight, ada_bias, qkv_weight, qv_bias, proj_weight, proj_bias,
           fc1_weight, fc1_bias, fc2_weight, fc2_bias, cotangent):
    plan = Plan(latents, condition, qkv_weight, fc1_weight)
    if plan.near:
        return shards_near(plan, latents, condition, ada_weight, ada_bias, qkv_weight, qv_bias, proj_weight, proj_bias,
                           fc1_weight, fc1_bias, fc2_weight, fc2_bias, cotangent)
    row, col = lax.axis_index("row"), lax.axis_index("col")
    rows, cols, width, tokens = plan.rows, plan.cols, plan.width, plan.tokens
    depth, hc, fc = plan.depth_rows, plan.head_cols, plan.ff_cols
    heads = cols * hc // HEAD_DIM
    groups = rows * plan.lats

    blocks = [qkv_weight.reshape(depth, 3 * hc), proj_weight.T, fc1_weight, fc2_weight.T]
    qkv_w, proj_w, fc1_w, fc2_w = gather_plain(blocks)
    home = row * plan.lats + col // plan.share
    values, grad_out = latents.astype(f32), cotangent.astype(f32)

    cond_all = lax.all_gather(condition, "row", axis=0, tiled=True).astype(f32)
    cond_act = jax.nn.silu(cond_all).astype(bf16)
    cond_mine = lax.dynamic_slice(cond_act, (0, row * depth), (groups, depth))
    ada_flat = ada_weight.reshape(depth, 6 * hc)
    partial = lax.psum(nn(cond_mine, ada_flat), "row") + ada_bias.astype(f32).reshape(1, 6 * hc)
    small = jnp.concatenate(
        [partial.reshape(-1)] + [b.astype(f32).reshape(-1) for b in (proj_bias, fc2_bias, fc1_bias, qv_bias)])
    small = lax.all_gather(small, "col", axis=0, tiled=False)
    sizes = [groups * 6 * hc, hc, hc, fc, 2 * hc]
    mod_all, proj_b, fc2_b, fc1_b, qv_b = jnp.split(small, [sum(sizes[:i + 1]) for i in range(4)], axis=1)
    mod = lax.dynamic_index_in_dim(mod_all.reshape(cols, groups, 6, hc), home, 1, keepdims=False)
    mod = mod.transpose(1, 0, 2).reshape(6, 1, width)
    shift_one, scale_one, gate_one, shift_two, scale_two, gate_two = (mod[k] for k in range(6))
    proj_b, fc2_b, fc1_b = proj_b.reshape(width), fc2_b.reshape(width), fc1_b.reshape(-1)
    q_b, v_b = qv_b[:, :hc].reshape(heads, 1, HEAD_DIM), qv_b[:, hc:].reshape(heads, 1, HEAD_DIM)

    def to_heads(flat):
        return flat.reshape(tokens, heads, HEAD_DIM).transpose(1, 0, 2)

    def from_heads(value):
        return value.transpose(1, 0, 2).reshape(tokens, cols, hc)

    normal_one, inverse_one = layer_norm(values)
    normed_one = (normal_one * (1.0 + scale_one) + shift_one).astype(bf16)
    projected = nn(normed_one, qkv_w).reshape(tokens, cols, 3 * hc)
    query = (to_heads(projected[:, :, :hc]) + q_b).astype(bf16)
    key = to_heads(projected[:, :, hc:2 * hc]).astype(bf16)
    value = (to_heads(projected[:, :, 2 * hc:]) + v_b).astype(bf16)
    cuts = [[s * plan.share + i for i in range(plan.share)] for s in range(cols // plan.share)]
    key_all = lax.all_gather(key, "col", axis=1, tiled=True, axis_index_groups=cuts)
    value_all = lax.all_gather(value, "col", axis=1, tiled=True, axis_index_groups=cuts)
    att, lse = attend_plain(query, key_all, value_all)
    att_flat = from_heads(att).reshape(tokens, width)
    branch_a = nt(att_flat, proj_w) + proj_b
    middle = values + gate_one * branch_a

    normal_two, inverse_two = layer_norm(middle)
    normed_two = (normal_two * (1.0 + scale_two) + shift_two).astype(bf16)
    hidden, slope = gelu_and_slope(nn(normed_two, fc1_w) + fc1_b)
    hidden = hidden.astype(bf16)
    branch_m = nt(hidden, fc2_w) + fc2_b
    output = (middle + gate_two * branch_m).astype(bf16)

    gate_two_grad = jnp.sum(grad_out * branch_m, axis=0)
    m_grad = grad_out * gate_two
    fc2_bias_part = jnp.sum(m_grad, axis=0)
    m_low = m_grad.astype(bf16)
    fc2_grad = tn(m_low, hidden).astype(bf16)
    pre_grad = nn(m_low, fc2_w) * slope
    fc1_bias_part = jnp.sum(pre_grad, axis=0)
    pre_low = pre_grad.astype(bf16)
    fc1_grad = tn(normed_two, pre_low).astype(bf16)
    normed_two_grad = nt(pre_low, fc1_w)
    middle_part, shift_two_grad, scale_two_grad = norm_back(normed_two_grad, normal_two, inverse_two, scale_two)
    middle_grad = grad_out + middle_part
    gate_one_grad = jnp.sum(middle_grad * branch_a, axis=0)
    a_grad = middle_grad * gate_one
    proj_bias_part = jnp.sum(a_grad, axis=0)
    a_low = a_grad.astype(bf16)
    proj_grad = tn(a_low, att_flat).astype(bf16)
    att_grad = to_heads(nn(a_low, proj_w).astype(bf16))
    query_grad, key_grad, value_grad = attend_back_plain(query, key_all, value_all, lse, att_grad)
    key_grad, value_grad = (
        lax.psum_scatter(g.astype(bf16), "col", scatter_dimension=1, tiled=True, axis_index_groups=cuts).astype(f32)
        for g in (key_grad, value_grad))
    q_bias_part, v_bias_part = jnp.sum(query_grad, axis=1), jnp.sum(value_grad, axis=1)
    qkv_low = jnp.concatenate([from_heads(g.astype(bf16)) for g in (query_grad, key_grad, value_grad)], axis=2)
    qkv_low = qkv_low.reshape(tokens, 3 * width)
    qkv_grad = tn(normed_one, qkv_low).astype(bf16)
    normed_one_grad = nt(qkv_low, qkv_w)
    fc2_sum, fc1_sum, qkv_sum, proj_sum = scatter_plain([fc2_grad, fc1_grad, qkv_grad, proj_grad])
    input_part, shift_one_grad, scale_one_grad = norm_back(normed_one_grad, normal_one, inverse_one, scale_one)
    latents_grad = middle_grad + input_part

    mod_grad = jnp.stack(
        [shift_one_grad, scale_one_grad, gate_one_grad, shift_two_grad, scale_two_grad, gate_two_grad], axis=0)
    mod_grad = lax.all_gather(mod_grad, ("row", "col"), axis=0, tiled=False)
    mod_grad = mod_grad.reshape(groups, plan.share, 6, width).sum(axis=1)
    mod_mine = lax.dynamic_slice(mod_grad, (0, 0, col * hc), (groups, 6, hc))
    ada_bsum = jnp.sum(mod_mine, axis=0)
    mod_low = mod_mine.astype(bf16).reshape(groups, 6 * hc)
    ada_wsum = tn(cond_mine, mod_low).reshape(depth, 6, hc)
    cond_part = lax.dynamic_update_slice(jnp.zeros((groups, width), f32), nt(mod_low, ada_flat), (0, row * depth))
    parts = [cond_part, proj_bias_part, fc2_bias_part, q_bias_part, v_bias_part, fc1_bias_part]
    totals = lax.psum(jnp.concatenate([part.reshape(-1) for part in parts]), ("row", "col"))
    ends, spot = [], 0
    for part in parts:
        ends.append(totals[spot:spot + part.size])
        spot += part.size

    def mine(flat):
        size = flat.size // cols
        return lax.dynamic_slice(flat, (col * size,), (size,))

    cond_summed = lax.dynamic_slice(ends[0].reshape(groups, width), (row * plan.lats, 0), (plan.lats, width))
    silu_value, silu_pull = jax.vjp(jax.nn.silu, condition.astype(f32))
    condition_grad = silu_pull(cond_summed)[0]
    qv_bsum = jnp.stack([mine(ends[3]), mine(ends[4])], axis=0)
    return (
        output, latents_grad, condition_grad, ada_wsum, ada_bsum, qkv_sum.reshape(depth, 3, hc), qv_bsum,
        proj_sum.T, mine(ends[1]), fc1_sum, mine(ends[5]), fc2_sum.T, mine(ends[2]))


def solution(mesh):
    token, grid, turned = P(("row", "col"), None), P("row", "col"), P("col", "row")
    cube, wide, flat = P("row", None, "col"), P(None, "col"), P("col")
    return jax.shard_map(
        shards,
        mesh=mesh,
        in_specs=(token, P("row", None), cube, wide, cube, wide, turned, flat, grid, flat, turned, flat, token),
        out_specs=(token, token, P("row", None), cube, wide, cube, wide, turned, flat, grid, flat, turned, flat),
        check_vma=False,
    )
```

```python
import functools
import math
import jax
import jax.numpy as jnp
from jax import lax
from jax.experimental import pallas as pl
from jax.experimental.pallas import tpu as pltpu
from jax.sharding import PartitionSpec as P

HEAD_DIM = 72
SEQ = 1024
norm_eps = 1e-06
bf16, f32 = jnp.bfloat16, jnp.float32

MESH = pl.DeviceIdType.MESH
ANY = pl.BlockSpec(memory_space=pl.ANY)


class Place:
    def __init__(self):
        row, col = lax.axis_index("row"), lax.axis_index("col")
        self.row, self.col = row, col
        self.depth = lax.axis_size("col") // 2
        self.y, self.h = row // 2, row % 2
        self.z, self.x = col // 2, col % 2
        self.p = jnp.where(self.h == 0, self.y, self.x)
        self.q = jnp.where(self.h == 0, self.x, self.y)
        flip_x, flip_y = (row, col + 1 - 2 * self.x), (row + 2 - 4 * self.y, col)
        self.to_q = tuple(jnp.where(self.h == 0, a, b) for a, b in zip(flip_x, flip_y))
        self.to_p = tuple(jnp.where(self.h == 0, b, a) for a, b in zip(flip_x, flip_y))
        self.to_core = (row + 1 - 2 * self.h, col)

    def to_z(self, z):
        return (self.row, 2 * z + self.x)

    def diagonal(self):
        return (self.row + 1 - 2 * self.h, self.col + 1 - 2 * self.x)

    def yx(self, p, q):
        return jnp.where(self.h == 0, p, q), jnp.where(self.h == 0, q, p)

    def partners(self):
        near = [self.to_q, self.to_p, self.to_core]
        return near + [self.to_z((self.z + k) % self.depth) for k in range(1, self.depth)]


def greet(partners):
    barrier = pltpu.get_barrier_semaphore()
    for partner in partners:
        pl.semaphore_signal(barrier, inc=1, device_id=partner, device_id_type=MESH)
    pl.semaphore_wait(barrier, len(partners))


def block_at(ref, rows, lanes, r, c):
    return ref.at[pl.ds(pl.multiple_of(r * rows, 16), rows), pl.ds(pl.multiple_of(c * lanes, 128), lanes)]


class Gather:
    def __init__(self, place, ins, outs, sems):
        self.at, self.ins, self.outs = place, ins, outs
        self.local, self.zs, self.zzs, self.qs, self.ps, self.ks = sems
        self.early = place.h == 0

    @staticmethod
    def scratch(count, depth):
        dma = pltpu.SemaphoreType.DMA
        return [dma((count,)), dma((count, 2, depth)), dma((count, 2, depth)), dma((count, 2, depth)), dma((count, 2, depth, 2)),
                dma((count, 2, depth, 2))]

    def block(self, a, p, q, z):
        y, x = self.at.yx(p, q)
        rows, lanes = self.ins[a].shape
        return block_at(self.outs[a], rows, lanes, 2 * y + self.at.h, 2 * z + x)

    def zc(self, t):
        return (self.at.z + self.at.depth - t) % self.at.depth

    def copy(self, src, dst, sems, index, to):
        return pltpu.make_async_remote_copy(
            src_ref=src, dst_ref=dst, send_sem=sems.at[(index[0], 0) + index[1:]], recv_sem=sems.at[(index[0], 1) + index[1:]],
            device_id=to, device_id_type=MESH)

    def spot(self, a, t, j=0):
        p, q = self.at.p, self.at.q
        return self.block(a, p if j < 2 else 1 - p, q if j % 2 == 0 else 1 - q, self.zc(t))

    def source(self, a, t, j=0):
        return self.ins[a] if t == 0 and j == 0 else self.spot(a, t, j)

    def c_local(self, a):
        return pltpu.make_async_copy(self.ins[a], self.spot(a, 0), self.local.at[a])

    def c_z(self, a, k, j):
        place, sems = self.at, (self.zs, self.zzs)[j]
        return pltpu.make_async_remote_copy(
            src_ref=self.source(a, 0, j), dst_ref=self.spot(a, 0, j), send_sem=sems.at[a, 0, k], recv_sem=sems.at[a, 1, place.z],
            device_id=place.to_z((place.z + k) % place.depth), device_id_type=MESH)

    def r_z(self, a, t, j):
        place, sems = self.at, (self.zs, self.zzs)[j]
        return pltpu.make_async_remote_copy(
            src_ref=self.source(a, 0, j), dst_ref=self.spot(a, t, j), send_sem=sems.at[a, 0, 0], recv_sem=sems.at[a, 1, self.zc(t)],
            device_id=place.to_q, device_id_type=MESH)

    def c_q(self, a, t):
        return self.copy(self.source(a, t), self.spot(a, t), self.qs, (a, self.zc(t)), self.at.to_q)

    def c_p(self, a, t, j):
        return self.copy(self.source(a, t, j), self.spot(a, t, j), self.ps, (a, self.zc(t), j), self.at.to_p)

    def c_k(self, a, t, j):
        rows, lanes = self.ins[a].shape
        r = 2 * j + self.at.h
        spot = block_at(self.outs[a], rows, 2 * lanes, r, self.zc(t))
        return self.copy(spot, spot, self.ks, (a, self.zc(t), j), self.at.to_core)

    def start(self, a):
        self.c_q(a, 0).start()
        for k in range(1, self.at.depth):
            self.c_z(a, k, 0).start()
        self.c_local(a).start()

    def forward(self, a):
        @pl.when(self.early)
        def _():
            self.c_q(a, 0).wait_recv()
            for k in range(1, self.at.depth):
                self.c_z(a, k, 1).start()

    def stage(self, a, t, n):
        late = jnp.logical_not(self.early)
        if n == 0:
            if t > 0:
                self.r_z(a, t, 0).wait_recv()
                pl.when(late)(self.c_q(a, t).start)
            self.c_p(a, t, 0).start()
        elif n == 1:
            pl.when(late)(self.c_q(a, t).wait_recv)
            if t > 0:
                pl.when(self.early)(self.r_z(a, t, 1).wait_recv)
            self.c_p(a, t, 1).start()
        elif n == 2:
            self.c_p(a, t, 0).wait_recv()
            if t == 0:
                self.c_local(a).wait()
        elif n == 3:
            self.c_p(a, t, 1).wait_recv()
            for j in range(2):
                self.c_k(a, t, j).start()
        else:
            for j in range(2):
                self.c_k(a, t, j).wait_recv()

    def finish(self, a):
        self.c_q(a, 0).wait_send()
        for k in range(1, self.at.depth):
            self.c_z(a, k, 0).wait_send()

        @pl.when(self.early)
        def _():
            for k in range(1, self.at.depth):
                self.c_z(a, k, 1).wait_send()

        @pl.when(jnp.logical_not(self.early))
        def _():
            for t in range(1, self.at.depth):
                self.c_q(a, t).wait_send()

        for t in range(self.at.depth):
            for j in range(2):
                self.c_p(a, t, j).wait_send()
            for j in range(2):
                self.c_k(a, t, j).wait_send()


class LineGather(Gather):
    def __init__(self, place, ins, outs, sems, mid=(), both=()):
        super().__init__(place, ins, outs, sems)
        z = place.z
        self.core0, self.mid, self.both = place.h == 0, mid, both
        self.middle = jnp.logical_and(z > 0, z < place.depth - 1)
        low = z < 2
        self.inner = place.to_z(jnp.where(low, z + 1, z - 1))
        self.outer = place.to_z(jnp.where(low, jnp.maximum(z - 1, 0), jnp.minimum(z + 1, place.depth - 1)))
        self.order = [z, z + 1 - 2 * (z % 2), jnp.where(low, 2, 1), jnp.where(low, 3, 0)]

    @staticmethod
    def scratch(count, depth):
        dma = pltpu.SemaphoreType.DMA
        return [dma((count,)), dma((count, 2, 5)), dma((count, 2, 5)), dma((count, 2, depth)), dma((count, 2, depth, 2)),
                dma((count, 2, depth, 2))]

    def z_first(self, a):
        return self.at.h < 2 if a in self.both else self.core0

    def zc(self, t):
        return self.order[t]

    def c_z(self, a, t, j, n):
        sems = (self.zs, self.zzs)[j]
        return pltpu.make_async_remote_copy(
            src_ref=self.source(a, t, j), dst_ref=self.spot(a, t, j), send_sem=sems.at[a, 0, n], recv_sem=sems.at[a, 1, self.zc(t)],
            device_id=self.inner if n in (0, 2) else self.outer, device_id_type=MESH)

    def z_start(self, a, j):
        self.c_z(a, 0, j, 0).start()
        pl.when(self.middle)(self.c_z(a, 0, j, 1).start)

    def z_got(self, a, t, j):
        self.c_z(a, t, j, 0).wait_recv()
        pl.when(self.middle)(self.c_z(a, t, j, 1 + t).start)

    def z_sent(self, a, j):
        self.c_z(a, 0, j, 0).wait_send()

        @pl.when(self.middle)
        def _():
            self.c_z(a, 0, j, 1).wait_send()
            for t in range(1, self.at.depth):
                self.c_z(a, t, j, 1 + t).wait_send()

    def start(self, a):
        self.c_q(a, 0).start()
        self.z_start(a, 0)
        self.c_local(a).start()

    def forward(self, a):
        if a in self.mid:
            @pl.when(self.z_first(a))
            def _():
                self.c_q(a, 0).wait_recv()
                self.z_start(a, 1)

    def stage(self, a, t, n):
        mid, early = a in self.mid, self.z_first(a)
        late = jnp.logical_not(early)
        if n == 0:
            if t > 0:
                self.z_got(a, t, 0)
                if mid:
                    pl.when(late)(self.c_q(a, t).start)
                else:
                    self.c_q(a, t).start()
            self.c_p(a, t, 0).start()
        elif n == 1:
            if not mid:
                self.c_q(a, t).wait_recv()
            else:
                pl.when(late)(self.c_q(a, t).wait_recv)
                if t > 0:
                    pl.when(early)(lambda: self.z_got(a, t, 1))
            self.c_p(a, t, 1).start()
        elif n == 2:
            self.c_p(a, t, 0).wait_recv()
            if t == 0:
                self.c_local(a).wait()
        elif n == 3:
            self.c_p(a, t, 1).wait_recv()
            for j in range(2):
                self.c_k(a, t, j).start()
        else:
            for j in range(2):
                self.c_k(a, t, j).wait_recv()

    def finish(self, a):
        self.c_q(a, 0).wait_send()
        self.z_sent(a, 0)

        def rest():
            for t in range(1, self.at.depth):
                self.c_q(a, t).wait_send()

        if a in self.mid:
            pl.when(self.z_first(a))(lambda: self.z_sent(a, 1))
            pl.when(jnp.logical_not(self.z_first(a)))(rest)
        else:
            rest()
        for t in range(self.at.depth):
            for j in range(2):
                self.c_p(a, t, j).wait_send()
            for j in range(2):
                self.c_k(a, t, j).wait_send()


def nt(a, b):
    return lax.dot_general(a, b, (((1,), (1,)), ((), ())), preferred_element_type=f32)


def nn(a, b):
    return lax.dot_general(a, b, (((1,), (0,)), ((), ())), preferred_element_type=f32)


def tn(a, b):
    return lax.dot_general(a, b, (((0,), (0,)), ((), ())), preferred_element_type=f32)


SOFT = HEAD_DIM ** (-0.5) * math.log2(math.e)


VECS = 24


def softmax_head(q, k, k2):
    one, two = nt(k, q), nt(k2, q)
    top = jnp.maximum(jnp.max(one, axis=0, keepdims=True), jnp.max(two, axis=0, keepdims=True)) * SOFT
    one, two = jnp.exp2(one * SOFT - top), jnp.exp2(two * SOFT - top)
    total = jnp.sum(one, axis=0, keepdims=True) + jnp.sum(two, axis=0, keepdims=True)
    return one.astype(bf16), two.astype(bf16), total, top + jnp.log2(total)


def norm_rows(values):
    mean = jnp.mean(values, axis=-1, keepdims=True)
    centred = values - mean
    inverse = lax.rsqrt(jnp.mean(centred * centred, axis=-1, keepdims=True) + norm_eps)
    return centred * inverse, inverse


def gelu_both(u):
    c = math.sqrt(2.0 / math.pi)
    square = u * u
    inner = jnp.tanh(u * (c + (c * 0.044715) * square))
    half = 0.5 * (1.0 + inner)
    slope = half + (0.5 * u) * (1.0 - inner * inner) * (c + (3 * c * 0.044715) * square)
    return u * half, slope


class Swap:
    def __init__(self, place, src, dst, sems, i):
        self.stay = place.h == place.x
        self.local = pltpu.make_async_copy(src, dst, sems.at[i, 0])
        self.remote = pltpu.make_async_remote_copy(
            src_ref=src, dst_ref=dst, send_sem=sems.at[i, 0], recv_sem=sems.at[i, 1],
            device_id=place.diagonal(), device_id_type=MESH)

    def start(self):
        pl.when(self.stay)(self.local.start)
        pl.when(jnp.logical_not(self.stay))(self.remote.start)

    def wait(self):
        pl.when(self.stay)(self.local.wait)
        pl.when(jnp.logical_not(self.stay))(self.remote.wait)


def unfold_into(left, target):
    rows = target.shape[0] // 4
    half = rows // 2
    for r in range(4):
        tile = left[r * half:(r + 1) * half, :].astype(f32)
        target[r * rows:r * rows + half, :] = jnp.concatenate([tile[:, :64], tile[:, 128:192]], axis=1).astype(bf16)
        target[r * rows + half:(r + 1) * rows, :] = jnp.concatenate([tile[:, 64:128], tile[:, 192:]], axis=1).astype(bf16)


GROUPS = (2, 1, 1)


def forward_kernel(*refs):
    lat, cot, cond, ada, bias = refs[:5]
    blocks, refs = refs[5:9], refs[9:]
    fulls, refs = refs[:4], refs[4:]
    (o_w, o_cot, o_x, o_n1, o_q, o_k, o_v, o_k2, o_v2, o_lse, o_att, o_ba, o_mid, o_n2, o_hid, o_slo, o_out, o_vec, o_act), refs = refs[:19], refs[19:]
    (x_v, n1, q_v, k_v, v_v, k2_v, v2_v, lse_v, ot, att, ba, mid, n2, hid, slo, acc, wbuf, lbuf, out_v, cot_v, vec,
     c_send, c_recv, s_send, s_recv, m_own, m_oth), refs = refs[:27], refs[27:]
    ag_sems, (swap_sems, c_sems, s_sems, m_sems, o_sems, kv_sems, w_sems, save_sems, wsave_sems) = refs[:6], refs[6:]

    place = Place()
    depth, rows_n = place.depth, 4
    row, col = place.row, place.col
    cols_n = 2 * depth
    tokens, width = x_v.shape
    hc = width // cols_n
    drows = ada.shape[0]
    q_main, p_main = 384, 128
    half = tokens // 2

    row_peers = [((row + k) % rows_n, col) for k in range(1, rows_n)]
    col_peers = [(row, (col + k) % cols_n) for k in range(1, cols_n)]
    greet(place.partners() + row_peers + col_peers + [place.diagonal()])

    def send(src, dst, s_sem, r_sem, to):
        return pltpu.make_async_remote_copy(
            src_ref=src, dst_ref=dst, send_sem=s_sem, recv_sem=r_sem, device_id=to, device_id_type=MESH)

    cond_value = cond[...]
    act = (cond_value / (1.0 + jnp.exp(-cond_value))).astype(bf16).astype(f32)
    for r in range(rows_n):
        c_send[r] = act[:, r * drows:(r + 1) * drows]

    def cond_copy(k):
        to = (row + k) % rows_n
        return send(c_send.at[to], c_recv.at[row], c_sems.at[0, k], c_sems.at[1, row], (to, col))

    def cond_got(k):
        src = (row + k) % rows_n
        return send(c_send.at[src], c_recv.at[src], c_sems.at[0, k], c_sems.at[1, src], (src, col))

    for k in range(1, rows_n):
        cond_copy(k).start()
    swap_x = Swap(place, lat, x_v, swap_sems, 0)
    swap_x.start()

    work = LineGather(place, blocks, fulls, ag_sems, range(4), (2,))
    for a in range(2):
        work.start(a)

    members, first = [], 0
    for size in GROUPS:
        members.append(list(range(first, first + size)))
        first += size
    chunks = [(g, t) for g in range(len(GROUPS)) for t in range(depth)]
    events = []
    for s in range(len(chunks) + 4):
        if s % depth == 2 and s < 2 * depth:
            events.append((s // depth + 1, "start"))
        if s in (1, 3, depth + 3):
            events.append(((s + 1) // depth, "forward"))
        events += [(s - n, n) for n in range(5) if 0 <= s - n < len(chunks)]
    at = [0]

    def pump(count):
        for s, n in events[at[0]:at[0] + count]:
            if n in ("start", "forward"):
                for a in members[s]:
                    (work.start if n == "start" else work.forward)(a)
                continue
            g, t = chunks[s]
            for a in members[g]:
                work.stage(a, t, n)
        at[0] += count

    def pump_to(s, n):
        pump(max(0, events.index((s, n)) + 1 - at[0]))

    pump_to(0, 0)
    c_recv[row] = c_send[row]
    for k in range(1, rows_n):
        cond_got(k).wait_recv()
    act_all = c_recv[...].reshape(rows_n * 8, drows).astype(bf16)
    s_send[...] = nn(act_all, ada[...]).reshape(rows_n, 8, 6 * hc)

    def sum_copy(k):
        to = (row + k) % rows_n
        return send(s_send.at[to], s_recv.at[row], s_sems.at[0, k], s_sems.at[1, row], (to, col))

    def sum_got(k):
        src = (row + k) % rows_n
        return send(s_send.at[src], s_recv.at[src], s_sems.at[0, k], s_sems.at[1, src], (src, col))

    for k in range(1, rows_n):
        sum_copy(k).start()
    pump_to(0, 1)
    s_recv[row] = s_send[row]
    for k in range(1, rows_n):
        sum_got(k).wait_recv()
    m_own[col] = s_recv[0] + s_recv[1] + s_recv[2] + s_recv[3] + bias[...]

    def mod_copy(k):
        return send(m_own.at[col], m_own.at[col], m_sems.at[0, k], m_sems.at[1, col], (row, (col + k) % cols_n))

    def mod_got(k):
        src = (col + k) % cols_n
        return send(m_own.at[src], m_own.at[src], m_sems.at[0, k], m_sems.at[1, src], (row, src))

    for k in range(1, cols_n):
        mod_copy(k).start()
    pump_to(0, 2)
    for k in range(1, cols_n):
        mod_got(k).wait_recv()
    other = send(m_own, m_oth, o_sems.at[0], o_sems.at[1], place.to_core)
    other.start()
    pump_to(0, 3)
    other.wait_recv()
    stay = place.h == place.x
    for c in range(cols_n):
        line = jnp.where(stay, m_own[c, pl.ds(place.z, 1), :], m_oth[c, pl.ds(place.z, 1), :])
        for k in range(6):
            vec[k:k + 1, c * hc:(c + 1) * hc] = line[:, k * hc:(k + 1) * hc]
        line = m_own[c, 4:5, :]
        vec[6:7, c * hc:(c + 1) * hc] = line[:, 576:576 + hc]
        vec[7:8, c * hc:(c + 1) * hc] = line[:, 576 + hc:]
        z, i = c // 2, c % 2
        vec[16 + z:17 + z, i * 512:(i + 1) * 512] = line[:, :512]
        vec[16 + z:17 + z, 1024 + i * 64:1024 + (i + 1) * 64] = line[:, 512:576]

    swap_x.wait()
    swap_dy = Swap(place, cot, o_cot, swap_sems, 1)
    swap_dy.start()
    part = 128

    def row_parts(body):
        @pl.loop(0, tokens // part)
        def _(i):
            body(pl.ds(pl.multiple_of(i * part, part), part))

    def first_norm(at_rows):
        normal, _ = norm_rows(x_v[at_rows, :].astype(f32))
        n1[at_rows, :] = (normal * (1.0 + vec[1:2, :]) + vec[0:1, :]).astype(bf16)

    row_parts(first_norm)

    saves = []

    def save(src, dst):
        copy = pltpu.make_async_copy(src, dst, save_sems.at[len(saves)])
        copy.start()
        saves.append(copy)

    save(x_v, o_x)
    save(n1, o_n1)
    save(c_recv, o_act)

    def fetch(s):
        g, t = chunks[s]
        zc, slot = work.zc(t), s % depth
        main = fulls[members[g][0]]
        if g == 0:
            cuts = [(512 * i, q_main, q_main * i) for i in range(2)] + [(512 * i + q_main, p_main, 2 * q_main + p_main * i) for i in range(2)]
        else:
            cuts = [(256 * i, 256, 256 * i) for i in range(4)]
        copies = []
        for n, (spot, size, to) in enumerate(cuts):
            src = main.at[:, pl.ds(pl.multiple_of(zc * 1024 + spot, 128), size)]
            copies.append(pltpu.make_async_copy(src, wbuf.at[slot, :, to:to + size], w_sems.at[s % 2, n]))
        for i in range(2):
            src = fulls[1].at[:, pl.ds(pl.multiple_of(zc * 768 + 384 * i + 128 * g, 128), 128)]
            copies.append(pltpu.make_async_copy(src, lbuf.at[s % 2, :, 128 * i:128 * (i + 1)], w_sems.at[s % 2, 4 + i]))
        return copies

    def fetch_start(s):
        pump_to(s, 4)
        if s >= depth:
            weight_save(s - depth).wait()
        for copy in fetch(s):
            copy.start()

    def fetch_wait(s):
        for copy in fetch(s):
            copy.wait()
        unfold_into(lbuf.at[s % 2], wbuf.at[s % depth, :, 1024:1152])
        weight_save(s).start()

    def weight_save(s):
        g, t = chunks[s]
        return pltpu.make_async_copy(wbuf.at[s % depth], o_w.at[g, work.zc(t)], wsave_sems.at[s])

    def swap_kv(i, h):
        src, dst = ((k_v, k2_v), (v_v, v2_v))[i]
        return send(src.at[h], dst.at[h], kv_sems.at[0, i, h], kv_sems.at[1, i, h], place.to_core)

    def project(s):
        t, slot = chunks[s][1], s % depth
        zc = work.zc(t)

        @pl.loop(0, 2)
        def _(i):
            at_rows = pl.ds(pl.multiple_of(i * half, half), half)
            main = nn(n1[at_rows, :], wbuf[slot, :, :2 * q_main])
            left = nn(n1[at_rows, :], wbuf[slot, :, 1024:1152])
            for j in range(2):
                biases = m_own[2 * zc + j]
                own = main[:, j * q_main:(j + 1) * q_main]
                tail = left[:, j * 64:j * 64 + 3 * hc - q_main]
                for e in range(2):
                    h = 4 * zc + 2 * j + e
                    a = e * HEAD_DIM
                    q_v[h, at_rows, :] = (own[:, a:a + HEAD_DIM] + biases[5:6, a:a + HEAD_DIM]).astype(bf16)
                    k_v[h, at_rows, :] = own[:, hc + a:hc + a + HEAD_DIM].astype(bf16)
                    if e == 0:
                        value = own[:, 2 * hc:2 * hc + HEAD_DIM]
                    else:
                        value = jnp.concatenate([own[:, 2 * hc + HEAD_DIM:], tail], axis=1)
                    v_v[h, at_rows, :] = (value + biases[5:6, hc + a:hc + a + HEAD_DIM]).astype(bf16)

        for i in range(4):
            swap_kv(0, 4 * zc + i).start()
            swap_kv(1, 4 * zc + i).start()

    def attention(s):
        zc = work.zc(chunks[s][1])
        start = at[0]

        @pl.loop(0, 4)
        def _(i):
            h = 4 * zc + i
            swap_kv(0, h).wait_recv()
            swap_kv(1, h).wait_recv()
            one, two, total, lse = softmax_head(q_v[h], k_v[h], k2_v[h])
            ot[i] = (tn(v_v[h], one) + tn(v2_v[h], two)) / total
            lse_v[h] = lse
            for k in range(4):
                at[0] = start + k

                @pl.when(i == k)
                def _():
                    pump(1)

        at[0] = start + 4
        att[zc, :, 2 * p_main:] = jnp.zeros((tokens, 128), bf16)
        for j in range(2):
            pair = jnp.concatenate([ot[2 * j], ot[2 * j + 1]], axis=0).T.astype(bf16)
            att[zc, :, j * p_main:(j + 1) * p_main] = pair[:, :p_main]
            att[zc, :, 2 * p_main + 64 * j + 48:2 * p_main + 64 * j + 64] = pair[:, p_main:]

        @pl.loop(0, 2)
        def _(i):
            at_rows = pl.ds(pl.multiple_of(i * half, half), half)
            term = nt(att[zc, at_rows, :], wbuf[s % depth, :, 2 * q_main:])
            if s == 0:
                acc[at_rows, :] = term
            else:
                acc[at_rows, :] += term

    fetch_start(0)
    for s in range(depth):
        fetch_wait(s)
        project(s)
        fetch_start(s + 1)
        if s > 0:
            attention(s - 1)
    attention(depth - 1)
    for src, dst in ((q_v, o_q), (k_v, o_k), (v_v, o_v), (k2_v, o_k2), (v2_v, o_v2), (lse_v, o_lse), (att, o_att)):
        save(src, dst)

    def second_norm(at_rows):
        branch = acc[at_rows, :] + vec[6:7, :]
        ba[at_rows, :] = branch.astype(bf16)
        middle = x_v[at_rows, :].astype(f32) + vec[2:3, :] * branch
        mid[at_rows, :] = middle
        normal, _ = norm_rows(middle)
        n2[at_rows, :] = (normal * (1.0 + vec[4:5, :]) + vec[3:4, :]).astype(bf16)

    row_parts(second_norm)
    for src, dst in ((ba, o_ba), (mid, o_mid), (n2, o_n2)):
        save(src, dst)

    for s in range(depth, 2 * depth):
        fetch_wait(s)
        fetch_start(s + 1)
        zc = work.zc(chunks[s][1])

        def up(at_rows):
            u = nn(n2[at_rows, :], wbuf[s % depth]) + vec[pl.ds(16 + zc, 1), :]
            value, slope = gelu_both(u)
            hid[zc, at_rows, :] = value.astype(bf16)
            slo[zc, at_rows, :] = slope.astype(bf16)

        row_parts(up)
    save(hid, o_hid)
    save(slo, o_slo)
    for s in range(2 * depth, 3 * depth):
        fetch_wait(s)
        if s + 1 < 3 * depth:
            fetch_start(s + 1)
        zc = work.zc(chunks[s][1])

        def down(at_rows):
            term = nt(hid[zc, at_rows, :], wbuf[s % depth])
            if s == 2 * depth:
                acc[at_rows, :] = term
            else:
                acc[at_rows, :] += term

        row_parts(down)

    swap_dy.wait()
    load_dy = pltpu.make_async_copy(o_cot, cot_v, w_sems.at[0, 0])
    load_dy.start()
    load_dy.wait()
    vec[8:9, :] = jnp.zeros((1, width), f32)

    def finish(at_rows):
        branch = acc[at_rows, :] + vec[7:8, :]
        out_v[at_rows, :] = (mid[at_rows, :] + vec[5:6, :] * branch).astype(bf16)
        vec[8:9, :] += jnp.sum(cot_v[at_rows, :].astype(f32) * branch, axis=0, keepdims=True)

    row_parts(finish)
    save(out_v, o_out)
    save(vec, o_vec)

    for a in range(4):
        work.finish(a)
    for k in range(1, rows_n):
        cond_copy(k).wait_send()
        sum_copy(k).wait_send()
    for k in range(1, cols_n):
        mod_copy(k).wait_send()
    other.wait_send()

    @pl.loop(0, 4 * depth)
    def _(h):
        swap_kv(0, h).wait_send()
        swap_kv(1, h).wait_send()

    for s in range(2 * depth, 3 * depth):
        weight_save(s).wait()
    for copy in saves:
        copy.wait()


def forward(lat, cot, cond, ada, bias, blocks, collective_id):
    rows, cols = lax.axis_size("row"), lax.axis_size("col")
    depth = cols // 2
    tokens, width = lat.shape
    heads = width // HEAD_DIM
    lanes = 1152
    hc6 = ada.shape[1]
    shape = jax.ShapeDtypeStruct
    head = shape((heads, tokens, HEAD_DIM), bf16)
    token = shape((tokens, width), bf16)
    outs = [shape((rows * b.shape[0], cols * b.shape[1]), bf16) for b in blocks] + [
        shape((3, depth, width, lanes), bf16), token, token, token, head, head, head, head, head,
        shape((heads, 1, tokens), f32), shape((depth, tokens, 384), bf16), token, shape((tokens, width), f32), token,
        shape((depth, tokens, lanes), bf16), shape((depth, tokens, lanes), bf16), token, shape((VECS, width), f32), shape((rows, 8, ada.shape[0]), f32)]
    dma, vm = pltpu.SemaphoreType.DMA, pltpu.VMEM
    t16, h16 = vm((tokens, width), bf16), vm((heads, tokens, HEAD_DIM), bf16)
    drows = ada.shape[0]
    scratch = [
        t16, t16, h16, h16, h16, h16, h16, vm((heads, 1, tokens), f32), vm((4, HEAD_DIM, tokens), f32),
        vm((depth, tokens, 384), bf16), t16, vm((tokens, width), f32), t16, vm((depth, tokens, lanes), bf16),
        vm((depth, tokens, lanes), bf16), vm((tokens, width), f32), vm((depth, width, lanes), bf16), vm((2, width // 2, 256), bf16),
        t16, t16, vm((VECS, width), f32), vm((rows, 8, drows), f32), vm((rows, 8, drows), f32), vm((rows, 8, hc6), f32),
        vm((rows, 8, hc6), f32), vm((cols, 8, hc6), f32), vm((cols, 8, hc6), f32)]
    scratch += LineGather.scratch(len(blocks), depth)
    scratch += [dma((2, 2)), dma((2, rows)), dma((2, rows)), dma((2, cols)), dma((2,)), dma((2, 2, heads)), dma((2, 6)), dma((32,)),
                dma((3 * depth,))]
    vmem = pl.BlockSpec(memory_space=pltpu.VMEM)
    got = pl.pallas_call(
        forward_kernel,
        out_shape=outs,
        in_specs=[ANY, ANY, vmem, vmem, vmem] + [ANY] * len(blocks),
        out_specs=[ANY] * len(outs),
        scratch_shapes=scratch,
        compiler_params=pltpu.CompilerParams(collective_id=collective_id, has_side_effects=True, vmem_limit_bytes=62 * 2**20),
        name="forward",
    )(lat, cot, cond, ada, bias, *blocks)
    return got[len(blocks):]


SLOTS = 4


def backward_kernel(*refs):
    (w, dy_h, x_h, n1_h, q_h, k_h, v_h, k2_h, v2_h, att_h, ba_h, mid_h, n2_h, hid_h, slo_h, out_h), refs = refs[:16], refs[16:]
    (lse, vec, act, ada, cond), refs = refs[:5], refs[5:]
    (o_out, o_lat, o_pq, o_fc2, o_fc1, o_qkv, o_proj, o_ada, o_rows, o_cond), refs = refs[:10], refs[10:]
    (acc, give, r0, r1, r1l, r2, r2l, r3, r3l, lf, lx), refs = refs[:11], refs[11:]
    (wbuf, hs, pre, pq, turn, tmp, ml, gm, gx, att, heads, grad_o, delta, kv_give, kv_got, own, gv, att_w), refs = refs[:18], refs[18:]
    (tt, tc, um, vm_, modl, cp, cr, cf), refs = refs[:8], refs[8:]
    (swap_sems, s0, s1, s2, s3, lx_sems, w_sems, hs_sems, slo_sems, tmp_sems, head_sems, kv_sems, pq_sems, t_sems, u_sems, v_sems, cr_sems, cf_sems, att_sems) = refs

    place = Place()
    depth, rows_n = place.depth, 4
    row, col, h = place.row, place.col, place.h
    cols_n = 2 * depth
    tokens, width = ml.shape
    hc = width // cols_n
    drows = ada.shape[0]
    lrows = drows // 2
    half, part = tokens // 2, 128
    q_main, p_main = 384, 128
    scale = HEAD_DIM ** (-0.5)
    row_peers = [((row + k) % rows_n, col) for k in range(1, rows_n)]
    col_peers = [(row, (col + k) % cols_n) for k in range(1, cols_n)]
    flip_x, flip_y = (row, col + 1 - 2 * place.x), (row + 2 - 4 * place.y, col)
    greet(place.partners() + row_peers + col_peers + [place.diagonal()])

    def send(src, dst, s_sem, r_sem, to):
        return pltpu.make_async_remote_copy(
            src_ref=src, dst_ref=dst, send_sem=s_sem, recv_sem=r_sem, device_id=to, device_id_type=MESH)

    def row_parts(body):
        @pl.loop(0, tokens // part)
        def _(i):
            body(pl.ds(pl.multiple_of(i * part, part), part))

    def row_halves(body):
        @pl.loop(0, 2)
        def _(i):
            body(pl.ds(pl.multiple_of(i * half, half), half))

    low = place.z < 2
    middle = jnp.logical_and(place.z > 0, place.z < depth - 1)
    inner = place.to_z(jnp.where(low, place.z + 1, place.z - 1))
    outer = place.to_z(jnp.where(low, jnp.maximum(place.z - 1, 0), jnp.minimum(place.z + 1, depth - 1)))
    far = [jnp.where(low, 3, 0), jnp.where(low, 2, 1), place.z + 1 - 2 * (place.z % 2), place.z]

    def zc(t):
        return far[t]

    def load(src, i):
        copy = pltpu.make_async_copy(src, tmp.at[i], tmp_sems.at[i])
        copy.start()
        return copy

    def weight_load(u):
        return pltpu.make_async_copy(w.at[2 - u // depth, zc(u % depth)], wbuf.at[u % 2], w_sems.at[u % 2])

    def slope_load(u):
        return pltpu.make_async_copy(slo_h.at[zc(u)], pre.at[zc(u)], slo_sems.at[u])

    def weight_use(u):
        weight_load(u).wait()
        if u + 1 < 3 * depth:
            weight_load(u + 1).start()


    def tick_loads(s):
        g, t = s // depth, s % depth
        if g == 0:
            return [pltpu.make_async_copy(hid_h.at[zc(t)], hs.at[s % 2], hs_sems.at[s % 2, 0])]
        if g == 1:
            return []
        return [pltpu.make_async_copy(o_pq.at[zc(t)], hs.at[s % 2, :, :896], hs_sems.at[s % 2, 0]),
                pltpu.make_async_copy(att_h.at[zc(t)], att_w.at[s % 2], hs_sems.at[s % 2, 1])]

    def tick_prefetch(s):
        if s < 3 * depth:
            if s // depth == 2:
                pq_wait(s % depth)
            for copy in tick_loads(s):
                copy.start()

    saved = set()

    def pq_wait(t):
        if t not in saved:
            saved.add(t)
            pq_save(t).wait()

    def pq_save(t):
        return pltpu.make_async_copy(pq, o_pq.at[zc(t)], pq_sems.at[t])

    def c0(s, y):
        return send(give.at[s % 2, y], r0.at[s % 2, y], s0.at[0, s % 2, y], s0.at[1, s % 2, y], place.to_core)

    def spots(s, y, x):
        return (acc.at[s % SLOTS, y, :, pl.ds(pl.multiple_of(x * 512, 512), 512)],
                acc.at[s % SLOTS, y, pl.ds(pl.multiple_of(x * lrows, 16), lrows), 1024:1152])

    def c1(s, j):
        main, left = spots(s, *place.yx(1 - place.p, j))
        k = s % 4
        return [send(main, r1.at[k, j], s1.at[0, k, j, 0], s1.at[1, k, j, 0], place.to_p),
                send(left, r1l.at[k, j], s1.at[0, k, j, 1], s1.at[1, k, j, 1], place.to_p)]

    zq = h == 0
    qz = jnp.logical_not(zq)

    def c2(s):
        main, left = spots(s, *place.yx(place.p, 1 - place.q))
        k = jnp.where(zq, s // depth, s % 4) if s % depth == depth - 1 else s % 4
        return [send(main, r2.at[k], s2.at[0, k, 0], s2.at[1, k, 0], place.to_q),
                send(left, r2l.at[k], s2.at[0, k, 1], s2.at[1, k, 1], place.to_q)]

    def z_copy(s, j, inward, slot):
        g, t = s // depth, s % depth
        main, left = spots(s, *place.yx(place.p, place.q if j == 0 else 1 - place.q))
        to = inner if inward else outer
        return [send(main, r3.at[j, slot], s3.at[0, j, g, t, 0], s3.at[1, j, slot, 0, 0], to),
                send(left, r3l.at[j, slot], s3.at[0, j, g, t, 1], s3.at[1, j, slot, 0, 1], to)]

    def z_stage(s, j, inside):
        g, t = s // depth, s % depth
        par = g % 2
        if t == depth - 1:
            return
        if inside:
            slot = (par, 2, 3 + par)[t]
            for copy in z_copy(s, j, True, slot):
                copy.wait_recv()
            for into, other in zip(spots(s, *place.yx(place.p, place.q if j == 0 else 1 - place.q)), (r3.at[j, slot], r3l.at[j, slot])):
                add_into(into, other)
            copies = z_copy(s, j, t < 2, (3 + par, 5 + par, 5 + par)[t])
        else:
            copies = z_copy(s, j, True, (par, 2, 7 + par)[t])
        for copy in copies:
            copy.start()

    def z_stages(s, twice, inside):
        where = jnp.logical_and(zq if twice else qz, middle if inside else jnp.logical_not(middle))

        @pl.when(where)
        def _():
            z_stage(s, 0, inside)
            if twice:
                z_stage(s, 1, inside)

    def z_got(g, j):
        par = g % 2
        last = (g + 1) * depth - 1
        for copy in z_copy(last, j, True, 5 + par):
            copy.wait_recv()

        @pl.when(middle)
        def _():
            for copy in z_copy(last, j, True, 7 + par):
                copy.wait_recv()

    def z_sum(g, j, value, refs, index):
        par = g % 2
        value = value + refs[(j, 5 + par) + index].astype(f32)
        return jnp.where(middle, value + refs[(j, 7 + par) + index].astype(f32), value)

    def sent(s):
        for j in range(2):
            for copy in c1(s, j):
                copy.wait_send()
        if s % depth < depth - 1:
            for copy in z_copy(s, 0, True, 0):
                copy.wait_send()

            @pl.when(zq)
            def _():
                for copy in z_copy(s, 1, True, 0):
                    copy.wait_send()

            @pl.when(qz)
            def _():
                for copy in c2(s):
                    copy.wait_send()
        else:
            for copy in c2(s):
                copy.wait_send()

    def add_into(into, other):
        n = into.shape[0]

        @pl.loop(0, n // 48)
        def _(i):
            at_rows = pl.ds(pl.multiple_of(i * 48, 16), 48)
            into[at_rows, :] = into[at_rows, :] + other[at_rows, :]

    def tick_a(s):
        g, t = s // depth, s % depth
        k = s % SLOTS
        if s >= SLOTS:
            sent(s - SLOTS)
        if s >= 2:
            for y in range(2):
                c0(s - 2, y).wait_send()
        for copy in tick_loads(s):
            copy.wait()

        def rows_of(r):
            at_rows = pl.ds(pl.multiple_of(r * drows, 16), drows)
            if g == 0:
                return nn(turn[0, at_rows, :], hs[s % 2]).astype(bf16)
            if g == 1:
                return nn(turn[0, at_rows, :], pre[zc(t)]).astype(bf16)
            one = nn(turn[1, at_rows, :], hs[s % 2, :, :896])
            two = nn(turn[0, at_rows, :], att_w[s % 2])
            return jnp.concatenate(
                [one[:, :q_main], two[:, :p_main], one[:, q_main:2 * q_main], two[:, p_main:2 * p_main],
                 one[:, 2 * q_main:] + two[:, 2 * p_main:]], axis=1).astype(bf16)

        @pl.loop(0, 2)
        def _(y):
            give[s % 2, y] = rows_of(2 * y + 1 - h)
            acc[k, y] = rows_of(2 * y + h)

        for y in range(2):
            c0(s, y).start()
        if s + 1 < 3 * depth - 1:
            tick_prefetch(s + 1)

    def tick_b(s):
        if s < 3 * depth:
            for y in range(2):
                c0(s, y).wait_recv()
            for y in range(2):
                add_into(acc.at[s % SLOTS, y], r0.at[s % 2, y])
            for j in range(2):
                for copy in c1(s, j):
                    copy.start()
        if 0 <= s - 1 < 3 * depth:
            n = s - 1
            for j in range(2):
                for copy in c1(n, j):
                    copy.wait_recv()
            for into, other in zip(spots(n, *place.yx(place.p, 1 - place.q)), (r1.at[n % 4, 1 - place.q], r1l.at[n % 4, 1 - place.q])):
                add_into(into, other)

            @pl.when(qz)
            def _():
                for copy in c2(n):
                    copy.start()

            for into, other in zip(spots(n, *place.yx(place.p, place.q)), (r1.at[n % 4, place.q], r1l.at[n % 4, place.q])):
                add_into(into, other)
            z_stages(n, True, False)
        if 0 <= s - 2 < 3 * depth:
            n = s - 2

            @pl.when(qz)
            def _():
                for copy in c2(n):
                    copy.wait_recv()
                for into, other in zip(spots(n, *place.yx(place.p, place.q)), (r2.at[n % 4], r2l.at[n % 4])):
                    add_into(into, other)

            z_stages(n, False, False)
            z_stages(n, True, True)
            if n % depth == depth - 1:
                pl.when(zq)(lambda: hand_over(n))
        if 0 <= s - 3 < 3 * depth:
            z_stages(s - 3, False, True)
            if (s - 3) % depth == depth - 1:
                total((s - 3) // depth)

    def hand_over(n):
        g = n // depth
        z_got(g, 1)
        main, left = spots(n, *place.yx(place.p, 1 - place.q))

        @pl.loop(0, drows // 48)
        def _(i):
            at_rows = pl.ds(pl.multiple_of(i * 48, 16), 48)
            main[at_rows, :] = z_sum(g, 1, main[at_rows, :].astype(f32), r3, (at_rows,)).astype(bf16)

        left[...] = z_sum(g, 1, left[...].astype(f32), r3l, ()).astype(bf16)
        for copy in c2(n):
            copy.start()

    def left_copy(g):
        return send(lf.at[g], lx.at[g], lx_sems.at[0, g], lx_sems.at[1, g], flip_x)

    def total(g):
        last = (g + 1) * depth - 1
        z_got(g, 0)
        main, left = spots(last, *place.yx(place.p, place.q))

        def write(handed):
            if handed:
                for copy in c2(last):
                    copy.wait_recv()

            @pl.loop(0, drows // 48)
            def _(i):
                at_rows = pl.ds(pl.multiple_of(i * 48, 16), 48)
                value = z_sum(g, 0, main[at_rows, :].astype(f32), r3, (at_rows,))
                if handed:
                    value = value + r2[g, at_rows, :].astype(f32)
                if g == 0:
                    o_fc2[at_rows, :512] = value
                elif g == 1:
                    o_fc1[at_rows, :512] = value
                else:
                    o_qkv[at_rows, :q_main] = value[:, :q_main]
                    o_proj[at_rows, :p_main] = value[:, q_main:]

            value = z_sum(g, 0, left[...].astype(f32), r3l, ())
            lf[g] = value + r2l[g].astype(f32) if handed else value

        pl.when(zq)(lambda: write(True))
        pl.when(qz)(lambda: write(False))
        left_copy(g).start()

    def left_finish(g):
        left_copy(g).wait_recv()
        first = place.x == 0
        top = jnp.where(first, lf[g][:, :64], lx[g][:, 64:])
        bottom = jnp.where(first, lx[g][:, :64], lf[g][:, 64:])
        tail = 3 * hc - q_main
        for spot, value in ((0, top), (lrows, bottom)):
            if g == 0:
                o_fc2[spot:spot + lrows, 512:] = value
            elif g == 1:
                o_fc1[spot:spot + lrows, 512:] = value
            else:
                o_qkv[spot:spot + lrows, q_main:] = value[:, :tail]
                o_proj[spot:spot + lrows, p_main:] = value[:, tail:]

    def turn_into(i, src):
        @pl.loop(0, width // 128)
        def _(n):
            spot = pl.ds(pl.multiple_of(n * 128, 128), 128)
            turn[i, spot, :] = src[:, spot].T

    swap_out = Swap(place, out_h, o_out, swap_sems, 0)
    load_dy = load(dy_h, 0)
    weight_load(0).start()
    for u in range(depth):
        slope_load(u).start()
    tick_prefetch(0)
    swap_out.start()
    gv[...] = jnp.zeros_like(gv)
    tt[...] = jnp.zeros_like(tt)
    gv[5:6, :] = vec[8:9, :]
    load_dy.wait()

    def first(at_rows):
        grad = tmp[0, at_rows, :].astype(f32) * vec[5:6, :]
        gv[7:8, :] += jnp.sum(grad, axis=0, keepdims=True)
        ml[at_rows, :] = grad.astype(bf16)

    row_parts(first)
    turn_into(0, ml)

    def hidden_back(u):
        z = zc(u)
        weight_use(u)
        slope_load(u).wait()
        sums = gv.at[8:9, :]
        sums[...] = jnp.zeros((1, width), f32)

        def body(at_rows):
            grad = nn(ml[at_rows, :], wbuf[u % 2]) * pre[z, at_rows, :].astype(f32)
            sums[...] += jnp.sum(grad, axis=0, keepdims=True)
            pre[z, at_rows, :] = grad.astype(bf16)

        row_parts(body)
        for j in range(2):
            tt[2 * z + j, 1:2, :512] = sums[:, 512 * j:512 * (j + 1)]
            tt[2 * z + j, 1:2, 512:576] = sums[:, 1024 + 64 * j:1024 + 64 * (j + 1)]

    def normed_back(u):
        z = zc(u % depth)
        weight_use(u)

        def body(at_rows):
            term = nt(pre[z, at_rows, :], wbuf[u % 2])
            if u == depth:
                gx[at_rows, :] = term
            else:
                gx[at_rows, :] += term

        row_parts(body)

    tick_a(0)
    hidden_back(0)
    tick_b(0)
    hidden_back(1)
    hidden_back(2)
    hidden_back(3)
    tick_a(1)
    normed_back(depth)
    tick_b(1)
    normed_back(depth + 1)
    normed_back(depth + 2)
    tick_a(2)
    normed_back(depth + 3)
    tick_b(2)

    load_mid = pltpu.make_async_copy(mid_h, gm, tmp_sems.at[2])
    load_mid.start()
    load_ba, load_dy = load(ba_h, 1), load(dy_h, 0)
    load_mid.wait()
    load_ba.wait()
    load_dy.wait()

    def norm_grad(values, grads, shift_row, scale_row, scale_vec):
        normal, inverse = norm_rows(values)
        gv[shift_row:shift_row + 1, :] += jnp.sum(grads, axis=0, keepdims=True)
        gv[scale_row:scale_row + 1, :] += jnp.sum(grads * normal, axis=0, keepdims=True)
        inner = grads * (1.0 + scale_vec)
        one = jnp.mean(inner, axis=-1, keepdims=True)
        two = jnp.mean(inner * normal, axis=-1, keepdims=True)
        return inverse * (inner - one - normal * two)

    def second(at_rows):
        grad = norm_grad(gm[at_rows, :], gx[at_rows, :], 3, 4, vec[4:5, :]) + tmp[0, at_rows, :].astype(f32)
        gm[at_rows, :] = grad
        gv[2:3, :] += jnp.sum(grad * tmp[1, at_rows, :].astype(f32), axis=0, keepdims=True)
        grad = grad * vec[2:3, :]
        gv[6:7, :] += jnp.sum(grad, axis=0, keepdims=True)
        ml[at_rows, :] = grad.astype(bf16)

    row_parts(second)

    def heads_load(t):
        spot = pl.ds(4 * zc(t), 4)
        return [pltpu.make_async_copy(src.at[spot], heads.at[i], head_sems.at[i])
                for i, src in enumerate((q_h, k_h, v_h, k2_h, v2_h))]

    def att_load(t):
        return pltpu.make_async_copy(att_h.at[zc(t)], att, att_sems.at[0])

    def kv_swap(t, kind, i):
        return send(kv_give.at[kind, i], kv_got.at[t % 2, kind, i], kv_sems.at[0, 0, kind, i], kv_sems.at[1, t % 2, kind, i], place.to_core)

    def pair_of(value, j):
        spot = 2 * p_main + 64 * j + 48
        return jnp.concatenate([value[:, j * p_main:(j + 1) * p_main], value[:, spot:spot + 16]], axis=1)

    def attention_open(t):
        u = 2 * depth + t
        weight_use(u)
        att_load(t).wait()

        def body(at_rows):
            grads = nn(ml[at_rows, :], wbuf[u % 2, :, 2 * q_main:])
            results = att[at_rows, :].astype(f32)
            for j in range(2):
                grad = pair_of(grads, j).astype(bf16)
                product = (grad.astype(f32) * pair_of(results, j)).T
                for e in range(2):
                    grad_o[2 * j + e, at_rows, :] = grad[:, e * HEAD_DIM:(e + 1) * HEAD_DIM]
                    delta[2 * j + e, :, at_rows] = jnp.sum(product[e * HEAD_DIM:(e + 1) * HEAD_DIM, :], axis=0, keepdims=True)

        row_halves(body)
        for copy in heads_load(t):
            copy.wait()

    def attention_heads(t, between):
        @pl.loop(0, 4)
        def _(i):
            q, out_grad, shift, less = heads[0, i], grad_o[i], lse[4 * zc(t) + i], delta[i]

            def side(k, v):
                probs = jnp.exp2(nt(k, q) * SOFT - shift)
                grad = (probs * (nt(v, out_grad) - less)).astype(bf16)
                return nn(grad, q) * scale, nn(probs.astype(bf16), out_grad), tn(k, grad)

            dk, dv, dq_two = side(heads[3, i], heads[4, i])
            kv_give[0, i] = dk.astype(bf16)
            kv_give[1, i] = dv.astype(bf16)
            kv_swap(t, 0, i).start()
            kv_swap(t, 1, i).start()
            dk, dv, dq_one = side(heads[1, i], heads[2, i])
            own[1, i] = dk
            own[2, i] = dv
            own[0, i] = ((dq_one + dq_two) * scale).T
            for n, action in between:
                pl.when(i == n)(action)

    def attention_close(t):
        u = 2 * depth + t
        z = zc(t)
        if t + 1 < depth:
            for copy in heads_load(t + 1):
                copy.start()
            att_load(t + 1).start()
        for kind in range(2):
            for i in range(4):
                kv_swap(t, kind, i).wait()
        if t > 0:
            pq_wait(t - 1)

        def body(at_rows):
            for j in range(2):
                pieces, tails = [[], [], []], None
                for e in range(2):
                    i = 2 * j + e
                    dq = own[0, i, at_rows, :]
                    dk = own[1, i, at_rows, :] + kv_got[t % 2, 0, i, at_rows, :].astype(f32)
                    dv = own[2, i, at_rows, :] + kv_got[t % 2, 1, i, at_rows, :].astype(f32)
                    tt[2 * z + j, 2:3, e * HEAD_DIM:(e + 1) * HEAD_DIM] += jnp.sum(dq, axis=0, keepdims=True)
                    tt[2 * z + j, 2:3, hc + e * HEAD_DIM:hc + (e + 1) * HEAD_DIM] += jnp.sum(dv, axis=0, keepdims=True)
                    for n, value in enumerate((dq, dk, dv)):
                        pieces[n].append(value)
                last = pieces[2][1]
                cut = q_main - 2 * hc - HEAD_DIM
                line = pieces[0] + pieces[1] + [pieces[2][0], last[:, :cut]]
                pq[at_rows, j * q_main:(j + 1) * q_main] = jnp.concatenate(line, axis=1).astype(bf16)
                rest = jnp.concatenate([last[:, cut:], jnp.zeros((last.shape[0], 64 - HEAD_DIM + cut), f32)], axis=1)
                pq[at_rows, 2 * q_main + 64 * j:2 * q_main + 64 * (j + 1)] = rest.astype(bf16)
            term = nt(pq[at_rows, :2 * q_main], wbuf[u % 2, :, :2 * q_main]) + nt(pq[at_rows, 2 * q_main:], wbuf[u % 2, :, 1024:])
            if t == 0:
                gx[at_rows, :] = term
            else:
                gx[at_rows, :] += term

        row_halves(body)
        pq_save(t).start()

    for copy in heads_load(0):
        copy.start()
    att_load(0).start()
    load_n2 = load(n2_h, 0)
    tick_a(3)
    load_n2.wait()
    turn_into(0, tmp.at[0])
    load_x, load_n1 = load(x_h, 0), load(n1_h, 1)
    attention_open(0)
    tick_b(3)
    attention_heads(0, [(2, lambda: tick_a(4))])
    tick_b(4)
    attention_close(0)
    attention_open(1)
    tick_a(5)
    attention_heads(1, [(1, lambda: tick_b(5)), (3, lambda: tick_a(6))])
    attention_close(1)
    tick_b(6)
    tick_a(7)
    load_n1.wait()
    turn_into(1, tmp.at[1])
    turn_into(0, ml)
    attention_open(2)
    attention_heads(2, [(1, lambda: tick_b(7)), (3, lambda: tick_a(8))])
    attention_close(2)
    tick_b(8)
    attention_open(3)
    tick_a(9)
    attention_heads(3, [(1, lambda: tick_b(9)), (2, lambda: tick_a(10))])
    tick_b(10)
    attention_close(3)
    tick_prefetch(11)
    tick_a(11)
    load_x.wait()

    def third(at_rows):
        grad = norm_grad(tmp[0, at_rows, :].astype(f32), gx[at_rows, :], 0, 1, vec[1:2, :]) + gm[at_rows, :]
        tmp[1, at_rows, :] = grad.astype(bf16)

    def swap_lat(i):
        at_rows = pl.ds(pl.multiple_of(i * part, part), part)
        return Swap(place, tmp.at[1, at_rows], o_lat.at[at_rows], swap_sems, 1 + i)

    @pl.loop(0, tokens // part)
    def _(i):
        third(pl.ds(pl.multiple_of(i * part, part), part))
        swap_lat(i).start()


    for c in range(cols_n):
        spot = slice(c * hc, (c + 1) * hc)
        for k in range(6):
            tt[c, 0:1, k * hc:(k + 1) * hc] = gv[k:k + 1, spot]
        tt[c, 1:2, 576:576 + hc] = gv[6:7, spot]
        tt[c, 1:2, 576 + hc:] = gv[7:8, spot]
    copy_t = send(tt, tc, t_sems.at[0], t_sems.at[1], place.to_core)
    copy_t.start()
    tick_b(11)
    copy_t.wait()
    tt[...] = tt[...] + tc[...]

    def u_copy(k):
        to = (col + k) % cols_n
        return send(tt.at[to], um.at[col], u_sems.at[0, k], u_sems.at[1, col], (row, to))

    def u_got(k):
        src = (col + k) % cols_n
        return send(tt.at[src], um.at[src], u_sems.at[0, k], u_sems.at[1, src], (row, src))

    for k in range(1, cols_n):
        u_copy(k).start()
    um[col] = tt[col]
    tick_b(12)
    for k in range(1, cols_n):
        u_got(k).wait_recv()
    copy_v = send(um, vm_, v_sems.at[0], v_sems.at[1], flip_y)
    copy_v.start()
    tick_b(13)
    copy_v.wait_recv()
    modl[...] = jnp.zeros_like(modl)
    sums = um[0] + vm_[0]
    for c in range(1, cols_n):
        sums = sums + um[c] + vm_[c]
    o_rows[...] = sums
    for c in range(cols_n):
        modl[2 * place.y + c % 2, c // 2:c // 2 + 1, :] = um[c, 0:1, :]
        modl[2 - 2 * place.y + c % 2, c // 2:c // 2 + 1, :] = vm_[c, 0:1, :]
    low = modl[...].reshape(rows_n * 8, 6 * hc).astype(bf16)
    o_ada[...] = tn(act[...].reshape(rows_n * 8, drows).astype(bf16), low)
    cp[...] = nt(low, ada[...]).reshape(rows_n, 8, drows)

    def cr_copy(k):
        return send(cp, cr.at[col], cr_sems.at[0, k], cr_sems.at[1, col], (row, (col + k) % cols_n))

    def cr_got(k):
        src = (col + k) % cols_n
        return send(cp, cr.at[src], cr_sems.at[0, k], cr_sems.at[1, src], (row, src))

    for k in range(1, cols_n):
        cr_copy(k).start()
    tick_b(14)
    left_finish(0)
    left_finish(1)
    for k in range(1, cols_n):
        cr_got(k).wait_recv()
        cr_copy(k).wait_send()
    cr[col] = cp[...]
    cp[...] = sum(cr[c] for c in range(cols_n))

    def cf_copy(k):
        to = (row + k) % rows_n
        return send(cp.at[to], cf.at[row], cf_sems.at[0, k], cf_sems.at[1, row], (to, col))

    def cf_got(k):
        src = (row + k) % rows_n
        return send(cp.at[src], cf.at[src], cf_sems.at[0, k], cf_sems.at[1, src], (src, col))

    for k in range(1, rows_n):
        cf_copy(k).start()
    cf[row] = cp[row]
    left_finish(2)
    for k in range(1, rows_n):
        cf_got(k).wait_recv()
    cond_value = cond[...]
    gate = 1.0 / (1.0 + jnp.exp(-cond_value))
    slope = gate * (1.0 + cond_value * (1.0 - gate))
    for r in range(rows_n):
        spot = slice(r * drows, (r + 1) * drows)
        o_cond[:, spot] = cf[r] * slope[:, spot]

    for s in range(3 * depth - SLOTS, 3 * depth):
        sent(s)
    for s in range(3 * depth - 2, 3 * depth):
        for y in range(2):
            c0(s, y).wait_send()
    for g in range(3):
        left_copy(g).wait_send()
    for k in range(1, cols_n):
        u_copy(k).wait_send()
    copy_v.wait_send()
    for k in range(1, rows_n):
        cf_copy(k).wait_send()
    for i in range(tokens // part):
        swap_lat(i).wait()
    swap_out.wait()


def backward(saved, out, lse, vec, act, ada, cond, collective_id):
    rows, cols = lax.axis_size("row"), lax.axis_size("col")
    depth = cols // 2
    tokens, width = out.shape
    heads, drows, hc6 = width // HEAD_DIM, ada.shape[0], ada.shape[1]
    hc, lanes, lrows = width // cols, 1152, drows // 2
    shape, dma, vm = jax.ShapeDtypeStruct, pltpu.SemaphoreType.DMA, pltpu.VMEM
    token = shape((tokens, width), bf16)
    outs = [token, token, shape((depth, tokens, 896), bf16), shape((drows, 576), f32), shape((drows, 576), f32),
            shape((drows, 3 * hc), f32), shape((drows, hc), f32), shape((drows, hc6), f32), shape((8, hc6), f32),
            shape((8, width), f32)]
    head = (tokens, HEAD_DIM)
    scratch = [
        vm((SLOTS, 2, drows, lanes), bf16), vm((2, 2, drows, lanes), bf16), vm((2, 2, drows, lanes), bf16),
        vm((4, 2, drows, 512), bf16), vm((4, 2, lrows, 128), bf16), vm((4, drows, 512), bf16), vm((4, lrows, 128), bf16),
        vm((2, 9, drows, 512), bf16), vm((2, 9, lrows, 128), bf16), vm((3, lrows, 128), f32), vm((3, lrows, 128), f32),
        vm((2, width, lanes), bf16), vm((2, tokens, lanes), bf16), vm((depth, tokens, lanes), bf16), vm((tokens, 896), bf16),
        vm((2, width, tokens), bf16), vm((2, tokens, width), bf16), vm((tokens, width), bf16), vm((tokens, width), f32),
        vm((tokens, width), f32), vm((tokens, 384), bf16), vm((5, 4) + head, bf16),
        vm((4,) + head, bf16), vm((4, 1, tokens), f32), vm((2, 4) + head, bf16), vm((2, 2, 4) + head, bf16), vm((3, 4) + head, f32),
        vm((16, width), f32), vm((2, tokens, 384), bf16),
        vm((cols, 8, hc6), f32), vm((cols, 8, hc6), f32), vm((cols, 8, hc6), f32), vm((cols, 8, hc6), f32), vm((rows, 8, hc6), f32),
        vm((rows, 8, drows), f32), vm((cols, rows, 8, drows), f32), vm((rows, 8, drows), f32)]
    scratch += [
        dma((1 + tokens // 128, 2)), dma((2, 2, 2)), dma((2, 4, 2, 2)), dma((2, 4, 2)), dma((2, 2, 9, depth, 2)), dma((2, 3)), dma((2,)), dma((2, 2)),
        dma((depth,)), dma((3,)), dma((5,)), dma((2, 2, 2, 4)), dma((depth,)), dma((2,)), dma((2, cols)), dma((2,)), dma((2, cols)),
        dma((2, rows)), dma((2,))]
    vmem = pl.BlockSpec(memory_space=pltpu.VMEM)
    return pl.pallas_call(
        backward_kernel,
        out_shape=outs,
        in_specs=[ANY] * 16 + [vmem] * 5,
        out_specs=[ANY] * 3 + [vmem] * 7,
        scratch_shapes=scratch,
        compiler_params=pltpu.CompilerParams(collective_id=collective_id, has_side_effects=True, vmem_limit_bytes=63 * 2**20),
        name="backward",
    )(*saved, out, lse, vec, act, ada, cond)


class Plan:
    def __init__(self, latents, condition, qkv_weight, fc1_weight):
        self.rows, self.cols = lax.axis_size("row"), lax.axis_size("col")
        self.tokens, self.width = latents.shape
        self.lats = condition.shape[0]
        self.depth_rows = qkv_weight.shape[0]
        self.head_cols = qkv_weight.shape[2]
        self.ff_cols = fc1_weight.shape[1]
        self.share = SEQ // self.tokens
        self.near = (
            self.rows == 4 and self.share == 2 and self.cols == 8 and self.lats == self.cols // 2
            and (self.depth_rows, self.head_cols, self.ff_cols) == (288, 2 * HEAD_DIM, 576) and self.width == 1152)


def fold(left):
    rows, lanes = left.shape
    return left.reshape(2, rows // 2, lanes).transpose(1, 0, 2).reshape(rows // 2, 2 * lanes)


def gather_plain(blocks):
    return [lax.all_gather(lax.all_gather(b, "row", axis=0, tiled=True), "col", axis=1, tiled=True) for b in blocks]


def scatter_plain(fulls):
    parts = [lax.psum_scatter(g, "row", scatter_dimension=0, tiled=True) for g in fulls]
    return [lax.psum_scatter(g, "col", scatter_dimension=1, tiled=True).astype(f32) for g in parts]


def attend_plain(q, k, v):
    def one(item):
        scores = nt(item[0], item[1]) * HEAD_DIM ** (-0.5)
        top = jnp.max(scores, axis=-1, keepdims=True)
        probs = jnp.exp(scores - top)
        total = jnp.sum(probs, axis=-1, keepdims=True)
        return nn((probs / total).astype(bf16), item[2]).astype(bf16), top + jnp.log(total)

    return lax.map(one, (q, k, v))


def attend_back_plain(q, k, v, lse, att_grad):
    def one(item):
        q, k, v, lse, out_grad = item
        probs = jnp.exp(nt(q, k) * HEAD_DIM ** (-0.5) - lse)
        probs_grad = nt(out_grad, v)
        inner = jnp.sum(probs * probs_grad, axis=-1, keepdims=True)
        grad = (probs * (probs_grad - inner) * HEAD_DIM ** (-0.5)).astype(bf16)
        return nn(grad, k), tn(grad, q), tn(probs.astype(bf16), out_grad)

    return lax.map(one, (q, k, v, lse, att_grad))


def gelu_and_slope(u):
    c = math.sqrt(2.0 / math.pi)
    inner = jnp.tanh(c * (u + 0.044715 * u * u * u))
    value = 0.5 * u * (1.0 + inner)
    slope = 0.5 * (1.0 + inner) + 0.5 * u * (1.0 - inner * inner) * c * (1.0 + 3 * 0.044715 * u * u)
    return value, slope


def layer_norm(values):
    mean = jnp.mean(values, axis=-1, keepdims=True)
    centred = values - mean
    inverse = lax.rsqrt(jnp.mean(centred * centred, axis=-1, keepdims=True) + norm_eps)
    return centred * inverse, inverse


def norm_back(rows_grad, normal, inverse, scale):
    normal_grad = rows_grad * (1.0 + scale)
    first = jnp.mean(normal_grad, axis=-1, keepdims=True)
    second = jnp.mean(normal_grad * normal, axis=-1, keepdims=True)
    value_grad = inverse * (normal_grad - first - normal * second)
    return value_grad, jnp.sum(rows_grad, axis=0), jnp.sum(rows_grad * normal, axis=0)


def shards_near(plan, latents, condition, ada_weight, ada_bias, qkv_weight, qv_bias, proj_weight, proj_bias,
                fc1_weight, fc1_bias, fc2_weight, fc2_bias, cotangent):
    depth, hc, fc = plan.depth_rows, plan.head_cols, plan.ff_cols
    q_main, p_main, f_main = 384, 128, 512
    qkv_flat = qkv_weight.reshape(depth, 3 * hc)
    proj_t, fc2_t = proj_weight.T, fc2_weight.T
    main_a = jnp.concatenate([qkv_flat[:, :q_main], proj_t[:, :p_main]], axis=1)
    left = jnp.concatenate([fold(jnp.concatenate([qkv_flat[:, q_main:], proj_t[:, p_main:]], axis=1)),
                            fold(fc1_weight[:, f_main:]), fold(fc2_t[:, f_main:])], axis=1)
    blocks = [main_a, left, fc1_weight[:, :f_main], fc2_t[:, :f_main]]
    cond = jnp.pad(condition.astype(f32), ((0, 8 - plan.lats), (0, 0)))
    ada = ada_weight.reshape(depth, 6 * hc)
    flat = lax.optimization_barrier(jnp.concatenate([fc1_bias, proj_bias, fc2_bias, qv_bias.reshape(-1)]).astype(f32))
    line = flat[:6 * hc].reshape(1, 6 * hc)
    tail = jnp.pad(flat[6 * hc:].reshape(1, 2 * hc), ((0, 0), (0, 4 * hc)))
    bias = jnp.concatenate([jnp.broadcast_to(ada_bias.astype(f32).reshape(1, 6 * hc), (plan.lats, 6 * hc)), line, tail,
                            jnp.zeros((8 - plan.lats - 2, 6 * hc), f32)], axis=0)
    (w, dy, x, n1, q, k, v, k2, v2, lse, att, ba, mid, n2, hid, slo, out, vec, act) = forward(
        latents, cotangent, cond, ada, bias, blocks, 0)
    output, lat_grad, _, fc2_sum, fc1_sum, qkv_sum, proj_sum, ada_sum, rows, cond_grad = backward(
        (w, dy, x, n1, q, k, v, k2, v2, att, ba, mid, n2, hid, slo), out, lse, vec, act, ada, cond, 1)
    return (
        output, lat_grad.astype(f32), cond_grad[:plan.lats], ada_sum.reshape(depth, 6, hc), rows[0].reshape(6, hc),
        qkv_sum.reshape(depth, 3, hc), rows[2, :2 * hc].reshape(2, hc), proj_sum.T, rows[1, fc:fc + hc],
        fc1_sum, rows[1, :fc], fc2_sum.T, rows[1, fc + hc:])


def shards(latents, condition, ada_weight, ada_bias, qkv_weight, qv_bias, proj_weight, proj_bias,
           fc1_weight, fc1_bias, fc2_weight, fc2_bias, cotangent):
    plan = Plan(latents, condition, qkv_weight, fc1_weight)
    if plan.near:
        return shards_near(plan, latents, condition, ada_weight, ada_bias, qkv_weight, qv_bias, proj_weight, proj_bias,
                           fc1_weight, fc1_bias, fc2_weight, fc2_bias, cotangent)
    row, col = lax.axis_index("row"), lax.axis_index("col")
    rows, cols, width, tokens = plan.rows, plan.cols, plan.width, plan.tokens
    depth, hc, fc = plan.depth_rows, plan.head_cols, plan.ff_cols
    heads = cols * hc // HEAD_DIM
    groups = rows * plan.lats

    blocks = [qkv_weight.reshape(depth, 3 * hc), proj_weight.T, fc1_weight, fc2_weight.T]
    qkv_w, proj_w, fc1_w, fc2_w = gather_plain(blocks)
    home = row * plan.lats + col // plan.share
    values, grad_out = latents.astype(f32), cotangent.astype(f32)

    cond_all = lax.all_gather(condition, "row", axis=0, tiled=True).astype(f32)
    cond_act = jax.nn.silu(cond_all).astype(bf16)
    cond_mine = lax.dynamic_slice(cond_act, (0, row * depth), (groups, depth))
    ada_flat = ada_weight.reshape(depth, 6 * hc)
    partial = lax.psum(nn(cond_mine, ada_flat), "row") + ada_bias.astype(f32).reshape(1, 6 * hc)
    small = jnp.concatenate(
        [partial.reshape(-1)] + [b.astype(f32).reshape(-1) for b in (proj_bias, fc2_bias, fc1_bias, qv_bias)])
    small = lax.all_gather(small, "col", axis=0, tiled=False)
    sizes = [groups * 6 * hc, hc, hc, fc, 2 * hc]
    mod_all, proj_b, fc2_b, fc1_b, qv_b = jnp.split(small, [sum(sizes[:i + 1]) for i in range(4)], axis=1)
    mod = lax.dynamic_index_in_dim(mod_all.reshape(cols, groups, 6, hc), home, 1, keepdims=False)
    mod = mod.transpose(1, 0, 2).reshape(6, 1, width)
    shift_one, scale_one, gate_one, shift_two, scale_two, gate_two = (mod[k] for k in range(6))
    proj_b, fc2_b, fc1_b = proj_b.reshape(width), fc2_b.reshape(width), fc1_b.reshape(-1)
    q_b, v_b = qv_b[:, :hc].reshape(heads, 1, HEAD_DIM), qv_b[:, hc:].reshape(heads, 1, HEAD_DIM)

    def to_heads(flat):
        return flat.reshape(tokens, heads, HEAD_DIM).transpose(1, 0, 2)

    def from_heads(value):
        return value.transpose(1, 0, 2).reshape(tokens, cols, hc)

    normal_one, inverse_one = layer_norm(values)
    normed_one = (normal_one * (1.0 + scale_one) + shift_one).astype(bf16)
    projected = nn(normed_one, qkv_w).reshape(tokens, cols, 3 * hc)
    query = (to_heads(projected[:, :, :hc]) + q_b).astype(bf16)
    key = to_heads(projected[:, :, hc:2 * hc]).astype(bf16)
    value = (to_heads(projected[:, :, 2 * hc:]) + v_b).astype(bf16)
    cuts = [[s * plan.share + i for i in range(plan.share)] for s in range(cols // plan.share)]
    key_all = lax.all_gather(key, "col", axis=1, tiled=True, axis_index_groups=cuts)
    value_all = lax.all_gather(value, "col", axis=1, tiled=True, axis_index_groups=cuts)
    att, lse = attend_plain(query, key_all, value_all)
    att_flat = from_heads(att).reshape(tokens, width)
    branch_a = nt(att_flat, proj_w) + proj_b
    middle = values + gate_one * branch_a

    normal_two, inverse_two = layer_norm(middle)
    normed_two = (normal_two * (1.0 + scale_two) + shift_two).astype(bf16)
    hidden, slope = gelu_and_slope(nn(normed_two, fc1_w) + fc1_b)
    hidden = hidden.astype(bf16)
    branch_m = nt(hidden, fc2_w) + fc2_b
    output = (middle + gate_two * branch_m).astype(bf16)

    gate_two_grad = jnp.sum(grad_out * branch_m, axis=0)
    m_grad = grad_out * gate_two
    fc2_bias_part = jnp.sum(m_grad, axis=0)
    m_low = m_grad.astype(bf16)
    fc2_grad = tn(m_low, hidden).astype(bf16)
    pre_grad = nn(m_low, fc2_w) * slope
    fc1_bias_part = jnp.sum(pre_grad, axis=0)
    pre_low = pre_grad.astype(bf16)
    fc1_grad = tn(normed_two, pre_low).astype(bf16)
    normed_two_grad = nt(pre_low, fc1_w)
    middle_part, shift_two_grad, scale_two_grad = norm_back(normed_two_grad, normal_two, inverse_two, scale_two)
    middle_grad = grad_out + middle_part
    gate_one_grad = jnp.sum(middle_grad * branch_a, axis=0)
    a_grad = middle_grad * gate_one
    proj_bias_part = jnp.sum(a_grad, axis=0)
    a_low = a_grad.astype(bf16)
    proj_grad = tn(a_low, att_flat).astype(bf16)
    att_grad = to_heads(nn(a_low, proj_w).astype(bf16))
    query_grad, key_grad, value_grad = attend_back_plain(query, key_all, value_all, lse, att_grad)
    key_grad, value_grad = (
        lax.psum_scatter(g.astype(bf16), "col", scatter_dimension=1, tiled=True, axis_index_groups=cuts).astype(f32)
        for g in (key_grad, value_grad))
    q_bias_part, v_bias_part = jnp.sum(query_grad, axis=1), jnp.sum(value_grad, axis=1)
    qkv_low = jnp.concatenate([from_heads(g.astype(bf16)) for g in (query_grad, key_grad, value_grad)], axis=2)
    qkv_low = qkv_low.reshape(tokens, 3 * width)
    qkv_grad = tn(normed_one, qkv_low).astype(bf16)
    normed_one_grad = nt(qkv_low, qkv_w)
    fc2_sum, fc1_sum, qkv_sum, proj_sum = scatter_plain([fc2_grad, fc1_grad, qkv_grad, proj_grad])
    input_part, shift_one_grad, scale_one_grad = norm_back(normed_one_grad, normal_one, inverse_one, scale_one)
    latents_grad = middle_grad + input_part

    mod_grad = jnp.stack(
        [shift_one_grad, scale_one_grad, gate_one_grad, shift_two_grad, scale_two_grad, gate_two_grad], axis=0)
    mod_grad = lax.all_gather(mod_grad, ("row", "col"), axis=0, tiled=False)
    mod_grad = mod_grad.reshape(groups, plan.share, 6, width).sum(axis=1)
    mod_mine = lax.dynamic_slice(mod_grad, (0, 0, col * hc), (groups, 6, hc))
    ada_bsum = jnp.sum(mod_mine, axis=0)
    mod_low = mod_mine.astype(bf16).reshape(groups, 6 * hc)
    ada_wsum = tn(cond_mine, mod_low).reshape(depth, 6, hc)
    cond_part = lax.dynamic_update_slice(jnp.zeros((groups, width), f32), nt(mod_low, ada_flat), (0, row * depth))
    parts = [cond_part, proj_bias_part, fc2_bias_part, q_bias_part, v_bias_part, fc1_bias_part]
    totals = lax.psum(jnp.concatenate([part.reshape(-1) for part in parts]), ("row", "col"))
    ends, spot = [], 0
    for part in parts:
        ends.append(totals[spot:spot + part.size])
        spot += part.size

    def mine(flat):
        size = flat.size // cols
        return lax.dynamic_slice(flat, (col * size,), (size,))

    cond_summed = lax.dynamic_slice(ends[0].reshape(groups, width), (row * plan.lats, 0), (plan.lats, width))
    silu_value, silu_pull = jax.vjp(jax.nn.silu, condition.astype(f32))
    condition_grad = silu_pull(cond_summed)[0]
    qv_bsum = jnp.stack([mine(ends[3]), mine(ends[4])], axis=0)
    return (
        output, latents_grad, condition_grad, ada_wsum, ada_bsum, qkv_sum.reshape(depth, 3, hc), qv_bsum,
        proj_sum.T, mine(ends[1]), fc1_sum, mine(ends[5]), fc2_sum.T, mine(ends[2]))


def solution(mesh):
    token, grid, turned = P(("row", "col"), None), P("row", "col"), P("col", "row")
    cube, wide, flat = P("row", None, "col"), P(None, "col"), P("col")
    return jax.shard_map(
        shards,
        mesh=mesh,
        in_specs=(token, P("row", None), cube, wide, cube, wide, turned, flat, grid, flat, turned, flat, token),
        out_specs=(token, token, P("row", None), cube, wide, cube, wide, turned, flat, grid, flat, turned, flat),
        check_vma=False,
    )
```
